32 devices in a mesh: dp: 16 (over z, x, core), mp: 2 (over y).
Axes of the slice: x: 2, y: 2, z: 4, core: 2. Of those that a mesh axis runs over, the one named last changes fastest.
Arguments:
- tokens: bfloat16 [4096, 2048], P('dp', 'mp'), may hold values from -6 to 6
- gain_rnn: bfloat16 [2048], replicated, may hold values from 0.5 to 1.5
- rnn_in: bfloat16 [2048, 2, 2816], P('dp', None, 'mp'), may hold values from -0.125 to 0.125
- gate_recur: bfloat16 [16, 176, 176], P('mp'), may hold values from -0.4375 to 0.4375
- gate_input: bfloat16 [16, 176, 176], P('mp'), may hold values from -0.4375 to 0.4375
- bias_recur: float32 [2816], P('mp'), may hold values from -3 to 3
- bias_input: float32 [2816], P('mp'), may hold values from -3 to 3
- decay_param: float32 [2816], P('mp'), may hold values from -1 to 7
- conv_weight: float32 [4, 2816], P(None, 'mp'), may hold values from -3 to 3
- conv_bias: float32 [2816], P('mp'), may hold values from -2 to 2
- rnn_out: bfloat16 [2048, 2816], P('dp', 'mp'), may hold values from -0.4375 to 0.4375
- gain_mlp: bfloat16 [2048], replicated, may hold values from 0.5 to 1.5
- mlp_in: bfloat16 [2048, 2, 6144], P('dp', None, 'mp'), may hold values from -0.125 to 0.125
- mlp_out: bfloat16 [2048, 6144], P('dp', 'mp'), may hold values from -0.15625 to 0.15625
- lengths: int32 [16, 4], P('dp'), may hold values from 1 to 153, 256 in all within a row
- out_grad: bfloat16 [4096, 2048], P('dp', 'mp'), may hold values from -6 to 6
Outputs:
- layer_output: bfloat16 [4096, 2048], P('dp', 'mp')
- tokens_grad: bfloat16 [4096, 2048], P('dp', 'mp')
- gain_rnn_grad: float32 [2048], P('mp')
- rnn_in_grad: float32 [2048, 2, 2816], P('dp', None, 'mp')
- gate_recur_grad: float32 [16, 176, 176], P('mp')
- gate_input_grad: float32 [16, 176, 176], P('mp')
- bias_recur_grad: float32 [2816], P('mp')
- bias_input_grad: float32 [2816], P('mp')
- decay_param_grad: float32 [2816], P('mp')
- conv_weight_grad: float32 [4, 2816], P(None, 'mp')
- conv_bias_grad: float32 [2816], P('mp')
- rnn_out_grad: float32 [2048, 2816], P('dp', 'mp')
- gain_mlp_grad: float32 [2048], P('mp')
- mlp_in_grad: float32 [2048, 2, 6144], P('dp', None, 'mp')
- mlp_out_grad: float32 [2048, 6144], P('dp', 'mp')
The draws below stay inside these ranges and needn't reach their ends.
Inputs may be any that keep to these rules, and one draw needn't show every extreme that they name: `lengths`: row b lists the pieces of buffer b in order: 3 sequences, then the padding at the buffer's end; together they fill all 256 slots, and every row has a piece of exactly 153.
All inputs are finite; a program needn't handle non-finite values.
Results may differ from the reference program's by a relative error of at most 0.012.
Values may be sent and summed in bfloat16 or wider, within the bound.
A program may use at most 256 MiB of HBM per device.

```python
import math
import jax
import jax.numpy as jnp
import numpy as np
from jax import lax

D = 2048
HEADS = 16
HEAD_W = 176
FF = 6144
CONV = 4
TOK_DEV = 256
SEGS = 4
RNN = 2816
MOST_LEN = 153
BUFFERS = 16
TOKENS = 4096


def with_spikes(values, key, source, target, blocks, factor):
    owner, partner = [(jnp.arange(values.shape[axis_at]) // (values.shape[axis_at] // blocks)).reshape([-1 if axis == axis_at else 1 for axis in range(values.ndim)]) for axis_at in (source, target)]
    chosen = jax.random.permutation(key, blocks)[partner]
    strong = (owner == chosen) | (owner == (partner + blocks // 2) % blocks)
    return jnp.where(strong, factor * values, values)


def block_scale(stream_key, shape, cuts, least, largest):
    gain, own = 1.0, jax.random.fold_in(stream_key, 6)
    for position, shards_of in cuts:
        steps = jnp.exp(jax.random.uniform(jax.random.fold_in(own, position), (shards_of,), jnp.float32, least / len(cuts), largest / len(cuts)))
        gain = gain * jnp.repeat(steps, shape[position] // shards_of).reshape([-1 if axis == position else 1 for axis in range(len(shape))])
    return gain


def profile(amount, total, most, slope):
    portions = [(1 << 20) // math.isqrt(standing ** slope) + 1 for standing in range(2, amount + 1)]
    spare, holding = total - most - (amount - 1), [1] * (amount - 1)
    while spare > 0:
        free = [i for i in range(amount - 1) if holding[i] < most]
        mass, left = sum([portions[i] for i in free]), spare
        for i in free:
            extra = min(most - holding[i], max(1, left * portions[i] // mass), spare)
            holding[i] = holding[i] + extra
            spare = spare - extra
    return np.array([most] + holding)


def uneven(rng, number_of, total, limit, slope):
    if number_of == 2:
        one = jax.random.randint(rng, (), max(1, total - limit), min(limit, total - 1) + 1)
        return jnp.stack([one, total - one])
    tallies = jnp.asarray(profile(number_of, total, limit, slope), jnp.int32)
    pairs = (number_of - 1) // 2
    giver, receiver = tallies[1:1 + 2 * pairs:2], tallies[2:2 + 2 * pairs:2]
    room = jnp.minimum(giver - 1, limit - receiver)
    moved = jax.random.randint(jax.random.fold_in(rng, 1), (pairs,), 0, 1 << 20) % (room + 1)
    tallies = tallies.at[1:1 + 2 * pairs:2].set(giver - moved).at[2:2 + 2 * pairs:2].set(receiver + moved)
    return tallies[jax.random.permutation(jax.random.fold_in(rng, 2), number_of)]


def noise(stream_key, dims, spread, most, split=(), held_as=jnp.bfloat16):
    values = spread * jax.random.normal(stream_key, dims, jnp.float32)
    if split:
        values = values * block_scale(stream_key, dims, split, -0.22, 0.18)
    return jnp.clip(values, -most, most).astype(held_as)


def gaussian_with(key, extent, deviation, reach, pieces, heavy, kind=jnp.bfloat16):
    values = deviation * jax.random.normal(key, extent, jnp.float32)
    if pieces:
        values = values * block_scale(key, extent, pieces, -0.22, 0.18)
    return jnp.clip(with_spikes(values, jax.random.fold_in(key, 3), *heavy), -reach, reach).astype(kind)


def setup_inputs(seed: int = 0) -> dict:
    keys = jax.random.split(jax.random.key(seed), 17)
    return {
        "tokens": gaussian_with(keys[0], (TOKENS, D), 1.0, 6.0, ((0, 16), (1, 2)), (0, 1, 16, 2.0)),
        "gain_rnn": jnp.clip(1.0 + 0.1 * jax.random.normal(keys[1], (D,), jnp.float32), 0.5, 1.5).astype(jnp.bfloat16),
        "rnn_in": noise(keys[2], (D, 2, RNN), D ** -0.5, 0.125, ((0, 16), (2, 2))),
        "gate_recur": noise(keys[3], (HEADS, HEAD_W, HEAD_W), HEAD_W ** -0.5, 0.4375, ((0, 2),)),
        "gate_input": noise(keys[4], (HEADS, HEAD_W, HEAD_W), HEAD_W ** -0.5, 0.4375, ((0, 2),)),
        "bias_recur": noise(keys[5], (RNN,), 0.5, 3.0, ((0, 2),), jnp.float32),
        "bias_input": noise(keys[6], (RNN,), 0.5, 3.0, ((0, 2),), jnp.float32),
        "decay_param": jnp.clip(-1.0 + 8.0 * jax.random.uniform(keys[7], (RNN,), jnp.float32) ** block_scale(keys[7], (RNN,), ((0, 2),), -0.2, 0.2), -1.0, 7.0),
        "conv_weight": noise(keys[8], (CONV, RNN), CONV ** -0.5, 3.0, ((1, 2),), jnp.float32),
        "conv_bias": noise(keys[9], (RNN,), 0.3, 2.0, ((0, 2),), jnp.float32),
        "rnn_out": noise(keys[10], (D, RNN), (RNN // 16) ** -0.5, 0.4375, ((0, 16), (1, 2))),
        "gain_mlp": jnp.clip(1.0 + 0.1 * jax.random.normal(keys[11], (D,), jnp.float32), 0.5, 1.5).astype(jnp.bfloat16),
        "mlp_in": noise(keys[12], (D, 2, FF), D ** -0.5, 0.125, ((0, 16), (2, 2))),
        "mlp_out": noise(keys[13], (D, FF), (FF // 4) ** -0.5, 0.15625, ((0, 16), (1, 2))),
        "lengths": jax.vmap(lambda own: uneven(own, SEGS, TOK_DEV, MOST_LEN, 2))(jax.random.split(keys[14], BUFFERS)).reshape((BUFFERS, SEGS)).astype(jnp.int32),
        "out_grad": gaussian_with(keys[15], (TOKENS, D), 1.0, 6.0, ((0, 16), (1, 2)), (0, 1, 16, 2.0)),
    }


@jax.custom_vjp
def low(v):
    return lax.optimization_barrier(v.astype(jnp.bfloat16)).astype(jnp.float32)

@jax.custom_vjp
def low_back(v):
    return v

def low_keep(v):
    return (low(v), None)

def low_pass(kept, grad):
    return (grad,)

def back_keep(v):
    return (v, None)

def back_low(kept, grad):
    return (low(grad),)
low.defvjp(low_keep, low_pass)
low_back.defvjp(back_keep, back_low)
norm_eps = 1e-06
root_eps = 0.001
highest = lax.Precision.HIGHEST

def segment_info(length_row, length_total):
    ends = jnp.cumsum(length_row).astype(jnp.int32)
    starts = (ends - length_row).astype(jnp.int32)
    places = jnp.arange(length_total, dtype=jnp.int32)
    inside = (places[:, None] >= starts[None, :]) & (places[:, None] < ends[None, :])
    first_place = lax.optimization_barrier(jnp.sum(jnp.where(inside, starts[None, :], 0), axis=1)).astype(jnp.int32)
    live_mask = (places < ends[-2]).astype(jnp.float32)[:, None]
    keep_mask = (places != first_place).astype(jnp.float32)[:, None]
    return (places, first_place, live_mask, keep_mask)

def rms_scale(values):
    return lax.rsqrt(lax.optimization_barrier(jnp.mean(values * values, axis=1, keepdims=True)) + norm_eps)

def combine(earlier, later):
    return (earlier[0] * later[0], later[0] * earlier[1] + later[1])

def conv_causal(inner_branch, conv_weight, conv_bias, places, first_place):
    channels = inner_branch.shape[1]
    conv_out = conv_bias + conv_weight[0] * inner_branch
    for offset in range(1, CONV):
        moved = jnp.concatenate([jnp.zeros((offset, channels), jnp.float32), inner_branch[:-offset]], axis=0)
        valid = (places - offset >= first_place).astype(jnp.float32)[:, None]
        conv_out = conv_out + conv_weight[offset] * moved * valid
    return conv_out

def layer(block, params, length_row):
    gain_rnn, rnn_in, gate_recur, gate_input, bias_recur, bias_input, decay_param, conv_weight, conv_bias, rnn_out, gain_mlp, mlp_in, mlp_out = params
    places, first_place, live_mask, keep_mask = segment_info(length_row, TOK_DEV)
    normed = low(block * rms_scale(block) * gain_rnn)
    both_proj = low_back(jnp.einsum('td,dkr->tkr', normed, rnn_in, precision=highest))
    inner_branch = both_proj[:, 0]
    gate_value = jax.nn.gelu(both_proj[:, 1])
    conv_out = conv_causal(inner_branch, conv_weight, conv_bias, places, first_place)
    heads_in = low(conv_out).reshape(TOK_DEV, HEADS, HEAD_W)
    pre_recur = low_back(jnp.einsum('thi,hij->thj', heads_in, gate_recur, precision=highest)).reshape(TOK_DEV, RNN) + bias_recur
    pre_input = low_back(jnp.einsum('thi,hij->thj', heads_in, gate_input, precision=highest)).reshape(TOK_DEV, RNN) + bias_input
    rate_gate = jax.nn.sigmoid(pre_recur)
    input_gate = jax.nn.sigmoid(pre_input)
    decay_step = jnp.exp(-8.0 * rate_gate * jax.nn.softplus(-decay_param))
    root_scale = jnp.sqrt(1.0 - decay_step * decay_step + root_eps)
    push_term = root_scale * input_gate * conv_out
    hidden_state = lax.associative_scan(combine, (decay_step * keep_mask, push_term), axis=0)[1]
    mixed_low = low(hidden_state * gate_value)
    branch = low_back(jnp.dot(mixed_low, rnn_out.T, precision=highest))
    middle = block + branch
    middle_low = low(middle)
    normed_two = low(middle_low * rms_scale(middle_low) * gain_mlp)
    pair_proj = low_back(jnp.einsum('td,dkf->tkf', normed_two, mlp_in, precision=highest))
    activation = low(jax.nn.gelu(pair_proj[:, 0]) * pair_proj[:, 1])
    branch_two = low_back(jnp.dot(activation, mlp_out.T, precision=highest))
    return live_mask * (middle + branch_two)

def widen(argument):
    return argument.astype(jnp.float32)

def reference(tokens, gain_rnn, rnn_in, gate_recur, gate_input, bias_recur, bias_input, decay_param, conv_weight, conv_bias, rnn_out, gain_mlp, mlp_in, mlp_out, lengths, out_grad):
    params = (widen(gain_rnn), widen(rnn_in), widen(gate_recur), widen(gate_input), widen(bias_recur), widen(bias_input), widen(decay_param), widen(conv_weight), widen(conv_bias), widen(rnn_out), widen(gain_mlp), widen(mlp_in), widen(mlp_out))
    blocks = widen(tokens).reshape(BUFFERS, TOK_DEV, D)

    def forward(blocks_in, params_in):

        def one_buffer(entries):
            return layer(entries[0], params_in, entries[1])
        return lax.map(jax.checkpoint(one_buffer), (blocks_in, lengths))
    result, pullback = jax.vjp(forward, blocks, params)
    grad_blocks, grad_params = pullback(widen(out_grad).reshape(BUFFERS, TOK_DEV, D))
    layer_output = result.reshape(TOKENS, D).astype(jnp.bfloat16)
    tokens_grad = grad_blocks.reshape(TOKENS, D).astype(jnp.bfloat16)
    return (layer_output, tokens_grad, grad_params[0], grad_params[1], grad_params[2], grad_params[3], grad_params[4], grad_params[5], grad_params[6], grad_params[7], grad_params[8], grad_params[9], grad_params[10], grad_params[11], grad_params[12])
```

```python
import functools

import jax
import jax.numpy as jnp
from jax import lax
from jax.experimental import pallas as pl
from jax.experimental.pallas import tpu as pltpu
from jax.sharding import PartitionSpec as P

norm_eps = 1e-06
root_eps = 0.001
bf16 = jnp.bfloat16
f32 = jnp.float32
contract_cols = (((1,), (1,)), ((), ()))
contract_rows = (((0,), (0,)), ((), ()))
gelu_scale = 0.7978845608028654
gelu_cubic = 0.044715
held_buffers = 4
scan_unroll = 8
lanes = 128


def pairs(n_dp, move):
    found = []
    for i in range(n_dp):
        target = move((i // 4) % 4, (i // 2) % 2, i % 2)
        if target is not None:
            z, x, c = target
            found.append((i, i // 16 * 16 + z * 4 + x * 2 + c))
    return found


def gelu_parts(v):
    tanh_value = jnp.tanh(gelu_scale * (v + gelu_cubic * v * v * v))
    value = 0.5 * v * (1.0 + tanh_value)
    slope = 0.5 * (1.0 + tanh_value) + 0.5 * v * (1.0 - tanh_value * tanh_value) * (
        gelu_scale * (1.0 + 3.0 * gelu_cubic * v * v)
    )
    return value, slope


def shifted(value, offset):
    return pltpu.roll(value, offset % value.shape[0], 0)


def store_lanes(ref, at, value):
    chunks = ref.shape[0]
    spare = chunks * lanes - value.shape[1]
    if spare:
        value = jnp.concatenate([value, jnp.zeros((value.shape[0], spare), f32)], axis=1)
    for i in range(chunks):
        ref[i, at, :] = value[:, i * lanes : (i + 1) * lanes]


def load_lanes(ref, at, width):
    return jnp.concatenate([ref[i, at, :] for i in range(ref.shape[0])], axis=1)[:, :width]


def scan_rows(coef_ref, push_ref, rows, reverse):
    chunks = coef_ref.shape[0]

    def step(i, carried):
        carried = list(carried)
        for j in range(scan_unroll):
            t = i * scan_unroll + j
            at = pl.ds(rows - 1 - t if reverse else t, held_buffers, stride=rows)
            for k in range(chunks):
                if reverse:
                    value = push_ref[k, at, :] + carried[k]
                    carried[k] = coef_ref[k, at, :] * value
                else:
                    value = coef_ref[k, at, :] * carried[k] + push_ref[k, at, :]
                    carried[k] = value
                push_ref[k, at, :] = value
        return tuple(carried)

    start = tuple(jnp.zeros((held_buffers, lanes), f32) for _ in range(chunks))
    lax.fori_loop(0, rows // scan_unroll, step, start)


def recur_forward(
    both_ref, mask_ref, vec_ref, wr_ref, wi_ref,
    mixed_ref, state_ref, conv_ref, rate_ref, igate_ref,
    coef_ref, push_ref,
):
    width = state_ref.shape[1]
    rows = both_ref.shape[0] // held_buffers

    def gates(b, carry):
        at = pl.ds(b * rows, rows)
        inner = both_ref[at, :width]
        mask = mask_ref[at, :]
        conv = vec_ref[4:5, :] + vec_ref[0:1, :] * inner
        for k in range(1, 4):
            conv = conv + vec_ref[k : k + 1, :] * (shifted(inner, k) * mask[:, k : k + 1])
        conv_low = conv.astype(bf16)
        rate = jax.nn.sigmoid(
            jnp.dot(conv_low, wr_ref[...], preferred_element_type=f32) + vec_ref[5:6, :]
        )
        igate = jax.nn.sigmoid(
            jnp.dot(conv_low, wi_ref[...], preferred_element_type=f32) + vec_ref[6:7, :]
        )
        decay = jnp.exp(-8.0 * rate * vec_ref[7:8, :])
        root = jnp.sqrt(1.0 - decay * decay + root_eps)
        store_lanes(coef_ref, at, decay * mask[:, 0:1])
        store_lanes(push_ref, at, root * igate * conv)
        conv_ref[at, :] = conv
        rate_ref[at, :] = rate
        igate_ref[at, :] = igate
        return carry

    lax.fori_loop(0, held_buffers, gates, 0)

    scan_rows(coef_ref, push_ref, rows, False)

    def mix(b, carry):
        at = pl.ds(b * rows, rows)
        gate = gelu_parts(both_ref[at, width:])[0]
        state = load_lanes(push_ref, at, width)
        state_ref[at, :] = state
        mixed_ref[at, :] = (state * gate).astype(bf16)
        return carry

    lax.fori_loop(0, held_buffers, mix, 0)


def recur_backward(
    dmix_ref, both_ref, state_ref, conv_ref, rate_ref, igate_ref, mask_ref, vec_ref, wr_ref, wi_ref,
    dboth_ref, sums_ref, gr_ref, gi_ref,
    coef_ref, push_ref,
):
    width = state_ref.shape[1]
    rows = both_ref.shape[0] // held_buffers

    def first(b, carry):
        at = pl.ds(b * rows, rows)
        gate, slope = gelu_parts(both_ref[at, width:])
        d_mixed = dmix_ref[at, :]
        store_lanes(push_ref, at, d_mixed * gate)
        dboth_ref[at, width:] = (slope * d_mixed * state_ref[at, :]).astype(bf16)
        store_lanes(
            coef_ref, at, jnp.exp(-8.0 * rate_ref[at, :] * vec_ref[7:8, :]) * mask_ref[at, 0:1]
        )
        return carry

    lax.fori_loop(0, held_buffers, first, 0)

    scan_rows(coef_ref, push_ref, rows, True)
    sums_ref[...] = jnp.zeros_like(sums_ref)
    gr_ref[...] = jnp.zeros_like(gr_ref)
    gi_ref[...] = jnp.zeros_like(gi_ref)

    def add_sum(k, value):
        sums_ref[k : k + 1, :] += jnp.sum(value, axis=0, keepdims=True)

    def last(b, carry):
        at = pl.ds(b * rows, rows)
        inner = both_ref[at, :width]
        mask = mask_ref[at, :]
        keep = mask[:, 0:1]
        softened = vec_ref[7:8, :]
        rate, igate, conv = rate_ref[at, :], igate_ref[at, :], conv_ref[at, :]
        d_push = load_lanes(push_ref, at, width)
        decay = jnp.exp(-8.0 * rate * softened)
        square = 1.0 - decay * decay + root_eps
        root = jnp.sqrt(square)
        d_root = d_push * igate * conv
        d_igate = d_push * root * conv
        before = shifted(state_ref[at, :], 1) * keep
        d_decay = d_push * before - d_root * decay / root
        d_log = d_decay * decay
        slow = d_log * rate
        d_pre_recur = (-8.0 * softened) * slow * (1.0 - rate)
        d_pre_input = d_igate * igate * (1.0 - igate)
        add_sum(7, slow)
        add_sum(5, d_pre_recur)
        add_sum(6, d_pre_input)
        low_recur = d_pre_recur.astype(bf16)
        low_input = d_pre_input.astype(bf16)
        conv_low = conv.astype(bf16)
        gr_ref[...] += lax.dot_general(
            conv_low, low_recur, contract_rows, preferred_element_type=f32
        )
        gi_ref[...] += lax.dot_general(
            conv_low, low_input, contract_rows, preferred_element_type=f32
        )
        d_conv = d_push * root * igate
        d_conv = d_conv + lax.dot_general(
            low_recur, wr_ref[...], contract_cols, preferred_element_type=f32
        )
        d_conv = d_conv + lax.dot_general(
            low_input, wi_ref[...], contract_cols, preferred_element_type=f32
        )
        add_sum(4, d_conv)
        add_sum(0, d_conv * inner)
        d_inner = vec_ref[0:1, :] * d_conv
        for k in range(1, 4):
            kept = d_conv * mask[:, k : k + 1]
            add_sum(k, kept * shifted(inner, k))
            d_inner = d_inner + vec_ref[k : k + 1, :] * shifted(kept, -k)
        dboth_ref[at, :width] = d_inner.astype(bf16)
        return carry

    lax.fori_loop(0, held_buffers, last, 0)


def whole_vmem(count):
    return [pl.BlockSpec(memory_space=pltpu.VMEM)] * count


def run_recur_forward(both, mask, vectors, wr, wi):
    rows, width = both.shape[0], both.shape[1] // 2
    wide = jax.ShapeDtypeStruct((rows, width), f32)
    return pl.pallas_call(
        recur_forward,
        out_shape=(jax.ShapeDtypeStruct((rows, width), bf16), wide, wide, wide, wide),
        in_specs=whole_vmem(5),
        out_specs=whole_vmem(5),
        scratch_shapes=[pltpu.VMEM((pl.cdiv(width, lanes), rows, lanes), f32)] * 2,
        compiler_params=pltpu.CompilerParams(vmem_limit_bytes=56 * 2**20),
        cost_estimate=pl.CostEstimate(
            flops=4 * rows * width * width, bytes_accessed=rows * width * 30, transcendentals=rows * width * 5
        ),
        name="recur_forward",
    )(both, mask, vectors, wr, wi)


def run_recur_backward(d_mixed, both, state, conv, rate, igate, mask, vectors, wr, wi):
    rows, width = state.shape
    square = jax.ShapeDtypeStruct((width, width), f32)
    return pl.pallas_call(
        recur_backward,
        out_shape=(
            jax.ShapeDtypeStruct((rows, 2 * width), bf16),
            jax.ShapeDtypeStruct((8, width), f32),
            square,
            square,
        ),
        in_specs=whole_vmem(10),
        out_specs=whole_vmem(4),
        scratch_shapes=[pltpu.VMEM((pl.cdiv(width, lanes), rows, lanes), f32)] * 2,
        compiler_params=pltpu.CompilerParams(vmem_limit_bytes=56 * 2**20),
        cost_estimate=pl.CostEstimate(
            flops=8 * rows * width * width, bytes_accessed=rows * width * 40, transcendentals=rows * width * 5
        ),
        name="recur_backward",
    )(d_mixed, both, state, conv, rate, igate, mask, vectors, wr, wi)


def block_diagonal(blocks):
    count, size = blocks.shape[0], blocks.shape[1]
    rows = [
        jnp.pad(blocks[h], ((0, 0), (h * size, (count - 1 - h) * size))) for h in range(count)
    ]
    return jnp.concatenate(rows, axis=0)


def diagonal_blocks(square, count):
    size = square.shape[0] // count
    return jnp.stack(
        [square[h * size : (h + 1) * size, h * size : (h + 1) * size] for h in range(count)]
    )


def masks_of(lengths, rows):
    ends = jnp.cumsum(lengths, axis=1)
    starts = ends - lengths
    places = jnp.arange(rows, dtype=jnp.int32)[None, :, None]
    inside = (places >= starts[:, None, :]) & (places < ends[:, None, :])
    first_place = jnp.sum(jnp.where(inside, starts[:, None, :], 0), axis=2)
    places = places[:, :, 0]
    live = (places < ends[:, 2:3]).astype(f32)
    columns = [(places != first_place).astype(f32)]
    for k in range(1, 4):
        columns.append((places - k >= first_place).astype(f32))
    columns += [live] + [jnp.zeros_like(live)] * 3
    return jnp.stack(columns, axis=2).reshape(lengths.shape[0] * rows, 8), live


def local(
    n_dp,
    tokens,
    gain_rnn,
    rnn_in,
    gate_recur,
    gate_input,
    bias_recur,
    bias_input,
    decay_param,
    conv_weight,
    conv_bias,
    rnn_out,
    gain_mlp,
    mlp_in,
    mlp_out,
    lengths,
    out_grad,
):
    outer_count = n_dp // 16
    rows_here = rnn_in.shape[0]
    model = gain_rnn.shape[0]
    half_model = model // 2
    buffer_rows = tokens.shape[0]
    own_rows = 2 * buffer_rows
    index = lax.axis_index("dp")
    y = lax.axis_index("mp")
    c = index % 2
    x = (index // 2) % 2
    z = (index // 4) % 4
    outer = jnp.where(z < 2, 0, 3)
    far = 3 - z
    far_outer = 3 - outer
    worker = (z == 1) | (z == 2)

    def mover(move):
        table = pairs(n_dp, move)
        return lambda value: lax.ppermute(value, "dp", table)

    swap_c = mover(lambda z, x, c: (z, x, 1 - c))
    swap_x = mover(lambda z, x, c: (z, 1 - x, c))
    swap_x_work = mover(lambda z, x, c: (z, 1 - x, c) if z in (1, 2) else None)
    swap_x_ends = mover(lambda z, x, c: (z, 1 - x, c) if z in (0, 3) else None)
    inward = mover(lambda z, x, c: {0: (1, x, c), 3: (2, x, c)}.get(z))
    outward = mover(lambda z, x, c: {1: (0, x, c), 2: (3, x, c)}.get(z))
    across = mover(lambda z, x, c: {1: (2, x, c), 2: (1, x, c)}.get(z))

    def swap_y(value):
        return lax.ppermute(value, "mp", [(0, 1), (1, 0)])

    def pick_c(first, second):
        return jnp.where(c == 0, first, second)

    def pick_y(first, second):
        return jnp.where(y == 0, first, second)

    group_rows = outer_count * rows_here
    block_rows = 2 * group_rows

    def over_outer(value):
        if outer_count == 1:
            return value
        groups = [[w * 16 + i for w in range(outer_count)] for i in range(16)]
        return lax.all_gather(value, "dp", axis_index_groups=groups, axis=0, tiled=True)

    def offset_of(z_at, x_at):
        z_place = z_at ^ (2 * y) if outer_count == 1 else z_at
        return (z_place * 2 + x_at) * block_rows

    def gather_weight(first_quarter, second_quarter):
        first_quarter, second_quarter = over_outer(first_quarter), over_outer(second_quarter)
        arrived = swap_c(pick_c(second_quarter, first_quarter))
        own = pick_c(
            jnp.concatenate([first_quarter, arrived], axis=0),
            jnp.concatenate([arrived, second_quarter], axis=0),
        )
        own_x = swap_x(own)
        from_outer = inward(own)
        from_outer_x = inward(own_x)
        from_far = across(own)
        from_far_outer = across(from_outer)
        from_far_x = swap_x_work(from_far)
        from_far_outer_x = across(from_outer_x)
        whole = jnp.zeros((model, own.shape[1]), bf16)
        for piece, z_at, x_at in (
            (own, z, x),
            (own_x, z, 1 - x),
            (from_outer, outer, x),
            (from_outer_x, outer, 1 - x),
            (from_far, far, x),
            (from_far_x, far, 1 - x),
            (from_far_outer, far_outer, x),
            (from_far_outer_x, far_outer, 1 - x),
        ):
            whole = lax.dynamic_update_slice(whole, piece, (offset_of(z_at, x_at), 0))
        if outer_count > 1:
            whole = whole.reshape(16, outer_count, rows_here, -1).swapaxes(0, 1)
            whole = whole.reshape(model, -1)
            whole = pick_y(whole, jnp.roll(whole, half_model, axis=0))
        return whole

    def scatter_grad(partial):
        if outer_count > 1:
            partial = pick_y(partial, jnp.roll(partial, half_model, axis=0))
            partial = partial.reshape(outer_count, 16, rows_here, -1).swapaxes(0, 1)
            partial = partial.reshape(model, -1)

        def block(z_at, x_at):
            start = (offset_of(z_at, x_at), 0)
            return lax.dynamic_slice(partial, start, (block_rows, partial.shape[1])).astype(f32)

        def sum_x(z_at):
            return block(z_at, x) + swap_x_work(block(z_at, 1 - x).astype(bf16)).astype(f32)

        to_far_outer = across(sum_x(far_outer).astype(bf16)).astype(f32)
        to_far = across(sum_x(far).astype(bf16)).astype(f32)
        out_x = outward((block(outer, x) + to_far_outer).astype(bf16)).astype(f32)
        out_other = outward(block(outer, 1 - x).astype(bf16))
        worker_total = sum_x(z) + to_far
        end_total = out_x + swap_x_ends(out_other).astype(f32)
        total = jnp.where(worker, worker_total, end_total).astype(bf16)
        top, bottom = total[:group_rows], total[group_rows:]
        mine = pick_c(top, bottom)
        arrived = swap_c(pick_c(bottom, top))
        first, second = pick_c(mine, arrived).astype(f32), pick_c(arrived, mine).astype(f32)
        if outer_count > 1:
            groups = [[w * 16 + i for w in range(outer_count)] for i in range(16)]
            first, second = (
                lax.psum_scatter(
                    v, "dp", axis_index_groups=groups, scatter_dimension=0, tiled=True
                )
                for v in (first, second)
            )
        return first, second

    def whole_features(half_rows):
        return jnp.concatenate([half_rows, swap_y(half_rows)], axis=1)

    def all_rows(rows_value):
        return jnp.concatenate([rows_value, swap_c(rows_value)], axis=0)

    def sum_partials(product):
        theirs = product(slice(own_rows, 2 * own_rows)).astype(bf16)
        theirs = swap_c(theirs)
        mine = product(slice(0, own_rows)) + theirs.astype(f32)
        arrived = swap_y(mine[:, half_model:].astype(bf16))
        return mine[:, :half_model] + arrived.astype(f32)

    def relative(vector):
        first, second = vector[:half_model], vector[half_model:]
        return jnp.concatenate([pick_y(first, second), pick_y(second, first)])

    def scale_of(rows_value):
        return lax.rsqrt(jnp.mean(rows_value * rows_value, axis=1, keepdims=True) + norm_eps)

    def norm_back(source, scale_rows, gain, grad_rows):
        weighted = grad_rows * gain
        part = jnp.sum(weighted * source, axis=1, keepdims=True)
        inner_mean = (part + swap_y(part)) / model
        back_rows = scale_rows * weighted - source * (scale_rows * scale_rows * scale_rows) * inner_mean
        return back_rows, jnp.sum(grad_rows * source * scale_rows, axis=0)

    def quarters(value, axis):
        size = value.shape[axis] // 2
        return (
            lax.slice_in_dim(value, 0, size, axis=axis),
            lax.slice_in_dim(value, size, 2 * size, axis=axis),
        )

    def pair_quarters(weight):
        first, second = quarters(weight, 2)
        return tuple(jnp.concatenate([v[:, 0], v[:, 1]], axis=1) for v in (first, second))

    def quarter(value, axis=0):
        return pick_c(*quarters(value, axis))

    gain_one, gain_two = relative(gain_rnn.astype(f32)), relative(gain_mlp.astype(f32))
    tokens_two = jnp.concatenate([tokens, inward(tokens)], axis=0)
    lengths_two = jnp.concatenate([lengths, inward(lengths)], axis=0)
    mask, live = masks_of(jnp.concatenate([lengths_two, swap_c(lengths_two)], axis=0), buffer_rows)
    live = live.reshape(-1, 1)[:own_rows]

    rnn_in_all = gather_weight(*pair_quarters(rnn_in))
    source = whole_features(tokens_two).astype(f32)
    scale_one = scale_of(source)
    normed = all_rows((source * scale_one * gain_one).astype(bf16))
    rnn_out_all = gather_weight(*quarters(rnn_out, 1))
    mlp_in_all = gather_weight(*pair_quarters(mlp_in))
    mlp_out_all = gather_weight(*quarters(mlp_out, 1))
    grad_two = jnp.concatenate([out_grad, inward(out_grad)], axis=0)
    live_grad = live * grad_two.astype(f32)
    grad_low = all_rows(whole_features(live_grad.astype(bf16)))

    both = jnp.dot(normed, rnn_in_all, preferred_element_type=f32)
    softened = jax.nn.softplus(-quarter(decay_param))
    vectors = jnp.concatenate(
        [
            quarter(conv_weight, 1),
            jnp.stack([quarter(conv_bias), quarter(bias_recur), quarter(bias_input), softened]),
        ],
        axis=0,
    )
    heads = gate_recur.shape[0] // 2
    wr = block_diagonal(quarter(gate_recur))
    wi = block_diagonal(quarter(gate_input))
    mixed, state, conv, rate, igate = run_recur_forward(both, mask, vectors, wr, wi)
    branch = sum_partials(
        lambda at: lax.dot_general(
            mixed[at], rnn_out_all, contract_cols, preferred_element_type=f32
        )
    )
    middle = tokens_two.astype(f32) + branch
    middle_low = middle.astype(bf16)
    middle_all = whole_features(middle_low).astype(f32)
    scale_two = scale_of(middle_all)
    normed_two = all_rows((middle_all * scale_two * gain_two).astype(bf16))
    pair = jnp.dot(normed_two, mlp_in_all, preferred_element_type=f32)
    hidden = pair.shape[1] // 2
    gate_mlp, up = pair[:, :hidden], pair[:, hidden:]
    gate_mlp_value, gate_mlp_slope = gelu_parts(gate_mlp)
    act = (gate_mlp_value * up).astype(bf16)
    mlp_out_partial = lax.dot_general(grad_low, act, contract_rows, preferred_element_type=f32)
    mlp_out_grad = scatter_grad(mlp_out_partial.astype(bf16))
    d_act = jnp.dot(grad_low, mlp_out_all, preferred_element_type=f32)
    d_pair = jnp.concatenate(
        [(gate_mlp_slope * d_act * up).astype(bf16), (d_act * gate_mlp_value).astype(bf16)], axis=1
    )
    e_two = sum_partials(
        lambda at: lax.dot_general(
            d_pair[at], mlp_in_all, contract_cols, preferred_element_type=f32
        )
    )
    mlp_in_partial = lax.dot_general(normed_two, d_pair, contract_rows, preferred_element_type=f32)
    mlp_in_grad = scatter_grad(mlp_in_partial.astype(bf16))
    back_two, gain_two_term = norm_back(
        middle_low.astype(f32), scale_two, gain_two[:half_model], e_two
    )
    d_middle = live_grad + back_two
    d_branch = all_rows(whole_features(d_middle.astype(bf16)))
    d_mixed = jnp.dot(d_branch, rnn_out_all, preferred_element_type=f32)
    rnn_out_partial = lax.dot_general(d_branch, mixed, contract_rows, preferred_element_type=f32)
    rnn_out_grad = scatter_grad(rnn_out_partial.astype(bf16))
    branch_two = sum_partials(
        lambda at: lax.dot_general(act[at], mlp_out_all, contract_cols, preferred_element_type=f32)
    )
    output_two = (live * (middle + branch_two)).astype(bf16)

    d_both, sums, square_recur, square_input = run_recur_backward(
        d_mixed, both, state, conv, rate, igate, mask, vectors, wr, wi
    )
    rnn_in_partial = lax.dot_general(normed, d_both, contract_rows, preferred_element_type=f32)
    rnn_in_grad = scatter_grad(rnn_in_partial.astype(bf16))
    e_one = sum_partials(
        lambda at: lax.dot_general(
            d_both[at], rnn_in_all, contract_cols, preferred_element_type=f32
        )
    )
    back_one, gain_one_term = norm_back(
        tokens_two.astype(f32), scale_one, gain_one[:half_model], e_one
    )
    tokens_grad_two = (d_middle + back_one).astype(bf16)

    def settle(two):
        return jnp.where(worker, two[:buffer_rows], outward(two[buffer_rows:]))

    layer_output = settle(output_two)
    tokens_grad = settle(tokens_grad_two)

    def total(value, dtype=f32):
        value = jnp.where(worker, value, 0).astype(dtype)
        if outer_count > 1:
            groups = [[w * 16 + i for w in range(outer_count)] for i in range(16)]
            value = lax.psum(value, "dp", axis_index_groups=groups)
        value = value + swap_x(value)
        value = value + across(value)
        return jnp.where(worker, value, outward(value))

    def both_quarters(value, axis=0):
        arrived = swap_c(value)
        return pick_c(
            jnp.concatenate([value, arrived], axis=axis), jnp.concatenate([arrived, value], axis=axis)
        )

    sums = both_quarters(total(sums), 1)
    blocks = jnp.concatenate(
        [diagonal_blocks(square_recur, heads), diagonal_blocks(square_input, heads)], axis=2
    )
    blocks = both_quarters(total(blocks, bf16)).astype(f32)
    gains = total(jnp.stack([gain_one_term, gain_two_term]))
    gains = gains + swap_c(gains)
    size = gate_recur.shape[1]

    def pair_layout(halves):
        columns = halves[0].shape[1] // 2
        return jnp.stack(
            [
                jnp.concatenate([v[:, k * columns : (k + 1) * columns] for v in halves], axis=1)
                for k in range(2)
            ],
            axis=1,
        )

    return (
        layer_output,
        tokens_grad,
        gains[0],
        pair_layout(rnn_in_grad),
        blocks[:, :, :size],
        blocks[:, :, size:],
        sums[5],
        sums[6],
        8.0 * jax.nn.sigmoid(-decay_param) * sums[7],
        sums[:4],
        sums[4],
        jnp.concatenate(rnn_out_grad, axis=1),
        gains[1],
        pair_layout(mlp_in_grad),
        jnp.concatenate(mlp_out_grad, axis=1),
    )


def solution(mesh):
    return jax.shard_map(
        functools.partial(local, mesh.shape["dp"]),
        mesh=mesh,
        in_specs=(
            P("dp", "mp"),
            P(),
            P("dp", None, "mp"),
            P("mp", None, None),
            P("mp", None, None),
            P("mp"),
            P("mp"),
            P("mp"),
            P(None, "mp"),
            P("mp"),
            P("dp", "mp"),
            P(),
            P("dp", None, "mp"),
            P("dp", "mp"),
            P("dp", None),
            P("dp", "mp"),
        ),
        out_specs=(
            P("dp", "mp"),
            P("dp", "mp"),
            P("mp"),
            P("dp", None, "mp"),
            P("mp", None, None),
            P("mp", None, None),
            P("mp"),
            P("mp"),
            P("mp"),
            P(None, "mp"),
            P("mp"),
            P("dp", "mp"),
            P("mp"),
            P("dp", None, "mp"),
            P("dp", "mp"),
        ),
        check_vma=False,
    )
```

```python
import functools

import jax
import jax.numpy as jnp
from jax import lax
from jax.experimental import pallas as pl
from jax.experimental.pallas import tpu as pltpu
from jax.sharding import PartitionSpec as P

norm_eps = 1e-06
root_eps = 0.001
bf16 = jnp.bfloat16
f32 = jnp.float32
contract_cols = (((1,), (1,)), ((), ()))
contract_rows = (((0,), (0,)), ((), ()))
gelu_scale = 0.7978845608028654
gelu_cubic = 0.044715
held_buffers = 4
scan_unroll = 8
blocks = 8
chunk_rows = 256
lanes = 128
by_mesh = pl.DeviceIdType.MESH


def pairs(n_dp, move):
    count = n_dp // 16
    found = []
    for i in range(n_dp):
        w, c, x, z = i % count, i // count % 2, i // count // 2 % 2, i // count // 4
        target = move(z, x, c)
        if target is not None:
            z, x, c = target
            found.append((i, ((z * 2 + x) * 2 + c) * count + w))
    return found


def gelu_parts(v):
    tanh_value = jnp.tanh(gelu_scale * (v + gelu_cubic * v * v * v))
    value = 0.5 * v * (1.0 + tanh_value)
    slope = 0.5 * (1.0 + tanh_value) + 0.5 * v * (1.0 - tanh_value * tanh_value) * (
        gelu_scale * (1.0 + 3.0 * gelu_cubic * v * v)
    )
    return value, slope


def shifted(value, offset):
    return pltpu.roll(value, offset % value.shape[0], 0)


def store_lanes(ref, at, value):
    chunks = ref.shape[0]
    spare = chunks * lanes - value.shape[1]
    if spare:
        value = jnp.concatenate([value, jnp.zeros((value.shape[0], spare), f32)], axis=1)
    for i in range(chunks):
        ref[i, at, :] = value[:, i * lanes : (i + 1) * lanes]


def load_lanes(ref, at, width):
    return jnp.concatenate([ref[i, at, :] for i in range(ref.shape[0])], axis=1)[:, :width]


def scan_rows(coef_ref, push_ref, rows, reverse):
    chunks = coef_ref.shape[0]

    def step(i, carried):
        carried = list(carried)
        for j in range(scan_unroll):
            t = i * scan_unroll + j
            at = pl.ds(rows - 1 - t if reverse else t, held_buffers, stride=rows)
            for k in range(chunks):
                if reverse:
                    value = push_ref[k, at, :] + carried[k]
                    carried[k] = coef_ref[k, at, :] * value
                else:
                    value = coef_ref[k, at, :] * carried[k] + push_ref[k, at, :]
                    carried[k] = value
                push_ref[k, at, :] = value
        return tuple(carried)

    start = tuple(jnp.zeros((held_buffers, lanes), f32) for _ in range(chunks))
    lax.fori_loop(0, rows // scan_unroll, step, start)


def columns_at(cols_ref, b, size):
    return pl.ds(pl.multiple_of(cols_ref[b], size), size)


def gathered(ref, at, cols_ref, size):
    return jnp.concatenate([ref[at, columns_at(cols_ref, b, size)] for b in range(blocks)], axis=1)


def stacked(refs, columns=slice(None)):
    return jnp.concatenate([ref[:, columns] for ref in refs], axis=0)


def project(mine_ref, theirs_ref, weight_refs, cols_ref, use):
    size = weight_refs[0].shape[0]
    own = mine_ref.shape[0]
    for part, ref in enumerate((mine_ref, theirs_ref)):

        def chunk(i, carry, part=part, ref=ref):
            at = pl.ds(pl.multiple_of(i * chunk_rows, chunk_rows), chunk_rows)
            rows = gathered(ref, at, cols_ref, size)
            use(
                pl.multiple_of(part * own + i * chunk_rows, chunk_rows),
                jnp.dot(rows, stacked(weight_refs), preferred_element_type=f32),
            )
            return carry

        lax.fori_loop(0, own // chunk_rows, chunk, 0)


def columns_at(cols, b, size):
    return pl.ds(pl.multiple_of(cols[b], size), size)


def gathered(ref, at, cols, size):
    return jnp.concatenate([ref[at, columns_at(cols, b, size)] for b in range(blocks)], axis=1)


def stacked(weight_ref):
    return weight_ref[...].reshape(-1, weight_ref.shape[2])


def project(mine_ref, theirs_ref, weight_ref, cols, use):
    size = weight_ref.shape[1]
    own = mine_ref.shape[0]
    for part, ref in enumerate((mine_ref, theirs_ref)):

        def chunk(i, carry, part=part, ref=ref):
            at = pl.ds(pl.multiple_of(i * chunk_rows, chunk_rows), chunk_rows)
            rows = gathered(ref, at, cols, size)
            use(
                pl.multiple_of(part * own + i * chunk_rows, chunk_rows),
                jnp.dot(rows, stacked(weight_ref), preferred_element_type=f32),
            )
            return carry

        lax.fori_loop(0, own // chunk_rows, chunk, 0)


def buffer_rows_at(b, rows):
    return pl.ds(pl.multiple_of(b * rows, rows), rows)


def conv_of(inner, mask, vec_ref):
    conv = vec_ref[4:5, :] + vec_ref[0:1, :] * inner
    for k in range(1, 4):
        conv = conv + vec_ref[k : k + 1, :] * (shifted(inner, k) * mask[:, k : k + 1])
    return conv


def gates_of(conv_low, vec_ref, wr_ref, wi_ref):
    rate = jax.nn.sigmoid(
        jnp.dot(conv_low, wr_ref[...], preferred_element_type=f32) + vec_ref[5:6, :]
    )
    igate = jax.nn.sigmoid(
        jnp.dot(conv_low, wi_ref[...], preferred_element_type=f32) + vec_ref[6:7, :]
    )
    return rate, igate


def recur_state(both_ref, mask_ref, vec_ref, wr_ref, wi_ref, coef_ref, push_ref):
    width = both_ref.shape[1] // 2
    rows = both_ref.shape[0] // held_buffers

    def gates(b, carry):
        at = buffer_rows_at(b, rows)
        mask = mask_ref[at, :]
        conv = conv_of(both_ref[at, :width], mask, vec_ref)
        rate, igate = gates_of(conv.astype(bf16), vec_ref, wr_ref, wi_ref)
        decay = jnp.exp(-8.0 * rate * vec_ref[7:8, :])
        root = jnp.sqrt(1.0 - decay * decay + root_eps)
        store_lanes(coef_ref, at, decay * mask[:, 0:1])
        store_lanes(push_ref, at, root * igate * conv)
        return carry

    lax.fori_loop(0, held_buffers, gates, 0)
    scan_rows(coef_ref, push_ref, rows, False)


def recur_mixed(both_ref, state_ref, mixed_ref):
    width = both_ref.shape[1] // 2
    rows = both_ref.shape[0] // held_buffers

    def mix(b, carry):
        at = buffer_rows_at(b, rows)
        gate = gelu_parts(both_ref[at, width:])[0]
        mixed_ref[at, :] = (load_lanes(state_ref, at, width) * gate).astype(bf16)
        return carry

    lax.fori_loop(0, held_buffers, mix, 0)


class Place:
    def __init__(self, count):
        self.me = lax.axis_index("dp")
        self.y = lax.axis_index("mp")
        self.c = self.me // count % 2
        self.x = self.me // (2 * count) % 2
        self.z = self.me // (4 * count)
        self.core = {"dp": self.me + (1 - 2 * self.c) * count}
        self.beside = {"dp": self.me + (1 - 2 * self.x) * 2 * count}
        self.over_y = {"mp": 1 - self.y}
        sign = 1 - 2 * (self.z // 2)
        self.ahead = {"dp": self.me + sign * 4 * count}
        self.behind = {"dp": self.me - sign * 4 * count}
        self.works = (self.z + 1) // 2 == 1
        self.serves = (self.z + 1) // 2 != 1

    def columns(self, size):
        outer = self.z // 2 * 3
        far, far_outer = 3 - self.z, 3 - outer
        return [
            ((at_z + 2 * self.y) % 4 * 2 + at_x) * size
            for at_z in (self.z, outer, far, far_outer)
            for at_x in (self.x, 1 - self.x)
        ]

    def meet(self):
        barrier = pltpu.get_barrier_semaphore()

        def greet(partners):
            for partner in partners:
                pl.semaphore_signal(barrier, inc=1, device_id=partner, device_id_type=by_mesh)
            pl.semaphore_wait(barrier, len(partners))

        @pl.when(self.works)
        def _():
            greet((self.core, self.beside, self.over_y, self.ahead, self.behind))

        @pl.when(self.serves)
        def _():
            greet((self.core, self.beside, self.ahead))


def remote(src, dst, send, recv, where):
    return pltpu.make_async_remote_copy(
        src_ref=src,
        dst_ref=dst,
        send_sem=send,
        recv_sem=recv,
        device_id=where,
        device_id_type=by_mesh,
    )


def normed_rows(source_ref, gain_ref, gain_row, scale_ref, scale_row, out_ref, first, count):
    size = 128

    def chunk(i, carry):
        at = pl.ds(pl.multiple_of(first + i * size, size), size)
        rows = source_ref[at, :].astype(f32)
        scale = lax.rsqrt(jnp.mean(rows * rows, axis=1, keepdims=True) + norm_eps)
        scale_ref[scale_row, at, :] = jnp.broadcast_to(scale, (size, lanes))
        out_ref[at, :] = (rows * scale * gain_ref[gain_row : gain_row + 1, :]).astype(bf16)
        return carry

    lax.fori_loop(0, count // size, chunk, 0)


def forward_kernel(
    count,
    keep_ri, keep_ro, keep_mi, keep_mo, give_ri, give_ro, give_mi, give_mo,
    tokens_ref, grad_ref, mask_in, gain_ref, vec_ref, wr_ref, wi_ref,
    g_ri, g_ro, g_mi, g_mo,
    both_ref, state_ref, mixed_ref, mask_ref, middle_ref, tok_ref,
    one_mine, one_theirs, two_mine, two_theirs, low_mine, low_theirs, scale_ref,
    coef_ref, w_ri, w_ro, grad_all, part_out, part_in, part_sum, y_out, y_in, mid_ref,
    w_send, w_recv, w_local, load_sem, m_send, m_recv, m_local,
):
    at = Place(count)
    half_rows = keep_ri.shape[0]
    size = 2 * half_rows
    model = tok_ref.shape[1]
    half_model = model // 2
    rows = tokens_ref.shape[0]
    own = 2 * rows
    cols = at.columns(size)
    whole, keeps, gives = (g_ri, g_ro, g_mi, g_mo), (keep_ri, keep_ro, keep_mi, keep_mo), (
        give_ri, give_ro, give_mi, give_mo,
    )
    ri, ro, mi, mo = range(4)
    top, bottom = pl.ds(0, half_rows), pl.ds(half_rows, half_rows)
    core_rows = pl.ds(pl.multiple_of(at.c * half_rows, half_rows), half_rows)

    def hop(w, k):
        g = whole[w]
        src, dst, where = (
            (gives[w], g.at[0, core_rows], at.core),
            (g.at[0], g.at[1], at.beside),
            (g.at[0], g.at[2], at.ahead),
            (g.at[1], g.at[3], at.ahead),
            (g.at[0], g.at[4], at.ahead),
            (g.at[4], g.at[5], at.beside),
            (g.at[2], g.at[6], at.ahead),
            (g.at[3, top], g.at[7, top], at.ahead),
            (g.at[6, bottom], g.at[7, bottom], at.beside),
        )[k]
        return remote(src, dst, w_send.at[w, k], w_recv.at[w, k], where)

    def kept(w):
        return pltpu.make_async_copy(keeps[w], whole[w].at[0, core_rows], w_local.at[w])

    def begin(w):
        kept(w).start()
        hop(w, 0).start()

    def own_block(w, hops):
        kept(w).wait()
        hop(w, 0).wait()
        for k in hops:
            hop(w, k).start()

    def pass_on(w, arrived, sent):
        hop(w, arrived).wait_recv()
        hop(w, sent).start()

    def move(k, src, dst, where):
        return remote(src, dst, m_send.at[k], m_recv.at[k], where)

    first, second = pl.ds(0, rows), pl.ds(rows, rows)
    left, right = pl.ds(0, half_model), pl.ds(half_model, half_model)
    mine_rows, their_rows = pl.ds(0, own), pl.ds(own, own)
    token_in = move(0, tokens_ref, tok_ref.at[second, left], at.ahead)
    token_y = move(1, tokens_ref, tok_ref.at[first, right], at.over_y)
    token_y_two = move(2, tok_ref.at[second, left], tok_ref.at[second, right], at.over_y)
    grad_in = move(3, grad_ref, grad_all.at[second, left], at.ahead)
    grad_y = move(4, grad_ref, grad_all.at[first, right], at.over_y)
    grad_y_two = move(5, grad_all.at[second, left], grad_all.at[second, right], at.over_y)
    mask_move = move(6, mask_in, mask_ref.at[second], at.ahead)
    mask_core = move(7, mask_ref.at[mine_rows], mask_ref.at[their_rows], at.core)
    one_core = move(8, one_mine, one_theirs, at.core)
    low_core = move(9, low_mine, low_theirs, at.core)
    halves = (first, second)
    part_core = [move(10 + i, part_out.at[h], part_in.at[h], at.core) for i, h in enumerate(halves)]
    part_y = [move(12 + i, y_out.at[h], y_in.at[h], at.over_y) for i, h in enumerate(halves)]
    mid_y = [
        move(14 + i, mid_ref.at[h, left], mid_ref.at[h, right], at.over_y)
        for i, h in enumerate(halves)
    ]
    two_core = [move(16 + i, two_mine.at[h], two_theirs.at[h], at.core) for i, h in enumerate(halves)]
    token_here = pltpu.make_async_copy(tokens_ref, tok_ref.at[first, left], m_local.at[0])
    grad_here = pltpu.make_async_copy(grad_ref, grad_all.at[first, left], m_local.at[1])
    mask_here = pltpu.make_async_copy(mask_in, mask_ref.at[first], m_local.at[2])

    def load(w, target, b):
        return pltpu.make_async_copy(whole[w].at[b], target.at[b], load_sem.at[w, b])

    at.meet()

    @pl.when(at.serves)
    def _():
        mask_move.start()
        token_in.start()
        for w in (ri, ro, mi, mo):
            begin(w)
        for w in (ri, ro):
            own_block(w, (1, 2))
        for w in (ri, ro):
            pass_on(w, 1, 3)
        grad_in.start()
        for w in (mi, mo):
            own_block(w, (1, 2))
        for w in (mi, mo):
            pass_on(w, 1, 3)
        for w in (ri, ro, mi, mo):
            for k in (1, 2, 3):
                hop(w, k).wait_send()
        for moved in (mask_move, token_in, grad_in):
            moved.wait_send()

    @pl.when(at.works)
    def _():
        token_here.start()
        mask_here.start()
        token_y.start()
        begin(ri)
        begin(ro)
        grad_here.start()
        begin(mi)
        begin(mo)
        own_block(ri, (1, 4))
        own_block(ro, (1, 4))
        mask_here.wait()
        mask_move.wait_recv()
        mask_core.start()
        token_in.wait_recv()
        token_y_two.start()
        pass_on(ri, 2, 6)
        pass_on(ri, 4, 5)
        token_here.wait()
        token_y.wait_recv()
        normed_rows(tok_ref, gain_ref, 0, scale_ref, 0, one_mine, 0, rows)
        token_y_two.wait_recv()
        normed_rows(tok_ref, gain_ref, 0, scale_ref, 0, one_mine, rows, rows)
        one_core.start()
        pass_on(ro, 2, 6)
        pass_on(ro, 4, 5)
        pass_on(ri, 3, 7)
        pass_on(ri, 6, 8)
        own_block(mi, (1, 4))
        pass_on(ro, 3, 7)
        pass_on(ro, 6, 8)
        grad_y.start()
        for w, target in ((ri, w_ri), (ro, w_ro)):
            hop(w, 1).wait_recv()
            for k in (5, 7, 8):
                hop(w, k).wait_recv()
            for b in range(blocks):
                load(w, target, b).start()
        for b in range(blocks):
            load(ri, w_ri, b).wait()
        one_core.wait_recv()
        mask_core.wait_recv()

        def keep_both(start, value):
            both_ref[pl.ds(start, chunk_rows), :] = value

        project(one_mine, one_theirs, w_ri, cols, keep_both)
        grad_in.wait_recv()
        grad_y_two.start()
        recur_state(both_ref, mask_ref, vec_ref, wr_ref, wi_ref, coef_ref, state_ref)
        pass_on(mi, 2, 6)
        pass_on(mi, 4, 5)
        own_block(mo, (1, 4))
        recur_mixed(both_ref, state_ref, mixed_ref)
        for b in range(blocks):
            load(ro, w_ro, b).wait()

        def branch(start, out_ref, out_at):
            for b in range(blocks):
                out_ref[out_at, columns_at(cols, b, size)] = lax.dot_general(
                    mixed_ref[pl.ds(start, rows), :],
                    w_ro[b],
                    contract_cols,
                    preferred_element_type=f32,
                ).astype(out_ref.dtype)

        for i, h in enumerate(halves):
            branch(own + i * rows, part_out, h)
            part_core[i].start()
        for i, h in enumerate(halves):
            branch(i * rows, part_sum, first)
            part_core[i].wait_recv()
            middle_ref[h, :] = part_sum[:, left] + part_in[h, left].astype(f32)
            y_out[h, :] = (part_sum[:, right] + part_in[h, right].astype(f32)).astype(bf16)
            part_y[i].start()
        pass_on(mi, 3, 7)
        grad_here.wait()
        grad_y.wait_recv()
        grad_y_two.wait_recv()
        low_mine[...] = (grad_all[...].astype(f32) * mask_ref[mine_rows, 4:5]).astype(bf16)
        low_core.start()
        for i, h in enumerate(halves):
            part_y[i].wait_recv()
            middle = middle_ref[h, :] + y_in[h, :].astype(f32) + tok_ref[h, left].astype(f32)
            middle_ref[h, :] = middle
            mid_ref[h, left] = middle.astype(bf16)
            mid_y[i].start()
        pass_on(mi, 6, 8)
        pass_on(mo, 2, 6)
        pass_on(mo, 4, 5)
        for i, h in enumerate(halves):
            mid_y[i].wait_recv()
            normed_rows(mid_ref, gain_ref, 1, scale_ref, 1, two_mine, i * rows, rows)
            two_core[i].start()
        pass_on(mo, 3, 7)
        pass_on(mo, 6, 8)
        for w in (mi, mo):
            for k in (1, 5, 7, 8):
                hop(w, k).wait_recv()
        low_core.wait_recv()
        for moved in two_core:
            moved.wait_recv()
        for w in (ri, ro, mi, mo):
            for k in (1, 4, 5, 6, 7, 8):
                hop(w, k).wait_send()
        for moved in (
            token_y, token_y_two, grad_y, grad_y_two, mask_core, one_core, low_core,
            *part_core, *part_y, *mid_y, *two_core,
        ):
            moved.wait_send()


def recur_backward(
    mine_ref, theirs_ref, weight_ref, cols_ref,
    both_ref, state_ref, mask_ref, vec_ref, wr_ref, wi_ref,
    dboth_ref, sums_ref, gr_ref, gi_ref,
    coef_ref, push_ref, dmix_ref,
):
    def keep_mixed(start, value):
        dmix_ref[pl.ds(start, chunk_rows), :] = value

    project(mine_ref, theirs_ref, weight_ref, cols_ref, keep_mixed)
    width = dmix_ref.shape[1]
    rows = both_ref.shape[0] // held_buffers

    def first(b, carry):
        at = buffer_rows_at(b, rows)
        gate, slope = gelu_parts(both_ref[at, width:])
        d_mixed = dmix_ref[at, :]
        mask = mask_ref[at, :]
        conv_low = conv_of(both_ref[at, :width], mask, vec_ref).astype(bf16)
        rate = gates_of(conv_low, vec_ref, wr_ref, wi_ref)[0]
        store_lanes(push_ref, at, d_mixed * gate)
        dboth_ref[at, width:] = (slope * d_mixed * load_lanes(state_ref, at, width)).astype(bf16)
        store_lanes(coef_ref, at, jnp.exp(-8.0 * rate * vec_ref[7:8, :]) * mask[:, 0:1])
        return carry

    lax.fori_loop(0, held_buffers, first, 0)

    scan_rows(coef_ref, push_ref, rows, True)
    sums_ref[...] = jnp.zeros_like(sums_ref)
    gr_ref[...] = jnp.zeros_like(gr_ref)
    gi_ref[...] = jnp.zeros_like(gi_ref)

    def add_sum(k, value):
        sums_ref[k : k + 1, :] += jnp.sum(value, axis=0, keepdims=True)

    def last(b, carry):
        at = buffer_rows_at(b, rows)
        inner = both_ref[at, :width]
        mask = mask_ref[at, :]
        keep = mask[:, 0:1]
        softened = vec_ref[7:8, :]
        conv = conv_of(inner, mask, vec_ref)
        conv_low = conv.astype(bf16)
        rate, igate = gates_of(conv_low, vec_ref, wr_ref, wi_ref)
        d_push = load_lanes(push_ref, at, width)
        decay = jnp.exp(-8.0 * rate * softened)
        square = 1.0 - decay * decay + root_eps
        root = jnp.sqrt(square)
        d_root = d_push * igate * conv
        d_igate = d_push * root * conv
        before = shifted(load_lanes(state_ref, at, width), 1) * keep
        d_decay = d_push * before - d_root * decay / root
        d_log = d_decay * decay
        slow = d_log * rate
        d_pre_recur = (-8.0 * softened) * slow * (1.0 - rate)
        d_pre_input = d_igate * igate * (1.0 - igate)
        add_sum(7, slow)
        add_sum(5, d_pre_recur)
        add_sum(6, d_pre_input)
        low_recur = d_pre_recur.astype(bf16)
        low_input = d_pre_input.astype(bf16)
        gr_ref[...] += lax.dot_general(
            conv_low, low_recur, contract_rows, preferred_element_type=f32
        )
        gi_ref[...] += lax.dot_general(
            conv_low, low_input, contract_rows, preferred_element_type=f32
        )
        d_conv = d_push * root * igate
        d_conv = d_conv + lax.dot_general(
            low_recur, wr_ref[...], contract_cols, preferred_element_type=f32
        )
        d_conv = d_conv + lax.dot_general(
            low_input, wi_ref[...], contract_cols, preferred_element_type=f32
        )
        add_sum(4, d_conv)
        add_sum(0, d_conv * inner)
        d_inner = vec_ref[0:1, :] * d_conv
        for k in range(1, 4):
            kept = d_conv * mask[:, k : k + 1]
            add_sum(k, kept * shifted(inner, k))
            d_inner = d_inner + vec_ref[k : k + 1, :] * shifted(kept, -k)
        dboth_ref[at, :width] = d_inner.astype(bf16)
        return carry

    lax.fori_loop(0, held_buffers, last, 0)


def mlp_forward(mine_ref, theirs_ref, gate_weight, up_weight, cols_ref, act_ref, slope_ref, value_ref):
    size = gate_weight.shape[1]
    own = mine_ref.shape[0]
    for part, ref in enumerate((mine_ref, theirs_ref)):

        def chunk(i, carry, part=part, ref=ref):
            rows = gathered(
                ref, pl.ds(pl.multiple_of(i * chunk_rows, chunk_rows), chunk_rows), cols_ref, size
            )
            gate = jnp.dot(rows, stacked(gate_weight), preferred_element_type=f32)
            up = jnp.dot(rows, stacked(up_weight), preferred_element_type=f32)
            value, slope = gelu_parts(gate)
            at = pl.ds(pl.multiple_of(part * own + i * chunk_rows, chunk_rows), chunk_rows)
            act_ref[at, :] = (value * up).astype(bf16)
            slope_ref[at, :] = (slope * up).astype(bf16)
            value_ref[at, :] = value.astype(bf16)
            return carry

        lax.fori_loop(0, own // chunk_rows, chunk, 0)


def mlp_backward(mine_ref, theirs_ref, weight_ref, cols_ref, slope_ref, value_ref, d_gate_ref, d_up_ref):
    def use(start, d_act):
        at = pl.ds(start, chunk_rows)
        d_gate_ref[at, :] = (d_act * slope_ref[at, :].astype(f32)).astype(bf16)
        d_up_ref[at, :] = (d_act * value_ref[at, :].astype(f32)).astype(bf16)

    project(mine_ref, theirs_ref, weight_ref, cols_ref, use)


def rows_back(part_tiles, *refs):
    count = len(part_tiles)
    row_refs, (weight_ref, cols_ref, out_ref, total_ref) = refs[:count], refs[count:]
    size = weight_ref.shape[1]
    step = pl.program_id(0)

    @pl.when(step == 0)
    def _():
        total_ref[...] = jnp.zeros_like(total_ref)

    first = 0
    for tiles, row_ref in zip(part_tiles, row_refs):

        @pl.when((step >= first) & (step < first + tiles))
        def _(row_ref=row_ref):
            for b in range(blocks):
                total_ref[:, columns_at(cols_ref, b, size)] += lax.dot_general(
                    row_ref[...], weight_ref[b], contract_cols, preferred_element_type=f32
                )

        first += tiles

    @pl.when(step == first - 1)
    def _():
        out_ref[...] = total_ref[...].astype(out_ref.dtype)


def weight_partial(part_tiles, mine_ref, theirs_ref, cols_ref, *refs):
    count = len(part_tiles)
    column_refs, out_ref = refs[:count], refs[count]
    size = out_ref.shape[1]
    own = mine_ref.shape[0]
    step = pl.program_id(0)
    first = 0
    for tiles, column_ref in zip(part_tiles, column_refs):

        @pl.when((step >= first) & (step < first + tiles))
        def _(column_ref=column_ref):
            for b in range(blocks):
                at = columns_at(cols_ref, b, size)
                total = lax.dot_general(
                    mine_ref[:, at], column_ref[:own, :], contract_rows, preferred_element_type=f32
                )
                total = total + lax.dot_general(
                    theirs_ref[:, at], column_ref[own:, :], contract_rows, preferred_element_type=f32
                )
                out_ref[b] = total.astype(bf16)

        first += tiles


in_vmem = pl.BlockSpec(memory_space=pltpu.VMEM)
in_smem = pl.BlockSpec(memory_space=pltpu.SMEM)
in_any = pl.BlockSpec(memory_space=pl.ANY)
no_cost = pl.CostEstimate(flops=0, bytes_accessed=0, transcendentals=0)
kernel_params = pltpu.CompilerParams(vmem_limit_bytes=60 * 2**20)
copy_sem = pltpu.SemaphoreType.DMA


def lane_shape(rows, width):
    return (pl.cdiv(width, lanes), rows, lanes)


def run_forward(count, keeps, gives, tokens, out_grad, mask, gains, vectors, wr, wi):
    rows, half_model = tokens.shape
    own, model, width = 2 * rows, 2 * half_model, wr.shape[0]
    size = 2 * keeps[0].shape[0]
    shape = jax.ShapeDtypeStruct
    gathered_shapes = [shape((blocks, size, v.shape[1]), bf16) for v in keeps]
    wide = shape((own, model), bf16)
    return pl.pallas_call(
        functools.partial(forward_kernel, count),
        out_shape=(
            *gathered_shapes,
            shape((2 * own, 2 * width), f32),
            shape(lane_shape(2 * own, width), f32),
            shape((2 * own, width), bf16),
            shape((2 * own, lanes), f32),
            shape((own, half_model), f32),
            *[wide] * 7,
            shape((2, own, lanes), f32),
        ),
        in_specs=[in_any] * 11 + [in_vmem] * 4,
        out_specs=[in_any] * 4 + [in_vmem] * 13,
        scratch_shapes=[
            pltpu.VMEM(lane_shape(2 * own, width), f32),
            pltpu.VMEM((blocks, size, 2 * width), bf16),
            pltpu.VMEM((blocks, size, width), bf16),
            pltpu.VMEM((own, model), bf16),
            pltpu.VMEM((own, model), bf16),
            pltpu.VMEM((own, model), bf16),
            pltpu.VMEM((rows, model), f32),
            pltpu.VMEM((own, half_model), bf16),
            pltpu.VMEM((own, half_model), bf16),
            pltpu.VMEM((own, model), bf16),
            copy_sem((4, 9)),
            copy_sem((4, 9)),
            copy_sem((4,)),
            copy_sem((2, blocks)),
            copy_sem((18,)),
            copy_sem((18,)),
            copy_sem((3,)),
        ],
        compiler_params=pltpu.CompilerParams(
            vmem_limit_bytes=60 * 2**20, collective_id=0, has_side_effects=True
        ),
        cost_estimate=no_cost,
        name="gather_and_recur",
    )(*keeps, *gives, tokens, out_grad, mask, gains, vectors, wr, wi)


def run_recur_backward(d_branch, weight, cols, both, state, mask, vectors, wr, wi):
    rows, width = both.shape[0], wr.shape[0]
    square = jax.ShapeDtypeStruct((width, width), f32)
    return pl.pallas_call(
        recur_backward,
        out_shape=(
            jax.ShapeDtypeStruct((rows, 2 * width), bf16),
            jax.ShapeDtypeStruct((8, width), f32),
            square,
            square,
        ),
        in_specs=[in_vmem] * 3 + [in_smem] + [in_vmem] * 6,
        out_specs=[in_vmem] * 4,
        scratch_shapes=[pltpu.VMEM(lane_shape(rows, width), f32)] * 2
        + [pltpu.VMEM((rows, width), f32)],
        compiler_params=kernel_params,
        cost_estimate=no_cost,
        name="recur_backward",
    )(*d_branch, weight, cols, both, state, mask, vectors, wr, wi)


def run_mlp_forward(normed, weight, cols):
    own, model = normed[0].shape
    size, hidden = weight.shape[1], weight.shape[2] // 2
    tile = 256
    tiles = hidden // tile
    out = jax.ShapeDtypeStruct((2 * own, hidden), bf16)
    return pl.pallas_call(
        mlp_forward,
        grid=(tiles,),
        out_shape=(out, out, out),
        in_specs=[pl.BlockSpec((own, model), lambda n: (0, 0))] * 2
        + [pl.BlockSpec((blocks, size, tile), lambda n: (0, 0, n))]
        + [pl.BlockSpec((blocks, size, tile), lambda n: (0, 0, n + tiles))]
        + [in_smem],
        out_specs=[pl.BlockSpec((2 * own, tile), lambda n: (0, n))] * 3,
        compiler_params=kernel_params,
        cost_estimate=no_cost,
        name="mlp_forward",
    )(*normed, weight, weight, cols)


def run_mlp_backward(grad_low, weight, cols, slope, value):
    own, model = grad_low[0].shape
    size, hidden = weight.shape[1:]
    tile = 256
    out = jax.ShapeDtypeStruct((2 * own, hidden), bf16)
    column = pl.BlockSpec((2 * own, tile), lambda n: (0, n))
    return pl.pallas_call(
        mlp_backward,
        grid=(hidden // tile,),
        out_shape=(out, out),
        in_specs=[pl.BlockSpec((own, model), lambda n: (0, 0))] * 2
        + [pl.BlockSpec((blocks, size, tile), lambda n: (0, 0, n))]
        + [in_smem, column, column],
        out_specs=[column, column],
        compiler_params=kernel_params,
        cost_estimate=no_cost,
        name="mlp_backward",
    )(*grad_low, weight, cols, slope, value)


def tile_of(width):
    return 512 if width % 512 == 0 else width


def part_specs(parts, rows, row_block, tile):
    specs, tiles, first = [], [], 0
    for part in parts:
        count = part.shape[1] // tile

        def index(n, first=first, count=count):
            return (row_block, jnp.clip(n - first, 0, count - 1))

        specs.append(pl.BlockSpec((rows, tile), index))
        tiles.append(count)
        first += count
    return specs, tuple(tiles)


def run_rows_back(name, parts, weight, cols, row_block, dtype):
    own = parts[0].shape[0] // 2
    size = weight.shape[1]
    tile = tile_of(parts[0].shape[1])
    specs, tiles = part_specs(parts, own, row_block, tile)
    return pl.pallas_call(
        functools.partial(rows_back, tiles),
        grid=(sum(tiles),),
        out_shape=jax.ShapeDtypeStruct((own, size * blocks), dtype),
        in_specs=specs
        + [pl.BlockSpec((blocks, size, tile), lambda n: (0, 0, n)), in_smem],
        out_specs=pl.BlockSpec((own, size * blocks), lambda n: (0, 0)),
        scratch_shapes=[pltpu.VMEM((own, size * blocks), f32)],
        compiler_params=kernel_params,
        cost_estimate=no_cost,
        name=name,
    )(*parts, weight, cols)


def run_weight_partial(name, rows, parts, cols):
    own, model = rows[0].shape
    size = model // blocks
    tile = tile_of(parts[0].shape[1])
    specs, tiles = part_specs(parts, 2 * own, 0, tile)
    return pl.pallas_call(
        functools.partial(weight_partial, tiles),
        grid=(sum(tiles),),
        out_shape=jax.ShapeDtypeStruct((blocks, size, sum(tiles) * tile), bf16),
        in_specs=[pl.BlockSpec((own, model), lambda n: (0, 0))] * 2 + [in_smem] + specs,
        out_specs=pl.BlockSpec((blocks, size, tile), lambda n: (0, 0, n)),
        compiler_params=kernel_params,
        cost_estimate=no_cost,
        name=name,
    )(*rows, cols, *parts)


def block_diagonal(blocks):
    count, size = blocks.shape[0], blocks.shape[1]
    rows = [
        jnp.pad(blocks[h], ((0, 0), (h * size, (count - 1 - h) * size))) for h in range(count)
    ]
    return jnp.concatenate(rows, axis=0)


def diagonal_blocks(square, count):
    size = square.shape[0] // count
    return jnp.stack(
        [square[h * size : (h + 1) * size, h * size : (h + 1) * size] for h in range(count)]
    )


def masks_of(lengths, rows):
    ends = jnp.cumsum(lengths, axis=1)
    starts = ends - lengths
    places = jnp.arange(rows, dtype=jnp.int32)[None, :, None]
    inside = (places >= starts[:, None, :]) & (places < ends[:, None, :])
    first_place = jnp.sum(jnp.where(inside, starts[:, None, :], 0), axis=2)
    places = places[:, :, 0]
    live = (places < ends[:, 2:3]).astype(f32)
    columns = [(places != first_place).astype(f32)]
    for k in range(1, 4):
        columns.append((places - k >= first_place).astype(f32))
    columns += [live] + [jnp.zeros_like(live)] * 3
    return jnp.stack(columns, axis=2).reshape(lengths.shape[0] * rows, 8), live


def local(
    n_dp,
    tokens,
    gain_rnn,
    rnn_in,
    gate_recur,
    gate_input,
    bias_recur,
    bias_input,
    decay_param,
    conv_weight,
    conv_bias,
    rnn_out,
    gain_mlp,
    mlp_in,
    mlp_out,
    lengths,
    out_grad,
):
    outer_count = n_dp // 16
    rows_here = rnn_in.shape[0]
    model = gain_rnn.shape[0]
    half_model = model // 2
    buffer_rows = tokens.shape[0]
    own_rows = 2 * buffer_rows
    index = lax.axis_index("dp")
    y = lax.axis_index("mp")
    c = index // outer_count % 2
    x = index // (2 * outer_count) % 2
    z = index // (4 * outer_count)
    outer = jnp.where(z < 2, 0, 3)
    far = 3 - z
    far_outer = 3 - outer
    worker = (z == 1) | (z == 2)

    def mover(move):
        table = pairs(n_dp, move)
        return lambda value: lax.ppermute(value, "dp", table)

    swap_c = mover(lambda z, x, c: (z, x, 1 - c))
    swap_x = mover(lambda z, x, c: (z, 1 - x, c))
    swap_x_work = mover(lambda z, x, c: (z, 1 - x, c) if z in (1, 2) else None)
    swap_x_ends = mover(lambda z, x, c: (z, 1 - x, c) if z in (0, 3) else None)
    inward = mover(lambda z, x, c: {0: (1, x, c), 3: (2, x, c)}.get(z))
    outward = mover(lambda z, x, c: {1: (0, x, c), 2: (3, x, c)}.get(z))
    across = mover(lambda z, x, c: {1: (2, x, c), 2: (1, x, c)}.get(z))

    def swap_y(value):
        return lax.ppermute(value, "mp", [(0, 1), (1, 0)])

    def pick_c(first, second):
        return jnp.where(c == 0, first, second)

    def pick_y(first, second):
        return jnp.where(y == 0, first, second)

    group_rows = outer_count * rows_here
    block_rows = 2 * group_rows

    outer_groups = [[i * outer_count + w for w in range(outer_count)] for i in range(16)]

    def over_outer(value):
        if outer_count == 1:
            return value
        return lax.all_gather(value, "dp", axis_index_groups=outer_groups, axis=0, tiled=True)

    cols = jnp.stack(
        [
            ((at_z + 2 * y) % 4 * 2 + at_x) * block_rows
            for at_z in (z, outer, far, far_outer)
            for at_x in (x, 1 - x)
        ]
    ).astype(jnp.int32)

    def added(*values):
        return sum(v.astype(f32) for v in values).astype(bf16)

    def scatter_grad(pieces, by_x):
        own, own_x, near, near_x, across_one, across_x, across_near, across_near_x = pieces
        if by_x:
            across_near = added(across_near, swap_x_work(across_near_x))
            across_one = added(across_one, swap_x_work(across_x))
        else:
            near_x = added(near_x, across(across_near_x))
            across_one = added(across_one, swap_x_work(across_x))
        near = added(near, across(across_near))
        out_other = outward(near_x)
        own_sum = swap_x_work(own_x)
        far_sum = across(across_one)
        out_near = outward(near)
        worker_total = own.astype(f32) + own_sum.astype(f32) + far_sum.astype(f32)
        end_total = out_near.astype(f32) + swap_x_ends(out_other).astype(f32)
        total = jnp.where(worker, worker_total, end_total).astype(bf16)
        top, bottom = total[:group_rows], total[group_rows:]
        mine = pick_c(top, bottom)
        arrived = swap_c(pick_c(bottom, top))
        first, second = pick_c(mine, arrived).astype(f32), pick_c(arrived, mine).astype(f32)
        if outer_count > 1:
            first, second = (
                lax.psum_scatter(
                    v, "dp", axis_index_groups=outer_groups, scatter_dimension=0, tiled=True
                )
                for v in (first, second)
            )
        return first, second

    def whole_features(half_rows):
        return jnp.concatenate([half_rows, swap_y(half_rows)], axis=1)

    def both_cores(rows_value):
        return rows_value, swap_c(rows_value)

    def sum_partials(name, parts, weight):
        theirs = swap_c(run_rows_back(name + "_theirs", parts, weight, cols, 1, bf16))
        mine = run_rows_back(name + "_mine", parts, weight, cols, 0, f32) + theirs.astype(f32)
        arrived = swap_y(mine[:, half_model:].astype(bf16))
        return mine[:, :half_model] + arrived.astype(f32)

    def relative(vector):
        first, second = vector[:half_model], vector[half_model:]
        return jnp.concatenate([pick_y(first, second), pick_y(second, first)])

    def norm_back(source, scale_rows, gain, grad_rows):
        weighted = grad_rows * gain
        part = jnp.sum(weighted * source, axis=1, keepdims=True)
        inner_mean = (part + swap_y(part)) / model
        back_rows = scale_rows * weighted - source * (scale_rows * scale_rows * scale_rows) * inner_mean
        return back_rows, jnp.sum(grad_rows * source * scale_rows, axis=0)

    def quarters(value, axis):
        size = value.shape[axis] // 2
        return (
            lax.slice_in_dim(value, 0, size, axis=axis),
            lax.slice_in_dim(value, size, 2 * size, axis=axis),
        )

    def pair_quarters(weight):
        first, second = quarters(weight, 2)
        return tuple(jnp.concatenate([v[:, 0], v[:, 1]], axis=1) for v in (first, second))

    def quarter(value, axis=0):
        return pick_c(*quarters(value, axis))

    gain_one, gain_two = relative(gain_rnn.astype(f32)), relative(gain_mlp.astype(f32))
    mask, _ = masks_of(lengths, buffer_rows)
    mask = jnp.pad(mask, ((0, 0), (0, lanes - mask.shape[1])))
    softened = jax.nn.softplus(-quarter(decay_param))
    vectors = jnp.concatenate(
        [
            quarter(conv_weight, 1),
            jnp.stack([quarter(conv_bias), quarter(bias_recur), quarter(bias_input), softened]),
        ],
        axis=0,
    )
    heads = gate_recur.shape[0] // 2
    wr = block_diagonal(quarter(gate_recur))
    wi = block_diagonal(quarter(gate_input))
    split = (
        pair_quarters(rnn_in),
        quarters(rnn_out, 1),
        pair_quarters(mlp_in),
        quarters(mlp_out, 1),
    )
    split = [(over_outer(first), over_outer(second)) for first, second in split]
    keeps = [pick_c(first, second) for first, second in split]
    gives = [pick_c(second, first) for first, second in split]
    gains = jnp.stack([gain_one, gain_two])
    (
        rnn_in_all, rnn_out_all, mlp_in_all, mlp_out_all,
        both, state, mixed, mask, middle, tokens_all,
        *rows_kept, scales,
    ) = run_forward(outer_count, keeps, gives, tokens, out_grad, mask, gains, vectors, wr, wi)
    normed, normed_two, grad_low = rows_kept[0:2], rows_kept[2:4], rows_kept[4:6]
    scale_one, scale_two = scales[0, :, :1], scales[1, :, :1]
    tokens_two = tokens_all[:, :half_model]
    live = mask[:own_rows, 4:5]
    live_grad = grad_low[0][:, :half_model].astype(f32)
    middle_low = middle.astype(bf16)

    act, gate_slope, gate_value = run_mlp_forward(normed_two, mlp_in_all, cols)
    mlp_out_grad = scatter_grad(
        run_weight_partial("mlp_out_partial", grad_low, (act,), cols), True
    )
    d_pair = run_mlp_backward(grad_low, mlp_out_all, cols, gate_slope, gate_value)
    e_two = sum_partials("mlp_in_back", d_pair, mlp_in_all)
    mlp_in_grad = scatter_grad(
        run_weight_partial("mlp_in_partial", normed_two, d_pair, cols), False
    )
    back_two, gain_two_term = norm_back(
        middle_low.astype(f32), scale_two, gain_two[:half_model], e_two
    )
    d_middle = live_grad + back_two
    d_branch = both_cores(whole_features(d_middle.astype(bf16)))
    rnn_out_grad = scatter_grad(
        run_weight_partial("rnn_out_partial", d_branch, (mixed,), cols), True
    )
    branch_two = sum_partials("mlp_out", (act,), mlp_out_all)
    output_two = (live * (middle + branch_two)).astype(bf16)

    d_both, sums, square_recur, square_input = run_recur_backward(
        d_branch, rnn_out_all, cols, both, state, mask, vectors, wr, wi
    )
    rnn_in_grad = scatter_grad(run_weight_partial("rnn_in_partial", normed, (d_both,), cols), True)
    e_one = sum_partials("rnn_in_back", (d_both,), rnn_in_all)
    back_one, gain_one_term = norm_back(
        tokens_two.astype(f32), scale_one, gain_one[:half_model], e_one
    )
    tokens_grad_two = (d_middle + back_one).astype(bf16)

    def settle(two):
        return jnp.where(worker, two[:buffer_rows], outward(two[buffer_rows:]))

    layer_output = settle(output_two)
    tokens_grad = settle(tokens_grad_two)

    def total(value, dtype=f32):
        value = jnp.where(worker, value, 0).astype(dtype)
        if outer_count > 1:
            value = lax.psum(value, "dp", axis_index_groups=outer_groups)
        value = value + swap_x(value)
        value = value + across(value)
        return jnp.where(worker, value, outward(value))

    def both_quarters(value, axis=0):
        arrived = swap_c(value)
        return pick_c(
            jnp.concatenate([value, arrived], axis=axis), jnp.concatenate([arrived, value], axis=axis)
        )

    sums = both_quarters(total(sums), 1)
    gate_grads = jnp.concatenate(
        [diagonal_blocks(square_recur, heads), diagonal_blocks(square_input, heads)], axis=2
    )
    gate_grads = both_quarters(total(gate_grads, bf16)).astype(f32)
    gains = total(jnp.stack([gain_one_term, gain_two_term]))
    gains = gains + swap_c(gains)
    size = gate_recur.shape[1]

    def pair_layout(halves):
        columns = halves[0].shape[1] // 2
        return jnp.stack(
            [
                jnp.concatenate([v[:, k * columns : (k + 1) * columns] for v in halves], axis=1)
                for k in range(2)
            ],
            axis=1,
        )

    return (
        layer_output,
        tokens_grad,
        gains[0],
        pair_layout(rnn_in_grad),
        gate_grads[:, :, :size],
        gate_grads[:, :, size:],
        sums[5],
        sums[6],
        8.0 * jax.nn.sigmoid(-decay_param) * sums[7],
        sums[:4],
        sums[4],
        jnp.concatenate(rnn_out_grad, axis=1),
        gains[1],
        pair_layout(mlp_in_grad),
        jnp.concatenate(mlp_out_grad, axis=1),
    )


def solution(mesh):
    return jax.shard_map(
        functools.partial(local, mesh.shape["dp"]),
        mesh=mesh,
        in_specs=(
            P("dp", "mp"),
            P(),
            P("dp", None, "mp"),
            P("mp", None, None),
            P("mp", None, None),
            P("mp"),
            P("mp"),
            P("mp"),
            P(None, "mp"),
            P("mp"),
            P("dp", "mp"),
            P(),
            P("dp", None, "mp"),
            P("dp", "mp"),
            P("dp", None),
            P("dp", "mp"),
        ),
        out_specs=(
            P("dp", "mp"),
            P("dp", "mp"),
            P("mp"),
            P("dp", None, "mp"),
            P("mp", None, None),
            P("mp", None, None),
            P("mp"),
            P("mp"),
            P("mp"),
            P(None, "mp"),
            P("mp"),
            P("dp", "mp"),
            P("mp"),
            P("dp", None, "mp"),
            P("dp", "mp"),
        ),
        check_vma=False,
    )
```

```python
import functools

import jax
import jax.numpy as jnp
from jax import lax
from jax.experimental import pallas as pl
from jax.experimental.pallas import tpu as pltpu
from jax.sharding import PartitionSpec as P

norm_eps = 1e-06
root_eps = 0.001
bf16 = jnp.bfloat16
f32 = jnp.float32
contract_cols = (((1,), (1,)), ((), ()))
contract_rows = (((0,), (0,)), ((), ()))
gelu_scale = 0.7978845608028654
gelu_cubic = 0.044715
held_buffers = 4
scan_unroll = 8
blocks = 8
chunk_rows = 256
lanes = 128
by_mesh = pl.DeviceIdType.MESH


def pairs(n_dp, move):
    count = n_dp // 16
    found = []
    for i in range(n_dp):
        w, c, x, z = i % count, i // count % 2, i // count // 2 % 2, i // count // 4
        target = move(z, x, c)
        if target is not None:
            z, x, c = target
            found.append((i, ((z * 2 + x) * 2 + c) * count + w))
    return found


def gelu_parts(v):
    tanh_value = jnp.tanh(gelu_scale * (v + gelu_cubic * v * v * v))
    value = 0.5 * v * (1.0 + tanh_value)
    slope = 0.5 * (1.0 + tanh_value) + 0.5 * v * (1.0 - tanh_value * tanh_value) * (
        gelu_scale * (1.0 + 3.0 * gelu_cubic * v * v)
    )
    return value, slope


def shifted(value, offset):
    return pltpu.roll(value, offset % value.shape[0], 0)


def store_lanes(ref, at, value):
    chunks = ref.shape[0]
    spare = chunks * lanes - value.shape[1]
    if spare:
        value = jnp.concatenate([value, jnp.zeros((value.shape[0], spare), f32)], axis=1)
    for i in range(chunks):
        ref[i, at, :] = value[:, i * lanes : (i + 1) * lanes]


def load_lanes(ref, at, width):
    return jnp.concatenate([ref[i, at, :] for i in range(ref.shape[0])], axis=1)[:, :width]


def scan_rows(coef_ref, push_ref, rows, reverse):
    chunks = coef_ref.shape[0]

    def step(i, carried):
        carried = list(carried)
        for j in range(scan_unroll):
            t = i * scan_unroll + j
            at = pl.ds(rows - 1 - t if reverse else t, held_buffers, stride=rows)
            for k in range(chunks):
                if reverse:
                    value = push_ref[k, at, :] + carried[k]
                    carried[k] = coef_ref[k, at, :] * value
                else:
                    value = coef_ref[k, at, :] * carried[k] + push_ref[k, at, :]
                    carried[k] = value
                push_ref[k, at, :] = value
        return tuple(carried)

    start = tuple(jnp.zeros((held_buffers, lanes), f32) for _ in range(chunks))
    lax.fori_loop(0, rows // scan_unroll, step, start)


def columns_at(cols_ref, b, size):
    return pl.ds(pl.multiple_of(cols_ref[b], size), size)


def gathered(ref, at, cols_ref, size):
    return jnp.concatenate([ref[at, columns_at(cols_ref, b, size)] for b in range(blocks)], axis=1)


def stacked(refs, columns=slice(None)):
    return jnp.concatenate([ref[:, columns] for ref in refs], axis=0)


def project(mine_ref, theirs_ref, weight_refs, cols_ref, use):
    size = weight_refs[0].shape[0]
    own = mine_ref.shape[0]
    for part, ref in enumerate((mine_ref, theirs_ref)):

        def chunk(i, carry, part=part, ref=ref):
            at = pl.ds(pl.multiple_of(i * chunk_rows, chunk_rows), chunk_rows)
            rows = gathered(ref, at, cols_ref, size)
            use(
                pl.multiple_of(part * own + i * chunk_rows, chunk_rows),
                jnp.dot(rows, stacked(weight_refs), preferred_element_type=f32),
            )
            return carry

        lax.fori_loop(0, own // chunk_rows, chunk, 0)


def columns_at(cols, b, size):
    return pl.ds(pl.multiple_of(cols[b], size), size)


def gathered(ref, at, cols, size):
    return jnp.concatenate([ref[at, columns_at(cols, b, size)] for b in range(blocks)], axis=1)


def stacked(weight_ref):
    return weight_ref[...].reshape(-1, weight_ref.shape[2])


def project(mine_ref, theirs_ref, weight_ref, cols, use):
    size = weight_ref.shape[1]
    own = mine_ref.shape[0]
    for part, ref in enumerate((mine_ref, theirs_ref)):

        def chunk(i, carry, part=part, ref=ref):
            at = pl.ds(pl.multiple_of(i * chunk_rows, chunk_rows), chunk_rows)
            rows = gathered(ref, at, cols, size)
            use(
                pl.multiple_of(part * own + i * chunk_rows, chunk_rows),
                jnp.dot(rows, stacked(weight_ref), preferred_element_type=f32),
            )
            return carry

        lax.fori_loop(0, own // chunk_rows, chunk, 0)


def buffer_rows_at(b, rows):
    return pl.ds(pl.multiple_of(b * rows, rows), rows)


def conv_of(inner, mask, vec_ref):
    conv = vec_ref[4:5, :] + vec_ref[0:1, :] * inner
    for k in range(1, 4):
        conv = conv + vec_ref[k : k + 1, :] * (shifted(inner, k) * mask[:, k : k + 1])
    return conv


def gates_of(conv_low, vec_ref, wr_ref, wi_ref):
    rate = jax.nn.sigmoid(
        jnp.dot(conv_low, wr_ref[...], preferred_element_type=f32) + vec_ref[5:6, :]
    )
    igate = jax.nn.sigmoid(
        jnp.dot(conv_low, wi_ref[...], preferred_element_type=f32) + vec_ref[6:7, :]
    )
    return rate, igate


def recur_state(both_ref, mask_ref, vec_ref, wr_ref, wi_ref, coef_ref, push_ref):
    width = both_ref.shape[1] // 2
    rows = both_ref.shape[0] // held_buffers

    def gates(b, carry):
        at = buffer_rows_at(b, rows)
        mask = mask_ref[at, :]
        conv = conv_of(both_ref[at, :width], mask, vec_ref)
        rate, igate = gates_of(conv.astype(bf16), vec_ref, wr_ref, wi_ref)
        decay = jnp.exp(-8.0 * rate * vec_ref[7:8, :])
        root = jnp.sqrt(1.0 - decay * decay + root_eps)
        store_lanes(coef_ref, at, decay * mask[:, 0:1])
        store_lanes(push_ref, at, root * igate * conv)
        return carry

    lax.fori_loop(0, held_buffers, gates, 0)
    scan_rows(coef_ref, push_ref, rows, False)


def recur_mixed(both_ref, state_ref, mixed_ref):
    width = both_ref.shape[1] // 2
    rows = both_ref.shape[0] // held_buffers

    def mix(b, carry):
        at = buffer_rows_at(b, rows)
        gate = gelu_parts(both_ref[at, width:])[0]
        mixed_ref[at, :] = (load_lanes(state_ref, at, width) * gate).astype(bf16)
        return carry

    lax.fori_loop(0, held_buffers, mix, 0)


class Place:
    def __init__(self, count):
        self.me = lax.axis_index("dp")
        self.y = lax.axis_index("mp")
        self.c = self.me // count % 2
        self.x = self.me // (2 * count) % 2
        self.z = self.me // (4 * count)
        self.core = {"dp": self.me + (1 - 2 * self.c) * count}
        self.beside = {"dp": self.me + (1 - 2 * self.x) * 2 * count}
        self.over_y = {"mp": 1 - self.y}
        sign = 1 - 2 * (self.z // 2)
        self.ahead = {"dp": self.me + sign * 4 * count}
        self.behind = {"dp": self.me - sign * 4 * count}
        self.works = (self.z + 1) // 2 == 1
        self.serves = (self.z + 1) // 2 != 1

    def columns(self, size):
        outer = self.z // 2 * 3
        far, far_outer = 3 - self.z, 3 - outer
        return [
            ((at_z + 2 * self.y) % 4 * 2 + at_x) * size
            for at_z in (self.z, outer, far, far_outer)
            for at_x in (self.x, 1 - self.x)
        ]

    def meet(self):
        barrier = pltpu.get_barrier_semaphore()

        def greet(partners):
            for partner in partners:
                pl.semaphore_signal(barrier, inc=1, device_id=partner, device_id_type=by_mesh)
            pl.semaphore_wait(barrier, len(partners))

        @pl.when(self.works)
        def _():
            greet((self.core, self.beside, self.over_y, self.ahead, self.behind))

        @pl.when(self.serves)
        def _():
            greet((self.core, self.beside, self.ahead))


def remote(src, dst, send, recv, where):
    return pltpu.make_async_remote_copy(
        src_ref=src,
        dst_ref=dst,
        send_sem=send,
        recv_sem=recv,
        device_id=where,
        device_id_type=by_mesh,
    )


def normed_rows(source_ref, gain_ref, gain_row, scale_ref, scale_row, out_ref, first, count):
    size = 128

    def chunk(i, carry):
        at = pl.ds(pl.multiple_of(first + i * size, size), size)
        rows = source_ref[at, :].astype(f32)
        scale = lax.rsqrt(jnp.mean(rows * rows, axis=1, keepdims=True) + norm_eps)
        scale_ref[scale_row, at, :] = jnp.broadcast_to(scale, (size, lanes))
        out_ref[at, :] = (rows * scale * gain_ref[gain_row : gain_row + 1, :]).astype(bf16)
        return carry

    lax.fori_loop(0, count // size, chunk, 0)


def forward_kernel(
    count,
    keep_ri, keep_ro, keep_mi, keep_mo, give_ri, give_ro, give_mi, give_mo,
    tokens_ref, grad_ref, mask_in, gain_ref, vec_ref, wr_ref, wi_ref,
    g_ri, g_ro, g_mi, g_mo,
    both_ref, state_ref, mixed_ref, mask_ref, middle_ref, tok_ref,
    one_mine, one_theirs, two_mine, two_theirs, low_mine, low_theirs, scale_ref,
    coef_ref, w_ri, w_ro, grad_all, part_out, part_in, part_sum, y_out, y_in, mid_ref,
    w_send, w_recv, w_local, load_sem, m_send, m_recv, m_local,
):
    at = Place(count)
    half_rows = keep_ri.shape[0]
    size = 2 * half_rows
    model = tok_ref.shape[1]
    half_model = model // 2
    rows = tokens_ref.shape[0]
    own = 2 * rows
    cols = at.columns(size)
    whole, keeps, gives = (g_ri, g_ro, g_mi, g_mo), (keep_ri, keep_ro, keep_mi, keep_mo), (
        give_ri, give_ro, give_mi, give_mo,
    )
    ri, ro, mi, mo = range(4)
    top, bottom = pl.ds(0, half_rows), pl.ds(half_rows, half_rows)
    core_rows = pl.ds(pl.multiple_of(at.c * half_rows, half_rows), half_rows)

    def hop(w, k):
        g = whole[w]
        src, dst, where = (
            (gives[w], g.at[0, core_rows], at.core),
            (g.at[0], g.at[1], at.beside),
            (g.at[0], g.at[2], at.ahead),
            (g.at[1], g.at[3], at.ahead),
            (g.at[0], g.at[4], at.ahead),
            (g.at[4], g.at[5], at.beside),
            (g.at[2], g.at[6], at.ahead),
            (g.at[3, top], g.at[7, top], at.ahead),
            (g.at[6, bottom], g.at[7, bottom], at.beside),
        )[k]
        return remote(src, dst, w_send.at[w, k], w_recv.at[w, k], where)

    def kept(w):
        return pltpu.make_async_copy(keeps[w], whole[w].at[0, core_rows], w_local.at[w])

    def begin(w):
        kept(w).start()
        hop(w, 0).start()

    def own_block(w, hops):
        kept(w).wait()
        hop(w, 0).wait()
        for k in hops:
            hop(w, k).start()

    def pass_on(w, arrived, sent):
        hop(w, arrived).wait_recv()
        hop(w, sent).start()

    def move(k, src, dst, where):
        return remote(src, dst, m_send.at[k], m_recv.at[k], where)

    first, second = pl.ds(0, rows), pl.ds(rows, rows)
    left, right = pl.ds(0, half_model), pl.ds(half_model, half_model)
    mine_rows, their_rows = pl.ds(0, own), pl.ds(own, own)
    token_in = move(0, tokens_ref, tok_ref.at[second, left], at.ahead)
    token_y = move(1, tokens_ref, tok_ref.at[first, right], at.over_y)
    token_y_two = move(2, tok_ref.at[second, left], tok_ref.at[second, right], at.over_y)
    grad_in = move(3, grad_ref, grad_all.at[second, left], at.ahead)
    grad_y = move(4, grad_ref, grad_all.at[first, right], at.over_y)
    grad_y_two = move(5, grad_all.at[second, left], grad_all.at[second, right], at.over_y)
    mask_move = move(6, mask_in, mask_ref.at[second], at.ahead)
    mask_core = move(7, mask_ref.at[mine_rows], mask_ref.at[their_rows], at.core)
    one_core = move(8, one_mine, one_theirs, at.core)
    low_core = move(9, low_mine, low_theirs, at.core)
    halves = (first, second)
    part_core = [move(10 + i, part_out.at[h], part_in.at[h], at.core) for i, h in enumerate(halves)]
    part_y = [move(12 + i, y_out.at[h], y_in.at[h], at.over_y) for i, h in enumerate(halves)]
    mid_y = [
        move(14 + i, mid_ref.at[h, left], mid_ref.at[h, right], at.over_y)
        for i, h in enumerate(halves)
    ]
    two_core = [move(16 + i, two_mine.at[h], two_theirs.at[h], at.core) for i, h in enumerate(halves)]
    token_here = pltpu.make_async_copy(tokens_ref, tok_ref.at[first, left], m_local.at[0])
    grad_here = pltpu.make_async_copy(grad_ref, grad_all.at[first, left], m_local.at[1])
    mask_here = pltpu.make_async_copy(mask_in, mask_ref.at[first], m_local.at[2])

    def load(w, target, b):
        return pltpu.make_async_copy(whole[w].at[b], target.at[b], load_sem.at[w, b])

    at.meet()

    @pl.when(at.serves)
    def _():
        mask_move.start()
        token_in.start()
        for w in (ri, ro, mi, mo):
            begin(w)
        for w in (ri, ro):
            own_block(w, (1, 2))
        for w in (ri, ro):
            pass_on(w, 1, 3)
        grad_in.start()
        for w in (mi, mo):
            own_block(w, (1, 2))
        for w in (mi, mo):
            pass_on(w, 1, 3)
        for w in (ri, ro, mi, mo):
            for k in (1, 2, 3):
                hop(w, k).wait_send()
        for moved in (mask_move, token_in, grad_in):
            moved.wait_send()

    @pl.when(at.works)
    def _():
        token_here.start()
        mask_here.start()
        token_y.start()
        begin(ri)
        begin(ro)
        grad_here.start()
        begin(mi)
        begin(mo)
        own_block(ri, (1, 4))
        own_block(ro, (1, 4))
        mask_here.wait()
        mask_move.wait_recv()
        mask_core.start()
        token_in.wait_recv()
        token_y_two.start()
        pass_on(ri, 2, 6)
        pass_on(ri, 4, 5)
        token_here.wait()
        token_y.wait_recv()
        normed_rows(tok_ref, gain_ref, 0, scale_ref, 0, one_mine, 0, rows)
        token_y_two.wait_recv()
        normed_rows(tok_ref, gain_ref, 0, scale_ref, 0, one_mine, rows, rows)
        one_core.start()
        pass_on(ro, 2, 6)
        pass_on(ro, 4, 5)
        pass_on(ri, 3, 7)
        pass_on(ri, 6, 8)
        own_block(mi, (1, 4))
        pass_on(ro, 3, 7)
        pass_on(ro, 6, 8)
        grad_y.start()
        for w, target in ((ri, w_ri), (ro, w_ro)):
            hop(w, 1).wait_recv()
            for k in (5, 7, 8):
                hop(w, k).wait_recv()
            for b in range(blocks):
                load(w, target, b).start()
        for b in range(blocks):
            load(ri, w_ri, b).wait()
        one_core.wait_recv()
        mask_core.wait_recv()

        def keep_both(start, value):
            both_ref[pl.ds(start, chunk_rows), :] = value

        project(one_mine, one_theirs, w_ri, cols, keep_both)
        grad_in.wait_recv()
        grad_y_two.start()
        recur_state(both_ref, mask_ref, vec_ref, wr_ref, wi_ref, coef_ref, state_ref)
        pass_on(mi, 2, 6)
        pass_on(mi, 4, 5)
        own_block(mo, (1, 4))
        recur_mixed(both_ref, state_ref, mixed_ref)
        for b in range(blocks):
            load(ro, w_ro, b).wait()

        def branch(start, out_ref, out_at):
            for b in range(blocks):
                out_ref[out_at, columns_at(cols, b, size)] = lax.dot_general(
                    mixed_ref[pl.ds(start, rows), :],
                    w_ro[b],
                    contract_cols,
                    preferred_element_type=f32,
                ).astype(out_ref.dtype)

        for i, h in enumerate(halves):
            branch(own + i * rows, part_out, h)
            part_core[i].start()
        for i, h in enumerate(halves):
            branch(i * rows, part_sum, first)
            part_core[i].wait_recv()
            middle_ref[h, :] = part_sum[:, left] + part_in[h, left].astype(f32)
            y_out[h, :] = (part_sum[:, right] + part_in[h, right].astype(f32)).astype(bf16)
            part_y[i].start()
        pass_on(mi, 3, 7)
        grad_here.wait()
        grad_y.wait_recv()
        grad_y_two.wait_recv()
        low_mine[...] = (grad_all[...].astype(f32) * mask_ref[mine_rows, 4:5]).astype(bf16)
        low_core.start()
        for i, h in enumerate(halves):
            part_y[i].wait_recv()
            middle = middle_ref[h, :] + y_in[h, :].astype(f32) + tok_ref[h, left].astype(f32)
            middle_ref[h, :] = middle
            mid_ref[h, left] = middle.astype(bf16)
            mid_y[i].start()
        pass_on(mi, 6, 8)
        pass_on(mo, 2, 6)
        pass_on(mo, 4, 5)
        for i, h in enumerate(halves):
            mid_y[i].wait_recv()
            normed_rows(mid_ref, gain_ref, 1, scale_ref, 1, two_mine, i * rows, rows)
            two_core[i].start()
        pass_on(mo, 3, 7)
        pass_on(mo, 6, 8)
        for w in (mi, mo):
            for k in (1, 5, 7, 8):
                hop(w, k).wait_recv()
        low_core.wait_recv()
        for moved in two_core:
            moved.wait_recv()
        for w in (ri, ro, mi, mo):
            for k in (1, 4, 5, 6, 7, 8):
                hop(w, k).wait_send()
        for moved in (
            token_y, token_y_two, grad_y, grad_y_two, mask_core, one_core, low_core,
            *part_core, *part_y, *mid_y, *two_core,
        ):
            moved.wait_send()


def recur_first(both_ref, state_ref, mask_ref, vec_ref, wr_ref, wi_ref, dmix_ref, dboth_ref, coef_ref, push_ref):
    width = dmix_ref.shape[1]
    rows = both_ref.shape[0] // held_buffers

    def first(b, carry):
        at = buffer_rows_at(b, rows)
        gate, slope = gelu_parts(both_ref[at, width:])
        d_mixed = dmix_ref[at, :]
        mask = mask_ref[at, :]
        conv_low = conv_of(both_ref[at, :width], mask, vec_ref).astype(bf16)
        rate = gates_of(conv_low, vec_ref, wr_ref, wi_ref)[0]
        store_lanes(push_ref, at, d_mixed * gate)
        dboth_ref[at, width:] = (slope * d_mixed * load_lanes(state_ref, at, width)).astype(bf16)
        store_lanes(coef_ref, at, jnp.exp(-8.0 * rate * vec_ref[7:8, :]) * mask[:, 0:1])
        return carry

    lax.fori_loop(0, held_buffers, first, 0)


def recur_last(
    both_ref, state_ref, mask_ref, vec_ref, wr_ref, wi_ref, push_ref,
    dboth_ref, sums_ref, gr_ref, gi_ref,
):
    width = both_ref.shape[1] // 2
    rows = both_ref.shape[0] // held_buffers
    sums_ref[...] = jnp.zeros_like(sums_ref)
    gr_ref[...] = jnp.zeros_like(gr_ref)
    gi_ref[...] = jnp.zeros_like(gi_ref)
    def add_sum(k, value):
        sums_ref[k : k + 1, :] += jnp.sum(value, axis=0, keepdims=True)

    def last(b, carry):
        at = buffer_rows_at(b, rows)
        inner = both_ref[at, :width]
        mask = mask_ref[at, :]
        keep = mask[:, 0:1]
        softened = vec_ref[7:8, :]
        conv = conv_of(inner, mask, vec_ref)
        conv_low = conv.astype(bf16)
        rate, igate = gates_of(conv_low, vec_ref, wr_ref, wi_ref)
        d_push = load_lanes(push_ref, at, width)
        decay = jnp.exp(-8.0 * rate * softened)
        square = 1.0 - decay * decay + root_eps
        root = jnp.sqrt(square)
        d_root = d_push * igate * conv
        d_igate = d_push * root * conv
        before = shifted(load_lanes(state_ref, at, width), 1) * keep
        d_decay = d_push * before - d_root * decay / root
        d_log = d_decay * decay
        slow = d_log * rate
        d_pre_recur = (-8.0 * softened) * slow * (1.0 - rate)
        d_pre_input = d_igate * igate * (1.0 - igate)
        add_sum(7, slow)
        add_sum(5, d_pre_recur)
        add_sum(6, d_pre_input)
        low_recur = d_pre_recur.astype(bf16)
        low_input = d_pre_input.astype(bf16)
        gr_ref[...] += lax.dot_general(
            conv_low, low_recur, contract_rows, preferred_element_type=f32
        )
        gi_ref[...] += lax.dot_general(
            conv_low, low_input, contract_rows, preferred_element_type=f32
        )
        d_conv = d_push * root * igate
        d_conv = d_conv + lax.dot_general(
            low_recur, wr_ref[...], contract_cols, preferred_element_type=f32
        )
        d_conv = d_conv + lax.dot_general(
            low_input, wi_ref[...], contract_cols, preferred_element_type=f32
        )
        add_sum(4, d_conv)
        add_sum(0, d_conv * inner)
        d_inner = vec_ref[0:1, :] * d_conv
        for k in range(1, 4):
            kept = d_conv * mask[:, k : k + 1]
            add_sum(k, kept * shifted(inner, k))
            d_inner = d_inner + vec_ref[k : k + 1, :] * shifted(kept, -k)
        dboth_ref[at, :width] = d_inner.astype(bf16)
        return carry

    lax.fori_loop(0, held_buffers, last, 0)


def mlp_forward(mine_ref, theirs_ref, gate_weight, up_weight, cols_ref, act_ref, slope_ref, value_ref):
    size = gate_weight.shape[1]
    own = mine_ref.shape[0]
    for part, ref in enumerate((mine_ref, theirs_ref)):

        def chunk(i, carry, part=part, ref=ref):
            rows = gathered(
                ref, pl.ds(pl.multiple_of(i * chunk_rows, chunk_rows), chunk_rows), cols_ref, size
            )
            gate = jnp.dot(rows, stacked(gate_weight), preferred_element_type=f32)
            up = jnp.dot(rows, stacked(up_weight), preferred_element_type=f32)
            value, slope = gelu_parts(gate)
            at = pl.ds(pl.multiple_of(part * own + i * chunk_rows, chunk_rows), chunk_rows)
            act_ref[at, :] = (value * up).astype(bf16)
            slope_ref[at, :] = (slope * up).astype(bf16)
            value_ref[at, :] = value.astype(bf16)
            return carry

        lax.fori_loop(0, own // chunk_rows, chunk, 0)


def mlp_backward(mine_ref, theirs_ref, weight_ref, cols_ref, slope_ref, value_ref, d_gate_ref, d_up_ref):
    def use(start, d_act):
        at = pl.ds(start, chunk_rows)
        d_gate_ref[at, :] = (d_act * slope_ref[at, :].astype(f32)).astype(bf16)
        d_up_ref[at, :] = (d_act * value_ref[at, :].astype(f32)).astype(bf16)

    project(mine_ref, theirs_ref, weight_ref, cols_ref, use)


def rows_back(part_tiles, *refs):
    count = len(part_tiles)
    row_refs, (weight_ref, cols_ref, out_ref, total_ref) = refs[:count], refs[count:]
    size = weight_ref.shape[1]
    step = pl.program_id(0)

    @pl.when(step == 0)
    def _():
        total_ref[...] = jnp.zeros_like(total_ref)

    first = 0
    for tiles, row_ref in zip(part_tiles, row_refs):

        @pl.when((step >= first) & (step < first + tiles))
        def _(row_ref=row_ref):
            for b in range(blocks):
                total_ref[:, columns_at(cols_ref, b, size)] += lax.dot_general(
                    row_ref[...], weight_ref[b], contract_cols, preferred_element_type=f32
                )

        first += tiles

    @pl.when(step == first - 1)
    def _():
        out_ref[...] = total_ref[...].astype(out_ref.dtype)


def weight_partial(part_tiles, mine_ref, theirs_ref, cols_ref, *refs):
    count = len(part_tiles)
    column_refs, out_ref = refs[:count], refs[count]
    size = out_ref.shape[1]
    own = mine_ref.shape[0]
    step = pl.program_id(0)
    first = 0
    for tiles, column_ref in zip(part_tiles, column_refs):

        @pl.when((step >= first) & (step < first + tiles))
        def _(column_ref=column_ref):
            for b in range(blocks):
                at = columns_at(cols_ref, b, size)
                total = lax.dot_general(
                    mine_ref[:, at], column_ref[:own, :], contract_rows, preferred_element_type=f32
                )
                total = total + lax.dot_general(
                    theirs_ref[:, at], column_ref[own:, :], contract_rows, preferred_element_type=f32
                )
                out_ref[b] = total.astype(bf16)

        first += tiles


class Sums:
    def __init__(self, at, partial, land, total, send, recv):
        self.at, self.partial, self.land, self.total = at, partial, land, total
        self.send, self.recv = send, recv
        self.half_rows = total.shape[1]
        self.top = pl.ds(0, self.half_rows)
        self.bottom = pl.ds(self.half_rows, self.half_rows)

    def rows_of(self, c):
        return pl.ds(pl.multiple_of(c * self.half_rows, self.half_rows), self.half_rows)

    def hop(self, k, last=None):
        d, land, at, top, bottom = self.partial, self.land, self.at, self.top, self.bottom
        src, dst, where = (
            lambda: (d.at[5], land.at[0], at.beside),
            lambda: (d.at[7, bottom], land.at[1, top], at.beside),
            lambda: (d.at[7, top], land.at[1, bottom], at.ahead),
            lambda: (d.at[6, top], land.at[2, top], at.ahead),
            lambda: (land.at[1, top], land.at[2, bottom], at.ahead),
            lambda: (d.at[3, bottom], land.at[0, bottom], at.behind),
            lambda: (land.at[1, bottom], land.at[0, top], at.behind),
            lambda: (d.at[1], land.at[3], at.beside),
            lambda: (land.at[0], land.at[4], at.ahead),
            lambda: (land.at[2], land.at[2], at.behind),
            lambda: (land.at[0], land.at[3], at.beside),
            lambda: (last.at[self.rows_of(1 - at.c)], self.total.at[1], at.core),
        )[k]()
        return remote(src, dst, self.send.at[k], self.recv.at[k], where)

    def start(self, *hops):
        for k in hops:
            self.hop(k).start()

    def received(self, *hops):
        for k in hops:
            self.hop(k).wait_recv()

    def sent(self, *hops):
        for k in hops:
            self.hop(k).wait_send()

    def step(self, k, add):
        d, land, top, bottom = self.partial, self.land, self.top, self.bottom
        if k == 4:
            self.received(1)
            add(land.at[1, top], d.at[6, bottom])
        elif k == 6:
            self.received(2)
            add(land.at[1, bottom], d.at[3, top])
        elif k == 8:
            self.received(0)
            add(land.at[0], d.at[4])
        elif k == 9:
            self.received(3, 4)
            add(land.at[2], d.at[2])
        self.start(k)


work_hops, serve_hops = (0, 1, 2, 3, 4, 5, 6, 7, 8, 9), (10,)


def add_rows(into, value, other=None):
    size = 32

    def chunk(i, carry):
        at = pl.ds(pl.multiple_of(i * size, size), size)
        total = into[at, :].astype(f32) + value[at, :].astype(f32)
        if other is not None:
            total = total + other[at, :].astype(f32)
        into[at, :] = total.astype(bf16)
        return carry

    lax.fori_loop(0, into.shape[0] // size, chunk, 0)


def norm_sums(e_ref, y_in, source_ref, gain_ref, gain_row, mean_ref, first, count):
    size, half = 64, e_ref.shape[1]

    def chunk(i, carry):
        at = pl.ds(pl.multiple_of(first + i * size, size), size)
        e = e_ref[at, :] + y_in[at, :].astype(f32)
        e_ref[at, :] = e
        source = source_ref[at, :half].astype(bf16).astype(f32)
        part = jnp.sum(e * gain_ref[gain_row : gain_row + 1, :half] * source, axis=1, keepdims=True)
        mean_ref[at, :] = jnp.broadcast_to(part, (size, lanes))
        return carry

    lax.fori_loop(0, count // size, chunk, 0)


def norm_rows_back(
    e_ref, source_ref, gain_ref, gain_row, scale_ref, mean_ref, mean_in, term_ref, model, first, count, use
):
    size, half = 64, e_ref.shape[1]

    def chunk(i, carry):
        at = pl.ds(pl.multiple_of(first + i * size, size), size)
        e = e_ref[at, :]
        source = source_ref[at, :half].astype(bf16).astype(f32)
        scale = scale_ref[gain_row, at, 0:1]
        inner = (mean_ref[at, 0:1] + mean_in[at, 0:1]) / model
        weighted = e * gain_ref[gain_row : gain_row + 1, :half]
        term_ref[gain_row : gain_row + 1, :] += jnp.sum(e * source * scale, axis=0, keepdims=True)
        use(at, scale * weighted - source * (scale * scale * scale * inner))
        return carry

    lax.fori_loop(0, count // size, chunk, 0)


def backward_kernel(
    count,
    d_mi, d_mo, e_theirs, e_mine, o_theirs, o_mine, low_ref,
    middle_ref, scale_ref, gain_ref, w_ro, both_ref, state_ref, mask_ref, vec_ref, wr_ref, wi_ref,
    land_mi, land_mo, total_mi, total_mo,
    out_ref, dmid_ref, db_mine, db_theirs, dboth_ref, sums_ref, gr_ref, gi_ref, term_ref,
    coef_ref, push_ref, dmix_ref, part_in, o_in, part_sum, y_out, y_in, oy_out, oy_in,
    mean_ref, mean_in, stage_a, stage_b,
    w_send, w_recv, m_send, m_recv, local_sem,
):
    at = Place(count)
    size = w_ro.shape[1]
    cols = at.columns(size)
    own, half_model = middle_ref.shape
    e_ref, low_left = dmid_ref, y_out
    model = 2 * half_model
    rows = own // 2
    mi = Sums(at, d_mi, land_mi, total_mi, w_send.at[0], w_recv.at[0])
    mo = Sums(at, d_mo, land_mo, total_mo, w_send.at[1], w_recv.at[1])
    first, second = pl.ds(0, rows), pl.ds(rows, rows)
    left, right = pl.ds(0, half_model), pl.ds(half_model, half_model)
    halves = (first, second)

    def move(k, src, dst, where):
        return remote(src, dst, m_send.at[k], m_recv.at[k], where)

    e_core = [move(i, e_theirs.at[h], part_in.at[h], at.core) for i, h in enumerate(halves)]
    o_core = [move(2 + i, o_theirs.at[h], o_in.at[h], at.core) for i, h in enumerate(halves)]
    e_y = [move(4 + i, y_out.at[h], y_in.at[h], at.over_y) for i, h in enumerate(halves)]
    o_y = [move(6 + i, oy_out.at[h], oy_in.at[h], at.over_y) for i, h in enumerate(halves)]
    mean_y = move(8, mean_ref, mean_in, at.over_y)
    db_y = [
        move(9 + i, db_mine.at[h, left], db_mine.at[h, right], at.over_y)
        for i, h in enumerate(halves)
    ]
    db_core = [move(11 + i, db_mine.at[h], db_theirs.at[h], at.core) for i, h in enumerate(halves)]
    out_move = move(13, out_ref.at[second], out_ref.at[first], at.behind)
    low_load = pltpu.make_async_copy(low_ref.at[:, left], low_left, local_sem.at[0])

    def fetch(src, dst, k):
        return pltpu.make_async_copy(src, dst, local_sem.at[k])

    def add(into, value):
        count_rows, width = into.shape
        a = stage_a.at[pl.ds(0, count_rows), pl.ds(0, width)]
        b = stage_b.at[pl.ds(0, count_rows), pl.ds(0, width)]
        loads = fetch(into, a, 1), fetch(value, b, 2)
        for v in loads:
            v.start()
        for v in loads:
            v.wait()
        add_rows(a, b)
        back = fetch(a, into, 3)
        back.start()
        back.wait()

    def finish(w, parts):
        count_rows, width = parts[0].shape
        a = stage_a.at[pl.ds(0, count_rows), pl.ds(0, width)]
        b = stage_b.at[pl.ds(0, count_rows), pl.ds(0, width)]
        loads = fetch(parts[0], a, 1), fetch(parts[1], b, 2)
        for v in loads:
            v.start()
        for v in loads:
            v.wait()
        add_rows(a, b)
        if len(parts) == 3:
            third = fetch(parts[2], b, 2)
            third.start()
            third.wait()
            add_rows(a, b)
        w.hop(11, a).start()
        kept = fetch(a.at[w.rows_of(at.c)], w.total.at[0], 3)
        kept.start()
        kept.wait()
        w.hop(11, a).wait()

    def part_fetch(source, h):
        return fetch(source.at[h], part_sum, 4)

    def join(i, h, source, arrived, landed, keep_value, sent_ref, over):
        part_fetch(source, h).wait()
        arrived[i].wait_recv()
        keep_value(i, part_sum[:, left] + landed[h, left].astype(f32))
        sent_ref[h, :] = (part_sum[:, right] + landed[h, right].astype(f32)).astype(bf16)
        over[i].start()

    def keep_e(i, value):
        e_ref[halves[i], :] = value

    def o_place(i, k):
        return k // 2, pl.ds(k % 2 * own + i * rows, rows)

    def keep_o(i, value):
        for k in range(half_model // lanes):
            chunk, o_rows = o_place(i, k)
            coef_ref[chunk, o_rows, :] = value[:, k * lanes : (k + 1) * lanes]

    def kept_o(i):
        parts = []
        for k in range(half_model // lanes):
            chunk, o_rows = o_place(i, k)
            parts.append(coef_ref[chunk, o_rows, :])
        return jnp.concatenate(parts, axis=1)

    at.meet()

    @pl.when(at.serves)
    def _():
        for w in (mo, mi):
            w.received(5, 6)
            w.start(10)
        for w in (mo, mi):
            w.received(9, 10)
            finish(w, (w.land.at[2], w.land.at[3]))
        out_move.wait_recv()
        for w in (mo, mi):
            w.sent(*serve_hops)

    @pl.when(at.works)
    def _():
        for moved in e_core:
            moved.start()
        part_fetch(e_mine, first).start()
        for w in (mo, mi):
            w.start(1, 2, 0, 3, 5, 7)
        term_ref[...] = jnp.zeros_like(term_ref)
        join(0, first, e_mine, e_core, part_in, keep_e, y_out, e_y)
        part_fetch(e_mine, second).start()
        join(1, second, e_mine, e_core, part_in, keep_e, y_out, e_y)
        part_fetch(o_mine, first).start()
        for moved in o_core:
            moved.start()
        mo.step(4, add)
        mo.step(6, add)
        join(0, first, o_mine, o_core, o_in, keep_o, oy_out, o_y)
        part_fetch(o_mine, second).start()
        join(1, second, o_mine, o_core, o_in, keep_o, oy_out, o_y)
        for i, h in enumerate(halves):
            e_y[i].wait_recv()
            norm_sums(e_ref, y_in, middle_ref, gain_ref, 1, mean_ref, i * rows, rows)
        mean_y.start()
        for moved in e_y:
            moved.wait_send()
        low_load.start()
        mo.step(8, add)
        low_load.wait()
        mean_y.wait_recv()

        def keep(row_at, back):
            d_middle = back + low_left[row_at, :].astype(f32)
            dmid_ref[row_at, :] = d_middle
            db_mine[row_at, left] = d_middle.astype(bf16)

        for i in range(2):
            norm_rows_back(
                e_ref, middle_ref, gain_ref, 1, scale_ref, mean_ref, mean_in, term_ref, model,
                i * rows, rows, keep,
            )
            db_y[i].start()
        mo.step(9, add)
        mi.step(6, add)
        mi.step(4, add)
        for i, h in enumerate(halves):
            o_y[i].wait_recv()
            out_ref[h, :] = (
                mask_ref[h, 4:5]
                * (middle_ref[h, :] + kept_o(i) + oy_in[h, :].astype(f32))
            ).astype(bf16)
        out_move.start()
        for i in range(2):
            db_y[i].wait_recv()
            db_core[i].start()
        for i in range(2):
            db_core[i].wait_recv()

        def keep_mixed(start, value):
            dmix_ref[pl.ds(start, chunk_rows), :] = value

        project(db_mine, db_theirs, w_ro, cols, keep_mixed)
        recur_first(
            both_ref, state_ref, mask_ref, vec_ref, wr_ref, wi_ref, dmix_ref, dboth_ref, coef_ref, push_ref
        )
        mi.step(8, add)
        scan_rows(coef_ref, push_ref, both_ref.shape[0] // held_buffers, True)
        mi.step(9, add)
        recur_last(
            both_ref, state_ref, mask_ref, vec_ref, wr_ref, wi_ref, push_ref,
            dboth_ref, sums_ref, gr_ref, gi_ref,
        )
        for w in (mo, mi):
            w.received(7, 8)
            finish(w, (w.partial.at[0], w.land.at[3], w.land.at[4]))
        for w in (mo, mi):
            w.sent(*work_hops)
        for moved in (*e_core, *o_core, *o_y, mean_y, *db_y, *db_core, out_move):
            moved.wait_send()


def finish_kernel(
    count,
    one_mine, one_theirs, db_mine, db_theirs, dboth_ref, mixed_ref, w_ri, tok_ref, scale_ref, gain_ref,
    dmid_ref, sums_ref, gates_ref, term_in,
    total_ri, total_ro, out_ref, gates_out, sums_out, term_out,
    d_ri, d_ro, land_ri, land_ro, tok_left, part_out, part_in, part_sum, y_out, y_in, e_ref,
    mean_ref, mean_in, last_ri, last_ro, gates_in, sums_in, term_ref, term_land,
    w_send, w_recv, m_send, m_recv, local_sem,
):
    at = Place(count)
    size = w_ri.shape[1]
    cols = at.columns(size)
    own, half_model = dmid_ref.shape
    model = 2 * half_model
    rows = own // 2
    ri = Sums(at, d_ri, land_ri, total_ri, w_send.at[0], w_recv.at[0])
    ro = Sums(at, d_ro, land_ro, total_ro, w_send.at[1], w_recv.at[1])
    first, second = pl.ds(0, rows), pl.ds(rows, rows)
    left, right = pl.ds(0, half_model), pl.ds(half_model, half_model)
    halves = (first, second)

    def move(k, src, dst, where):
        return remote(src, dst, m_send.at[k], m_recv.at[k], where)

    e_core = [move(i, part_out.at[h], part_in.at[h], at.core) for i, h in enumerate(halves)]
    e_y = [move(2 + i, y_out.at[h], y_in.at[h], at.over_y) for i, h in enumerate(halves)]
    mean_y = move(4, mean_ref, mean_in, at.over_y)
    out_move = move(5, out_ref.at[second], out_ref.at[first], at.behind)
    gates_x = move(6, gates_ref, gates_in.at[0], at.beside)
    gates_z = move(7, gates_in.at[0], gates_in.at[1], at.ahead)
    gates_end = move(8, gates_out.at[0], gates_out.at[0], at.behind)
    gates_core = move(9, gates_out.at[0], gates_out.at[1], at.core)
    sums_x = move(10, sums_ref, sums_in.at[0], at.beside)
    sums_z = move(11, sums_in.at[0], sums_in.at[1], at.ahead)
    sums_end = move(12, sums_out.at[0], sums_out.at[0], at.behind)
    sums_core = move(13, sums_out.at[0], sums_out.at[1], at.core)
    term_x = move(14, term_ref, term_land.at[0], at.beside)
    term_z = move(15, term_land.at[0], term_land.at[1], at.ahead)
    term_core = move(16, term_land.at[1], term_land.at[2], at.core)
    term_end = move(17, term_out, term_out, at.behind)
    tok_load = pltpu.make_async_copy(tok_ref.at[:, left], tok_left, local_sem.at[0])

    def add(into, value):
        add_rows(into, value)

    def finish(w, last, parts):
        last[...] = parts[0][...]
        add_rows(last, parts[1], parts[2] if len(parts) == 3 else None)
        w.hop(11, last).start()
        w.total[0] = last[w.rows_of(at.c), :]

    at.meet()

    @pl.when(at.serves)
    def _():
        for w in (ro, ri):
            w.received(5, 6)
            w.start(10)
        sums_end.wait_recv()
        sums_core.start()
        gates_end.wait_recv()
        gates_core.start()
        for w, last in ((ro, last_ro), (ri, last_ri)):
            w.received(9, 10)
            finish(w, last, (w.land.at[2], w.land.at[3]))
        for w, last in ((ro, last_ro), (ri, last_ri)):
            w.hop(11, last).wait()
            w.sent(*serve_hops)
        out_move.wait_recv()
        term_end.wait_recv()
        sums_core.wait()
        gates_core.wait()

    @pl.when(at.works)
    def _():
        tok_load.start()
        gates_x.start()
        sums_x.start()

        def partial(b):
            here = columns_at(cols, b, size)

            def product(mine_ref, theirs_ref, column_ref):
                total = lax.dot_general(
                    mine_ref[:, here], column_ref[:own, :], contract_rows, preferred_element_type=f32
                )
                total = total + lax.dot_general(
                    theirs_ref[:, here], column_ref[own:, :], contract_rows, preferred_element_type=f32
                )
                return total.astype(bf16)

            d_ro[b] = product(db_mine, db_theirs, mixed_ref)
            d_ri[b] = product(one_mine, one_theirs, dboth_ref)

        for b, hops in ((7, (1, 2)), (5, (0,)), (6, (3,)), (3, (5,)), (1, (7,))):
            partial(b)
            for w in (ro, ri):
                w.start(*hops)

        def back(start, out, out_at):
            for b in range(blocks):
                out[out_at, columns_at(cols, b, size)] = lax.dot_general(
                    dboth_ref[pl.ds(start, rows), :], w_ri[b], contract_cols, preferred_element_type=f32
                ).astype(out.dtype)

        for i, h in enumerate(halves):
            back(own + i * rows, part_out, h)
            e_core[i].start()
        for b in (4, 2, 0):
            partial(b)
        for w in (ro, ri):
            w.step(4, add)
            w.step(6, add)
            w.step(8, add)
        for i, h in enumerate(halves):
            back(i * rows, part_sum, first)
            e_core[i].wait_recv()
            e_ref[h, :] = part_sum[:, left] + part_in[h, left].astype(f32)
            y_out[h, :] = (part_sum[:, right] + part_in[h, right].astype(f32)).astype(bf16)
            e_y[i].start()
        sums_x.wait_recv()
        sums_in[0] = sums_in[0] + sums_ref[...]
        sums_z.start()
        gates_x.wait_recv()
        for k in range(2):
            add_rows(gates_in.at[0, k], gates_ref.at[k])
        gates_z.start()
        for w in (ro, ri):
            w.step(9, add)
        sums_z.wait_recv()
        sums_out[0] = sums_in[0] + sums_in[1]
        sums_end.start()
        sums_core.start()
        gates_z.wait_recv()
        for k in range(2):
            gates_out[0, k] = gates_in[0, k]
            add_rows(gates_out.at[0, k], gates_in.at[1, k])
        gates_end.start()
        gates_core.start()
        term_ref[...] = term_in[...]
        tok_load.wait()
        for i in range(2):
            e_y[i].wait_recv()
            norm_sums(e_ref, y_in, tok_left, gain_ref, 0, mean_ref, i * rows, rows)
        mean_y.start()
        for w, last in ((ro, last_ro), (ri, last_ri)):
            w.received(7, 8)
            finish(w, last, (w.partial.at[0], w.land.at[3], w.land.at[4]))
        mean_y.wait_recv()

        def keep(row_at, value):
            out_ref[row_at, :] = (value + dmid_ref[row_at, :]).astype(bf16)

        for i in (1, 0):
            norm_rows_back(
                e_ref, tok_left, gain_ref, 0, scale_ref, mean_ref, mean_in, term_ref, model,
                i * rows, rows, keep,
            )
            if i == 1:
                out_move.start()
        term_x.start()
        term_x.wait_recv()
        term_land[0] = term_land[0] + term_ref[...]
        term_z.start()
        term_z.wait_recv()
        term_land[1] = term_land[0] + term_land[1]
        term_core.start()
        term_core.wait_recv()
        term_out[...] = term_land[1] + term_land[2]
        term_end.start()
        for w, last in ((ro, last_ro), (ri, last_ri)):
            w.hop(11, last).wait()
            w.sent(*work_hops)
        sums_core.wait_recv()
        gates_core.wait_recv()
        for moved in (
            *e_core, *e_y, mean_y, out_move, gates_x, gates_z, gates_end, gates_core,
            sums_x, sums_z, sums_end, sums_core, term_x, term_z, term_core, term_end,
        ):
            moved.wait_send()


in_vmem = pl.BlockSpec(memory_space=pltpu.VMEM)
in_smem = pl.BlockSpec(memory_space=pltpu.SMEM)
in_any = pl.BlockSpec(memory_space=pl.ANY)
no_cost = pl.CostEstimate(flops=0, bytes_accessed=0, transcendentals=0)
kernel_params = pltpu.CompilerParams(vmem_limit_bytes=60 * 2**20)
copy_sem = pltpu.SemaphoreType.DMA


def lane_shape(rows, width):
    return (pl.cdiv(width, lanes), rows, lanes)


def run_forward(count, keeps, gives, tokens, out_grad, mask, gains, vectors, wr, wi):
    rows, half_model = tokens.shape
    own, model, width = 2 * rows, 2 * half_model, wr.shape[0]
    size = 2 * keeps[0].shape[0]
    shape = jax.ShapeDtypeStruct
    gathered_shapes = [shape((blocks, size, v.shape[1]), bf16) for v in keeps]
    wide = shape((own, model), bf16)
    return pl.pallas_call(
        functools.partial(forward_kernel, count),
        out_shape=(
            *gathered_shapes,
            shape((2 * own, 2 * width), f32),
            shape(lane_shape(2 * own, width), f32),
            shape((2 * own, width), bf16),
            shape((2 * own, lanes), f32),
            shape((own, half_model), f32),
            *[wide] * 7,
            shape((2, own, lanes), f32),
        ),
        in_specs=[in_any] * 11 + [in_vmem] * 4,
        out_specs=[in_any] * 4 + [in_vmem] * 13,
        scratch_shapes=[
            pltpu.VMEM(lane_shape(2 * own, width), f32),
            pltpu.VMEM((blocks, size, 2 * width), bf16),
            pltpu.VMEM((blocks, size, width), bf16),
            pltpu.VMEM((own, model), bf16),
            pltpu.VMEM((own, model), bf16),
            pltpu.VMEM((own, model), bf16),
            pltpu.VMEM((rows, model), f32),
            pltpu.VMEM((own, half_model), bf16),
            pltpu.VMEM((own, half_model), bf16),
            pltpu.VMEM((own, model), bf16),
            copy_sem((4, 9)),
            copy_sem((4, 9)),
            copy_sem((4,)),
            copy_sem((2, blocks)),
            copy_sem((18,)),
            copy_sem((18,)),
            copy_sem((3,)),
        ],
        compiler_params=comm_params(0),
        cost_estimate=no_cost,
        name="gather_and_recur",
    )(*keeps, *gives, tokens, out_grad, mask, gains, vectors, wr, wi)


def comm_params(collective):
    return pltpu.CompilerParams(
        vmem_limit_bytes=63 * 2**20, collective_id=collective, has_side_effects=True
    )


def run_backward(
    count, partials, e_parts, o_parts, low, middle, scales, gains, weight, both, state, mask, vectors, wr, wi
):
    own, half_model = middle.shape
    model, width, rows = 2 * half_model, wr.shape[0], own // 2
    size = weight.shape[1]
    shape = jax.ShapeDtypeStruct
    hidden = [v.shape[2] for v in partials]
    square = shape((width, width), f32)
    wide = shape((own, model), bf16)
    return pl.pallas_call(
        functools.partial(backward_kernel, count),
        out_shape=(
            *[shape((5, size, n), bf16) for n in hidden],
            *[shape((2, size // 2, n), bf16) for n in hidden],
            shape((own, half_model), bf16),
            shape((own, half_model), f32),
            wide,
            wide,
            shape((2 * own, 2 * width), bf16),
            shape((8, width), f32),
            square,
            square,
            shape((8, half_model), f32),
        ),
        in_specs=[in_any] * 7 + [in_vmem] * 10,
        out_specs=[in_any] * 4 + [in_vmem] * 9,
        scratch_shapes=[
            pltpu.VMEM(lane_shape(2 * own, width), f32),
            pltpu.VMEM(lane_shape(2 * own, width), f32),
            pltpu.VMEM((2 * own, width), f32),
            pltpu.VMEM((own, model), bf16),
            pltpu.VMEM((own, model), bf16),
            pltpu.VMEM((rows, model), f32),
            *[pltpu.VMEM((own, half_model), bf16)] * 4,
            pltpu.VMEM((own, lanes), f32),
            pltpu.VMEM((own, lanes), f32),
            pltpu.VMEM((size, max(hidden)), bf16),
            pltpu.VMEM((size, max(hidden)), bf16),
            copy_sem((2, 12)),
            copy_sem((2, 12)),
            copy_sem((14,)),
            copy_sem((14,)),
            copy_sem((5,)),
        ],
        compiler_params=comm_params(1),
        cost_estimate=no_cost,
        name="sum_and_recur_back",
    )(*partials, *e_parts, *o_parts, low, middle, scales, gains, weight, both, state, mask, vectors, wr, wi)


def run_finish(
    count, normed, d_branch, d_both, mixed, weight, tokens, scales, gains, d_middle, sums, gates, term
):
    own, half_model = d_middle.shape
    model, rows = 2 * half_model, own // 2
    size = weight.shape[1]
    widths = [weight.shape[2], mixed.shape[1]]
    shape = jax.ShapeDtypeStruct
    return pl.pallas_call(
        functools.partial(finish_kernel, count),
        out_shape=(
            *[shape((2, size // 2, n), bf16) for n in widths],
            shape((own, half_model), bf16),
            shape((2, *gates.shape), bf16),
            shape((2, *sums.shape), f32),
            shape(term.shape, f32),
        ),
        in_specs=[in_vmem] * 7 + [in_any] + [in_vmem] * 6,
        out_specs=[in_vmem] * 6,
        scratch_shapes=[
            *[pltpu.VMEM((blocks, size, n), bf16) for n in widths],
            *[pltpu.VMEM((5, size, n), bf16) for n in widths],
            pltpu.VMEM((own, half_model), bf16),
            pltpu.VMEM((own, model), bf16),
            pltpu.VMEM((own, model), bf16),
            pltpu.VMEM((rows, model), f32),
            pltpu.VMEM((own, half_model), bf16),
            pltpu.VMEM((own, half_model), bf16),
            pltpu.VMEM((own, half_model), f32),
            pltpu.VMEM((own, lanes), f32),
            pltpu.VMEM((own, lanes), f32),
            *[pltpu.VMEM((size, n), bf16) for n in widths],
            pltpu.VMEM((2, *gates.shape), bf16),
            pltpu.VMEM((2, *sums.shape), f32),
            pltpu.VMEM(term.shape, f32),
            pltpu.VMEM((3, *term.shape), f32),
            copy_sem((2, 12)),
            copy_sem((2, 12)),
            copy_sem((18,)),
            copy_sem((18,)),
            copy_sem((1,)),
        ],
        compiler_params=comm_params(2),
        cost_estimate=no_cost,
        name="sum_and_finish",
    )(*normed, *d_branch, d_both, mixed, weight, tokens, scales, gains, d_middle, sums, gates, term)


def run_mlp_forward(normed, weight, cols):
    own, model = normed[0].shape
    size, hidden = weight.shape[1], weight.shape[2] // 2
    tile = 256
    tiles = hidden // tile
    out = jax.ShapeDtypeStruct((2 * own, hidden), bf16)
    return pl.pallas_call(
        mlp_forward,
        grid=(tiles,),
        out_shape=(out, out, out),
        in_specs=[pl.BlockSpec((own, model), lambda n: (0, 0))] * 2
        + [pl.BlockSpec((blocks, size, tile), lambda n: (0, 0, n))]
        + [pl.BlockSpec((blocks, size, tile), lambda n: (0, 0, n + tiles))]
        + [in_smem],
        out_specs=[pl.BlockSpec((2 * own, tile), lambda n: (0, n))] * 3,
        compiler_params=kernel_params,
        cost_estimate=no_cost,
        name="mlp_forward",
    )(*normed, weight, weight, cols)


def run_mlp_backward(grad_low, weight, cols, slope, value):
    own, model = grad_low[0].shape
    size, hidden = weight.shape[1:]
    tile = 256
    out = jax.ShapeDtypeStruct((2 * own, hidden), bf16)
    column = pl.BlockSpec((2 * own, tile), lambda n: (0, n))
    return pl.pallas_call(
        mlp_backward,
        grid=(hidden // tile,),
        out_shape=(out, out),
        in_specs=[pl.BlockSpec((own, model), lambda n: (0, 0))] * 2
        + [pl.BlockSpec((blocks, size, tile), lambda n: (0, 0, n))]
        + [in_smem, column, column],
        out_specs=[column, column],
        compiler_params=kernel_params,
        cost_estimate=no_cost,
        name="mlp_backward",
    )(*grad_low, weight, cols, slope, value)


def tile_of(width):
    return 512 if width % 512 == 0 else width


def part_specs(parts, rows, row_block, tile):
    specs, tiles, first = [], [], 0
    for part in parts:
        count = part.shape[1] // tile

        def index(n, first=first, count=count):
            return (row_block, jnp.clip(n - first, 0, count - 1))

        specs.append(pl.BlockSpec((rows, tile), index))
        tiles.append(count)
        first += count
    return specs, tuple(tiles)


def run_rows_back(name, parts, weight, cols, row_block, dtype):
    own = parts[0].shape[0] // 2
    size = weight.shape[1]
    tile = tile_of(parts[0].shape[1])
    specs, tiles = part_specs(parts, own, row_block, tile)
    return pl.pallas_call(
        functools.partial(rows_back, tiles),
        grid=(sum(tiles),),
        out_shape=jax.ShapeDtypeStruct((own, size * blocks), dtype),
        in_specs=specs
        + [pl.BlockSpec((blocks, size, tile), lambda n: (0, 0, n)), in_smem],
        out_specs=pl.BlockSpec((own, size * blocks), lambda n: (0, 0)),
        scratch_shapes=[pltpu.VMEM((own, size * blocks), f32)],
        compiler_params=kernel_params,
        cost_estimate=no_cost,
        name=name,
    )(*parts, weight, cols)


def run_weight_partial(name, rows, parts, cols):
    own, model = rows[0].shape
    size = model // blocks
    tile = tile_of(parts[0].shape[1])
    specs, tiles = part_specs(parts, 2 * own, 0, tile)
    return pl.pallas_call(
        functools.partial(weight_partial, tiles),
        grid=(sum(tiles),),
        out_shape=jax.ShapeDtypeStruct((blocks, size, sum(tiles) * tile), bf16),
        in_specs=[pl.BlockSpec((own, model), lambda n: (0, 0))] * 2 + [in_smem] + specs,
        out_specs=pl.BlockSpec((blocks, size, tile), lambda n: (0, 0, n)),
        compiler_params=kernel_params,
        cost_estimate=no_cost,
        name=name,
    )(*rows, cols, *parts)


def block_diagonal(blocks):
    count, size = blocks.shape[0], blocks.shape[1]
    rows = [
        jnp.pad(blocks[h], ((0, 0), (h * size, (count - 1 - h) * size))) for h in range(count)
    ]
    return jnp.concatenate(rows, axis=0)


def diagonal_blocks(square, count):
    size = square.shape[0] // count
    return jnp.stack(
        [square[h * size : (h + 1) * size, h * size : (h + 1) * size] for h in range(count)]
    )


def masks_of(lengths, rows):
    ends = jnp.cumsum(lengths, axis=1)
    starts = ends - lengths
    places = jnp.arange(rows, dtype=jnp.int32)[None, :, None]
    inside = (places >= starts[:, None, :]) & (places < ends[:, None, :])
    first_place = jnp.sum(jnp.where(inside, starts[:, None, :], 0), axis=2)
    places = places[:, :, 0]
    live = (places < ends[:, 2:3]).astype(f32)
    columns = [(places != first_place).astype(f32)]
    for k in range(1, 4):
        columns.append((places - k >= first_place).astype(f32))
    columns += [live] + [jnp.zeros_like(live)] * 3
    return jnp.stack(columns, axis=2).reshape(lengths.shape[0] * rows, 8), live


def local(
    n_dp,
    tokens,
    gain_rnn,
    rnn_in,
    gate_recur,
    gate_input,
    bias_recur,
    bias_input,
    decay_param,
    conv_weight,
    conv_bias,
    rnn_out,
    gain_mlp,
    mlp_in,
    mlp_out,
    lengths,
    out_grad,
):
    outer_count = n_dp // 16
    rows_here = rnn_in.shape[0]
    model = gain_rnn.shape[0]
    half_model = model // 2
    buffer_rows = tokens.shape[0]
    own_rows = 2 * buffer_rows
    index = lax.axis_index("dp")
    y = lax.axis_index("mp")
    c = index // outer_count % 2
    x = index // (2 * outer_count) % 2
    z = index // (4 * outer_count)
    outer = jnp.where(z < 2, 0, 3)
    far = 3 - z
    far_outer = 3 - outer

    def pick_c(first, second):
        return jnp.where(c == 0, first, second)

    def pick_y(first, second):
        return jnp.where(y == 0, first, second)

    group_rows = outer_count * rows_here
    block_rows = 2 * group_rows

    outer_groups = [[i * outer_count + w for w in range(outer_count)] for i in range(16)]

    def over_outer(value):
        if outer_count == 1:
            return value
        return lax.all_gather(value, "dp", axis_index_groups=outer_groups, axis=0, tiled=True)

    cols = jnp.stack(
        [
            ((at_z + 2 * y) % 4 * 2 + at_x) * block_rows
            for at_z in (z, outer, far, far_outer)
            for at_x in (x, 1 - x)
        ]
    ).astype(jnp.int32)

    def settle_grad(total):
        first, second = pick_c(total[0], total[1]), pick_c(total[1], total[0])
        first, second = first.astype(f32), second.astype(f32)
        if outer_count > 1:
            first, second = (
                lax.psum_scatter(
                    v, "dp", axis_index_groups=outer_groups, scatter_dimension=0, tiled=True
                )
                for v in (first, second)
            )
        return first, second

    def over_groups(value):
        return lax.psum(value, "dp", axis_index_groups=outer_groups) if outer_count > 1 else value

    def relative(vector):
        first, second = vector[:half_model], vector[half_model:]
        return jnp.concatenate([pick_y(first, second), pick_y(second, first)])

    def quarters(value, axis):
        size = value.shape[axis] // 2
        return (
            lax.slice_in_dim(value, 0, size, axis=axis),
            lax.slice_in_dim(value, size, 2 * size, axis=axis),
        )

    def pair_quarters(weight):
        first, second = quarters(weight, 2)
        return tuple(jnp.concatenate([v[:, 0], v[:, 1]], axis=1) for v in (first, second))

    def quarter(value, axis=0):
        return pick_c(*quarters(value, axis))

    gain_one, gain_two = relative(gain_rnn.astype(f32)), relative(gain_mlp.astype(f32))
    mask, _ = masks_of(lengths, buffer_rows)
    mask = jnp.pad(mask, ((0, 0), (0, lanes - mask.shape[1])))
    softened = jax.nn.softplus(-quarter(decay_param))
    vectors = jnp.concatenate(
        [
            quarter(conv_weight, 1),
            jnp.stack([quarter(conv_bias), quarter(bias_recur), quarter(bias_input), softened]),
        ],
        axis=0,
    )
    heads = gate_recur.shape[0] // 2
    wr = block_diagonal(quarter(gate_recur))
    wi = block_diagonal(quarter(gate_input))
    split = (
        pair_quarters(rnn_in),
        quarters(rnn_out, 1),
        pair_quarters(mlp_in),
        quarters(mlp_out, 1),
    )
    split = [(over_outer(first), over_outer(second)) for first, second in split]
    keeps = [pick_c(first, second) for first, second in split]
    gives = [pick_c(second, first) for first, second in split]
    gains = jnp.stack([gain_one, gain_two])
    (
        rnn_in_all, rnn_out_all, mlp_in_all, mlp_out_all,
        both, state, mixed, mask, middle, tokens_all,
        *rows_kept, scales,
    ) = run_forward(outer_count, keeps, gives, tokens, out_grad, mask, gains, vectors, wr, wi)
    normed, normed_two, grad_low = rows_kept[0:2], rows_kept[2:4], rows_kept[4:6]

    act, gate_slope, gate_value = run_mlp_forward(normed_two, mlp_in_all, cols)
    d_pair = run_mlp_backward(grad_low, mlp_out_all, cols, gate_slope, gate_value)

    def both_halves(name, parts, weight):
        return (
            run_rows_back(name + "_theirs", parts, weight, cols, 1, bf16),
            run_rows_back(name + "_mine", parts, weight, cols, 0, f32),
        )

    partials = (
        run_weight_partial("mlp_in_partial", normed_two, d_pair, cols),
        run_weight_partial("mlp_out_partial", grad_low, (act,), cols),
    )
    (
        _, _, mlp_in_total, mlp_out_total,
        output_two, d_middle, d_branch, d_branch_theirs, d_both, sums, square_recur, square_input, term,
    ) = run_backward(
        outer_count,
        partials,
        both_halves("mlp_in_back", d_pair, mlp_in_all),
        both_halves("mlp_out", (act,), mlp_out_all),
        grad_low[0],
        middle,
        scales,
        gains,
        rnn_out_all,
        both,
        state,
        mask,
        vectors,
        wr,
        wi,
    )
    gates = jnp.stack(
        [
            diagonal_blocks(v, heads).reshape(-1, gate_recur.shape[1]).astype(bf16)
            for v in (square_recur, square_input)
        ]
    )
    rnn_in_total, rnn_out_total, tokens_grad_two, gates, sums, term = run_finish(
        outer_count,
        normed,
        (d_branch, d_branch_theirs),
        d_both,
        mixed,
        rnn_in_all,
        tokens_all,
        scales,
        gains,
        d_middle,
        sums,
        gates,
        term,
    )
    layer_output, tokens_grad = output_two[:buffer_rows], tokens_grad_two[:buffer_rows]
    mlp_in_grad, mlp_out_grad, rnn_in_grad, rnn_out_grad = (
        settle_grad(v) for v in (mlp_in_total, mlp_out_total, rnn_in_total, rnn_out_total)
    )

    def both_quarters(pair, axis):
        return over_groups(
            pick_c(
                jnp.concatenate([pair[0], pair[1]], axis=axis),
                jnp.concatenate([pair[1], pair[0]], axis=axis),
            )
        )

    sums = both_quarters(sums, 1)
    gates = both_quarters(gates.astype(f32), 1)
    gains_grad = over_groups(term[:2])
    size = gate_recur.shape[1]

    def pair_layout(halves):
        columns = halves[0].shape[1] // 2
        return jnp.stack(
            [
                jnp.concatenate([v[:, k * columns : (k + 1) * columns] for v in halves], axis=1)
                for k in range(2)
            ],
            axis=1,
        )

    return (
        layer_output,
        tokens_grad,
        gains_grad[0],
        pair_layout(rnn_in_grad),
        gates[0].reshape(-1, size, size),
        gates[1].reshape(-1, size, size),
        sums[5],
        sums[6],
        8.0 * jax.nn.sigmoid(-decay_param) * sums[7],
        sums[:4],
        sums[4],
        jnp.concatenate(rnn_out_grad, axis=1),
        gains_grad[1],
        pair_layout(mlp_in_grad),
        jnp.concatenate(mlp_out_grad, axis=1),
    )


def solution(mesh):
    return jax.shard_map(
        functools.partial(local, mesh.shape["dp"]),
        mesh=mesh,
        in_specs=(
            P("dp", "mp"),
            P(),
            P("dp", None, "mp"),
            P("mp", None, None),
            P("mp", None, None),
            P("mp"),
            P("mp"),
            P("mp"),
            P(None, "mp"),
            P("mp"),
            P("dp", "mp"),
            P(),
            P("dp", None, "mp"),
            P("dp", "mp"),
            P("dp", None),
            P("dp", "mp"),
        ),
        out_specs=(
            P("dp", "mp"),
            P("dp", "mp"),
            P("mp"),
            P("dp", None, "mp"),
            P("mp", None, None),
            P("mp", None, None),
            P("mp"),
            P("mp"),
            P("mp"),
            P(None, "mp"),
            P("mp"),
            P("dp", "mp"),
            P("mp"),
            P("dp", None, "mp"),
            P("dp", "mp"),
        ),
        check_vma=False,
    )
```

```python
import functools

import jax
import jax.numpy as jnp
from jax import lax
from jax.experimental import pallas as pl
from jax.experimental.pallas import tpu as pltpu
from jax.sharding import PartitionSpec as P

norm_eps = 1e-06
root_eps = 0.001
bf16 = jnp.bfloat16
f32 = jnp.float32
contract_cols = (((1,), (1,)), ((), ()))
contract_rows = (((0,), (0,)), ((), ()))
gelu_scale = 0.7978845608028654
gelu_cubic = 0.044715
held_buffers = 4
scan_unroll = 8
blocks = 8
chunk_rows = 256
lanes = 128
by_mesh = pl.DeviceIdType.MESH


def pairs(n_dp, move):
    count = n_dp // 16
    found = []
    for i in range(n_dp):
        w, c, x, z = i % count, i // count % 2, i // count // 2 % 2, i // count // 4
        target = move(z, x, c)
        if target is not None:
            z, x, c = target
            found.append((i, ((z * 2 + x) * 2 + c) * count + w))
    return found


def gelu_parts(v):
    tanh_value = jnp.tanh(gelu_scale * (v + gelu_cubic * v * v * v))
    value = 0.5 * v * (1.0 + tanh_value)
    slope = 0.5 * (1.0 + tanh_value) + 0.5 * v * (1.0 - tanh_value * tanh_value) * (
        gelu_scale * (1.0 + 3.0 * gelu_cubic * v * v)
    )
    return value, slope


def shifted(value, offset):
    return pltpu.roll(value, offset % value.shape[0], 0)


def store_lanes(ref, at, value):
    chunks = ref.shape[0]
    spare = chunks * lanes - value.shape[1]
    if spare:
        value = jnp.concatenate([value, jnp.zeros((value.shape[0], spare), f32)], axis=1)
    for i in range(chunks):
        ref[i, at, :] = value[:, i * lanes : (i + 1) * lanes]


def load_lanes(ref, at, width):
    return jnp.concatenate([ref[i, at, :] for i in range(ref.shape[0])], axis=1)[:, :width]


def scan_rows(coef_ref, push_ref, rows, reverse):
    chunks = coef_ref.shape[0]

    def step(i, carried):
        carried = list(carried)
        for j in range(scan_unroll):
            t = i * scan_unroll + j
            at = pl.ds(rows - 1 - t if reverse else t, held_buffers, stride=rows)
            for k in range(chunks):
                if reverse:
                    value = push_ref[k, at, :] + carried[k]
                    carried[k] = coef_ref[k, at, :] * value
                else:
                    value = coef_ref[k, at, :] * carried[k] + push_ref[k, at, :]
                    carried[k] = value
                push_ref[k, at, :] = value
        return tuple(carried)

    start = tuple(jnp.zeros((held_buffers, lanes), f32) for _ in range(chunks))
    lax.fori_loop(0, rows // scan_unroll, step, start)


def columns_at(cols_ref, b, size):
    return pl.ds(pl.multiple_of(cols_ref[b], size), size)


def gathered(ref, at, cols_ref, size):
    return jnp.concatenate([ref[at, columns_at(cols_ref, b, size)] for b in range(blocks)], axis=1)


def stacked(refs, columns=slice(None)):
    return jnp.concatenate([ref[:, columns] for ref in refs], axis=0)


def project(mine_ref, theirs_ref, weight_refs, cols_ref, use):
    size = weight_refs[0].shape[0]
    own = mine_ref.shape[0]
    for part, ref in enumerate((mine_ref, theirs_ref)):

        def chunk(i, carry, part=part, ref=ref):
            at = pl.ds(pl.multiple_of(i * chunk_rows, chunk_rows), chunk_rows)
            rows = gathered(ref, at, cols_ref, size)
            use(
                pl.multiple_of(part * own + i * chunk_rows, chunk_rows),
                jnp.dot(rows, stacked(weight_refs), preferred_element_type=f32),
            )
            return carry

        lax.fori_loop(0, own // chunk_rows, chunk, 0)


def columns_at(cols, b, size):
    return pl.ds(pl.multiple_of(cols[b], size), size)


def gathered(ref, at, cols, size):
    return jnp.concatenate([ref[at, columns_at(cols, b, size)] for b in range(blocks)], axis=1)


def stacked(weight_ref):
    return weight_ref[...].reshape(-1, weight_ref.shape[2])


def project(mine_ref, theirs_ref, weight_ref, cols, use):
    size = weight_ref.shape[1]
    own = mine_ref.shape[0]
    for part, ref in enumerate((mine_ref, theirs_ref)):

        def chunk(i, carry, part=part, ref=ref):
            at = pl.ds(pl.multiple_of(i * chunk_rows, chunk_rows), chunk_rows)
            rows = gathered(ref, at, cols, size)
            use(
                pl.multiple_of(part * own + i * chunk_rows, chunk_rows),
                jnp.dot(rows, stacked(weight_ref), preferred_element_type=f32),
            )
            return carry

        lax.fori_loop(0, own // chunk_rows, chunk, 0)


def buffer_rows_at(b, rows):
    return pl.ds(pl.multiple_of(b * rows, rows), rows)


def conv_of(inner, mask, vec_ref):
    conv = vec_ref[4:5, :] + vec_ref[0:1, :] * inner
    for k in range(1, 4):
        conv = conv + vec_ref[k : k + 1, :] * (shifted(inner, k) * mask[:, k : k + 1])
    return conv


def gates_of(conv_low, vec_ref, wr_ref, wi_ref):
    rate = jax.nn.sigmoid(
        jnp.dot(conv_low, wr_ref[...], preferred_element_type=f32) + vec_ref[5:6, :]
    )
    igate = jax.nn.sigmoid(
        jnp.dot(conv_low, wi_ref[...], preferred_element_type=f32) + vec_ref[6:7, :]
    )
    return rate, igate


def recur_state(both_ref, mask_ref, vec_ref, wr_ref, wi_ref, coef_ref, push_ref):
    width = both_ref.shape[1] // 2
    rows = both_ref.shape[0] // held_buffers

    def gates(b, carry):
        at = buffer_rows_at(b, rows)
        mask = mask_ref[at, :]
        conv = conv_of(both_ref[at, :width], mask, vec_ref)
        rate, igate = gates_of(conv.astype(bf16), vec_ref, wr_ref, wi_ref)
        decay = jnp.exp(-8.0 * rate * vec_ref[7:8, :])
        root = jnp.sqrt(1.0 - decay * decay + root_eps)
        store_lanes(coef_ref, at, decay * mask[:, 0:1])
        store_lanes(push_ref, at, root * igate * conv)
        return carry

    lax.fori_loop(0, held_buffers, gates, 0)
    scan_rows(coef_ref, push_ref, rows, False)


def recur_mixed(both_ref, state_ref, mixed_ref):
    width = both_ref.shape[1] // 2
    rows = both_ref.shape[0] // held_buffers

    def mix(b, carry):
        at = buffer_rows_at(b, rows)
        gate = gelu_parts(both_ref[at, width:])[0]
        mixed_ref[at, :] = (load_lanes(state_ref, at, width) * gate).astype(bf16)
        return carry

    lax.fori_loop(0, held_buffers, mix, 0)


class Place:
    def __init__(self, count):
        self.me = lax.axis_index("dp")
        self.y = lax.axis_index("mp")
        self.c = self.me // count % 2
        self.x = self.me // (2 * count) % 2
        self.z = self.me // (4 * count)
        self.core = {"dp": self.me + (1 - 2 * self.c) * count}
        self.beside = {"dp": self.me + (1 - 2 * self.x) * 2 * count}
        self.over_y = {"mp": 1 - self.y}
        sign = 1 - 2 * (self.z // 2)
        self.ahead = {"dp": self.me + sign * 4 * count}
        self.behind = {"dp": self.me - sign * 4 * count}
        self.works = (self.z + 1) // 2 == 1
        self.serves = (self.z + 1) // 2 != 1

    def columns(self, size):
        outer = self.z // 2 * 3
        far, far_outer = 3 - self.z, 3 - outer
        return [
            ((at_z + 2 * self.y) % 4 * 2 + at_x) * size
            for at_z in (self.z, outer, far, far_outer)
            for at_x in (self.x, 1 - self.x)
        ]

    def meet(self):
        barrier = pltpu.get_barrier_semaphore()

        def greet(partners):
            for partner in partners:
                pl.semaphore_signal(barrier, inc=1, device_id=partner, device_id_type=by_mesh)
            pl.semaphore_wait(barrier, len(partners))

        @pl.when(self.works)
        def _():
            greet((self.core, self.beside, self.over_y, self.ahead, self.behind))

        @pl.when(self.serves)
        def _():
            greet((self.core, self.beside, self.ahead))


def remote(src, dst, send, recv, where):
    return pltpu.make_async_remote_copy(
        src_ref=src,
        dst_ref=dst,
        send_sem=send,
        recv_sem=recv,
        device_id=where,
        device_id_type=by_mesh,
    )


def normed_rows(source_ref, gain_ref, gain_row, scale_ref, scale_row, out_ref, first, count):
    size = 128

    def chunk(i, carry):
        at = pl.ds(pl.multiple_of(first + i * size, size), size)
        rows = source_ref[at, :].astype(f32)
        scale = lax.rsqrt(jnp.mean(rows * rows, axis=1, keepdims=True) + norm_eps)
        scale_ref[scale_row, at, :] = jnp.broadcast_to(scale, (size, lanes))
        out_ref[at, :] = (rows * scale * gain_ref[gain_row : gain_row + 1, :]).astype(bf16)
        return carry

    lax.fori_loop(0, count // size, chunk, 0)


def forward_kernel(
    count,
    keep_ri, keep_ro, keep_mi, keep_mo, give_ri, give_ro, give_mi, give_mo,
    tokens_ref, grad_ref, mask_in, gain_ref, vec_ref, wr_ref, wi_ref,
    g_ri, g_ro, g_mi, g_mo, *refs,
):
    results, refs = refs[:13], refs[13:]
    (
        both_ref, state_ref, mixed_ref, mask_ref, middle_ref, tok_ref,
        one_mine, one_theirs, two_mine, two_theirs, low_mine, low_theirs, scale_ref,
    ) = held = refs[:13]
    refs = refs[13:]
    (
    coef_ref, w_ri, w_ro, grad_all, part_out, part_in, part_sum, y_out, y_in, mid_ref,
    w_send, w_recv, w_local, load_sem, m_send, m_recv, m_local, out_sem,
    ) = refs
    at = Place(count)
    half_rows = keep_ri.shape[0]
    size = 2 * half_rows
    model = tok_ref.shape[1]
    half_model = model // 2
    rows = tokens_ref.shape[0]
    own = 2 * rows
    cols = at.columns(size)
    whole, keeps, gives = (g_ri, g_ro, g_mi, g_mo), (keep_ri, keep_ro, keep_mi, keep_mo), (
        give_ri, give_ro, give_mi, give_mo,
    )
    ri, ro, mi, mo = range(4)
    top, bottom = pl.ds(0, half_rows), pl.ds(half_rows, half_rows)
    core_rows = pl.ds(pl.multiple_of(at.c * half_rows, half_rows), half_rows)

    def hop(w, k):
        g = whole[w]
        src, dst, where = (
            (gives[w], g.at[0, core_rows], at.core),
            (g.at[0], g.at[1], at.beside),
            (g.at[0], g.at[2], at.ahead),
            (g.at[1], g.at[3], at.ahead),
            (g.at[0], g.at[4], at.ahead),
            (g.at[4], g.at[5], at.beside),
            (g.at[2], g.at[6], at.ahead),
            (g.at[3, top], g.at[7, top], at.ahead),
            (g.at[6, bottom], g.at[7, bottom], at.beside),
        )[k]
        return remote(src, dst, w_send.at[w, k], w_recv.at[w, k], where)

    def kept(w):
        return pltpu.make_async_copy(keeps[w], whole[w].at[0, core_rows], w_local.at[w])

    def begin(w):
        kept(w).start()
        hop(w, 0).start()

    def own_block(w, hops):
        kept(w).wait()
        hop(w, 0).wait()
        for k in hops:
            hop(w, k).start()

    def pass_on(w, arrived, sent):
        hop(w, arrived).wait_recv()
        hop(w, sent).start()

    def move(k, src, dst, where):
        return remote(src, dst, m_send.at[k], m_recv.at[k], where)

    first, second = pl.ds(0, rows), pl.ds(rows, rows)
    left, right = pl.ds(0, half_model), pl.ds(half_model, half_model)
    mine_rows, their_rows = pl.ds(0, own), pl.ds(own, own)
    token_in = move(0, tokens_ref, tok_ref.at[second, left], at.ahead)
    token_y = move(1, tokens_ref, tok_ref.at[first, right], at.over_y)
    token_y_two = move(2, tok_ref.at[second, left], tok_ref.at[second, right], at.over_y)
    grad_in = move(3, grad_ref, grad_all.at[second, left], at.ahead)
    grad_y = move(4, grad_ref, grad_all.at[first, right], at.over_y)
    grad_y_two = move(5, grad_all.at[second, left], grad_all.at[second, right], at.over_y)
    mask_move = move(6, mask_in, mask_ref.at[second], at.ahead)
    mask_core = move(7, mask_ref.at[mine_rows], mask_ref.at[their_rows], at.core)
    one_core = move(8, one_mine, one_theirs, at.core)
    low_core = move(9, low_mine, low_theirs, at.core)
    halves = (first, second)
    part_core = [move(10 + i, part_out.at[h], part_in.at[h], at.core) for i, h in enumerate(halves)]
    part_y = [move(12 + i, y_out.at[h], y_in.at[h], at.over_y) for i, h in enumerate(halves)]
    mid_y = [
        move(14 + i, mid_ref.at[h, left], mid_ref.at[h, right], at.over_y)
        for i, h in enumerate(halves)
    ]
    two_core = [move(16 + i, two_mine.at[h], two_theirs.at[h], at.core) for i, h in enumerate(halves)]
    token_here = pltpu.make_async_copy(tokens_ref, tok_ref.at[first, left], m_local.at[0])
    grad_here = pltpu.make_async_copy(grad_ref, grad_all.at[first, left], m_local.at[1])
    mask_here = pltpu.make_async_copy(mask_in, mask_ref.at[first], m_local.at[2])

    def load(w, target, b):
        return pltpu.make_async_copy(whole[w].at[b], target.at[b], load_sem.at[w, b])

    def keep_out(k):
        source = held[k].at[:, left] if k == 5 else held[k]
        return pltpu.make_async_copy(source, results[k], out_sem.at[k])

    at.meet()

    @pl.when(at.serves)
    def _():
        mask_move.start()
        token_in.start()
        for w in (ri, ro, mi, mo):
            begin(w)
        for w in (ri, ro):
            own_block(w, (1, 2))
        for w in (ri, ro):
            pass_on(w, 1, 3)
        grad_in.start()
        for w in (mi, mo):
            own_block(w, (1, 2))
        for w in (mi, mo):
            pass_on(w, 1, 3)
        for w in (ri, ro, mi, mo):
            for k in (1, 2, 3):
                hop(w, k).wait_send()
        for moved in (mask_move, token_in, grad_in):
            moved.wait_send()

    @pl.when(at.works)
    def _():
        token_here.start()
        mask_here.start()
        token_y.start()
        begin(ri)
        begin(ro)
        grad_here.start()
        begin(mi)
        begin(mo)
        own_block(ri, (1, 4))
        own_block(ro, (1, 4))
        mask_here.wait()
        mask_move.wait_recv()
        mask_core.start()
        token_in.wait_recv()
        token_y_two.start()
        pass_on(ri, 2, 6)
        pass_on(ri, 4, 5)
        token_here.wait()
        token_y.wait_recv()
        normed_rows(tok_ref, gain_ref, 0, scale_ref, 0, one_mine, 0, rows)
        token_y_two.wait_recv()
        normed_rows(tok_ref, gain_ref, 0, scale_ref, 0, one_mine, rows, rows)
        one_core.start()
        pass_on(ro, 2, 6)
        pass_on(ro, 4, 5)
        pass_on(ri, 3, 7)
        pass_on(ri, 6, 8)
        own_block(mi, (1, 4))
        pass_on(ro, 3, 7)
        pass_on(ro, 6, 8)
        grad_y.start()
        for w, target in ((ri, w_ri), (ro, w_ro)):
            hop(w, 1).wait_recv()
            for k in (5, 7, 8):
                hop(w, k).wait_recv()
            for b in range(blocks):
                load(w, target, b).start()
        for b in range(blocks):
            load(ri, w_ri, b).wait()
        one_core.wait_recv()
        mask_core.wait_recv()

        def keep_both(start, value):
            both_ref[pl.ds(start, chunk_rows), :] = value

        keep_out(3).start()
        keep_out(5).start()
        keep_out(6).start()
        keep_out(7).start()
        project(one_mine, one_theirs, w_ri, cols, keep_both)
        keep_out(0).start()
        grad_in.wait_recv()
        grad_y_two.start()
        recur_state(both_ref, mask_ref, vec_ref, wr_ref, wi_ref, coef_ref, state_ref)
        keep_out(1).start()
        pass_on(mi, 2, 6)
        pass_on(mi, 4, 5)
        own_block(mo, (1, 4))
        recur_mixed(both_ref, state_ref, mixed_ref)
        keep_out(2).start()
        for b in range(blocks):
            load(ro, w_ro, b).wait()

        def branch(start, out_ref, out_at):
            for b in range(blocks):
                out_ref[out_at, columns_at(cols, b, size)] = lax.dot_general(
                    mixed_ref[pl.ds(start, rows), :],
                    w_ro[b],
                    contract_cols,
                    preferred_element_type=f32,
                ).astype(out_ref.dtype)

        for i, h in enumerate(halves):
            branch(own + i * rows, part_out, h)
            part_core[i].start()
        for i, h in enumerate(halves):
            branch(i * rows, part_sum, first)
            part_core[i].wait_recv()
            middle_ref[h, :] = part_sum[:, left] + part_in[h, left].astype(f32)
            y_out[h, :] = (part_sum[:, right] + part_in[h, right].astype(f32)).astype(bf16)
            part_y[i].start()
        pass_on(mi, 3, 7)
        grad_here.wait()
        grad_y.wait_recv()
        grad_y_two.wait_recv()
        low_mine[...] = (grad_all[...].astype(f32) * mask_ref[mine_rows, 4:5]).astype(bf16)
        low_core.start()
        keep_out(10).start()
        for i, h in enumerate(halves):
            part_y[i].wait_recv()
            middle = middle_ref[h, :] + y_in[h, :].astype(f32) + tok_ref[h, left].astype(f32)
            middle_ref[h, :] = middle
            mid_ref[h, left] = middle.astype(bf16)
            mid_y[i].start()
        keep_out(4).start()
        pass_on(mi, 6, 8)
        pass_on(mo, 2, 6)
        pass_on(mo, 4, 5)
        for i, h in enumerate(halves):
            mid_y[i].wait_recv()
            normed_rows(mid_ref, gain_ref, 1, scale_ref, 1, two_mine, i * rows, rows)
            two_core[i].start()
        keep_out(8).start()
        keep_out(12).start()
        pass_on(mo, 3, 7)
        pass_on(mo, 6, 8)
        for w in (mi, mo):
            for k in (1, 5, 7, 8):
                hop(w, k).wait_recv()
        low_core.wait_recv()
        keep_out(11).start()
        for moved in two_core:
            moved.wait_recv()
        keep_out(9).start()
        for w in (ri, ro, mi, mo):
            for k in (1, 4, 5, 6, 7, 8):
                hop(w, k).wait_send()
        for moved in (
            token_y, token_y_two, grad_y, grad_y_two, mask_core, one_core, low_core,
            *part_core, *part_y, *mid_y, *two_core,
        ):
            moved.wait_send()
        for k in range(13):
            keep_out(k).wait()


def recur_first(both_ref, state_ref, mask_ref, vec_ref, wr_ref, wi_ref, dmix_ref, dboth_ref, coef_ref, push_ref):
    width = dmix_ref.shape[1]
    rows = both_ref.shape[0] // held_buffers

    def first(b, carry):
        at = buffer_rows_at(b, rows)
        gate, slope = gelu_parts(both_ref[at, width:])
        d_mixed = dmix_ref[at, :]
        mask = mask_ref[at, :]
        conv_low = conv_of(both_ref[at, :width], mask, vec_ref).astype(bf16)
        rate = gates_of(conv_low, vec_ref, wr_ref, wi_ref)[0]
        store_lanes(push_ref, at, d_mixed * gate)
        dboth_ref[at, width:] = (slope * d_mixed * load_lanes(state_ref, at, width)).astype(bf16)
        store_lanes(coef_ref, at, jnp.exp(-8.0 * rate * vec_ref[7:8, :]) * mask[:, 0:1])
        return carry

    lax.fori_loop(0, held_buffers, first, 0)


def recur_last(
    both_ref, state_ref, mask_ref, vec_ref, wr_ref, wi_ref, push_ref,
    dboth_ref, sums_ref, gr_ref, gi_ref,
):
    width = both_ref.shape[1] // 2
    rows = both_ref.shape[0] // held_buffers
    sums_ref[...] = jnp.zeros_like(sums_ref)
    gr_ref[...] = jnp.zeros_like(gr_ref)
    gi_ref[...] = jnp.zeros_like(gi_ref)
    def add_sum(k, value):
        sums_ref[k : k + 1, :] += jnp.sum(value, axis=0, keepdims=True)

    def last(b, carry):
        at = buffer_rows_at(b, rows)
        inner = both_ref[at, :width]
        mask = mask_ref[at, :]
        keep = mask[:, 0:1]
        softened = vec_ref[7:8, :]
        conv = conv_of(inner, mask, vec_ref)
        conv_low = conv.astype(bf16)
        rate, igate = gates_of(conv_low, vec_ref, wr_ref, wi_ref)
        d_push = load_lanes(push_ref, at, width)
        decay = jnp.exp(-8.0 * rate * softened)
        square = 1.0 - decay * decay + root_eps
        root = jnp.sqrt(square)
        d_root = d_push * igate * conv
        d_igate = d_push * root * conv
        before = shifted(load_lanes(state_ref, at, width), 1) * keep
        d_decay = d_push * before - d_root * decay / root
        d_log = d_decay * decay
        slow = d_log * rate
        d_pre_recur = (-8.0 * softened) * slow * (1.0 - rate)
        d_pre_input = d_igate * igate * (1.0 - igate)
        add_sum(7, slow)
        add_sum(5, d_pre_recur)
        add_sum(6, d_pre_input)
        low_recur = d_pre_recur.astype(bf16)
        low_input = d_pre_input.astype(bf16)
        gr_ref[...] += lax.dot_general(
            conv_low, low_recur, contract_rows, preferred_element_type=f32
        )
        gi_ref[...] += lax.dot_general(
            conv_low, low_input, contract_rows, preferred_element_type=f32
        )
        d_conv = d_push * root * igate
        d_conv = d_conv + lax.dot_general(
            low_recur, wr_ref[...], contract_cols, preferred_element_type=f32
        )
        d_conv = d_conv + lax.dot_general(
            low_input, wi_ref[...], contract_cols, preferred_element_type=f32
        )
        add_sum(4, d_conv)
        add_sum(0, d_conv * inner)
        d_inner = vec_ref[0:1, :] * d_conv
        for k in range(1, 4):
            kept = d_conv * mask[:, k : k + 1]
            add_sum(k, kept * shifted(inner, k))
            d_inner = d_inner + vec_ref[k : k + 1, :] * shifted(kept, -k)
        dboth_ref[at, :width] = d_inner.astype(bf16)
        return carry

    lax.fori_loop(0, held_buffers, last, 0)


def mlp_forward(mine_ref, theirs_ref, gate_weight, up_weight, cols_ref, act_ref, slope_ref, value_ref):
    size = gate_weight.shape[1]
    own = mine_ref.shape[0]
    for part, ref in enumerate((mine_ref, theirs_ref)):

        def chunk(i, carry, part=part, ref=ref):
            rows = gathered(
                ref, pl.ds(pl.multiple_of(i * chunk_rows, chunk_rows), chunk_rows), cols_ref, size
            )
            gate = jnp.dot(rows, stacked(gate_weight), preferred_element_type=f32)
            up = jnp.dot(rows, stacked(up_weight), preferred_element_type=f32)
            value, slope = gelu_parts(gate)
            at = pl.ds(pl.multiple_of(part * own + i * chunk_rows, chunk_rows), chunk_rows)
            act_ref[at, :] = (value * up).astype(bf16)
            slope_ref[at, :] = (slope * up).astype(bf16)
            value_ref[at, :] = value.astype(bf16)
            return carry

        lax.fori_loop(0, own // chunk_rows, chunk, 0)


class Sums:
    def __init__(self, at, partial, land, total, send, recv):
        self.at, self.partial, self.land, self.total = at, partial, land, total
        self.send, self.recv = send, recv
        self.half_rows = total.shape[1]
        self.top = pl.ds(0, self.half_rows)
        self.bottom = pl.ds(self.half_rows, self.half_rows)

    def rows_of(self, c):
        return pl.ds(pl.multiple_of(c * self.half_rows, self.half_rows), self.half_rows)

    def hop(self, k, last=None):
        d, land, at, top, bottom = self.partial, self.land, self.at, self.top, self.bottom
        src, dst, where = (
            lambda: (d.at[5], land.at[0], at.beside),
            lambda: (d.at[7, bottom], land.at[1, top], at.beside),
            lambda: (d.at[7, top], land.at[1, bottom], at.ahead),
            lambda: (d.at[6, top], land.at[2, top], at.ahead),
            lambda: (land.at[1, top], land.at[2, bottom], at.ahead),
            lambda: (d.at[3, bottom], land.at[0, bottom], at.behind),
            lambda: (land.at[1, bottom], land.at[0, top], at.behind),
            lambda: (d.at[1], land.at[3], at.beside),
            lambda: (land.at[0], land.at[4], at.ahead),
            lambda: (land.at[2], land.at[2], at.behind),
            lambda: (land.at[0], land.at[3], at.beside),
            lambda: (last.at[self.rows_of(1 - at.c)], self.total.at[1], at.core),
        )[k]()
        return remote(src, dst, self.send.at[k], self.recv.at[k], where)

    def start(self, *hops):
        for k in hops:
            self.hop(k).start()

    def received(self, *hops):
        for k in hops:
            self.hop(k).wait_recv()

    def sent(self, *hops):
        for k in hops:
            self.hop(k).wait_send()

    def step(self, k, add):
        d, land, top, bottom = self.partial, self.land, self.top, self.bottom
        if k == 4:
            self.received(1)
            add(land.at[1, top], d.at[6, bottom])
        elif k == 6:
            self.received(2)
            add(land.at[1, bottom], d.at[3, top])
        elif k == 8:
            self.received(0)
            add(land.at[0], d.at[4])
        elif k == 9:
            self.received(3, 4)
            add(land.at[2], d.at[2])
        self.start(k)


work_hops, serve_hops = (0, 1, 2, 3, 4, 5, 6, 7, 8, 9), (10,)


def add_rows(into, value, other=None):
    size = 32 if into.shape[0] % 32 == 0 else 16

    def chunk(i, carry):
        at = pl.ds(pl.multiple_of(i * size, size), size)
        total = into[at, :].astype(f32) + value[at, :].astype(f32)
        if other is not None:
            total = total + other[at, :].astype(f32)
        into[at, :] = total.astype(bf16)
        return carry

    lax.fori_loop(0, into.shape[0] // size, chunk, 0)


def norm_sums(e_ref, y_in, source_ref, gain_ref, gain_row, mean_ref, first, count):
    size, half = 64, e_ref.shape[1]

    def chunk(i, carry):
        at = pl.ds(pl.multiple_of(first + i * size, size), size)
        e = e_ref[at, :] + y_in[at, :].astype(f32)
        e_ref[at, :] = e
        source = source_ref[at, :half].astype(bf16).astype(f32)
        part = jnp.sum(e * gain_ref[gain_row : gain_row + 1, :half] * source, axis=1, keepdims=True)
        mean_ref[at, :] = jnp.broadcast_to(part, (size, lanes))
        return carry

    lax.fori_loop(0, count // size, chunk, 0)


def norm_rows_back(
    e_ref, source_ref, gain_ref, gain_row, scale_ref, mean_ref, mean_in, term_ref, model, first, count, use
):
    size, half = 64, e_ref.shape[1]

    def chunk(i, carry):
        at = pl.ds(pl.multiple_of(first + i * size, size), size)
        e = e_ref[at, :]
        source = source_ref[at, :half].astype(bf16).astype(f32)
        scale = scale_ref[gain_row, at, 0:1]
        inner = (mean_ref[at, 0:1] + mean_in[at, 0:1]) / model
        weighted = e * gain_ref[gain_row : gain_row + 1, :half]
        term_ref[gain_row : gain_row + 1, :] += jnp.sum(e * source * scale, axis=0, keepdims=True)
        use(at, scale * weighted - source * (scale * scale * scale * inner))
        return carry

    lax.fori_loop(0, count // size, chunk, 0)


def stream_tiles(count, fetch, body):
    fetch(0, 0).start()

    def step(t, carry):
        slot = t % 2

        @pl.when(t + 1 < count)
        def _():
            fetch(t + 1, 1 - slot).start()

        fetch(t, slot).wait()
        body(t, slot)
        return carry

    lax.fori_loop(0, count, step, 0)


def backward_kernel(
    count,
    weight_mi, weight_mo, act_in, slope_in, value_in, two_mine, two_theirs, low_mine, low_theirs,
    middle_in, weight_in, both_in, state_in,
    scale_ref, gain_ref, mask_ref, vec_ref, wr_ref, wi_ref,
    d_mi, d_mo, land_mi, land_mo, total_mi, total_mo, dmid_out, mine_out, theirs_out, dboth_out,
    out_ref, sums_ref, gates_ref, term_ref,
    middle_ref, dmid_ref, db_mine, db_theirs,
    part_out, part_in, o_in, y_out, y_in, oy_out, oy_in, mean_ref, mean_in, stage_a, stage_b,
    w_send, w_recv, m_send, m_recv, local_sem, load_sem, out_sem, tile_sem, keep_sem,
):
    at = Place(count)
    size = weight_mi.shape[1]
    cols = at.columns(size)
    own, half_model = middle_ref.shape
    model = 2 * half_model
    rows = own // 2
    hidden = act_in.shape[1]
    width = weight_in.shape[2]
    e_ref, low_left = dmid_ref, y_out
    mi = Sums(at, d_mi, land_mi, total_mi, w_send.at[0], w_recv.at[0])
    mo = Sums(at, d_mo, land_mo, total_mo, w_send.at[1], w_recv.at[1])
    first, second = pl.ds(0, rows), pl.ds(rows, rows)
    left, right = pl.ds(0, half_model), pl.ds(half_model, half_model)
    halves = (first, second)

    def move(k, src, dst, where):
        return remote(src, dst, m_send.at[k], m_recv.at[k], where)

    e_core = [move(i, part_out.at[h], part_in.at[h], at.core) for i, h in enumerate(halves)]
    o_core = [move(2 + i, part_out.at[h], o_in.at[h], at.core) for i, h in enumerate(halves)]
    e_y = [move(4 + i, y_out.at[h], y_in.at[h], at.over_y) for i, h in enumerate(halves)]
    o_y = [move(6 + i, oy_out.at[h], oy_in.at[h], at.over_y) for i, h in enumerate(halves)]
    mean_y = move(8, mean_ref, mean_in, at.over_y)
    db_y = [
        move(9 + i, db_mine.at[h, left], db_mine.at[h, right], at.over_y)
        for i, h in enumerate(halves)
    ]
    db_core = [move(11 + i, db_mine.at[h], db_theirs.at[h], at.core) for i, h in enumerate(halves)]
    out_move = move(13, out_ref.at[second], out_ref.at[first], at.behind)
    low_load = pltpu.make_async_copy(low_mine.at[:, left], low_left, local_sem.at[0])
    middle_load = pltpu.make_async_copy(middle_in, middle_ref, local_sem.at[4])
    keep_out = [
        pltpu.make_async_copy(src, dst, out_sem.at[k])
        for k, (src, dst) in enumerate(
            ((dmid_ref, dmid_out), (db_mine, mine_out), (db_theirs, theirs_out))
        )
    ]

    def fetch(src, dst, k):
        return pltpu.make_async_copy(src, dst, local_sem.at[k])

    def add(into, value):
        count_rows, wide = into.shape
        a = stage_a.at[pl.ds(0, count_rows), pl.ds(0, wide)]
        b = stage_b.at[pl.ds(0, count_rows), pl.ds(0, wide)]
        loads = fetch(into, a, 1), fetch(value, b, 2)
        for v in loads:
            v.start()
        for v in loads:
            v.wait()
        add_rows(a, b)
        back = fetch(a, into, 3)
        back.start()
        back.wait()

    def finish(w, parts):
        count_rows, wide = parts[0].shape
        a = stage_a.at[pl.ds(0, count_rows), pl.ds(0, wide)]
        b = stage_b.at[pl.ds(0, count_rows), pl.ds(0, wide)]
        loads = fetch(parts[0], a, 1), fetch(parts[1], b, 2)
        for v in loads:
            v.start()
        for v in loads:
            v.wait()
        add_rows(a, b)
        if len(parts) == 3:
            third = fetch(parts[2], b, 2)
            third.start()
            third.wait()
            add_rows(a, b)
        w.hop(11, a).start()
        kept = fetch(a.at[w.rows_of(at.c)], w.total.at[0], 3)
        kept.start()
        kept.wait()
        w.hop(11, a).wait()

    at.meet()

    @pl.when(at.serves)
    def _():
        for w in (mo, mi):
            w.received(5, 6)
            w.start(10)
        for w in (mo, mi):
            w.received(9, 10)
            finish(w, (w.land.at[2], w.land.at[3]))
        out_move.wait_recv()
        for w in (mo, mi):
            w.sent(*serve_hops)

    def partial_blocks(w, lhs, column_ref, room, order):
        wide = column_ref.shape[1]
        tile = 512
        writes = []

        def write(i, b):
            return pltpu.make_async_copy(
                room.at[i % 2, :, pl.ds(0, wide)], w.partial.at[b], keep_sem.at[i % 2]
            )

        for i, (b, hops) in enumerate(order):
            if i >= 2:
                write(i - 2, order[i - 2][0]).wait()
                w.start(*order[i - 2][1])
            here = columns_at(cols, b, size)

            def column(t, carry, i=i, here=here):
                wide_at = pl.ds(pl.multiple_of(t * tile, tile), tile)
                total = lax.dot_general(
                    lhs[0, :, here], column_ref[:own, wide_at], contract_rows, preferred_element_type=f32
                )
                total = total + lax.dot_general(
                    lhs[1, :, here], column_ref[own:, wide_at], contract_rows, preferred_element_type=f32
                )
                room[i % 2, :, wide_at] = total.astype(bf16)
                return carry

            lax.fori_loop(0, wide // tile, column, 0)
            write(i, b).start()
        for i in (len(order) - 2, len(order) - 1):
            write(i, order[i][0]).wait()
            w.start(*order[i][1])

    def rows_product(weight, row_ref, room, wide, which, out):
        def block(b):
            return pltpu.make_async_copy(
                weight.at[b], room.at[b % 2, :, pl.ds(0, wide)], tile_sem.at[b % 2]
            )

        block(0).start()
        for b in range(blocks):
            if b + 1 < blocks:
                block(b + 1).start()
            block(b).wait()
            here = columns_at(cols, b, size)

            def chunk(i, carry, b=b, here=here):
                start = pl.multiple_of(i * chunk_rows, chunk_rows)
                out[pl.ds(start, chunk_rows), here] = lax.dot_general(
                    row_ref[pl.ds(which * own + start, chunk_rows), :],
                    room[b % 2, :, pl.ds(0, wide)],
                    contract_cols,
                    preferred_element_type=f32,
                ).astype(out.dtype)
                return carry

            lax.fori_loop(0, own // chunk_rows, chunk, 0)

    def join(i, h, mine_ref, arrived, landed, keep_value, sent_ref, over):
        arrived[i].wait_recv()
        keep_value(h, mine_ref[h, left] + landed[h, left].astype(f32))
        sent_ref[h, :] = (mine_ref[h, right] + landed[h, right].astype(f32)).astype(bf16)
        over[i].start()

    def mlp_part(lhs, act_ref, pair_ref, tiles, room, mine_ref):
        lhs_low = fetch(low_mine, lhs.at[0], 1), fetch(low_theirs, lhs.at[1], 2)
        lhs_two = fetch(two_mine, lhs.at[0], 1), fetch(two_theirs, lhs.at[1], 2)
        act_load = pltpu.make_async_copy(act_in, act_ref, load_sem.at[0])
        pair_load = [
            pltpu.make_async_copy(src, pair_ref.at[:, pl.ds(k * hidden, hidden)], load_sem.at[1 + k])
            for k, src in enumerate((slope_in, value_in))
        ]
        for v in (*lhs_low, act_load, *pair_load):
            v.start()
        middle_load.start()
        for v in (*lhs_low, act_load):
            v.wait()
        partial_blocks(
            mo,
            lhs,
            act_ref,
            room,
            ((7, (1, 2)), (5, (0,)), (6, (3,)), (3, (5,)), (1, (7,)), (4, ()), (2, ()), (0, ())),
        )
        for v in pair_load:
            v.wait()
        tile = tiles.shape[3]

        def back(t, slot):
            gate_at = pl.ds(pl.multiple_of(t * tile, tile), tile)
            up_at = pl.ds(pl.multiple_of(hidden + t * tile, tile), tile)

            def use(start, d_act):
                row_at = pl.ds(start, chunk_rows)
                for where in (gate_at, up_at):
                    pair_ref[row_at, where] = (d_act * pair_ref[row_at, where].astype(f32)).astype(bf16)

            project(lhs.at[0], lhs.at[1], tiles.at[slot], cols, use)

        stream_tiles(
            hidden // tile,
            lambda t, slot: pltpu.make_async_copy(
                weight_mo.at[:, :, pl.ds(pl.multiple_of(t * tile, tile), tile)],
                tiles.at[slot],
                tile_sem.at[slot],
            ),
            back,
        )
        for v in lhs_two:
            v.start()
        mo.step(4, add_late)
        mo.step(6, add_late)
        for v in lhs_two:
            v.wait()
        rows_product(weight_mi, pair_ref, room, 2 * hidden, 1, part_out)
        for moved in e_core:
            moved.start()
        mo.step(8, add)
        rows_product(weight_mi, pair_ref, room, 2 * hidden, 0, mine_ref)

        def keep_e(h, value):
            e_ref[h, :] = value

        for i, h in enumerate(halves):
            join(i, h, mine_ref, e_core, part_in, keep_e, y_out, e_y)
        mo.step(9, add)
        partial_blocks(
            mi,
            lhs,
            pair_ref,
            room,
            ((7, (1, 2)), (5, (0,)), (6, (3,)), (3, (5,)), (1, (7,)), (4, ()), (2, ()), (0, ())),
        )
        middle_load.wait()
        for i, h in enumerate(halves):
            e_y[i].wait_recv()
            norm_sums(e_ref, y_in, middle_ref, gain_ref, 1, mean_ref, i * rows, rows)
        mean_y.start()
        for moved in e_y:
            moved.wait_send()
        low_load.start()
        mi.step(6, add)
        low_load.wait()
        mean_y.wait_recv()

        def keep(row_at, value):
            d_middle = value + low_left[row_at, :].astype(f32)
            dmid_ref[row_at, :] = d_middle
            db_mine[row_at, left] = d_middle.astype(bf16)

        for i in range(2):
            norm_rows_back(
                e_ref, middle_ref, gain_ref, 1, scale_ref, mean_ref, mean_in, term_ref, model,
                i * rows, rows, keep,
            )
            db_y[i].start()
        for moved in e_core:
            moved.wait_send()
        rows_product(weight_mo, act_ref, room, hidden, 1, part_out)
        for moved in o_core:
            moved.start()
        mi.step(4, add)
        rows_product(weight_mo, act_ref, room, hidden, 0, mine_ref)

        def keep_o(h, value):
            middle_ref[h, :] = middle_ref[h, :] + value

        for i in range(2):
            db_y[i].wait_recv()
            db_core[i].start()
        for i, h in enumerate(halves):
            join(i, h, mine_ref, o_core, o_in, keep_o, oy_out, o_y)

    def add_late(into, value):
        count_rows, wide = into.shape
        a = stage_a.at[pl.ds(0, count_rows), pl.ds(0, wide)]
        b = stage_b.at[pl.ds(0, count_rows), pl.ds(0, wide)]
        loads = fetch(into, a, 5), fetch(value, b, 6)
        for v in loads:
            v.start()
        for v in loads:
            v.wait()
        add_rows(a, b)
        back = fetch(a, into, 3)
        back.start()
        back.wait()

    def recur_part(w_ro, both_ref, state_ref, dboth_ref, coef_ref, push_ref, dmix_ref, gr_ref, gi_ref):
        loads = [
            pltpu.make_async_copy(src, dst, load_sem.at[k])
            for k, (src, dst) in enumerate(
                ((weight_in, w_ro), (both_in, both_ref), (state_in, state_ref))
            )
        ]
        for v in loads:
            v.start()
        for i in range(2):
            db_core[i].wait_recv()
        for v in keep_out:
            v.start()
        for v in loads:
            v.wait()

        def keep_mixed(start, value):
            dmix_ref[pl.ds(start, chunk_rows), :] = value

        project(db_mine, db_theirs, w_ro, cols, keep_mixed)
        recur_first(
            both_ref, state_ref, mask_ref, vec_ref, wr_ref, wi_ref, dmix_ref, dboth_ref, coef_ref, push_ref
        )
        for i, h in enumerate(halves):
            o_y[i].wait_recv()
            out_ref[h, :] = (
                mask_ref[h, 4:5] * (middle_ref[h, :] + oy_in[h, :].astype(f32))
            ).astype(bf16)
        out_move.start()
        mi.step(8, add)
        scan_rows(coef_ref, push_ref, both_ref.shape[0] // held_buffers, True)
        mi.step(9, add)
        recur_last(
            both_ref, state_ref, mask_ref, vec_ref, wr_ref, wi_ref, push_ref,
            dboth_ref, sums_ref, gr_ref, gi_ref,
        )
        keep_both = pltpu.make_async_copy(dboth_ref, dboth_out, out_sem.at[3])
        keep_both.start()
        block = gates_ref.shape[0]
        packed = [
            ref[h * block : (h + 1) * block, h * block : (h + 1) * block].astype(bf16)
            for ref in (gr_ref, gi_ref)
            for h in range(width // block)
        ]
        gates_ref[...] = jnp.concatenate(packed, axis=1)
        keep_both.wait()

    @pl.when(at.works)
    def _():
        term_ref[...] = jnp.zeros_like(term_ref)
        pl.run_scoped(
            mlp_part,
            pltpu.VMEM((2, own, model), bf16),
            pltpu.VMEM((2 * own, hidden), bf16),
            pltpu.VMEM((2 * own, 2 * hidden), bf16),
            pltpu.VMEM((2, blocks, size, 256), bf16),
            pltpu.VMEM((2, size, 2 * hidden), bf16),
            pltpu.VMEM((own, model), f32),
        )
        pl.run_scoped(
            recur_part,
            pltpu.VMEM((blocks, size, width), bf16),
            pltpu.VMEM(both_in.shape, f32),
            pltpu.VMEM(state_in.shape, f32),
            pltpu.VMEM(dboth_out.shape, bf16),
            pltpu.VMEM(state_in.shape, f32),
            pltpu.VMEM(state_in.shape, f32),
            pltpu.VMEM((2 * own, width), f32),
            pltpu.VMEM((width, width), f32),
            pltpu.VMEM((width, width), f32),
        )
        for w in (mo, mi):
            w.received(7, 8)
            finish(w, (w.partial.at[0], w.land.at[3], w.land.at[4]))
        for w in (mo, mi):
            w.sent(*work_hops)
        for v in keep_out:
            v.wait()
        for moved in (*o_core, *o_y, mean_y, *db_y, *db_core, out_move):
            moved.wait_send()


def finish_kernel(
    count,
    *refs,
):
    sources, refs = refs[:9], refs[9:]
    (
        scale_ref, gain_ref, sums_ref, gates_ref, term_in,
        total_r, out_ref, recur_out, input_out, sums_out, term_out,
    ) = refs[:11]
    refs = refs[11:]
    one_mine, one_theirs, db_mine, db_theirs, dboth_ref, mixed_ref, w_ri, tok_left, dmid_ref = refs[:9]
    (
        d_r, land_r, part_out, part_in, part_sum, y_out, y_in, e_ref,
        mean_ref, mean_in, last_r, gates_in, gates_out, sums_in, term_ref, term_land,
        w_send, w_recv, m_send, m_recv, load_sem,
    ) = refs[9:]
    at = Place(count)
    size = w_ri.shape[1]
    cols = at.columns(size)
    own, half_model = dmid_ref.shape
    model = 2 * half_model
    rows = own // 2
    pair_width = dboth_ref.shape[1]
    w = Sums(at, d_r, land_r, total_r, w_send, w_recv)
    first, second = pl.ds(0, rows), pl.ds(rows, rows)
    left, right = pl.ds(0, half_model), pl.ds(half_model, half_model)
    halves = (first, second)

    def move(k, src, dst, where):
        return remote(src, dst, m_send.at[k], m_recv.at[k], where)

    e_core = [move(i, part_out.at[h], part_in.at[h], at.core) for i, h in enumerate(halves)]
    e_y = [move(2 + i, y_out.at[h], y_in.at[h], at.over_y) for i, h in enumerate(halves)]
    mean_y = move(4, mean_ref, mean_in, at.over_y)
    out_move = move(5, out_ref.at[second], out_ref.at[first], at.behind)
    gates_x = move(6, gates_ref, gates_in.at[0], at.beside)
    gates_z = move(7, gates_in.at[0], gates_in.at[1], at.ahead)
    gates_end = move(8, gates_out.at[0], gates_out.at[0], at.behind)
    gates_core = move(9, gates_out.at[0], gates_out.at[1], at.core)
    sums_x = move(10, sums_ref, sums_in.at[0], at.beside)
    sums_z = move(11, sums_in.at[0], sums_in.at[1], at.ahead)
    sums_end = move(12, sums_out.at[0], sums_out.at[0], at.behind)
    sums_core = move(13, sums_out.at[0], sums_out.at[1], at.core)
    term_x = move(14, term_ref, term_land.at[0], at.beside)
    term_z = move(15, term_land.at[0], term_land.at[1], at.ahead)
    term_core = move(16, term_land.at[1], term_land.at[2], at.core)
    term_end = move(17, term_out, term_out, at.behind)
    loads = [
        pltpu.make_async_copy(src, dst, load_sem.at[k]) for k, (src, dst) in enumerate(zip(sources, refs))
    ]

    def add(into, value):
        add_rows(into, value)

    def finish(parts):
        last_r[...] = parts[0][...]
        add_rows(last_r, parts[1], parts[2] if len(parts) == 3 else None)
        w.hop(11, last_r).start()
        w.total[0] = last_r[w.rows_of(at.c), :]

    def unpack(place, quarter):
        block = recur_out.shape[1]
        count_heads = recur_out.shape[0] // 2
        for k, out in enumerate((recur_out, input_out)):
            for h in range(count_heads):
                start = (k * count_heads + h) * block
                out[quarter * count_heads + h] = gates_out[place, :, start : start + block].astype(f32)

    at.meet()

    @pl.when(at.serves)
    def _():
        sums_end.wait_recv()
        sums_core.start()
        w.received(5, 6)
        w.start(10)
        gates_end.wait_recv()
        gates_core.start()
        w.received(9, 10)
        finish((w.land.at[2], w.land.at[3]))
        w.hop(11, last_r).wait()
        w.sent(*serve_hops)
        out_move.wait_recv()
        term_end.wait_recv()
        sums_core.wait()
        unpack(0, at.c)
        gates_core.wait()
        unpack(1, 1 - at.c)

    @pl.when(at.works)
    def _():
        for k in (4, 0, 1, 5, 2, 3, 6, 7, 8):
            loads[k].start()
        sums_x.start()
        for k in (4, 0, 1, 5, 2, 3):
            loads[k].wait()

        def partial(b):
            here = columns_at(cols, b, size)

            def product(mine_ref, theirs_ref, column_ref):
                total = lax.dot_general(
                    mine_ref[:, here], column_ref[:own, :], contract_rows, preferred_element_type=f32
                )
                total = total + lax.dot_general(
                    theirs_ref[:, here], column_ref[own:, :], contract_rows, preferred_element_type=f32
                )
                return total.astype(bf16)

            d_r[b, :, :pair_width] = product(one_mine, one_theirs, dboth_ref)
            d_r[b, :, pair_width:] = product(db_mine, db_theirs, mixed_ref)

        for b, hops in ((7, (1, 2)), (5, (0,)), (6, (3,)), (3, (5,))):
            partial(b)
            w.start(*hops)

        def back(start, out, out_at):
            for b in range(blocks):
                out[out_at, columns_at(cols, b, size)] = lax.dot_general(
                    dboth_ref[pl.ds(start, rows), :], w_ri[b], contract_cols, preferred_element_type=f32
                ).astype(out.dtype)

        loads[6].wait()
        for i, h in enumerate(halves):
            back(own + i * rows, part_out, h)
            e_core[i].start()
        w.step(4, add)
        w.step(6, add)
        for b in (4, 1):
            partial(b)
        for i, h in enumerate(halves):
            back(i * rows, part_sum, first)
            e_core[i].wait_recv()
            e_ref[h, :] = part_sum[:, left] + part_in[h, left].astype(f32)
            y_out[h, :] = (part_sum[:, right] + part_in[h, right].astype(f32)).astype(bf16)
            e_y[i].start()
        w.step(8, add)
        gates_x.start()
        w.start(7)
        sums_x.wait_recv()
        sums_in[0] = sums_in[0] + sums_ref[...]
        sums_z.start()
        for b in (2, 0):
            partial(b)
        w.step(9, add)
        sums_z.wait_recv()
        sums_out[0] = sums_in[0] + sums_in[1]
        sums_end.start()
        sums_core.start()
        gates_x.wait_recv()
        add_rows(gates_in.at[0], gates_ref)
        gates_z.start()
        term_ref[...] = term_in[...]
        for k in (7, 8):
            loads[k].wait()
        for i in range(2):
            e_y[i].wait_recv()
            norm_sums(e_ref, y_in, tok_left, gain_ref, 0, mean_ref, i * rows, rows)
        mean_y.start()
        gates_z.wait_recv()
        gates_out[0] = gates_in[0]
        add_rows(gates_out.at[0], gates_in.at[1])
        gates_end.start()
        gates_core.start()
        unpack(0, at.c)
        mean_y.wait_recv()

        def keep(row_at, value):
            out_ref[row_at, :] = (value + dmid_ref[row_at, :]).astype(bf16)

        for i in (1, 0):
            norm_rows_back(
                e_ref, tok_left, gain_ref, 0, scale_ref, mean_ref, mean_in, term_ref, model,
                i * rows, rows, keep,
            )
            if i == 1:
                out_move.start()
        term_x.start()
        term_x.wait_recv()
        term_land[0] = term_land[0] + term_ref[...]
        term_z.start()
        w.received(7, 8)
        finish((w.partial.at[0], w.land.at[3], w.land.at[4]))
        term_z.wait_recv()
        term_land[1] = term_land[0] + term_land[1]
        term_core.start()
        term_core.wait_recv()
        term_out[...] = term_land[1] + term_land[2]
        term_end.start()
        w.hop(11, last_r).wait()
        w.sent(*work_hops)
        sums_core.wait_recv()
        gates_core.wait_recv()
        unpack(1, 1 - at.c)
        for moved in (
            *e_core, *e_y, mean_y, out_move, gates_x, gates_z, gates_end, gates_core,
            sums_x, sums_z, sums_end, sums_core, term_x, term_z, term_core, term_end,
        ):
            moved.wait_send()


in_vmem = pl.BlockSpec(memory_space=pltpu.VMEM)
in_smem = pl.BlockSpec(memory_space=pltpu.SMEM)
in_any = pl.BlockSpec(memory_space=pl.ANY)
no_cost = pl.CostEstimate(flops=0, bytes_accessed=0, transcendentals=0)
kernel_params = pltpu.CompilerParams(vmem_limit_bytes=60 * 2**20)
copy_sem = pltpu.SemaphoreType.DMA


def lane_shape(rows, width):
    return (pl.cdiv(width, lanes), rows, lanes)


def run_forward(count, keeps, gives, tokens, out_grad, mask, gains, vectors, wr, wi):
    rows, half_model = tokens.shape
    own, model, width = 2 * rows, 2 * half_model, wr.shape[0]
    size = 2 * keeps[0].shape[0]
    shape = jax.ShapeDtypeStruct
    gathered_shapes = [shape((blocks, size, v.shape[1]), bf16) for v in keeps]
    wide = shape((own, model), bf16)
    kept = [
        shape((2 * own, 2 * width), f32),
        shape(lane_shape(2 * own, width), f32),
        shape((2 * own, width), bf16),
        shape((2 * own, lanes), f32),
        shape((own, half_model), f32),
        shape((own, half_model), bf16),
        *[wide] * 6,
        shape((2, own, lanes), f32),
    ]
    return pl.pallas_call(
        functools.partial(forward_kernel, count),
        out_shape=(*gathered_shapes, *kept),
        in_specs=[in_any] * 11 + [in_vmem] * 4,
        out_specs=[in_any] * 17,
        scratch_shapes=[
            *[pltpu.VMEM(wide.shape if i == 5 else v.shape, v.dtype) for i, v in enumerate(kept)],
            pltpu.VMEM(lane_shape(2 * own, width), f32),
            pltpu.VMEM((blocks, size, 2 * width), bf16),
            pltpu.VMEM((blocks, size, width), bf16),
            pltpu.VMEM((own, model), bf16),
            pltpu.VMEM((own, model), bf16),
            pltpu.VMEM((own, model), bf16),
            pltpu.VMEM((rows, model), f32),
            pltpu.VMEM((own, half_model), bf16),
            pltpu.VMEM((own, half_model), bf16),
            pltpu.VMEM((own, model), bf16),
            copy_sem((4, 9)),
            copy_sem((4, 9)),
            copy_sem((4,)),
            copy_sem((2, blocks)),
            copy_sem((18,)),
            copy_sem((18,)),
            copy_sem((3,)),
            copy_sem((13,)),
        ],
        compiler_params=comm_params(0),
        cost_estimate=no_cost,
        name="gather_and_recur",
    )(*keeps, *gives, tokens, out_grad, mask, gains, vectors, wr, wi)


def comm_params(collective):
    return pltpu.CompilerParams(
        vmem_limit_bytes=63 * 2**20, collective_id=collective, has_side_effects=True
    )


def run_backward(
    count, weights, mlp_kept, normed_two, grad_low, middle, weight, both, state,
    scales, gains, mask, vectors, wr, wi, block,
):
    own, half_model = middle.shape
    model, width, rows = 2 * half_model, wr.shape[0], own // 2
    size = weight.shape[1]
    shape = jax.ShapeDtypeStruct
    hidden = [v.shape[2] for v in weights]
    wide = shape((own, model), bf16)
    kept = (shape((own, half_model), f32), wide, wide)
    return pl.pallas_call(
        functools.partial(backward_kernel, count),
        out_shape=(
            *[shape(v.shape, bf16) for v in weights],
            *[shape((5, size, n), bf16) for n in hidden],
            *[shape((2, size // 2, n), bf16) for n in hidden],
            *kept,
            shape((2 * own, 2 * width), bf16),
            shape((own, half_model), bf16),
            shape((8, width), f32),
            shape((block, 2 * width), bf16),
            shape((8, half_model), f32),
        ),
        in_specs=[in_any] * 13 + [in_vmem] * 6,
        out_specs=[in_any] * 10 + [in_vmem] * 4,
        scratch_shapes=[
            pltpu.VMEM((own, half_model), f32),
            *[pltpu.VMEM(v.shape, v.dtype) for v in kept],
            *[pltpu.VMEM((own, model), bf16)] * 3,
            *[pltpu.VMEM((own, half_model), bf16)] * 4,
            pltpu.VMEM((own, lanes), f32),
            pltpu.VMEM((own, lanes), f32),
            pltpu.VMEM((size, max(hidden)), bf16),
            pltpu.VMEM((size, max(hidden)), bf16),
            copy_sem((2, 12)),
            copy_sem((2, 12)),
            copy_sem((14,)),
            copy_sem((14,)),
            copy_sem((7,)),
            copy_sem((4,)),
            copy_sem((4,)),
            copy_sem((2,)),
            copy_sem((2,)),
        ],
        compiler_params=comm_params(1),
        cost_estimate=no_cost,
        name="sum_and_back",
    )(
        *weights, *mlp_kept, *normed_two, *grad_low, middle, weight, both, state,
        scales, gains, mask, vectors, wr, wi,
    )


def run_finish(
    count, normed, d_branch, d_both, mixed, weight, tokens, d_middle, scales, gains, sums, gates, term
):
    own, half_model = d_middle.shape
    model, rows = 2 * half_model, own // 2
    size = weight.shape[1]
    width = weight.shape[2] + mixed.shape[1]
    shape = jax.ShapeDtypeStruct
    held = (*normed, *d_branch, d_both, mixed, weight, tokens, d_middle)
    block = gates.shape[0]
    square = shape((gates.shape[1] // block, block, block), f32)
    return pl.pallas_call(
        functools.partial(finish_kernel, count),
        out_shape=(
            shape((2, size // 2, width), bf16),
            shape((own, half_model), bf16),
            square,
            square,
            shape((2, *sums.shape), f32),
            shape(term.shape, f32),
        ),
        in_specs=[in_any] * 9 + [in_vmem] * 5,
        out_specs=[in_vmem] * 6,
        scratch_shapes=[
            *[pltpu.VMEM(v.shape, v.dtype) for v in held],
            pltpu.VMEM((blocks, size, width), bf16),
            pltpu.VMEM((5, size, width), bf16),
            pltpu.VMEM((own, model), bf16),
            pltpu.VMEM((own, model), bf16),
            pltpu.VMEM((rows, model), f32),
            pltpu.VMEM((own, half_model), bf16),
            pltpu.VMEM((own, half_model), bf16),
            pltpu.VMEM((own, half_model), f32),
            pltpu.VMEM((own, lanes), f32),
            pltpu.VMEM((own, lanes), f32),
            pltpu.VMEM((size, width), bf16),
            pltpu.VMEM((2, *gates.shape), bf16),
            pltpu.VMEM((2, *gates.shape), bf16),
            pltpu.VMEM((2, *sums.shape), f32),
            pltpu.VMEM(term.shape, f32),
            pltpu.VMEM((3, *term.shape), f32),
            copy_sem((12,)),
            copy_sem((12,)),
            copy_sem((18,)),
            copy_sem((18,)),
            copy_sem((9,)),
        ],
        compiler_params=comm_params(2),
        cost_estimate=no_cost,
        name="sum_and_finish",
    )(*held, scales, gains, sums, gates, term)


def run_mlp_forward(normed, weight, cols):
    own, model = normed[0].shape
    size, hidden = weight.shape[1], weight.shape[2] // 2
    tile = 256
    tiles = hidden // tile
    out = jax.ShapeDtypeStruct((2 * own, hidden), bf16)
    return pl.pallas_call(
        mlp_forward,
        grid=(tiles,),
        out_shape=(out, out, out),
        in_specs=[pl.BlockSpec((own, model), lambda n: (0, 0))] * 2
        + [pl.BlockSpec((blocks, size, tile), lambda n: (0, 0, n))]
        + [pl.BlockSpec((blocks, size, tile), lambda n: (0, 0, n + tiles))]
        + [in_smem],
        out_specs=[pl.BlockSpec((2 * own, tile), lambda n: (0, n))] * 3,
        compiler_params=kernel_params,
        cost_estimate=no_cost,
        name="mlp_forward",
    )(*normed, weight, weight, cols)


def block_diagonal(blocks):
    count, size = blocks.shape[0], blocks.shape[1]
    rows = [
        jnp.pad(blocks[h], ((0, 0), (h * size, (count - 1 - h) * size))) for h in range(count)
    ]
    return jnp.concatenate(rows, axis=0)


def diagonal_blocks(square, count):
    size = square.shape[0] // count
    return jnp.stack(
        [square[h * size : (h + 1) * size, h * size : (h + 1) * size] for h in range(count)]
    )


def masks_of(lengths, rows):
    ends = jnp.cumsum(lengths, axis=1)
    starts = ends - lengths
    places = jnp.arange(rows, dtype=jnp.int32)[None, :, None]
    inside = (places >= starts[:, None, :]) & (places < ends[:, None, :])
    first_place = jnp.sum(jnp.where(inside, starts[:, None, :], 0), axis=2)
    places = places[:, :, 0]
    live = (places < ends[:, 2:3]).astype(f32)
    columns = [(places != first_place).astype(f32)]
    for k in range(1, 4):
        columns.append((places - k >= first_place).astype(f32))
    columns += [live] + [jnp.zeros_like(live)] * 3
    return jnp.stack(columns, axis=2).reshape(lengths.shape[0] * rows, 8), live


def local(
    n_dp,
    tokens,
    gain_rnn,
    rnn_in,
    gate_recur,
    gate_input,
    bias_recur,
    bias_input,
    decay_param,
    conv_weight,
    conv_bias,
    rnn_out,
    gain_mlp,
    mlp_in,
    mlp_out,
    lengths,
    out_grad,
):
    outer_count = n_dp // 16
    rows_here = rnn_in.shape[0]
    model = gain_rnn.shape[0]
    half_model = model // 2
    buffer_rows = tokens.shape[0]
    own_rows = 2 * buffer_rows
    index = lax.axis_index("dp")
    y = lax.axis_index("mp")
    c = index // outer_count % 2
    x = index // (2 * outer_count) % 2
    z = index // (4 * outer_count)
    outer = jnp.where(z < 2, 0, 3)
    far = 3 - z
    far_outer = 3 - outer

    def pick_c(first, second):
        return jnp.where(c == 0, first, second)

    def pick_y(first, second):
        return jnp.where(y == 0, first, second)

    group_rows = outer_count * rows_here
    block_rows = 2 * group_rows

    outer_groups = [[i * outer_count + w for w in range(outer_count)] for i in range(16)]

    def over_outer(value):
        if outer_count == 1:
            return value
        return lax.all_gather(value, "dp", axis_index_groups=outer_groups, axis=0, tiled=True)

    cols = jnp.stack(
        [
            ((at_z + 2 * y) % 4 * 2 + at_x) * block_rows
            for at_z in (z, outer, far, far_outer)
            for at_x in (x, 1 - x)
        ]
    ).astype(jnp.int32)

    def settle_grad(total):
        first, second = pick_c(total[0], total[1]), pick_c(total[1], total[0])
        first, second = first.astype(f32), second.astype(f32)
        if outer_count > 1:
            first, second = (
                lax.psum_scatter(
                    v, "dp", axis_index_groups=outer_groups, scatter_dimension=0, tiled=True
                )
                for v in (first, second)
            )
        return first, second

    def over_groups(value):
        return lax.psum(value, "dp", axis_index_groups=outer_groups) if outer_count > 1 else value

    def relative(vector):
        first, second = vector[:half_model], vector[half_model:]
        return jnp.concatenate([pick_y(first, second), pick_y(second, first)])

    def quarters(value, axis):
        size = value.shape[axis] // 2
        return (
            lax.slice_in_dim(value, 0, size, axis=axis),
            lax.slice_in_dim(value, size, 2 * size, axis=axis),
        )

    def pair_quarters(weight):
        first, second = quarters(weight, 2)
        return tuple(jnp.concatenate([v[:, 0], v[:, 1]], axis=1) for v in (first, second))

    def quarter(value, axis=0):
        return pick_c(*quarters(value, axis))

    gain_one, gain_two = relative(gain_rnn.astype(f32)), relative(gain_mlp.astype(f32))
    mask, _ = masks_of(lengths, buffer_rows)
    mask = jnp.pad(mask, ((0, 0), (0, lanes - mask.shape[1])))
    softened = jax.nn.softplus(-quarter(decay_param))
    vectors = jnp.concatenate(
        [
            quarter(conv_weight, 1),
            jnp.stack([quarter(conv_bias), quarter(bias_recur), quarter(bias_input), softened]),
        ],
        axis=0,
    )
    heads = gate_recur.shape[0] // 2
    wr = block_diagonal(quarter(gate_recur))
    wi = block_diagonal(quarter(gate_input))
    split = (
        pair_quarters(rnn_in),
        quarters(rnn_out, 1),
        pair_quarters(mlp_in),
        quarters(mlp_out, 1),
    )
    split = [(over_outer(first), over_outer(second)) for first, second in split]
    keeps = [pick_c(first, second) for first, second in split]
    gives = [pick_c(second, first) for first, second in split]
    gains = jnp.stack([gain_one, gain_two])
    (
        rnn_in_all, rnn_out_all, mlp_in_all, mlp_out_all,
        both, state, mixed, mask, middle, tokens_all,
        *rows_kept, scales,
    ) = run_forward(outer_count, keeps, gives, tokens, out_grad, mask, gains, vectors, wr, wi)
    normed, normed_two, grad_low = rows_kept[0:2], rows_kept[2:4], rows_kept[4:6]

    act, gate_slope, gate_value = run_mlp_forward(normed_two, mlp_in_all, cols)
    (
        _, _, _, _, mlp_in_total, mlp_out_total, d_middle, d_branch, d_branch_theirs, d_both,
        output_two, sums, gates, term,
    ) = run_backward(
        outer_count,
        (mlp_in_all, mlp_out_all),
        (act, gate_slope, gate_value),
        normed_two,
        grad_low,
        middle,
        rnn_out_all,
        both,
        state,
        scales,
        gains,
        mask,
        vectors,
        wr,
        wi,
        gate_recur.shape[1],
    )
    rnn_total, tokens_grad_two, recur_grad, input_grad, sums, term = run_finish(
        outer_count,
        normed,
        (d_branch, d_branch_theirs),
        d_both,
        mixed,
        rnn_in_all,
        tokens_all,
        d_middle,
        scales,
        gains,
        sums,
        gates,
        term,
    )
    rnn_width = rnn_in.shape[2]
    rnn_in_total, rnn_out_total = rnn_total[:, :, :rnn_width], rnn_total[:, :, rnn_width:]
    layer_output, tokens_grad = output_two[:buffer_rows], tokens_grad_two[:buffer_rows]
    mlp_in_grad, mlp_out_grad, rnn_in_grad, rnn_out_grad = (
        settle_grad(v) for v in (mlp_in_total, mlp_out_total, rnn_in_total, rnn_out_total)
    )

    def both_quarters(pair, axis):
        return over_groups(
            pick_c(
                jnp.concatenate([pair[0], pair[1]], axis=axis),
                jnp.concatenate([pair[1], pair[0]], axis=axis),
            )
        )

    sums = both_quarters(sums, 1)
    recur_grad, input_grad = over_groups(recur_grad), over_groups(input_grad)
    gains_grad = over_groups(term[:2])

    def pair_layout(halves):
        columns = halves[0].shape[1] // 2
        return jnp.stack(
            [
                jnp.concatenate([v[:, k * columns : (k + 1) * columns] for v in halves], axis=1)
                for k in range(2)
            ],
            axis=1,
        )

    return (
        layer_output,
        tokens_grad,
        gains_grad[0],
        pair_layout(rnn_in_grad),
        recur_grad,
        input_grad,
        sums[5],
        sums[6],
        8.0 * jax.nn.sigmoid(-decay_param) * sums[7],
        sums[:4],
        sums[4],
        jnp.concatenate(rnn_out_grad, axis=1),
        gains_grad[1],
        pair_layout(mlp_in_grad),
        jnp.concatenate(mlp_out_grad, axis=1),
    )


def solution(mesh):
    return jax.shard_map(
        functools.partial(local, mesh.shape["dp"]),
        mesh=mesh,
        in_specs=(
            P("dp", "mp"),
            P(),
            P("dp", None, "mp"),
            P("mp", None, None),
            P("mp", None, None),
            P("mp"),
            P("mp"),
            P("mp"),
            P(None, "mp"),
            P("mp"),
            P("dp", "mp"),
            P(),
            P("dp", None, "mp"),
            P("dp", "mp"),
            P("dp", None),
            P("dp", "mp"),
        ),
        out_specs=(
            P("dp", "mp"),
            P("dp", "mp"),
            P("mp"),
            P("dp", None, "mp"),
            P("mp", None, None),
            P("mp", None, None),
            P("mp"),
            P("mp"),
            P("mp"),
            P(None, "mp"),
            P("mp"),
            P("dp", "mp"),
            P("mp"),
            P("dp", None, "mp"),
            P("dp", "mp"),
        ),
        check_vma=False,
    )
```

```python
import functools

import jax
import jax.numpy as jnp
from jax import lax
from jax.experimental import pallas as pl
from jax.experimental.pallas import tpu as pltpu
from jax.sharding import PartitionSpec as P

norm_eps = 1e-06
root_eps = 0.001
bf16 = jnp.bfloat16
f32 = jnp.float32
contract_cols = (((1,), (1,)), ((), ()))
contract_rows = (((0,), (0,)), ((), ()))
gelu_scale = 0.7978845608028654
gelu_cubic = 0.044715
held_buffers = 4
scan_unroll = 8
blocks = 8
chunk_rows = 512
lanes = 128
by_mesh = pl.DeviceIdType.MESH


def pairs(n_dp, move):
    count = n_dp // 16
    found = []
    for i in range(n_dp):
        w, c, x, z = i % count, i // count % 2, i // count // 2 % 2, i // count // 4
        target = move(z, x, c)
        if target is not None:
            z, x, c = target
            found.append((i, ((z * 2 + x) * 2 + c) * count + w))
    return found


def gelu_parts(v):
    tanh_value = jnp.tanh(gelu_scale * (v + gelu_cubic * v * v * v))
    value = 0.5 * v * (1.0 + tanh_value)
    slope = 0.5 * (1.0 + tanh_value) + 0.5 * v * (1.0 - tanh_value * tanh_value) * (
        gelu_scale * (1.0 + 3.0 * gelu_cubic * v * v)
    )
    return value, slope


def shifted(value, offset):
    return pltpu.roll(value, offset % value.shape[0], 0)


def store_lanes(ref, at, value):
    chunks = ref.shape[0]
    spare = chunks * lanes - value.shape[1]
    if spare:
        value = jnp.concatenate([value, jnp.zeros((value.shape[0], spare), f32)], axis=1)
    for i in range(chunks):
        ref[i, at, :] = value[:, i * lanes : (i + 1) * lanes]


def load_lanes(ref, at, width):
    return jnp.concatenate([ref[i, at, :] for i in range(ref.shape[0])], axis=1)[:, :width]


def scan_rows(coef_ref, push_ref, rows, reverse):
    chunks = coef_ref.shape[0]

    def step(i, carried):
        carried = list(carried)
        for j in range(scan_unroll):
            t = i * scan_unroll + j
            at = pl.ds(rows - 1 - t if reverse else t, held_buffers, stride=rows)
            for k in range(chunks):
                if reverse:
                    value = push_ref[k, at, :] + carried[k]
                    carried[k] = coef_ref[k, at, :] * value
                else:
                    value = coef_ref[k, at, :] * carried[k] + push_ref[k, at, :]
                    carried[k] = value
                push_ref[k, at, :] = value
        return tuple(carried)

    start = tuple(jnp.zeros((held_buffers, lanes), f32) for _ in range(chunks))
    lax.fori_loop(0, rows // scan_unroll, step, start)


def columns_at(cols_ref, b, size):
    return pl.ds(pl.multiple_of(cols_ref[b], size), size)


def gathered(ref, at, cols_ref, size):
    return jnp.concatenate([ref[at, columns_at(cols_ref, b, size)] for b in range(blocks)], axis=1)


def stacked(refs, columns=slice(None)):
    return jnp.concatenate([ref[:, columns] for ref in refs], axis=0)


def project(mine_ref, theirs_ref, weight_refs, cols_ref, use):
    size = weight_refs[0].shape[0]
    own = mine_ref.shape[0]
    for part, ref in enumerate((mine_ref, theirs_ref)):

        def chunk(i, carry, part=part, ref=ref):
            at = pl.ds(pl.multiple_of(i * chunk_rows, chunk_rows), chunk_rows)
            rows = gathered(ref, at, cols_ref, size)
            use(
                pl.multiple_of(part * own + i * chunk_rows, chunk_rows),
                jnp.dot(rows, stacked(weight_refs), preferred_element_type=f32),
            )
            return carry

        lax.fori_loop(0, own // chunk_rows, chunk, 0)


def columns_at(cols, b, size):
    return pl.ds(pl.multiple_of(cols[b], size), size)


def gathered(ref, at, cols, size):
    return jnp.concatenate([ref[at, columns_at(cols, b, size)] for b in range(blocks)], axis=1)


def stacked(weight_ref):
    return weight_ref[...].reshape(-1, weight_ref.shape[2])


def project(mine_ref, theirs_ref, weight, size, cols, use):
    own = mine_ref.shape[0]
    for part, ref in enumerate((mine_ref, theirs_ref)):

        def chunk(i, carry, part=part, ref=ref):
            at = pl.ds(pl.multiple_of(i * chunk_rows, chunk_rows), chunk_rows)
            rows = gathered(ref, at, cols, size)
            use(
                pl.multiple_of(part * own + i * chunk_rows, chunk_rows),
                jnp.dot(rows, weight(), preferred_element_type=f32),
            )
            return carry

        lax.fori_loop(0, own // chunk_rows, chunk, 0)


def buffer_rows_at(b, rows):
    return pl.ds(pl.multiple_of(b * rows, rows), rows)


def conv_of(inner, mask, vec_ref):
    conv = vec_ref[4:5, :] + vec_ref[0:1, :] * inner
    for k in range(1, 4):
        conv = conv + vec_ref[k : k + 1, :] * (shifted(inner, k) * mask[:, k : k + 1])
    return conv


def gates_of(conv_low, vec_ref, wr_ref, wi_ref):
    rate = jax.nn.sigmoid(
        jnp.dot(conv_low, wr_ref[...], preferred_element_type=f32) + vec_ref[5:6, :]
    )
    igate = jax.nn.sigmoid(
        jnp.dot(conv_low, wi_ref[...], preferred_element_type=f32) + vec_ref[6:7, :]
    )
    return rate, igate


def recur_state(both_ref, mask_ref, vec_ref, wr_ref, wi_ref, coef_ref, push_ref):
    width = both_ref.shape[1] // 2
    rows = both_ref.shape[0] // held_buffers

    def gates(b, carry):
        at = buffer_rows_at(b, rows)
        mask = mask_ref[at, :]
        conv = conv_of(both_ref[at, :width], mask, vec_ref)
        rate, igate = gates_of(conv.astype(bf16), vec_ref, wr_ref, wi_ref)
        decay = jnp.exp(-8.0 * rate * vec_ref[7:8, :])
        root = jnp.sqrt(1.0 - decay * decay + root_eps)
        store_lanes(coef_ref, at, decay * mask[:, 0:1])
        store_lanes(push_ref, at, root * igate * conv)
        return carry

    lax.fori_loop(0, held_buffers, gates, 0)
    scan_rows(coef_ref, push_ref, rows, False)


def recur_mixed(both_ref, state_ref, mixed_ref):
    width = both_ref.shape[1] // 2
    rows = both_ref.shape[0] // held_buffers

    def mix(b, carry):
        at = buffer_rows_at(b, rows)
        gate = gelu_parts(both_ref[at, width:])[0]
        mixed_ref[at, :] = (load_lanes(state_ref, at, width) * gate).astype(bf16)
        return carry

    lax.fori_loop(0, held_buffers, mix, 0)


def stream_tiles(first, last, fetch, body):
    fetch(first, first % 2).start()

    def step(t, carry):
        slot = t % 2

        @pl.when(t + 1 < last)
        def _():
            fetch(t + 1, 1 - slot).start()

        fetch(t, slot).wait()
        body(t, slot)
        return carry

    lax.fori_loop(first, last, step, 0)


class Tile:
    def __init__(self, weight, room, sems, first_column, tile):
        at = pl.ds(pl.multiple_of(first_column, tile), tile)
        self.copies = [
            pltpu.make_async_copy(
                weight.at[b, :, at], room.at[:, pl.ds(b * tile, tile)], sems.at[b]
            )
            for b in range(blocks)
        ]

    def start(self):
        for v in self.copies:
            v.start()

    def wait(self):
        for v in self.copies:
            v.wait()


def tile_rows(room, tile):
    return jnp.concatenate([room[:, b * tile : (b + 1) * tile] for b in range(blocks)], axis=0)


class Place:
    def __init__(self, count):
        self.me = lax.axis_index("dp")
        self.y = lax.axis_index("mp")
        self.c = self.me // count % 2
        self.x = self.me // (2 * count) % 2
        self.z = self.me // (4 * count)
        self.core = {"dp": self.me + (1 - 2 * self.c) * count}
        self.beside = {"dp": self.me + (1 - 2 * self.x) * 2 * count}
        self.over_y = {"mp": 1 - self.y}
        sign = 1 - 2 * (self.z // 2)
        self.ahead = {"dp": self.me + sign * 4 * count}
        self.behind = {"dp": self.me - sign * 4 * count}
        self.works = (self.z + 1) // 2 == 1
        self.serves = (self.z + 1) // 2 != 1

    def columns(self, size):
        outer = self.z // 2 * 3
        far, far_outer = 3 - self.z, 3 - outer
        return [
            ((at_z + 2 * self.y) % 4 * 2 + at_x) * size
            for at_z in (self.z, outer, far, far_outer)
            for at_x in (self.x, 1 - self.x)
        ]

    def meet(self):
        barrier = pltpu.get_barrier_semaphore()

        def greet(partners):
            for partner in partners:
                pl.semaphore_signal(barrier, inc=1, device_id=partner, device_id_type=by_mesh)
            pl.semaphore_wait(barrier, len(partners))

        @pl.when(self.works)
        def _():
            greet((self.core, self.beside, self.over_y, self.ahead, self.behind))

        @pl.when(self.serves)
        def _():
            greet((self.core, self.beside, self.ahead))


def remote(src, dst, send, recv, where):
    return pltpu.make_async_remote_copy(
        src_ref=src,
        dst_ref=dst,
        send_sem=send,
        recv_sem=recv,
        device_id=where,
        device_id_type=by_mesh,
    )


def normed_rows(source_ref, gain_ref, gain_row, scale_ref, scale_row, out_ref, first, count):
    size = 128

    def chunk(i, carry):
        at = pl.ds(pl.multiple_of(first + i * size, size), size)
        rows = source_ref[at, :].astype(f32)
        scale = lax.rsqrt(jnp.mean(rows * rows, axis=1, keepdims=True) + norm_eps)
        scale_ref[scale_row, at, :] = jnp.broadcast_to(scale, (size, lanes))
        out_ref[at, :] = (rows * scale * gain_ref[gain_row : gain_row + 1, :]).astype(bf16)
        return carry

    lax.fori_loop(0, count // size, chunk, 0)


def forward_kernel(
    count,
    s_ri, s_ro, s_mi, s_mo,
    tokens_ref, grad_ref, mask_in, gain_ref, vec_ref, wr_ref, wi_ref,
    g_ri, g_ro, g_mi, g_mo, *refs,
):
    results, mlp_out_refs, refs = refs[:13], refs[13:16], refs[16:]
    (
        state_ref, mask_ref, middle_ref, tok_ref,
        one_mine, one_theirs, two_mine, two_theirs, low_mine, low_theirs, scale_ref,
    ) = refs[:11]
    (
        grad_all, part_out, part_in, y_out, y_in, mid_ref,
        w_send, w_recv, w_local, load_sem, m_send, m_recv, m_local, out_sem, tile_sem, mlp_sem,
    ) = refs[11:]
    held = (
        None, state_ref, None, mask_ref, middle_ref, tok_ref,
        one_mine, one_theirs, two_mine, two_theirs, low_mine, low_theirs, scale_ref,
    )
    at = Place(count)
    half_rows = s_ri.shape[1]
    size = 2 * half_rows
    model = tok_ref.shape[1]
    half_model = model // 2
    rows = tokens_ref.shape[0]
    own = 2 * rows
    cols = at.columns(size)
    whole, splits = (g_ri, g_ro, g_mi, g_mo), (s_ri, s_ro, s_mi, s_mo)
    ri, ro, mi, mo = range(4)
    top, bottom = pl.ds(0, half_rows), pl.ds(half_rows, half_rows)
    core_rows = pl.ds(pl.multiple_of(at.c * half_rows, half_rows), half_rows)

    def hop(w, k):
        g = whole[w]
        src, dst, where = (
            (splits[w].at[1 - at.c], g.at[0, core_rows], at.core),
            (g.at[0], g.at[1], at.beside),
            (g.at[0], g.at[2], at.ahead),
            (g.at[1], g.at[3], at.ahead),
            (g.at[0], g.at[4], at.ahead),
            (g.at[4], g.at[5], at.beside),
            (g.at[2], g.at[6], at.ahead),
            (g.at[3, top], g.at[7, top], at.ahead),
            (g.at[6, bottom], g.at[7, bottom], at.beside),
        )[k]
        return remote(src, dst, w_send.at[w, k], w_recv.at[w, k], where)

    def kept(w):
        return pltpu.make_async_copy(splits[w].at[at.c], whole[w].at[0, core_rows], w_local.at[w])

    def begin(w):
        kept(w).start()
        hop(w, 0).start()

    def own_block(w, hops):
        kept(w).wait()
        hop(w, 0).wait()
        for k in hops:
            hop(w, k).start()

    def pass_on(w, arrived, sent):
        hop(w, arrived).wait_recv()
        hop(w, sent).start()

    def move(k, src, dst, where):
        return remote(src, dst, m_send.at[k], m_recv.at[k], where)

    first, second = pl.ds(0, rows), pl.ds(rows, rows)
    left, right = pl.ds(0, half_model), pl.ds(half_model, half_model)
    mine_rows, their_rows = pl.ds(0, own), pl.ds(own, own)
    token_in = move(0, tokens_ref, tok_ref.at[second, left], at.ahead)
    token_y = move(1, tokens_ref, tok_ref.at[first, right], at.over_y)
    token_y_two = move(2, tok_ref.at[second, left], tok_ref.at[second, right], at.over_y)
    grad_in = move(3, grad_ref, grad_all.at[second, left], at.ahead)
    grad_y = move(4, grad_ref, grad_all.at[first, right], at.over_y)
    grad_y_two = move(5, grad_all.at[second, left], grad_all.at[second, right], at.over_y)
    mask_move = move(6, mask_in, mask_ref.at[second], at.ahead)
    mask_core = move(7, mask_ref.at[mine_rows], mask_ref.at[their_rows], at.core)
    one_core = move(8, one_mine, one_theirs, at.core)
    low_core = move(9, low_mine, low_theirs, at.core)
    halves = (first, second)
    part_core = [move(10 + i, part_out.at[h], part_in.at[h], at.core) for i, h in enumerate(halves)]
    part_y = [move(12 + i, y_out.at[h], y_in.at[h], at.over_y) for i, h in enumerate(halves)]
    mid_y = [
        move(14 + i, mid_ref.at[h, left], mid_ref.at[h, right], at.over_y)
        for i, h in enumerate(halves)
    ]
    two_core = [move(16 + i, two_mine.at[h], two_theirs.at[h], at.core) for i, h in enumerate(halves)]
    token_here = pltpu.make_async_copy(tokens_ref, tok_ref.at[first, left], m_local.at[0])
    grad_here = pltpu.make_async_copy(grad_ref, grad_all.at[first, left], m_local.at[1])
    mask_here = pltpu.make_async_copy(mask_in, mask_ref.at[first], m_local.at[2])

    def load(w, target, b):
        return pltpu.make_async_copy(whole[w].at[b], target.at[b], load_sem.at[w, b])

    def keep_out(k, source=None):
        if source is None:
            source = held[k].at[:, left] if k == 5 else held[k]
        return pltpu.make_async_copy(source, results[k], out_sem.at[k])

    at.meet()

    @pl.when(at.serves)
    def _():
        mask_move.start()
        token_in.start()
        for w in (ri, ro, mi, mo):
            begin(w)
        for w in (ri, ro):
            own_block(w, (1, 2))
        for w in (ri, ro):
            pass_on(w, 1, 3)
        grad_in.start()
        for w in (mi, mo):
            own_block(w, (1, 2))
        for w in (mi, mo):
            pass_on(w, 1, 3)
        for w in (ri, ro, mi, mo):
            for k in (1, 2, 3):
                hop(w, k).wait_send()
        for moved in (mask_move, token_in, grad_in):
            moved.wait_send()

    def recur_part(both_ref, mixed_ref, coef_ref, w_ri, w_ro, part_sum):
        for w, target in ((ri, w_ri), (ro, w_ro)):
            hop(w, 1).wait_recv()
            for k in (5, 7, 8):
                hop(w, k).wait_recv()
            for b in range(blocks):
                load(w, target, b).start()
        for b in range(blocks):
            load(ri, w_ri, b).wait()
        one_core.wait_recv()
        mask_core.wait_recv()

        def keep_both(start, value):
            both_ref[pl.ds(start, chunk_rows), :] = value

        for k in (3, 5, 6, 7):
            keep_out(k).start()
        project(one_mine, one_theirs, lambda: stacked(w_ri), size, cols, keep_both)
        keep_out(0, both_ref).start()
        grad_in.wait_recv()
        grad_y_two.start()
        recur_state(both_ref, mask_ref, vec_ref, wr_ref, wi_ref, coef_ref, state_ref)
        keep_out(1).start()
        pass_on(mi, 2, 6)
        pass_on(mi, 4, 5)
        recur_mixed(both_ref, state_ref, mixed_ref)
        keep_out(2, mixed_ref).start()
        for b in range(blocks):
            load(ro, w_ro, b).wait()

        def branch(start, out_ref, out_at):
            for b in range(blocks):
                out_ref[out_at, columns_at(cols, b, size)] = lax.dot_general(
                    mixed_ref[pl.ds(start, rows), :],
                    w_ro[b],
                    contract_cols,
                    preferred_element_type=f32,
                ).astype(out_ref.dtype)

        for i, h in enumerate(halves):
            branch(own + i * rows, part_out, h)
            part_core[i].start()
        for i, h in enumerate(halves):
            branch(i * rows, part_sum, first)
            part_core[i].wait_recv()
            middle_ref[h, :] = part_sum[:, left] + part_in[h, left].astype(f32)
            y_out[h, :] = (part_sum[:, right] + part_in[h, right].astype(f32)).astype(bf16)
            part_y[i].start()
        keep_out(0, both_ref).wait()
        keep_out(2, mixed_ref).wait()

    def mlp_part(gate_room, up_room, act_room, slope_room, value_room):
        hidden = mlp_out_refs[0].shape[1]
        tile = act_room.shape[2]
        rooms = (act_room, slope_room, value_room)

        class Both:
            def __init__(self, t, slot):
                self.tiles = (
                    Tile(g_mi, gate_room.at[slot], tile_sem.at[slot, 0], t * tile, tile),
                    Tile(g_mi, up_room.at[slot], tile_sem.at[slot, 1], hidden + t * tile, tile),
                )

            def start(self):
                for v in self.tiles:
                    v.start()

            def wait(self):
                for v in self.tiles:
                    v.wait()

        def results_of(t, slot):
            columns = pl.ds(pl.multiple_of(t * tile, tile), tile)
            return [
                pltpu.make_async_copy(room.at[slot], out.at[:, columns], mlp_sem.at[slot, k])
                for k, (room, out) in enumerate(zip(rooms, mlp_out_refs))
            ]

        def body(t, slot):
            @pl.when(t >= 2)
            def _():
                for v in results_of(t - 2, slot):
                    v.wait()

            for part, ref in enumerate((two_mine, two_theirs)):
                row_values = gathered(ref, slice(None), cols, size)
                gate = jnp.dot(
                    row_values, tile_rows(gate_room.at[slot], tile), preferred_element_type=f32
                )
                up = jnp.dot(
                    row_values, tile_rows(up_room.at[slot], tile), preferred_element_type=f32
                )
                value, slope = gelu_parts(gate)
                row_at = pl.ds(part * own, own)
                act_room[slot, row_at, :] = (value * up).astype(bf16)
                slope_room[slot, row_at, :] = (slope * up).astype(bf16)
                value_room[slot, row_at, :] = value.astype(bf16)
            for v in results_of(t, slot):
                v.start()

        count_tiles = hidden // tile
        half_way = count_tiles // 2
        stream_tiles(0, half_way, Both, body)
        pass_on(mo, 3, 7)
        pass_on(mo, 6, 8)
        stream_tiles(half_way, count_tiles, Both, body)
        for t in (count_tiles - 2, count_tiles - 1):
            for v in results_of(t, t % 2):
                v.wait()

    @pl.when(at.works)
    def _():
        token_here.start()
        mask_here.start()
        token_y.start()
        begin(ri)
        begin(ro)
        grad_here.start()
        begin(mi)
        begin(mo)
        own_block(ri, (1, 4))
        own_block(ro, (1, 4))
        mask_here.wait()
        mask_move.wait_recv()
        mask_core.start()
        token_in.wait_recv()
        token_y_two.start()
        pass_on(ri, 2, 6)
        pass_on(ri, 4, 5)
        token_here.wait()
        token_y.wait_recv()
        normed_rows(tok_ref, gain_ref, 0, scale_ref, 0, one_mine, 0, rows)
        token_y_two.wait_recv()
        normed_rows(tok_ref, gain_ref, 0, scale_ref, 0, one_mine, rows, rows)
        one_core.start()
        pass_on(ro, 2, 6)
        pass_on(ro, 4, 5)
        pass_on(ri, 3, 7)
        pass_on(ri, 6, 8)
        own_block(mi, (1, 4))
        pass_on(ro, 3, 7)
        pass_on(ro, 6, 8)
        grad_y.start()
        width = vec_ref.shape[1]
        pl.run_scoped(
            recur_part,
            pltpu.VMEM((2 * own, 2 * width), f32),
            pltpu.VMEM((2 * own, width), bf16),
            pltpu.VMEM(state_ref.shape, f32),
            pltpu.VMEM(g_ri.shape, bf16),
            pltpu.VMEM(g_ro.shape, bf16),
            pltpu.VMEM((rows, model), f32),
        )
        grad_here.wait()
        grad_y.wait_recv()
        grad_y_two.wait_recv()
        low_mine[...] = (grad_all[...].astype(f32) * mask_ref[mine_rows, 4:5]).astype(bf16)
        low_core.start()
        keep_out(10).start()
        for i, h in enumerate(halves):
            part_y[i].wait_recv()
            middle = middle_ref[h, :] + y_in[h, :].astype(f32) + tok_ref[h, left].astype(f32)
            middle_ref[h, :] = middle
            mid_ref[h, left] = middle.astype(bf16)
            mid_y[i].start()
        keep_out(4).start()
        pass_on(mi, 3, 7)
        pass_on(mi, 6, 8)
        own_block(mo, (1, 4))
        for i, h in enumerate(halves):
            mid_y[i].wait_recv()
            normed_rows(mid_ref, gain_ref, 1, scale_ref, 1, two_mine, i * rows, rows)
            two_core[i].start()
        keep_out(8).start()
        keep_out(12).start()
        pass_on(mo, 2, 6)
        pass_on(mo, 4, 5)
        low_core.wait_recv()
        keep_out(11).start()
        for moved in two_core:
            moved.wait_recv()
        keep_out(9).start()
        for k in (1, 5, 7, 8):
            hop(mi, k).wait_recv()
        tile = 256
        pl.run_scoped(
            mlp_part,
            *[pltpu.VMEM((2, size, blocks * tile), bf16)] * 2,
            *[pltpu.VMEM((2, 2 * own, tile), bf16)] * 3,
        )
        for k in (1, 5, 7, 8):
            hop(mo, k).wait_recv()
        for w in (ri, ro, mi, mo):
            for k in (1, 4, 5, 6, 7, 8):
                hop(w, k).wait_send()
        for moved in (
            token_y, token_y_two, grad_y, grad_y_two, mask_core, one_core, low_core,
            *part_core, *part_y, *mid_y, *two_core,
        ):
            moved.wait_send()
        for k in range(13):
            if k not in (0, 2):
                keep_out(k).wait()


def recur_first(both_ref, state_ref, mask_ref, vec_ref, wr_ref, wi_ref, dmix_ref, dboth_ref, coef_ref, push_ref):
    width = dmix_ref.shape[1]
    rows = both_ref.shape[0] // held_buffers

    def first(b, carry):
        at = buffer_rows_at(b, rows)
        gate, slope = gelu_parts(both_ref[at, width:])
        d_mixed = dmix_ref[at, :]
        mask = mask_ref[at, :]
        conv_low = conv_of(both_ref[at, :width], mask, vec_ref).astype(bf16)
        rate = gates_of(conv_low, vec_ref, wr_ref, wi_ref)[0]
        store_lanes(push_ref, at, d_mixed * gate)
        dboth_ref[at, width:] = (slope * d_mixed * load_lanes(state_ref, at, width)).astype(bf16)
        store_lanes(coef_ref, at, jnp.exp(-8.0 * rate * vec_ref[7:8, :]) * mask[:, 0:1])
        return carry

    lax.fori_loop(0, held_buffers, first, 0)


def recur_last(
    both_ref, state_ref, mask_ref, vec_ref, wr_ref, wi_ref, push_ref,
    dboth_ref, sums_ref, gr_ref, gi_ref,
):
    width = both_ref.shape[1] // 2
    rows = both_ref.shape[0] // held_buffers
    sums_ref[...] = jnp.zeros_like(sums_ref)
    gr_ref[...] = jnp.zeros_like(gr_ref)
    gi_ref[...] = jnp.zeros_like(gi_ref)
    def add_sum(k, value):
        sums_ref[k : k + 1, :] += jnp.sum(value, axis=0, keepdims=True)

    def last(b, carry):
        at = buffer_rows_at(b, rows)
        inner = both_ref[at, :width]
        mask = mask_ref[at, :]
        keep = mask[:, 0:1]
        softened = vec_ref[7:8, :]
        conv = conv_of(inner, mask, vec_ref)
        conv_low = conv.astype(bf16)
        rate, igate = gates_of(conv_low, vec_ref, wr_ref, wi_ref)
        d_push = load_lanes(push_ref, at, width)
        decay = jnp.exp(-8.0 * rate * softened)
        square = 1.0 - decay * decay + root_eps
        root = jnp.sqrt(square)
        d_root = d_push * igate * conv
        d_igate = d_push * root * conv
        before = shifted(load_lanes(state_ref, at, width), 1) * keep
        d_decay = d_push * before - d_root * decay / root
        d_log = d_decay * decay
        slow = d_log * rate
        d_pre_recur = (-8.0 * softened) * slow * (1.0 - rate)
        d_pre_input = d_igate * igate * (1.0 - igate)
        add_sum(7, slow)
        add_sum(5, d_pre_recur)
        add_sum(6, d_pre_input)
        low_recur = d_pre_recur.astype(bf16)
        low_input = d_pre_input.astype(bf16)
        gr_ref[...] += lax.dot_general(
            conv_low, low_recur, contract_rows, preferred_element_type=f32
        )
        gi_ref[...] += lax.dot_general(
            conv_low, low_input, contract_rows, preferred_element_type=f32
        )
        d_conv = d_push * root * igate
        d_conv = d_conv + lax.dot_general(
            low_recur, wr_ref[...], contract_cols, preferred_element_type=f32
        )
        d_conv = d_conv + lax.dot_general(
            low_input, wi_ref[...], contract_cols, preferred_element_type=f32
        )
        add_sum(4, d_conv)
        add_sum(0, d_conv * inner)
        d_inner = vec_ref[0:1, :] * d_conv
        for k in range(1, 4):
            kept = d_conv * mask[:, k : k + 1]
            add_sum(k, kept * shifted(inner, k))
            d_inner = d_inner + vec_ref[k : k + 1, :] * shifted(kept, -k)
        dboth_ref[at, :width] = d_inner.astype(bf16)
        return carry

    lax.fori_loop(0, held_buffers, last, 0)


class Sums:
    def __init__(self, at, partial, land, total, send, recv):
        self.at, self.partial, self.land, self.total = at, partial, land, total
        self.send, self.recv = send, recv
        self.half_rows = total.shape[1]
        self.top = pl.ds(0, self.half_rows)
        self.bottom = pl.ds(self.half_rows, self.half_rows)

    def rows_of(self, c):
        return pl.ds(pl.multiple_of(c * self.half_rows, self.half_rows), self.half_rows)

    def hop(self, k, last=None):
        d, land, at, top, bottom = self.partial, self.land, self.at, self.top, self.bottom
        src, dst, where = (
            lambda: (d.at[5], land.at[0], at.beside),
            lambda: (d.at[7, bottom], land.at[1, top], at.beside),
            lambda: (d.at[7, top], land.at[1, bottom], at.ahead),
            lambda: (d.at[6, top], land.at[2, top], at.ahead),
            lambda: (land.at[1, top], land.at[2, bottom], at.ahead),
            lambda: (d.at[3, bottom], land.at[0, bottom], at.behind),
            lambda: (land.at[1, bottom], land.at[0, top], at.behind),
            lambda: (d.at[1], land.at[3], at.beside),
            lambda: (land.at[0], land.at[4], at.ahead),
            lambda: (land.at[2], land.at[2], at.behind),
            lambda: (land.at[0], land.at[3], at.beside),
            lambda: (last.at[self.rows_of(1 - at.c)], self.total.at[at.c], at.core),
        )[k]()
        return remote(src, dst, self.send.at[k], self.recv.at[k], where)

    def start(self, *hops):
        for k in hops:
            self.hop(k).start()

    def received(self, *hops):
        for k in hops:
            self.hop(k).wait_recv()

    def sent(self, *hops):
        for k in hops:
            self.hop(k).wait_send()

    def operands(self, k):
        d, land, top, bottom = self.partial, self.land, self.top, self.bottom
        return {
            4: (land.at[1, top], d.at[6, bottom]),
            6: (land.at[1, bottom], d.at[3, top]),
            8: (land.at[0], d.at[4]),
            9: (land.at[2], d.at[2]),
        }[k]

    def arrived(self, k):
        self.received(*{4: (1,), 6: (2,), 8: (0,), 9: (3, 4)}[k])

    def step(self, k, add):
        self.arrived(k)
        add(*self.operands(k))
        self.start(k)


work_hops, serve_hops = (0, 1, 2, 3, 4, 5, 6, 7, 8, 9), (10,)


def add_rows(into, value, other=None):
    size = 32 if into.shape[0] % 32 == 0 else 16

    def chunk(i, carry):
        at = pl.ds(pl.multiple_of(i * size, size), size)
        total = into[at, :].astype(f32) + value[at, :].astype(f32)
        if other is not None:
            total = total + other[at, :].astype(f32)
        into[at, :] = total.astype(bf16)
        return carry

    lax.fori_loop(0, into.shape[0] // size, chunk, 0)


def norm_sums(e_ref, y_in, source_ref, gain_ref, gain_row, mean_ref, first, count):
    size, half = 64, e_ref.shape[1]

    def chunk(i, carry):
        at = pl.ds(pl.multiple_of(first + i * size, size), size)
        e = e_ref[at, :] + y_in[at, :].astype(f32)
        e_ref[at, :] = e
        source = source_ref[at, :half].astype(bf16).astype(f32)
        part = jnp.sum(e * gain_ref[gain_row : gain_row + 1, :half] * source, axis=1, keepdims=True)
        mean_ref[at, :] = jnp.broadcast_to(part, (size, lanes))
        return carry

    lax.fori_loop(0, count // size, chunk, 0)


def norm_rows_back(
    e_ref, source_ref, gain_ref, gain_row, scale_ref, mean_ref, mean_in, term_ref, model, first, count, use
):
    size, half = 64, e_ref.shape[1]

    def chunk(i, carry):
        at = pl.ds(pl.multiple_of(first + i * size, size), size)
        e = e_ref[at, :]
        source = source_ref[at, :half].astype(bf16).astype(f32)
        scale = scale_ref[gain_row, at, 0:1]
        inner = (mean_ref[at, 0:1] + mean_in[at, 0:1]) / model
        weighted = e * gain_ref[gain_row : gain_row + 1, :half]
        term_ref[gain_row : gain_row + 1, :] += jnp.sum(e * source * scale, axis=0, keepdims=True)
        use(at, scale * weighted - source * (scale * scale * scale * inner))
        return carry

    lax.fori_loop(0, count // size, chunk, 0)


def backward_kernel(
    count,
    weight_mi, weight_mo, act_in, slope_in, value_in, two_mine, two_theirs, low_mine, low_theirs,
    middle_in, weight_in, both_in, state_in,
    scale_ref, gain_ref, mask_ref, vec_ref, wr_ref, wi_ref,
    d_mi, d_mo, land_mi, land_mo, total_mi, total_mo, dmid_out, mine_out, theirs_out, dboth_out,
    out_ref, sums_ref, gates_ref, term_ref,
    middle_ref, dmid_ref, db_mine, db_theirs,
    part_out, part_in, o_in, y_out, y_in, oy_out, oy_in, mean_ref, mean_in, stage_a, stage_b,
    w_send, w_recv, m_send, m_recv, local_sem, load_sem, out_sem, tile_sem, keep_sem,
):
    at = Place(count)
    size = weight_mi.shape[1]
    cols = at.columns(size)
    own, half_model = middle_ref.shape
    model = 2 * half_model
    rows = own // 2
    hidden = act_in.shape[1]
    width = weight_in.shape[2]
    e_ref, low_left = dmid_ref, y_out
    mi = Sums(at, d_mi, land_mi, total_mi, w_send.at[0], w_recv.at[0])
    mo = Sums(at, d_mo, land_mo, total_mo, w_send.at[1], w_recv.at[1])
    first, second = pl.ds(0, rows), pl.ds(rows, rows)
    left, right = pl.ds(0, half_model), pl.ds(half_model, half_model)
    halves = (first, second)

    def move(k, src, dst, where):
        return remote(src, dst, m_send.at[k], m_recv.at[k], where)

    e_core = [move(i, part_out.at[h], part_in.at[h], at.core) for i, h in enumerate(halves)]
    o_core = [move(2 + i, part_out.at[h], o_in.at[h], at.core) for i, h in enumerate(halves)]
    e_y = [move(4 + i, y_out.at[h], y_in.at[h], at.over_y) for i, h in enumerate(halves)]
    o_y = [move(6 + i, oy_out.at[h], oy_in.at[h], at.over_y) for i, h in enumerate(halves)]
    mean_y = move(8, mean_ref, mean_in, at.over_y)
    db_y = [
        move(9 + i, db_mine.at[h, left], db_mine.at[h, right], at.over_y)
        for i, h in enumerate(halves)
    ]
    db_core = [move(11 + i, db_mine.at[h], db_theirs.at[h], at.core) for i, h in enumerate(halves)]
    out_move = move(13, out_ref.at[second], out_ref.at[first], at.behind)
    low_load = pltpu.make_async_copy(low_mine.at[:, left], low_left, local_sem.at[6])
    middle_load = pltpu.make_async_copy(middle_in, middle_ref, local_sem.at[7])
    keep_out = [
        pltpu.make_async_copy(src, dst, out_sem.at[k])
        for k, (src, dst) in enumerate(
            ((dmid_ref, dmid_out), (db_mine, mine_out), (db_theirs, theirs_out))
        )
    ]

    def fetch(src, dst, k):
        return pltpu.make_async_copy(src, dst, local_sem.at[k])

    def staged(w, k):
        into, value = w.operands(k)
        count_rows, wide = into.shape
        at_rows = pl.ds(0, count_rows) if k != 6 else pl.ds(count_rows, count_rows)
        place = 3 if k == 6 else 0
        a = stage_a.at[at_rows, pl.ds(0, wide)]
        b = stage_b.at[at_rows, pl.ds(0, wide)]
        return a, b, fetch(into, a, place), fetch(value, b, place + 1), fetch(a, into, place + 2)

    def begin(w, *hops):
        for k in hops:
            w.arrived(k)
            _, _, load_a, load_b, _ = staged(w, k)
            load_a.start()
            load_b.start()

    def combine(w, *hops):
        for k in hops:
            a, b, load_a, load_b, back = staged(w, k)
            load_a.wait()
            load_b.wait()
            add_rows(a, b)
            back.start()

    def send_on(w, *hops):
        for k in hops:
            staged(w, k)[4].wait()
            w.start(k)

    def finish(w, parts):
        count_rows, wide = parts[0].shape
        a = stage_a.at[pl.ds(0, count_rows), pl.ds(0, wide)]
        b = stage_b.at[pl.ds(0, count_rows), pl.ds(0, wide)]
        loads = fetch(parts[0], a, 0), fetch(parts[1], b, 1)
        for v in loads:
            v.start()
        for v in loads:
            v.wait()
        add_rows(a, b)
        if len(parts) == 3:
            third = fetch(parts[2], b, 1)
            third.start()
            third.wait()
            add_rows(a, b)
        w.hop(11, a).start()
        kept = fetch(a.at[w.rows_of(at.c)], w.total.at[at.c], 2)
        kept.start()
        kept.wait()
        w.hop(11, a).wait()

    at.meet()

    @pl.when(at.serves)
    def _():
        for w in (mo, mi):
            w.received(5, 6)
            w.start(10)
        for w in (mo, mi):
            w.received(9, 10)
            finish(w, (w.land.at[2], w.land.at[3]))
        out_move.wait_recv()
        for w in (mo, mi):
            w.sent(*serve_hops)

    block_order = (
        (7, (1, 2)), (5, (0,)), (6, (3,)), (3, (5,)), (1, (7,)), (4, ()), (2, ()), (0, ()),
    )

    def partial_blocks(w, lhs, column_ref, room, between=()):
        wide = column_ref.shape[1]
        between = dict(between)

        def write(i):
            return pltpu.make_async_copy(
                room.at[i % 2, :, pl.ds(0, wide)], w.partial.at[block_order[i][0]], keep_sem.at[i % 2]
            )

        def leave(i):
            write(i).wait()
            w.start(*block_order[i][1])

        for i in range(blocks):
            if i >= 2:
                leave(i - 2)
            here = columns_at(cols, block_order[i][0], size)
            rows_here = jnp.concatenate([lhs[0, :, here], lhs[1, :, here]], axis=0)
            room[i % 2, :, :wide] = lax.dot_general(
                rows_here, column_ref[...], contract_rows, preferred_element_type=f32
            ).astype(bf16)
            write(i).start()
            if i in between:
                between[i]()
        leave(blocks - 2)
        leave(blocks - 1)

    def rows_product(weight, row_ref, room, wide, theirs_out, mine_out, between=()):
        between = dict(between)

        def block(b):
            return pltpu.make_async_copy(
                weight.at[b], room.at[b % 2, :, pl.ds(0, wide)], tile_sem.at[b % 2, 0]
            )

        block(0).start()
        for b in range(blocks):
            if b + 1 < blocks:
                block(b + 1).start()
            block(b).wait()
            here = columns_at(cols, b, size)
            for which, out in ((1, theirs_out), (0, mine_out)):
                out[:, here] = lax.dot_general(
                    row_ref[which * own : (which + 1) * own, :],
                    room[b % 2, :, :wide],
                    contract_cols,
                    preferred_element_type=f32,
                ).astype(out.dtype)
            if b in between:
                between[b]()

    def settle(w):
        w.received(7, 8)
        finish(w, (w.partial.at[0], w.land.at[3], w.land.at[4]))

    def join(i, h, mine_ref, arrived, landed, keep_value, sent_ref, over):
        arrived[i].wait_recv()
        keep_value(h, mine_ref[h, left] + landed[h, left].astype(f32))
        sent_ref[h, :] = (mine_ref[h, right] + landed[h, right].astype(f32)).astype(bf16)
        over[i].start()

    def mlp_part(lhs, act_ref, pair_ref, room, mine_ref):
        lhs_low = fetch(low_mine, lhs.at[0], 8), fetch(low_theirs, lhs.at[1], 9)
        lhs_two = fetch(two_mine, lhs.at[0], 8), fetch(two_theirs, lhs.at[1], 9)
        act_load = pltpu.make_async_copy(act_in, act_ref, load_sem.at[0])
        pair_load = [
            pltpu.make_async_copy(src, pair_ref.at[:, pl.ds(k * hidden, hidden)], load_sem.at[1 + k])
            for k, src in enumerate((slope_in, value_in))
        ]
        for v in (*lhs_low, act_load, *pair_load):
            v.start()
        middle_load.start()
        for v in (*lhs_low, act_load):
            v.wait()
        partial_blocks(mo, lhs, act_ref, room)
        for v in pair_load:
            v.wait()
        tile = 256

        def back(t, slot):
            gate_at = pl.ds(pl.multiple_of(t * tile, tile), tile)
            up_at = pl.ds(pl.multiple_of(hidden + t * tile, tile), tile)

            def use(start, d_act):
                row_at = pl.ds(start, chunk_rows)
                for where in (gate_at, up_at):
                    pair_ref[row_at, where] = (d_act * pair_ref[row_at, where].astype(f32)).astype(bf16)

            project(
                lhs.at[0], lhs.at[1], lambda: tile_rows(room.at[slot], tile), size, cols, use
            )

        stream_tiles(
            0,
            hidden // tile,
            lambda t, slot: Tile(weight_mo, room.at[slot], tile_sem.at[slot], t * tile, tile),
            back,
        )
        for v in lhs_two:
            v.start()
        begin(mo, 4, 6)
        rows_product(
            weight_mi,
            pair_ref,
            room,
            2 * hidden,
            part_out,
            mine_ref,
            (
                (1, lambda: combine(mo, 4, 6)),
                (2, lambda: send_on(mo, 4, 6)),
                (4, lambda: begin(mo, 8)),
                (6, lambda: combine(mo, 8)),
            ),
        )
        for moved in e_core:
            moved.start()
        send_on(mo, 8)

        def keep_e(h, value):
            e_ref[h, :] = value

        for i, h in enumerate(halves):
            join(i, h, mine_ref, e_core, part_in, keep_e, y_out, e_y)
        for v in lhs_two:
            v.wait()
        partial_blocks(
            mi,
            lhs,
            pair_ref,
            room,
            (
                (2, lambda: begin(mo, 9)),
                (4, lambda: combine(mo, 9)),
                (5, lambda: send_on(mo, 9)),
            ),
        )
        middle_load.wait()
        for i, h in enumerate(halves):
            e_y[i].wait_recv()
            norm_sums(e_ref, y_in, middle_ref, gain_ref, 1, mean_ref, i * rows, rows)
        mean_y.start()
        for moved in e_y:
            moved.wait_send()
        low_load.start()
        for moved in e_core:
            moved.wait_send()
        low_load.wait()
        mean_y.wait_recv()

        def keep(row_at, value):
            d_middle = value + low_left[row_at, :].astype(f32)
            dmid_ref[row_at, :] = d_middle
            db_mine[row_at, left] = d_middle.astype(bf16)

        for i in range(2):
            norm_rows_back(
                e_ref, middle_ref, gain_ref, 1, scale_ref, mean_ref, mean_in, term_ref, model,
                i * rows, rows, keep,
            )
            db_y[i].start()
        begin(mi, 4, 6)
        rows_product(
            weight_mo,
            act_ref,
            room,
            hidden,
            part_out,
            mine_ref,
            ((1, lambda: combine(mi, 4, 6)), (2, lambda: send_on(mi, 4, 6))),
        )
        for moved in o_core:
            moved.start()

        def keep_o(h, value):
            middle_ref[h, :] = middle_ref[h, :] + value

        for i in range(2):
            db_y[i].wait_recv()
            db_core[i].start()
        for i, h in enumerate(halves):
            join(i, h, mine_ref, o_core, o_in, keep_o, oy_out, o_y)

    def recur_part(w_ro, both_ref, state_ref, dboth_ref, coef_ref, push_ref, dmix_ref, gr_ref, gi_ref):
        loads = [
            pltpu.make_async_copy(src, dst, load_sem.at[k])
            for k, (src, dst) in enumerate(
                ((weight_in, w_ro), (both_in, both_ref), (state_in, state_ref))
            )
        ]
        for v in loads:
            v.start()
        begin(mi, 9)
        for i in range(2):
            db_core[i].wait_recv()
        for v in keep_out:
            v.start()
        combine(mi, 9)
        for v in loads:
            v.wait()
        send_on(mi, 9)
        begin(mi, 8)

        def keep_mixed(start, value):
            dmix_ref[pl.ds(start, chunk_rows), :] = value

        project(db_mine, db_theirs, lambda: stacked(w_ro), size, cols, keep_mixed)
        combine(mi, 8)
        send_on(mi, 8)
        recur_first(
            both_ref, state_ref, mask_ref, vec_ref, wr_ref, wi_ref, dmix_ref, dboth_ref, coef_ref, push_ref
        )
        for i, h in enumerate(halves):
            o_y[i].wait_recv()
            out_ref[h, :] = (
                mask_ref[h, 4:5] * (middle_ref[h, :] + oy_in[h, :].astype(f32))
            ).astype(bf16)
        out_move.start()
        scan_rows(coef_ref, push_ref, both_ref.shape[0] // held_buffers, True)
        recur_last(
            both_ref, state_ref, mask_ref, vec_ref, wr_ref, wi_ref, push_ref,
            dboth_ref, sums_ref, gr_ref, gi_ref,
        )
        keep_both = pltpu.make_async_copy(dboth_ref, dboth_out, out_sem.at[3])
        keep_both.start()
        block = gates_ref.shape[0]
        packed = [
            ref[h * block : (h + 1) * block, h * block : (h + 1) * block].astype(bf16)
            for ref in (gr_ref, gi_ref)
            for h in range(width // block)
        ]
        gates_ref[...] = jnp.concatenate(packed, axis=1)
        keep_both.wait()

    @pl.when(at.works)
    def _():
        term_ref[...] = jnp.zeros_like(term_ref)
        pl.run_scoped(
            mlp_part,
            pltpu.VMEM((2, own, model), bf16),
            pltpu.VMEM((2 * own, hidden), bf16),
            pltpu.VMEM((2 * own, 2 * hidden), bf16),
            pltpu.VMEM((2, size, 2 * hidden), bf16),
            pltpu.VMEM((own, model), f32),
        )
        pl.run_scoped(
            recur_part,
            pltpu.VMEM((blocks, size, width), bf16),
            pltpu.VMEM(both_in.shape, f32),
            pltpu.VMEM(state_in.shape, f32),
            pltpu.VMEM(dboth_out.shape, bf16),
            pltpu.VMEM(state_in.shape, f32),
            pltpu.VMEM(state_in.shape, f32),
            pltpu.VMEM((2 * own, width), f32),
            pltpu.VMEM((width, width), f32),
            pltpu.VMEM((width, width), f32),
        )
        for w in (mo, mi):
            settle(w)
        for w in (mo, mi):
            w.sent(*work_hops)
        for v in keep_out:
            v.wait()
        for moved in (*o_core, *o_y, mean_y, *db_y, *db_core, out_move):
            moved.wait_send()


def finish_kernel(
    count,
    *refs,
):
    sources, refs = refs[:9], refs[9:]
    (
        scale_ref, gain_ref, sums_ref, gates_ref, term_in,
        total_r, out_ref, recur_out, input_out, sums_out, term_out,
    ) = refs[:11]
    refs = refs[11:]
    one_mine, one_theirs, db_mine, db_theirs, dboth_ref, mixed_ref, w_ri, tok_left, dmid_ref = refs[:9]
    (
        d_r, land_r, part_out, part_in, part_sum, y_out, y_in, e_ref,
        mean_ref, mean_in, last_r, gates_in, gates_out, sums_in, term_ref, term_land,
        w_send, w_recv, m_send, m_recv, load_sem,
    ) = refs[9:]
    at = Place(count)
    size = w_ri.shape[1]
    cols = at.columns(size)
    own, half_model = dmid_ref.shape
    model = 2 * half_model
    rows = own // 2
    pair_width = dboth_ref.shape[1]
    w = Sums(at, d_r, land_r, total_r, w_send, w_recv)
    first, second = pl.ds(0, rows), pl.ds(rows, rows)
    left, right = pl.ds(0, half_model), pl.ds(half_model, half_model)
    halves = (first, second)

    def move(k, src, dst, where):
        return remote(src, dst, m_send.at[k], m_recv.at[k], where)

    e_core = [move(i, part_out.at[h], part_in.at[h], at.core) for i, h in enumerate(halves)]
    e_y = [move(2 + i, y_out.at[h], y_in.at[h], at.over_y) for i, h in enumerate(halves)]
    mean_y = move(4, mean_ref, mean_in, at.over_y)
    out_move = move(5, out_ref.at[second], out_ref.at[first], at.behind)
    gates_x = move(6, gates_ref, gates_in.at[0], at.beside)
    gates_z = move(7, gates_in.at[0], gates_in.at[1], at.ahead)
    gates_end = move(8, gates_out.at[0], gates_out.at[0], at.behind)
    gates_core = move(9, gates_out.at[0], gates_out.at[1], at.core)
    sums_x = move(10, sums_ref, sums_in.at[0], at.beside)
    sums_z = move(11, sums_in.at[0], sums_in.at[1], at.ahead)
    sums_end = move(12, sums_out.at[0], sums_out.at[0], at.behind)
    sums_core = move(13, sums_out.at[0], sums_out.at[1], at.core)
    term_x = move(14, term_ref, term_land.at[0], at.beside)
    term_z = move(15, term_land.at[0], term_land.at[1], at.ahead)
    term_core = move(16, term_land.at[1], term_land.at[2], at.core)
    term_end = move(17, term_out, term_out, at.behind)
    loads = [
        pltpu.make_async_copy(src, dst, load_sem.at[k]) for k, (src, dst) in enumerate(zip(sources, refs))
    ]

    def add(into, value):
        add_rows(into, value)

    def finish(parts):
        last_r[...] = parts[0][...]
        add_rows(last_r, parts[1], parts[2] if len(parts) == 3 else None)
        w.hop(11, last_r).start()
        w.total[at.c] = last_r[w.rows_of(at.c), :]

    def unpack(place, quarter):
        block = recur_out.shape[1]
        count_heads = recur_out.shape[0] // 2
        for k, out in enumerate((recur_out, input_out)):
            for h in range(count_heads):
                start = (k * count_heads + h) * block
                out[quarter * count_heads + h] = gates_out[place, :, start : start + block].astype(f32)

    at.meet()

    @pl.when(at.serves)
    def _():
        sums_end.wait_recv()
        sums_core.start()
        w.received(5, 6)
        w.start(10)
        gates_end.wait_recv()
        gates_core.start()
        w.received(9, 10)
        finish((w.land.at[2], w.land.at[3]))
        w.hop(11, last_r).wait()
        w.sent(*serve_hops)
        out_move.wait_recv()
        term_end.wait_recv()
        sums_core.wait()
        unpack(0, at.c)
        gates_core.wait()
        unpack(1, 1 - at.c)

    @pl.when(at.works)
    def _():
        gates_x.start()
        sums_x.start()
        for k in (4, 0, 1, 5, 2, 3, 6, 7, 8):
            loads[k].start()
        for k in (4, 0, 1, 5, 2, 3):
            loads[k].wait()

        def partial(b):
            here = columns_at(cols, b, size)

            def product(mine_ref, theirs_ref, column_ref):
                total = lax.dot_general(
                    mine_ref[:, here], column_ref[:own, :], contract_rows, preferred_element_type=f32
                )
                total = total + lax.dot_general(
                    theirs_ref[:, here], column_ref[own:, :], contract_rows, preferred_element_type=f32
                )
                return total.astype(bf16)

            d_r[b, :, :pair_width] = product(one_mine, one_theirs, dboth_ref)
            d_r[b, :, pair_width:] = product(db_mine, db_theirs, mixed_ref)

        for b, hops in ((7, (1, 2)), (5, (0,))):
            partial(b)
            w.start(*hops)
        sums_x.wait_recv()
        sums_in[0] = sums_in[0] + sums_ref[...]
        sums_z.start()
        gates_x.wait_recv()
        add_rows(gates_in.at[0], gates_ref)
        gates_z.start()
        for b, hops in ((6, (3,)), (3, (5,))):
            partial(b)
            w.start(*hops)

        def back(start, out, out_at):
            for b in range(blocks):
                out[out_at, columns_at(cols, b, size)] = lax.dot_general(
                    dboth_ref[pl.ds(start, rows), :], w_ri[b], contract_cols, preferred_element_type=f32
                ).astype(out.dtype)

        loads[6].wait()
        for i, h in enumerate(halves):
            back(own + i * rows, part_out, h)
            e_core[i].start()
        w.step(4, add)
        w.step(6, add)
        for b in (4, 1):
            partial(b)
        for i, h in enumerate(halves):
            back(i * rows, part_sum, first)
            e_core[i].wait_recv()
            e_ref[h, :] = part_sum[:, left] + part_in[h, left].astype(f32)
            y_out[h, :] = (part_sum[:, right] + part_in[h, right].astype(f32)).astype(bf16)
            e_y[i].start()
        sums_z.wait_recv()
        sums_out[0] = sums_in[0] + sums_in[1]
        sums_end.start()
        sums_core.start()
        gates_z.wait_recv()
        gates_out[0] = gates_in[0]
        add_rows(gates_out.at[0], gates_in.at[1])
        gates_end.start()
        gates_core.start()
        w.step(8, add)
        w.start(7)
        for b in (2, 0):
            partial(b)
        w.step(9, add)
        term_ref[...] = term_in[...]
        for k in (7, 8):
            loads[k].wait()
        for i in range(2):
            e_y[i].wait_recv()
            norm_sums(e_ref, y_in, tok_left, gain_ref, 0, mean_ref, i * rows, rows)
        mean_y.start()
        unpack(0, at.c)
        mean_y.wait_recv()

        def keep(row_at, value):
            out_ref[row_at, :] = (value + dmid_ref[row_at, :]).astype(bf16)

        for i in (1, 0):
            norm_rows_back(
                e_ref, tok_left, gain_ref, 0, scale_ref, mean_ref, mean_in, term_ref, model,
                i * rows, rows, keep,
            )
            if i == 1:
                out_move.start()
        term_x.start()
        term_x.wait_recv()
        term_land[0] = term_land[0] + term_ref[...]
        term_z.start()
        w.received(7, 8)
        finish((w.partial.at[0], w.land.at[3], w.land.at[4]))
        term_z.wait_recv()
        term_land[1] = term_land[0] + term_land[1]
        term_core.start()
        term_core.wait_recv()
        term_out[...] = term_land[1] + term_land[2]
        term_end.start()
        w.hop(11, last_r).wait()
        w.sent(*work_hops)
        sums_core.wait_recv()
        gates_core.wait_recv()
        unpack(1, 1 - at.c)
        for moved in (
            *e_core, *e_y, mean_y, out_move, gates_x, gates_z, gates_end, gates_core,
            sums_x, sums_z, sums_end, sums_core, term_x, term_z, term_core, term_end,
        ):
            moved.wait_send()


in_vmem = pl.BlockSpec(memory_space=pltpu.VMEM)
in_smem = pl.BlockSpec(memory_space=pltpu.SMEM)
in_any = pl.BlockSpec(memory_space=pl.ANY)
no_cost = pl.CostEstimate(flops=0, bytes_accessed=0, transcendentals=0)
kernel_params = pltpu.CompilerParams(vmem_limit_bytes=60 * 2**20)
copy_sem = pltpu.SemaphoreType.DMA


def lane_shape(rows, width):
    return (pl.cdiv(width, lanes), rows, lanes)


def run_forward(count, splits, tokens, out_grad, mask, gains, vectors, wr, wi):
    rows, half_model = tokens.shape
    own, model, width = 2 * rows, 2 * half_model, wr.shape[0]
    size = 2 * splits[0].shape[1]
    shape = jax.ShapeDtypeStruct
    gathered_shapes = [shape((blocks, size, v.shape[2]), bf16) for v in splits]
    wide = shape((own, model), bf16)
    kept = [
        shape((2 * own, 2 * width), f32),
        shape(lane_shape(2 * own, width), f32),
        shape((2 * own, width), bf16),
        shape((2 * own, lanes), f32),
        shape((own, half_model), f32),
        shape((own, half_model), bf16),
        *[wide] * 6,
        shape((2, own, lanes), f32),
    ]
    hidden = shape((2 * own, splits[3].shape[2]), bf16)
    return pl.pallas_call(
        functools.partial(forward_kernel, count),
        out_shape=(*gathered_shapes, *kept, *[hidden] * 3),
        in_specs=[in_any] * 7 + [in_vmem] * 4,
        out_specs=[in_any] * 20,
        scratch_shapes=[
            *[
                pltpu.VMEM(wide.shape if i == 5 else v.shape, v.dtype)
                for i, v in enumerate(kept)
                if i not in (0, 2)
            ],
            pltpu.VMEM((own, model), bf16),
            pltpu.VMEM((own, model), bf16),
            pltpu.VMEM((own, model), bf16),
            pltpu.VMEM((own, half_model), bf16),
            pltpu.VMEM((own, half_model), bf16),
            pltpu.VMEM((own, model), bf16),
            copy_sem((4, 9)),
            copy_sem((4, 9)),
            copy_sem((4,)),
            copy_sem((2, blocks)),
            copy_sem((18,)),
            copy_sem((18,)),
            copy_sem((3,)),
            copy_sem((13,)),
            copy_sem((2, 2, blocks)),
            copy_sem((2, 3)),
        ],
        compiler_params=comm_params(0),
        cost_estimate=no_cost,
        name="gather_and_recur",
    )(*splits, tokens, out_grad, mask, gains, vectors, wr, wi)


def comm_params(collective):
    return pltpu.CompilerParams(
        vmem_limit_bytes=255 * 2**18, collective_id=collective, has_side_effects=True
    )


def run_backward(
    count, weights, mlp_kept, normed_two, grad_low, middle, weight, both, state,
    scales, gains, mask, vectors, wr, wi, block,
):
    own, half_model = middle.shape
    model, width, rows = 2 * half_model, wr.shape[0], own // 2
    size = weight.shape[1]
    shape = jax.ShapeDtypeStruct
    hidden = [v.shape[2] for v in weights]
    wide = shape((own, model), bf16)
    kept = (shape((own, half_model), f32), wide, wide)
    return pl.pallas_call(
        functools.partial(backward_kernel, count),
        out_shape=(
            *[shape(v.shape, bf16) for v in weights],
            *[shape((5, size, n), bf16) for n in hidden],
            *[shape((2, size // 2, n), bf16) for n in hidden],
            *kept,
            shape((2 * own, 2 * width), bf16),
            shape((own, half_model), bf16),
            shape((8, width), f32),
            shape((block, 2 * width), bf16),
            shape((8, half_model), f32),
        ),
        in_specs=[in_any] * 13 + [in_vmem] * 6,
        out_specs=[in_any] * 10 + [in_vmem] * 4,
        scratch_shapes=[
            pltpu.VMEM((own, half_model), f32),
            *[pltpu.VMEM(v.shape, v.dtype) for v in kept],
            *[pltpu.VMEM((own, model), bf16)] * 3,
            *[pltpu.VMEM((own, half_model), bf16)] * 4,
            pltpu.VMEM((own, lanes), f32),
            pltpu.VMEM((own, lanes), f32),
            pltpu.VMEM((size, max(hidden)), bf16),
            pltpu.VMEM((size, max(hidden)), bf16),
            copy_sem((2, 12)),
            copy_sem((2, 12)),
            copy_sem((14,)),
            copy_sem((14,)),
            copy_sem((10,)),
            copy_sem((4,)),
            copy_sem((4,)),
            copy_sem((2, blocks)),
            copy_sem((2,)),
        ],
        compiler_params=comm_params(1),
        cost_estimate=no_cost,
        name="sum_and_back",
    )(
        *weights, *mlp_kept, *normed_two, *grad_low, middle, weight, both, state,
        scales, gains, mask, vectors, wr, wi,
    )


def run_finish(
    count, normed, d_branch, d_both, mixed, weight, tokens, d_middle, scales, gains, sums, gates, term
):
    own, half_model = d_middle.shape
    model, rows = 2 * half_model, own // 2
    size = weight.shape[1]
    width = weight.shape[2] + mixed.shape[1]
    shape = jax.ShapeDtypeStruct
    held = (*normed, *d_branch, d_both, mixed, weight, tokens, d_middle)
    block = gates.shape[0]
    square = shape((gates.shape[1] // block, block, block), f32)
    return pl.pallas_call(
        functools.partial(finish_kernel, count),
        out_shape=(
            shape((2, size // 2, width), bf16),
            shape((own, half_model), bf16),
            square,
            square,
            shape((2, *sums.shape), f32),
            shape(term.shape, f32),
        ),
        in_specs=[in_any] * 9 + [in_vmem] * 5,
        out_specs=[in_vmem] * 6,
        scratch_shapes=[
            *[pltpu.VMEM(v.shape, v.dtype) for v in held],
            pltpu.VMEM((blocks, size, width), bf16),
            pltpu.VMEM((5, size, width), bf16),
            pltpu.VMEM((own, model), bf16),
            pltpu.VMEM((own, model), bf16),
            pltpu.VMEM((rows, model), f32),
            pltpu.VMEM((own, half_model), bf16),
            pltpu.VMEM((own, half_model), bf16),
            pltpu.VMEM((own, half_model), f32),
            pltpu.VMEM((own, lanes), f32),
            pltpu.VMEM((own, lanes), f32),
            pltpu.VMEM((size, width), bf16),
            pltpu.VMEM((2, *gates.shape), bf16),
            pltpu.VMEM((2, *gates.shape), bf16),
            pltpu.VMEM((2, *sums.shape), f32),
            pltpu.VMEM(term.shape, f32),
            pltpu.VMEM((3, *term.shape), f32),
            copy_sem((12,)),
            copy_sem((12,)),
            copy_sem((18,)),
            copy_sem((18,)),
            copy_sem((9,)),
        ],
        compiler_params=comm_params(2),
        cost_estimate=no_cost,
        name="sum_and_finish",
    )(*held, scales, gains, sums, gates, term)


def block_diagonal(blocks):
    count, size = blocks.shape[0], blocks.shape[1]
    rows = [
        jnp.pad(blocks[h], ((0, 0), (h * size, (count - 1 - h) * size))) for h in range(count)
    ]
    return jnp.concatenate(rows, axis=0)


def diagonal_blocks(square, count):
    size = square.shape[0] // count
    return jnp.stack(
        [square[h * size : (h + 1) * size, h * size : (h + 1) * size] for h in range(count)]
    )


def masks_of(lengths, rows):
    ends = jnp.cumsum(lengths, axis=1)
    starts = ends - lengths
    places = jnp.arange(rows, dtype=jnp.int32)[None, :, None]
    inside = (places >= starts[:, None, :]) & (places < ends[:, None, :])
    first_place = jnp.sum(jnp.where(inside, starts[:, None, :], 0), axis=2)
    places = places[:, :, 0]
    live = (places < ends[:, 2:3]).astype(f32)
    columns = [(places != first_place).astype(f32)]
    for k in range(1, 4):
        columns.append((places - k >= first_place).astype(f32))
    columns += [live] + [jnp.zeros_like(live)] * 3
    return jnp.stack(columns, axis=2).reshape(lengths.shape[0] * rows, 8), live


def local(
    n_dp,
    tokens,
    gain_rnn,
    rnn_in,
    gate_recur,
    gate_input,
    bias_recur,
    bias_input,
    decay_param,
    conv_weight,
    conv_bias,
    rnn_out,
    gain_mlp,
    mlp_in,
    mlp_out,
    lengths,
    out_grad,
):
    outer_count = n_dp // 16
    rows_here = rnn_in.shape[0]
    model = gain_rnn.shape[0]
    half_model = model // 2
    buffer_rows = tokens.shape[0]
    own_rows = 2 * buffer_rows
    index = lax.axis_index("dp")
    y = lax.axis_index("mp")
    c = index // outer_count % 2
    x = index // (2 * outer_count) % 2
    z = index // (4 * outer_count)
    outer = jnp.where(z < 2, 0, 3)
    far = 3 - z
    far_outer = 3 - outer

    def pick_c(first, second):
        return jnp.where(c == 0, first, second)

    def pick_y(first, second):
        return jnp.where(y == 0, first, second)

    group_rows = outer_count * rows_here
    block_rows = 2 * group_rows

    outer_groups = [[i * outer_count + w for w in range(outer_count)] for i in range(16)]

    def over_outer(value):
        if outer_count == 1:
            return value
        return lax.all_gather(value, "dp", axis_index_groups=outer_groups, axis=1, tiled=True)

    cols = jnp.stack(
        [
            ((at_z + 2 * y) % 4 * 2 + at_x) * block_rows
            for at_z in (z, outer, far, far_outer)
            for at_x in (x, 1 - x)
        ]
    ).astype(jnp.int32)

    def settle_grad(total):
        total = total.astype(f32)
        if outer_count > 1:
            total = lax.psum_scatter(
                total, "dp", axis_index_groups=outer_groups, scatter_dimension=1, tiled=True
            )
        return total

    def joined_pair(total):
        _, row_count, columns = total.shape
        parts = settle_grad(total).reshape(2, -1, 2, columns // 2).transpose(1, 2, 0, 3)
        return parts.reshape(-1, 2, columns)

    def joined_out(total):
        return settle_grad(total).swapaxes(0, 1).reshape(-1, 2 * total.shape[2])

    def over_groups(value):
        return lax.psum(value, "dp", axis_index_groups=outer_groups) if outer_count > 1 else value

    def relative(vector):
        first, second = vector[:half_model], vector[half_model:]
        return jnp.concatenate([pick_y(first, second), pick_y(second, first)])

    def quarters(value, axis):
        size = value.shape[axis] // 2
        return (
            lax.slice_in_dim(value, 0, size, axis=axis),
            lax.slice_in_dim(value, size, 2 * size, axis=axis),
        )

    def quarter(value, axis=0):
        return pick_c(*quarters(value, axis))

    gain_one, gain_two = relative(gain_rnn.astype(f32)), relative(gain_mlp.astype(f32))
    mask, _ = masks_of(lengths, buffer_rows)
    mask = jnp.pad(mask, ((0, 0), (0, lanes - mask.shape[1])))
    softened = jax.nn.softplus(-quarter(decay_param))
    vectors = jnp.concatenate(
        [
            quarter(conv_weight, 1),
            jnp.stack([quarter(conv_bias), quarter(bias_recur), quarter(bias_input), softened]),
        ],
        axis=0,
    )
    heads = gate_recur.shape[0] // 2
    wr = block_diagonal(quarter(gate_recur))
    wi = block_diagonal(quarter(gate_input))
    def split_pair(weight):
        row_count, _, columns = weight.shape
        parts = weight.reshape(row_count, 2, 2, columns // 2).transpose(2, 0, 1, 3)
        return over_outer(parts.reshape(2, row_count, columns))

    def split_out(weight):
        row_count, columns = weight.shape
        return over_outer(weight.reshape(row_count, 2, columns // 2).swapaxes(0, 1))

    splits = (split_pair(rnn_in), split_out(rnn_out), split_pair(mlp_in), split_out(mlp_out))
    gains = jnp.stack([gain_one, gain_two])
    (
        rnn_in_all, rnn_out_all, mlp_in_all, mlp_out_all,
        both, state, mixed, mask, middle, tokens_all,
        *rows_kept, scales, act, gate_slope, gate_value,
    ) = run_forward(outer_count, splits, tokens, out_grad, mask, gains, vectors, wr, wi)
    normed, normed_two, grad_low = rows_kept[0:2], rows_kept[2:4], rows_kept[4:6]

    (
        _, _, _, _, mlp_in_total, mlp_out_total, d_middle, d_branch, d_branch_theirs, d_both,
        output_two, sums, gates, term,
    ) = run_backward(
        outer_count,
        (mlp_in_all, mlp_out_all),
        (act, gate_slope, gate_value),
        normed_two,
        grad_low,
        middle,
        rnn_out_all,
        both,
        state,
        scales,
        gains,
        mask,
        vectors,
        wr,
        wi,
        gate_recur.shape[1],
    )
    rnn_total, tokens_grad_two, recur_grad, input_grad, sums, term = run_finish(
        outer_count,
        normed,
        (d_branch, d_branch_theirs),
        d_both,
        mixed,
        rnn_in_all,
        tokens_all,
        d_middle,
        scales,
        gains,
        sums,
        gates,
        term,
    )
    rnn_width = rnn_in.shape[2]
    rnn_in_total, rnn_out_total = rnn_total[:, :, :rnn_width], rnn_total[:, :, rnn_width:]
    layer_output, tokens_grad = output_two[:buffer_rows], tokens_grad_two[:buffer_rows]
    def both_quarters(pair, axis):
        return over_groups(
            pick_c(
                jnp.concatenate([pair[0], pair[1]], axis=axis),
                jnp.concatenate([pair[1], pair[0]], axis=axis),
            )
        )

    sums = both_quarters(sums, 1)
    recur_grad, input_grad = over_groups(recur_grad), over_groups(input_grad)
    gains_grad = over_groups(term[:2])

    return (
        layer_output,
        tokens_grad,
        gains_grad[0],
        joined_pair(rnn_in_total),
        recur_grad,
        input_grad,
        sums[5],
        sums[6],
        8.0 * jax.nn.sigmoid(-decay_param) * sums[7],
        sums[:4],
        sums[4],
        joined_out(rnn_out_total),
        gains_grad[1],
        joined_pair(mlp_in_total),
        joined_out(mlp_out_total),
    )


def solution(mesh):
    return jax.shard_map(
        functools.partial(local, mesh.shape["dp"]),
        mesh=mesh,
        in_specs=(
            P("dp", "mp"),
            P(),
            P("dp", None, "mp"),
            P("mp", None, None),
            P("mp", None, None),
            P("mp"),
            P("mp"),
            P("mp"),
            P(None, "mp"),
            P("mp"),
            P("dp", "mp"),
            P(),
            P("dp", None, "mp"),
            P("dp", "mp"),
            P("dp", None),
            P("dp", "mp"),
        ),
        out_specs=(
            P("dp", "mp"),
            P("dp", "mp"),
            P("mp"),
            P("dp", None, "mp"),
            P("mp", None, None),
            P("mp", None, None),
            P("mp"),
            P("mp"),
            P("mp"),
            P(None, "mp"),
            P("mp"),
            P("dp", "mp"),
            P("mp"),
            P("dp", None, "mp"),
            P("dp", "mp"),
        ),
        check_vma=False,
    )
```

```python
import functools

import jax
import jax.numpy as jnp
from jax import lax
from jax.experimental import pallas as pl
from jax.experimental.pallas import tpu as pltpu
from jax.sharding import PartitionSpec as P

norm_eps = 1e-06
root_eps = 0.001
bf16 = jnp.bfloat16
f32 = jnp.float32
contract_cols = (((1,), (1,)), ((), ()))
contract_rows = (((0,), (0,)), ((), ()))
gelu_scale = 0.7978845608028654
gelu_cubic = 0.044715
held_buffers = 4
scan_unroll = 8
blocks = 8
chunk_rows = 512
lanes = 128
by_mesh = pl.DeviceIdType.MESH


def pairs(n_dp, move):
    count = n_dp // 16
    found = []
    for i in range(n_dp):
        w, c, x, z = i % count, i // count % 2, i // count // 2 % 2, i // count // 4
        target = move(z, x, c)
        if target is not None:
            z, x, c = target
            found.append((i, ((z * 2 + x) * 2 + c) * count + w))
    return found


def gelu_parts(v):
    tanh_value = jnp.tanh(gelu_scale * (v + gelu_cubic * v * v * v))
    value = 0.5 * v * (1.0 + tanh_value)
    slope = 0.5 * (1.0 + tanh_value) + 0.5 * v * (1.0 - tanh_value * tanh_value) * (
        gelu_scale * (1.0 + 3.0 * gelu_cubic * v * v)
    )
    return value, slope


def shifted(value, offset):
    return pltpu.roll(value, offset % value.shape[0], 0)


def store_lanes(ref, at, value):
    chunks = ref.shape[0]
    spare = chunks * lanes - value.shape[1]
    if spare:
        value = jnp.concatenate([value, jnp.zeros((value.shape[0], spare), f32)], axis=1)
    for i in range(chunks):
        ref[i, at, :] = value[:, i * lanes : (i + 1) * lanes]


def load_lanes(ref, at, width):
    return jnp.concatenate([ref[i, at, :] for i in range(ref.shape[0])], axis=1)[:, :width]


def scan_rows(coef_ref, push_ref, rows, reverse):
    chunks = coef_ref.shape[0]

    def step(i, carried):
        carried = list(carried)
        for j in range(scan_unroll):
            t = i * scan_unroll + j
            at = pl.ds(rows - 1 - t if reverse else t, held_buffers, stride=rows)
            for k in range(chunks):
                if reverse:
                    value = push_ref[k, at, :] + carried[k]
                    carried[k] = coef_ref[k, at, :] * value
                else:
                    value = coef_ref[k, at, :] * carried[k] + push_ref[k, at, :]
                    carried[k] = value
                push_ref[k, at, :] = value
        return tuple(carried)

    start = tuple(jnp.zeros((held_buffers, lanes), f32) for _ in range(chunks))
    lax.fori_loop(0, rows // scan_unroll, step, start)


def columns_at(cols_ref, b, size):
    return pl.ds(pl.multiple_of(cols_ref[b], size), size)


def gathered(ref, at, cols_ref, size):
    return jnp.concatenate([ref[at, columns_at(cols_ref, b, size)] for b in range(blocks)], axis=1)


def stacked(refs, columns=slice(None)):
    return jnp.concatenate([ref[:, columns] for ref in refs], axis=0)


def project(mine_ref, theirs_ref, weight_refs, cols_ref, use):
    size = weight_refs[0].shape[0]
    own = mine_ref.shape[0]
    for part, ref in enumerate((mine_ref, theirs_ref)):

        def chunk(i, carry, part=part, ref=ref):
            at = pl.ds(pl.multiple_of(i * chunk_rows, chunk_rows), chunk_rows)
            rows = gathered(ref, at, cols_ref, size)
            use(
                pl.multiple_of(part * own + i * chunk_rows, chunk_rows),
                jnp.dot(rows, stacked(weight_refs), preferred_element_type=f32),
            )
            return carry

        lax.fori_loop(0, own // chunk_rows, chunk, 0)


def columns_at(cols, b, size):
    return pl.ds(pl.multiple_of(cols[b], size), size)


def gathered(ref, at, cols, size):
    return jnp.concatenate([ref[at, columns_at(cols, b, size)] for b in range(blocks)], axis=1)


def stacked(weight_ref):
    return weight_ref[...].reshape(-1, weight_ref.shape[2])


def project(mine_ref, theirs_ref, weight, size, cols, use):
    own = mine_ref.shape[0]
    for part, ref in enumerate((mine_ref, theirs_ref)):

        def chunk(i, carry, part=part, ref=ref):
            at = pl.ds(pl.multiple_of(i * chunk_rows, chunk_rows), chunk_rows)
            rows = gathered(ref, at, cols, size)
            use(
                pl.multiple_of(part * own + i * chunk_rows, chunk_rows),
                jnp.dot(rows, weight(), preferred_element_type=f32),
            )
            return carry

        lax.fori_loop(0, own // chunk_rows, chunk, 0)


def buffer_rows_at(b, rows):
    return pl.ds(pl.multiple_of(b * rows, rows), rows)


def conv_of(inner, mask, vec_ref):
    conv = vec_ref[4:5, :] + vec_ref[0:1, :] * inner
    for k in range(1, 4):
        conv = conv + vec_ref[k : k + 1, :] * (shifted(inner, k) * mask[:, k : k + 1])
    return conv


def gates_of(conv_low, vec_ref, wr_ref, wi_ref):
    rate = jax.nn.sigmoid(
        jnp.dot(conv_low, wr_ref[...], preferred_element_type=f32) + vec_ref[5:6, :]
    )
    igate = jax.nn.sigmoid(
        jnp.dot(conv_low, wi_ref[...], preferred_element_type=f32) + vec_ref[6:7, :]
    )
    return rate, igate


def recur_state(both_ref, mask_ref, vec_ref, wr_ref, wi_ref, coef_ref, push_ref):
    width = both_ref.shape[1] // 2
    rows = both_ref.shape[0] // held_buffers

    def gates(b, carry):
        at = buffer_rows_at(b, rows)
        mask = mask_ref[at, :]
        conv = conv_of(both_ref[at, :width], mask, vec_ref)
        rate, igate = gates_of(conv.astype(bf16), vec_ref, wr_ref, wi_ref)
        decay = jnp.exp(-8.0 * rate * vec_ref[7:8, :])
        root = jnp.sqrt(1.0 - decay * decay + root_eps)
        store_lanes(coef_ref, at, decay * mask[:, 0:1])
        store_lanes(push_ref, at, root * igate * conv)
        return carry

    lax.fori_loop(0, held_buffers, gates, 0)
    scan_rows(coef_ref, push_ref, rows, False)


def recur_mixed(both_ref, state_ref, mixed_ref):
    width = both_ref.shape[1] // 2
    rows = both_ref.shape[0] // held_buffers

    def mix(b, carry):
        at = buffer_rows_at(b, rows)
        gate = gelu_parts(both_ref[at, width:])[0]
        mixed_ref[at, :] = (load_lanes(state_ref, at, width) * gate).astype(bf16)
        return carry

    lax.fori_loop(0, held_buffers, mix, 0)


def stream_tiles(first, last, fetch, body):
    fetch(first, first % 2).start()

    def step(t, carry):
        slot = t % 2

        @pl.when(t + 1 < last)
        def _():
            fetch(t + 1, 1 - slot).start()

        fetch(t, slot).wait()
        body(t, slot)
        return carry

    lax.fori_loop(first, last, step, 0)


class Tile:
    def __init__(self, weight, room, sems, first_column, tile):
        at = pl.ds(pl.multiple_of(first_column, tile), tile)
        self.copies = [
            pltpu.make_async_copy(
                weight.at[b, :, at], room.at[:, pl.ds(b * tile, tile)], sems.at[b]
            )
            for b in range(blocks)
        ]

    def start(self):
        for v in self.copies:
            v.start()

    def wait(self):
        for v in self.copies:
            v.wait()


def tile_rows(room, tile):
    return jnp.concatenate([room[:, b * tile : (b + 1) * tile] for b in range(blocks)], axis=0)


class Place:
    def __init__(self, count):
        self.me = lax.axis_index("dp")
        self.y = lax.axis_index("mp")
        self.c = self.me // count % 2
        self.x = self.me // (2 * count) % 2
        self.z = self.me // (4 * count)
        self.core = {"dp": self.me + (1 - 2 * self.c) * count}
        self.beside = {"dp": self.me + (1 - 2 * self.x) * 2 * count}
        self.over_y = {"mp": 1 - self.y}
        sign = 1 - 2 * (self.z // 2)
        self.ahead = {"dp": self.me + sign * 4 * count}
        self.behind = {"dp": self.me - sign * 4 * count}
        self.works = (self.z + 1) // 2 == 1
        self.serves = (self.z + 1) // 2 != 1

    def columns(self, size):
        outer = self.z // 2 * 3
        far, far_outer = 3 - self.z, 3 - outer
        return [
            ((at_z + 2 * self.y) % 4 * 2 + at_x) * size
            for at_z in (self.z, outer, far, far_outer)
            for at_x in (self.x, 1 - self.x)
        ]

    def meet(self):
        barrier = pltpu.get_barrier_semaphore()

        def greet(partners):
            for partner in partners:
                pl.semaphore_signal(barrier, inc=1, device_id=partner, device_id_type=by_mesh)
            pl.semaphore_wait(barrier, len(partners))

        @pl.when(self.works)
        def _():
            greet((self.core, self.beside, self.over_y, self.ahead, self.behind))

        @pl.when(self.serves)
        def _():
            greet((self.core, self.beside, self.ahead))


def remote(src, dst, send, recv, where):
    return pltpu.make_async_remote_copy(
        src_ref=src,
        dst_ref=dst,
        send_sem=send,
        recv_sem=recv,
        device_id=where,
        device_id_type=by_mesh,
    )


def normed_rows(source_ref, gain_ref, gain_row, scale_ref, scale_row, out_ref, first, count):
    size = 128

    def chunk(i, carry):
        at = pl.ds(pl.multiple_of(first + i * size, size), size)
        rows = source_ref[at, :].astype(f32)
        scale = lax.rsqrt(jnp.mean(rows * rows, axis=1, keepdims=True) + norm_eps)
        scale_ref[scale_row, at, :] = jnp.broadcast_to(scale, (size, lanes))
        out_ref[at, :] = (rows * scale * gain_ref[gain_row : gain_row + 1, :]).astype(bf16)
        return carry

    lax.fori_loop(0, count // size, chunk, 0)


def forward_kernel(
    count,
    s_ri, s_ro, s_mi, s_mo,
    tokens_ref, grad_ref, lengths_ref, gain_ref, taps_ref, biases_ref, recur_blocks, input_blocks,
    g_ri, g_ro, g_mi, g_mo, *refs,
):
    results, mlp_out_refs, refs = refs[:16], refs[16:19], refs[19:]
    (
        state_ref, mask_ref, middle_ref, tok_ref,
        one_mine, one_theirs, two_mine, two_theirs, low_mine, low_theirs, scale_ref,
        vec_ref, wr_ref, wi_ref,
    ) = refs[:14]
    (
        grad_all, part_out, part_in, y_out, y_in, mid_ref,
        w_send, w_recv, w_local, load_sem, m_send, m_recv, m_local, out_sem, tile_sem, mlp_sem,
    ) = refs[14:]
    held = (
        None, state_ref, None, mask_ref, middle_ref, tok_ref,
        one_mine, one_theirs, two_mine, two_theirs, low_mine, low_theirs, scale_ref,
        vec_ref, wr_ref, wi_ref,
    )
    at = Place(count)
    half_rows = s_ri.shape[1]
    size = 2 * half_rows
    model = tok_ref.shape[1]
    half_model = model // 2
    rows = tokens_ref.shape[0]
    own = 2 * rows
    cols = at.columns(size)
    whole, splits = (g_ri, g_ro, g_mi, g_mo), (s_ri, s_ro, s_mi, s_mo)
    ri, ro, mi, mo = range(4)
    top, bottom = pl.ds(0, half_rows), pl.ds(half_rows, half_rows)
    core_rows = pl.ds(pl.multiple_of(at.c * half_rows, half_rows), half_rows)

    def split(w, quarter):
        if w == mo:
            columns = whole[w].shape[2]
            return s_mo.at[:, pl.ds(pl.multiple_of(quarter * columns, lanes), columns)]
        return splits[w].at[quarter]

    def hop(w, k):
        g = whole[w]
        src, dst, where = (
            (split(w, 1 - at.c), g.at[0, core_rows], at.core),
            (g.at[0], g.at[1], at.beside),
            (g.at[0], g.at[2], at.ahead),
            (g.at[1], g.at[3], at.ahead),
            (g.at[0], g.at[4], at.ahead),
            (g.at[4], g.at[5], at.beside),
            (g.at[2], g.at[6], at.ahead),
            (g.at[3, top], g.at[7, top], at.ahead),
            (g.at[6, bottom], g.at[7, bottom], at.beside),
        )[k]
        return remote(src, dst, w_send.at[w, k], w_recv.at[w, k], where)

    def kept(w):
        return pltpu.make_async_copy(split(w, at.c), whole[w].at[0, core_rows], w_local.at[w])

    def begin(w):
        kept(w).start()
        hop(w, 0).start()

    def own_block(w, hops):
        kept(w).wait()
        hop(w, 0).wait()
        for k in hops:
            hop(w, k).start()

    def pass_on(w, arrived, sent):
        hop(w, arrived).wait_recv()
        hop(w, sent).start()

    def move(k, src, dst, where):
        return remote(src, dst, m_send.at[k], m_recv.at[k], where)

    first, second = pl.ds(0, rows), pl.ds(rows, rows)
    left, right = pl.ds(0, half_model), pl.ds(half_model, half_model)
    mine_rows, their_rows = pl.ds(0, own), pl.ds(own, own)
    token_in = move(0, tokens_ref, tok_ref.at[second, left], at.ahead)
    token_y = move(1, tokens_ref, tok_ref.at[first, right], at.over_y)
    token_y_two = move(2, tok_ref.at[second, left], tok_ref.at[second, right], at.over_y)
    grad_in = move(3, grad_ref, grad_all.at[second, left], at.ahead)
    grad_y = move(4, grad_ref, grad_all.at[first, right], at.over_y)
    grad_y_two = move(5, grad_all.at[second, left], grad_all.at[second, right], at.over_y)
    mask_move = move(6, mask_ref.at[first], mask_ref.at[second], at.ahead)
    mask_core = move(7, mask_ref.at[mine_rows], mask_ref.at[their_rows], at.core)
    one_core = move(8, one_mine, one_theirs, at.core)
    low_core = move(9, low_mine, low_theirs, at.core)
    halves = (first, second)
    part_core = [move(10 + i, part_out.at[h], part_in.at[h], at.core) for i, h in enumerate(halves)]
    part_y = [move(12 + i, y_out.at[h], y_in.at[h], at.over_y) for i, h in enumerate(halves)]
    mid_y = [
        move(14 + i, mid_ref.at[h, left], mid_ref.at[h, right], at.over_y)
        for i, h in enumerate(halves)
    ]
    two_core = [move(16 + i, two_mine.at[h], two_theirs.at[h], at.core) for i, h in enumerate(halves)]
    token_here = pltpu.make_async_copy(tokens_ref, tok_ref.at[first, left], m_local.at[0])
    grad_here = pltpu.make_async_copy(grad_ref, grad_all.at[first, left], m_local.at[1])

    def load(w, target, b):
        return pltpu.make_async_copy(whole[w].at[b], target.at[b], load_sem.at[w, b])

    def keep_out(k, source=None):
        if source is None:
            source = held[k].at[:, left] if k == 5 else held[k]
        return pltpu.make_async_copy(source, results[k], out_sem.at[k])

    def make_mask():
        place = lax.broadcasted_iota(jnp.int32, (rows, lanes), 0)
        lane = lax.broadcasted_iota(jnp.int32, (rows, lanes), 1)
        ends = [lengths_ref[0, 0]]
        for k in (1, 2):
            ends.append(ends[-1] + lengths_ref[0, k])
        start = jnp.zeros((rows, lanes), jnp.int32)
        for end in ends:
            start = jnp.where(place >= end, end, start)
        offset = place - start
        bound = jnp.where(lane == 0, 1, jnp.where(lane == 4, place + 1 - ends[2] + offset, lane))
        mask_ref[first, :] = jnp.where((offset >= bound) & (lane < 5), 1.0, 0.0)

    def make_parameters():
        width = vec_ref.shape[1]

        def quarter(ref, row):
            value = ref[row : row + 1, :]
            return jnp.where(at.c == 0, value[:, :width], value[:, width:])

        for k in range(4):
            vec_ref[k : k + 1, :] = quarter(taps_ref, k)
        for k in range(3):
            vec_ref[4 + k : 5 + k, :] = quarter(biases_ref, k)
        turned = -quarter(biases_ref, 3)
        vec_ref[7:8, :] = jnp.maximum(turned, 0.0) + jnp.log1p(jnp.exp(-jnp.abs(turned)))
        block = recur_blocks.shape[1]
        count_heads = width // block
        for source, target in ((recur_blocks, wr_ref), (input_blocks, wi_ref)):
            for h in range(count_heads):
                parts = [source[at.c * count_heads + h]]
                if h > 0:
                    parts.insert(0, jnp.zeros((block, h * block), bf16))
                if h + 1 < count_heads:
                    parts.append(jnp.zeros((block, (count_heads - 1 - h) * block), bf16))
                target[h * block : (h + 1) * block, :] = jnp.concatenate(parts, axis=1)

    at.meet()

    @pl.when(at.serves)
    def _():
        for w in (ri, ro, mi, mo):
            begin(w)
        token_in.start()
        make_mask()
        mask_move.start()
        own_block(ri, (1, 2))
        pass_on(ri, 1, 3)
        own_block(ro, (1, 2))
        pass_on(ro, 1, 3)
        own_block(mi, (1, 2))
        grad_in.start()
        pass_on(mi, 1, 3)
        own_block(mo, (1, 2))
        pass_on(mo, 1, 3)
        for w in (ri, ro, mi, mo):
            for k in (1, 2, 3):
                hop(w, k).wait_send()
        for moved in (mask_move, token_in, grad_in):
            moved.wait_send()

    def recur_part(both_ref, mixed_ref, coef_ref, w_ri, w_ro, part_sum):
        for w, target in ((ri, w_ri), (ro, w_ro)):
            hop(w, 1).wait_recv()
            for k in (5, 7, 8):
                hop(w, k).wait_recv()
            for b in range(blocks):
                load(w, target, b).start()
        for b in range(blocks):
            load(ri, w_ri, b).wait()
        one_core.wait_recv()
        mask_core.wait_recv()

        def keep_both(start, value):
            both_ref[pl.ds(start, chunk_rows), :] = value

        for k in (3, 5, 6, 7):
            keep_out(k).start()
        project(one_mine, one_theirs, lambda: stacked(w_ri), size, cols, keep_both)
        keep_out(0, both_ref).start()
        grad_in.wait_recv()
        grad_y_two.start()
        recur_state(both_ref, mask_ref, vec_ref, wr_ref, wi_ref, coef_ref, state_ref)
        keep_out(1).start()
        pass_on(mi, 2, 6)
        pass_on(mi, 4, 5)
        recur_mixed(both_ref, state_ref, mixed_ref)
        keep_out(2, mixed_ref).start()
        for b in range(blocks):
            load(ro, w_ro, b).wait()

        def branch(start, out_ref, out_at):
            for b in range(blocks):
                out_ref[out_at, columns_at(cols, b, size)] = lax.dot_general(
                    mixed_ref[pl.ds(start, rows), :],
                    w_ro[b],
                    contract_cols,
                    preferred_element_type=f32,
                ).astype(out_ref.dtype)

        for i, h in enumerate(halves):
            branch(own + i * rows, part_out, h)
            part_core[i].start()
        for i, h in enumerate(halves):
            branch(i * rows, part_sum, first)
            part_core[i].wait_recv()
            middle_ref[h, :] = part_sum[:, left] + part_in[h, left].astype(f32)
            y_out[h, :] = (part_sum[:, right] + part_in[h, right].astype(f32)).astype(bf16)
            part_y[i].start()
        keep_out(0, both_ref).wait()
        keep_out(2, mixed_ref).wait()

    def mlp_part(gate_room, up_room, act_room, slope_room, value_room):
        hidden = mlp_out_refs[0].shape[1]
        tile = act_room.shape[2]
        rooms = (act_room, slope_room, value_room)

        class Both:
            def __init__(self, t, slot):
                self.tiles = (
                    Tile(g_mi, gate_room.at[slot], tile_sem.at[slot, 0], t * tile, tile),
                    Tile(g_mi, up_room.at[slot], tile_sem.at[slot, 1], hidden + t * tile, tile),
                )

            def start(self):
                for v in self.tiles:
                    v.start()

            def wait(self):
                for v in self.tiles:
                    v.wait()

        def results_of(t, slot):
            columns = pl.ds(pl.multiple_of(t * tile, tile), tile)
            return [
                pltpu.make_async_copy(room.at[slot], out.at[:, columns], mlp_sem.at[slot, k])
                for k, (room, out) in enumerate(zip(rooms, mlp_out_refs))
            ]

        def body(t, slot):
            @pl.when(t >= 2)
            def _():
                for v in results_of(t - 2, slot):
                    v.wait()

            for part, ref in enumerate((two_mine, two_theirs)):
                row_values = gathered(ref, slice(None), cols, size)
                gate = jnp.dot(
                    row_values, tile_rows(gate_room.at[slot], tile), preferred_element_type=f32
                )
                up = jnp.dot(
                    row_values, tile_rows(up_room.at[slot], tile), preferred_element_type=f32
                )
                value, slope = gelu_parts(gate)
                row_at = pl.ds(part * own, own)
                act_room[slot, row_at, :] = (value * up).astype(bf16)
                slope_room[slot, row_at, :] = (slope * up).astype(bf16)
                value_room[slot, row_at, :] = value.astype(bf16)
            for v in results_of(t, slot):
                v.start()

        count_tiles = hidden // tile
        stream_tiles(0, 2, Both, body)
        pass_on(mo, 2, 6)
        pass_on(mo, 4, 5)
        stream_tiles(2, count_tiles, Both, body)
        pass_on(mo, 3, 7)
        pass_on(mo, 6, 8)
        for t in (count_tiles - 2, count_tiles - 1):
            for v in results_of(t, t % 2):
                v.wait()

    @pl.when(at.works)
    def _():
        begin(ri)
        begin(ro)
        token_here.start()
        token_y.start()
        grad_here.start()
        begin(mi)
        begin(mo)
        own_block(ri, (1, 4))
        own_block(ro, (1, 4))
        make_mask()
        pass_on(ri, 4, 5)
        token_in.wait_recv()
        token_y_two.start()
        pass_on(ri, 2, 6)
        pass_on(ro, 4, 5)
        token_here.wait()
        token_y.wait_recv()
        normed_rows(tok_ref, gain_ref, 0, scale_ref, 0, one_mine, 0, rows)
        token_y_two.wait_recv()
        normed_rows(tok_ref, gain_ref, 0, scale_ref, 0, one_mine, rows, rows)
        one_core.start()
        own_block(mi, (1, 4))
        make_parameters()
        keep_out(13).start()
        keep_out(14).start()
        keep_out(15).start()
        mask_move.wait_recv()
        mask_core.start()
        pass_on(ri, 3, 7)
        pass_on(ri, 6, 8)
        pass_on(ro, 2, 6)
        pass_on(ro, 3, 7)
        pass_on(ro, 6, 8)
        grad_y.start()
        width = vec_ref.shape[1]
        pl.run_scoped(
            recur_part,
            pltpu.VMEM((2 * own, 2 * width), f32),
            pltpu.VMEM((2 * own, width), bf16),
            pltpu.VMEM(state_ref.shape, f32),
            pltpu.VMEM(g_ri.shape, bf16),
            pltpu.VMEM(g_ro.shape, bf16),
            pltpu.VMEM((rows, model), f32),
        )
        grad_here.wait()
        grad_y.wait_recv()
        grad_y_two.wait_recv()
        low_mine[...] = (grad_all[...].astype(f32) * mask_ref[mine_rows, 4:5]).astype(bf16)
        low_core.start()
        keep_out(10).start()
        for i, h in enumerate(halves):
            part_y[i].wait_recv()
            middle = middle_ref[h, :] + y_in[h, :].astype(f32) + tok_ref[h, left].astype(f32)
            middle_ref[h, :] = middle
            mid_ref[h, left] = middle.astype(bf16)
            mid_y[i].start()
        keep_out(4).start()
        pass_on(mi, 3, 7)
        pass_on(mi, 6, 8)
        own_block(mo, (1, 4))
        for i, h in enumerate(halves):
            mid_y[i].wait_recv()
            normed_rows(mid_ref, gain_ref, 1, scale_ref, 1, two_mine, i * rows, rows)
            two_core[i].start()
        keep_out(8).start()
        keep_out(12).start()
        low_core.wait_recv()
        keep_out(11).start()
        for moved in two_core:
            moved.wait_recv()
        keep_out(9).start()
        for k in (1, 5, 7, 8):
            hop(mi, k).wait_recv()
        tile = 256
        pl.run_scoped(
            mlp_part,
            *[pltpu.VMEM((2, size, blocks * tile), bf16)] * 2,
            *[pltpu.VMEM((2, 2 * own, tile), bf16)] * 3,
        )
        for k in (1, 5, 7, 8):
            hop(mo, k).wait_recv()
        for w in (ri, ro, mi, mo):
            for k in (1, 4, 5, 6, 7, 8):
                hop(w, k).wait_send()
        for moved in (
            token_y, token_y_two, grad_y, grad_y_two, mask_core, one_core, low_core,
            *part_core, *part_y, *mid_y, *two_core,
        ):
            moved.wait_send()
        for k in range(16):
            if k not in (0, 2):
                keep_out(k).wait()


def recur_first(both_ref, state_ref, mask_ref, vec_ref, wr_ref, wi_ref, dmix_ref, dboth_ref, coef_ref, push_ref):
    width = dmix_ref.shape[1]
    rows = both_ref.shape[0] // held_buffers

    def first(b, carry):
        at = buffer_rows_at(b, rows)
        gate, slope = gelu_parts(both_ref[at, width:])
        d_mixed = dmix_ref[at, :]
        mask = mask_ref[at, :]
        conv_low = conv_of(both_ref[at, :width], mask, vec_ref).astype(bf16)
        rate = gates_of(conv_low, vec_ref, wr_ref, wi_ref)[0]
        store_lanes(push_ref, at, d_mixed * gate)
        dboth_ref[at, width:] = (slope * d_mixed * load_lanes(state_ref, at, width)).astype(bf16)
        store_lanes(coef_ref, at, jnp.exp(-8.0 * rate * vec_ref[7:8, :]) * mask[:, 0:1])
        return carry

    lax.fori_loop(0, held_buffers, first, 0)


def recur_last(
    both_ref, state_ref, mask_ref, vec_ref, wr_ref, wi_ref, push_ref,
    dboth_ref, sums_ref, gr_ref, gi_ref,
):
    width = both_ref.shape[1] // 2
    rows = both_ref.shape[0] // held_buffers
    sums_ref[...] = jnp.zeros_like(sums_ref)
    gr_ref[...] = jnp.zeros_like(gr_ref)
    gi_ref[...] = jnp.zeros_like(gi_ref)
    def add_sum(k, value):
        sums_ref[k : k + 1, :] += jnp.sum(value, axis=0, keepdims=True)

    def last(b, carry):
        at = buffer_rows_at(b, rows)
        inner = both_ref[at, :width]
        mask = mask_ref[at, :]
        keep = mask[:, 0:1]
        softened = vec_ref[7:8, :]
        conv = conv_of(inner, mask, vec_ref)
        conv_low = conv.astype(bf16)
        rate, igate = gates_of(conv_low, vec_ref, wr_ref, wi_ref)
        d_push = load_lanes(push_ref, at, width)
        decay = jnp.exp(-8.0 * rate * softened)
        square = 1.0 - decay * decay + root_eps
        root = jnp.sqrt(square)
        d_root = d_push * igate * conv
        d_igate = d_push * root * conv
        before = shifted(load_lanes(state_ref, at, width), 1) * keep
        d_decay = d_push * before - d_root * decay / root
        d_log = d_decay * decay
        slow = d_log * rate
        d_pre_recur = (-8.0 * softened) * slow * (1.0 - rate)
        d_pre_input = d_igate * igate * (1.0 - igate)
        add_sum(7, slow)
        add_sum(5, d_pre_recur)
        add_sum(6, d_pre_input)
        low_recur = d_pre_recur.astype(bf16)
        low_input = d_pre_input.astype(bf16)
        gr_ref[...] += lax.dot_general(
            conv_low, low_recur, contract_rows, preferred_element_type=f32
        )
        gi_ref[...] += lax.dot_general(
            conv_low, low_input, contract_rows, preferred_element_type=f32
        )
        d_conv = d_push * root * igate
        d_conv = d_conv + lax.dot_general(
            low_recur, wr_ref[...], contract_cols, preferred_element_type=f32
        )
        d_conv = d_conv + lax.dot_general(
            low_input, wi_ref[...], contract_cols, preferred_element_type=f32
        )
        add_sum(4, d_conv)
        add_sum(0, d_conv * inner)
        d_inner = vec_ref[0:1, :] * d_conv
        for k in range(1, 4):
            kept = d_conv * mask[:, k : k + 1]
            add_sum(k, kept * shifted(inner, k))
            d_inner = d_inner + vec_ref[k : k + 1, :] * shifted(kept, -k)
        dboth_ref[at, :width] = d_inner.astype(bf16)
        return carry

    lax.fori_loop(0, held_buffers, last, 0)


class Sums:
    def __init__(self, at, partial, land, total, send, recv):
        self.at, self.partial, self.land, self.total = at, partial, land, total
        self.send, self.recv = send, recv
        self.half_rows = total.shape[1]
        self.top = pl.ds(0, self.half_rows)
        self.bottom = pl.ds(self.half_rows, self.half_rows)

    def rows_of(self, c):
        return pl.ds(pl.multiple_of(c * self.half_rows, self.half_rows), self.half_rows)

    def hop(self, k, last=None):
        d, land, at, top, bottom = self.partial, self.land, self.at, self.top, self.bottom
        src, dst, where = (
            lambda: (d.at[5], land.at[0], at.beside),
            lambda: (d.at[7, bottom], land.at[1, top], at.beside),
            lambda: (d.at[7, top], land.at[1, bottom], at.ahead),
            lambda: (d.at[6, top], land.at[2, top], at.ahead),
            lambda: (land.at[1, top], land.at[2, bottom], at.ahead),
            lambda: (d.at[3, bottom], land.at[0, bottom], at.behind),
            lambda: (land.at[1, bottom], land.at[0, top], at.behind),
            lambda: (d.at[1], land.at[3], at.beside),
            lambda: (land.at[0], land.at[4], at.ahead),
            lambda: (land.at[2], land.at[2], at.behind),
            lambda: (land.at[0], land.at[3], at.beside),
            lambda: (last.at[self.rows_of(1 - at.c)], self.total.at[at.c], at.core),
        )[k]()
        return remote(src, dst, self.send.at[k], self.recv.at[k], where)

    def start(self, *hops):
        for k in hops:
            self.hop(k).start()

    def received(self, *hops):
        for k in hops:
            self.hop(k).wait_recv()

    def sent(self, *hops):
        for k in hops:
            self.hop(k).wait_send()

    def operands(self, k):
        d, land, top, bottom = self.partial, self.land, self.top, self.bottom
        return {
            4: (land.at[1, top], d.at[6, bottom]),
            6: (land.at[1, bottom], d.at[3, top]),
            8: (land.at[0], d.at[4]),
            9: (land.at[2], d.at[2]),
        }[k]

    def arrived(self, k):
        self.received(*{4: (1,), 6: (2,), 8: (0,), 9: (3, 4)}[k])

    def step(self, k, add):
        self.arrived(k)
        add(*self.operands(k))
        self.start(k)


work_hops, serve_hops = (0, 1, 2, 3, 4, 5, 6, 7, 8, 9), (10,)


def add_rows(into, value, other=None):
    size = 32 if into.shape[0] % 32 == 0 else 16

    def chunk(i, carry):
        at = pl.ds(pl.multiple_of(i * size, size), size)
        total = into[at, :].astype(f32) + value[at, :].astype(f32)
        if other is not None:
            total = total + other[at, :].astype(f32)
        into[at, :] = total.astype(bf16)
        return carry

    lax.fori_loop(0, into.shape[0] // size, chunk, 0)


def norm_sums(e_ref, y_in, source_ref, gain_ref, gain_row, mean_ref, first, count):
    size, half = 64, e_ref.shape[1]

    def chunk(i, carry):
        at = pl.ds(pl.multiple_of(first + i * size, size), size)
        e = e_ref[at, :] + y_in[at, :].astype(f32)
        e_ref[at, :] = e
        source = source_ref[at, :half].astype(bf16).astype(f32)
        part = jnp.sum(e * gain_ref[gain_row : gain_row + 1, :half] * source, axis=1, keepdims=True)
        mean_ref[at, :] = jnp.broadcast_to(part, (size, lanes))
        return carry

    lax.fori_loop(0, count // size, chunk, 0)


def norm_rows_back(
    e_ref, source_ref, gain_ref, gain_row, scale_ref, mean_ref, mean_in, term_ref, model, first, count, use
):
    size, half = 64, e_ref.shape[1]

    def chunk(i, carry):
        at = pl.ds(pl.multiple_of(first + i * size, size), size)
        e = e_ref[at, :]
        source = source_ref[at, :half].astype(bf16).astype(f32)
        scale = scale_ref[gain_row, at, 0:1]
        inner = (mean_ref[at, 0:1] + mean_in[at, 0:1]) / model
        weighted = e * gain_ref[gain_row : gain_row + 1, :half]
        term_ref[gain_row : gain_row + 1, :] += jnp.sum(e * source * scale, axis=0, keepdims=True)
        use(at, scale * weighted - source * (scale * scale * scale * inner))
        return carry

    lax.fori_loop(0, count // size, chunk, 0)


def backward_kernel(
    count,
    weight_mi, weight_mo, act_in, slope_in, value_in, two_mine, two_theirs, low_mine, low_theirs,
    middle_in, weight_in, both_in, state_in,
    scale_ref, gain_ref, mask_ref, vec_ref, wr_ref, wi_ref,
    d_mi, d_mo, land_mi, land_mo, total_mi, total_mo, dmid_out, mine_out, theirs_out, dboth_out,
    out_ref, sums_ref, gates_ref, term_ref,
    middle_ref, dmid_ref, db_mine, db_theirs,
    part_out, part_in, o_in, y_out, y_in, oy_out, oy_in, mean_ref, mean_in, stage_a, stage_b,
    w_send, w_recv, m_send, m_recv, local_sem, load_sem, out_sem, tile_sem, keep_sem,
):
    at = Place(count)
    size = weight_mi.shape[1]
    cols = at.columns(size)
    own, half_model = middle_ref.shape
    model = 2 * half_model
    rows = own // 2
    hidden = act_in.shape[1]
    width = weight_in.shape[2]
    e_ref, low_left = dmid_ref, y_out
    mi = Sums(at, d_mi, land_mi, total_mi, w_send.at[0], w_recv.at[0])
    mo = Sums(at, d_mo, land_mo, total_mo, w_send.at[1], w_recv.at[1])
    first, second = pl.ds(0, rows), pl.ds(rows, rows)
    left, right = pl.ds(0, half_model), pl.ds(half_model, half_model)
    halves = (first, second)

    def move(k, src, dst, where):
        return remote(src, dst, m_send.at[k], m_recv.at[k], where)

    e_core = [move(i, part_out.at[h], part_in.at[h], at.core) for i, h in enumerate(halves)]
    o_core = [move(2 + i, part_out.at[h], o_in.at[h], at.core) for i, h in enumerate(halves)]
    e_y = [move(4 + i, y_out.at[h], y_in.at[h], at.over_y) for i, h in enumerate(halves)]
    o_y = [move(6 + i, oy_out.at[h], oy_in.at[h], at.over_y) for i, h in enumerate(halves)]
    mean_y = move(8, mean_ref, mean_in, at.over_y)
    db_y = [
        move(9 + i, db_mine.at[h, left], db_mine.at[h, right], at.over_y)
        for i, h in enumerate(halves)
    ]
    db_core = [move(11 + i, db_mine.at[h], db_theirs.at[h], at.core) for i, h in enumerate(halves)]
    out_move = move(13, out_ref.at[second], out_ref.at[first], at.behind)
    low_load = pltpu.make_async_copy(low_mine.at[:, left], low_left, local_sem.at[6])
    middle_load = pltpu.make_async_copy(middle_in, middle_ref, local_sem.at[7])
    keep_out = [
        pltpu.make_async_copy(src, dst, out_sem.at[k])
        for k, (src, dst) in enumerate(
            ((dmid_ref, dmid_out), (db_mine, mine_out), (db_theirs, theirs_out))
        )
    ]

    def fetch(src, dst, k):
        return pltpu.make_async_copy(src, dst, local_sem.at[k])

    def staged(w, k):
        into, value = w.operands(k)
        count_rows, wide = into.shape
        at_rows = pl.ds(0, count_rows) if k != 6 else pl.ds(count_rows, count_rows)
        place = 3 if k == 6 else 0
        a = stage_a.at[at_rows, pl.ds(0, wide)]
        b = stage_b.at[at_rows, pl.ds(0, wide)]
        return a, b, fetch(into, a, place), fetch(value, b, place + 1), fetch(a, into, place + 2)

    def begin(w, *hops):
        for k in hops:
            w.arrived(k)
            _, _, load_a, load_b, _ = staged(w, k)
            load_a.start()
            load_b.start()

    def combine(w, *hops):
        for k in hops:
            a, b, load_a, load_b, back = staged(w, k)
            load_a.wait()
            load_b.wait()
            add_rows(a, b)
            back.start()

    def send_on(w, *hops):
        for k in hops:
            staged(w, k)[4].wait()
            w.start(k)

    def finish(w, parts):
        count_rows, wide = parts[0].shape
        a = stage_a.at[pl.ds(0, count_rows), pl.ds(0, wide)]
        b = stage_b.at[pl.ds(0, count_rows), pl.ds(0, wide)]
        loads = fetch(parts[0], a, 0), fetch(parts[1], b, 1)
        for v in loads:
            v.start()
        for v in loads:
            v.wait()
        add_rows(a, b)
        if len(parts) == 3:
            third = fetch(parts[2], b, 1)
            third.start()
            third.wait()
            add_rows(a, b)
        w.hop(11, a).start()
        kept = fetch(a.at[w.rows_of(at.c)], w.total.at[at.c], 2)
        kept.start()
        kept.wait()
        w.hop(11, a).wait()

    at.meet()

    @pl.when(at.serves)
    def _():
        for w in (mo, mi):
            w.received(5, 6)
            w.start(10)
        for w in (mo, mi):
            w.received(9, 10)
            finish(w, (w.land.at[2], w.land.at[3]))
        out_move.wait_recv()
        for w in (mo, mi):
            w.sent(*serve_hops)

    block_order = (
        (7, (1, 2)), (5, (0,)), (6, (3,)), (3, (5,)), (1, (7,)), (4, ()), (2, ()), (0, ()),
    )

    def partial_blocks(w, lhs, column_ref, room, between=()):
        wide = column_ref.shape[1]
        between = dict(between)

        def write(i):
            return pltpu.make_async_copy(
                room.at[i % 2, :, pl.ds(0, wide)], w.partial.at[block_order[i][0]], keep_sem.at[i % 2]
            )

        def leave(i):
            write(i).wait()
            w.start(*block_order[i][1])

        for i in range(blocks):
            if i >= 2:
                leave(i - 2)
            here = columns_at(cols, block_order[i][0], size)
            rows_here = jnp.concatenate([lhs[0, :, here], lhs[1, :, here]], axis=0)
            room[i % 2, :, :wide] = lax.dot_general(
                rows_here, column_ref[...], contract_rows, preferred_element_type=f32
            ).astype(bf16)
            write(i).start()
            if i in between:
                between[i]()
        leave(blocks - 2)
        leave(blocks - 1)

    def rows_product(weight, row_ref, room, wide, theirs_out, mine_out, between=()):
        between = dict(between)

        def block(b):
            return pltpu.make_async_copy(
                weight.at[b], room.at[b % 2, :, pl.ds(0, wide)], tile_sem.at[b % 2, 0]
            )

        block(0).start()
        for b in range(blocks):
            if b + 1 < blocks:
                block(b + 1).start()
            block(b).wait()
            here = columns_at(cols, b, size)
            for which, out in ((1, theirs_out), (0, mine_out)):
                out[:, here] = lax.dot_general(
                    row_ref[which * own : (which + 1) * own, :],
                    room[b % 2, :, :wide],
                    contract_cols,
                    preferred_element_type=f32,
                ).astype(out.dtype)
            if b in between:
                between[b]()

    def settle(w):
        w.received(7, 8)
        finish(w, (w.partial.at[0], w.land.at[3], w.land.at[4]))

    def join(i, h, mine_ref, arrived, landed, keep_value, sent_ref, over):
        arrived[i].wait_recv()
        keep_value(h, mine_ref[h, left] + landed[h, left].astype(f32))
        sent_ref[h, :] = (mine_ref[h, right] + landed[h, right].astype(f32)).astype(bf16)
        over[i].start()

    def mlp_part(lhs, act_ref, pair_ref, room, mine_ref):
        lhs_low = fetch(low_mine, lhs.at[0], 8), fetch(low_theirs, lhs.at[1], 9)
        lhs_two = fetch(two_mine, lhs.at[0], 8), fetch(two_theirs, lhs.at[1], 9)
        act_load = pltpu.make_async_copy(act_in, act_ref, load_sem.at[0])
        pair_load = [
            pltpu.make_async_copy(src, pair_ref.at[:, pl.ds(k * hidden, hidden)], load_sem.at[1 + k])
            for k, src in enumerate((slope_in, value_in))
        ]
        for v in (*lhs_low, act_load, *pair_load):
            v.start()
        middle_load.start()
        for v in (*lhs_low, act_load):
            v.wait()
        partial_blocks(mo, lhs, act_ref, room)
        for v in pair_load:
            v.wait()
        tile = 256

        def back(t, slot):
            gate_at = pl.ds(pl.multiple_of(t * tile, tile), tile)
            up_at = pl.ds(pl.multiple_of(hidden + t * tile, tile), tile)

            def use(start, d_act):
                row_at = pl.ds(start, chunk_rows)
                for where in (gate_at, up_at):
                    pair_ref[row_at, where] = (d_act * pair_ref[row_at, where].astype(f32)).astype(bf16)

            project(
                lhs.at[0], lhs.at[1], lambda: tile_rows(room.at[slot], tile), size, cols, use
            )

        stream_tiles(
            0,
            hidden // tile,
            lambda t, slot: Tile(weight_mo, room.at[slot], tile_sem.at[slot], t * tile, tile),
            back,
        )
        for v in lhs_two:
            v.start()
        begin(mo, 4, 6)
        rows_product(
            weight_mi,
            pair_ref,
            room,
            2 * hidden,
            part_out,
            mine_ref,
            (
                (1, lambda: combine(mo, 4, 6)),
                (2, lambda: send_on(mo, 4, 6)),
                (4, lambda: begin(mo, 8)),
                (6, lambda: combine(mo, 8)),
            ),
        )
        for moved in e_core:
            moved.start()
        send_on(mo, 8)

        def keep_e(h, value):
            e_ref[h, :] = value

        for i, h in enumerate(halves):
            join(i, h, mine_ref, e_core, part_in, keep_e, y_out, e_y)
        for v in lhs_two:
            v.wait()
        partial_blocks(
            mi,
            lhs,
            pair_ref,
            room,
            (
                (2, lambda: begin(mo, 9)),
                (4, lambda: combine(mo, 9)),
                (5, lambda: send_on(mo, 9)),
            ),
        )
        middle_load.wait()
        for i, h in enumerate(halves):
            e_y[i].wait_recv()
            norm_sums(e_ref, y_in, middle_ref, gain_ref, 1, mean_ref, i * rows, rows)
        mean_y.start()
        for moved in e_y:
            moved.wait_send()
        low_load.start()
        for moved in e_core:
            moved.wait_send()
        low_load.wait()
        mean_y.wait_recv()

        def keep(row_at, value):
            d_middle = value + low_left[row_at, :].astype(f32)
            dmid_ref[row_at, :] = d_middle
            db_mine[row_at, left] = d_middle.astype(bf16)

        for i in range(2):
            norm_rows_back(
                e_ref, middle_ref, gain_ref, 1, scale_ref, mean_ref, mean_in, term_ref, model,
                i * rows, rows, keep,
            )
            db_y[i].start()
        begin(mi, 4, 6)
        rows_product(
            weight_mo,
            act_ref,
            room,
            hidden,
            part_out,
            mine_ref,
            ((1, lambda: combine(mi, 4, 6)), (2, lambda: send_on(mi, 4, 6))),
        )
        for moved in o_core:
            moved.start()

        def keep_o(h, value):
            middle_ref[h, :] = middle_ref[h, :] + value

        for i in range(2):
            db_y[i].wait_recv()
            db_core[i].start()
        for i, h in enumerate(halves):
            join(i, h, mine_ref, o_core, o_in, keep_o, oy_out, o_y)

    def recur_part(w_ro, both_ref, state_ref, dboth_ref, coef_ref, push_ref, dmix_ref, gr_ref, gi_ref):
        loads = [
            pltpu.make_async_copy(src, dst, load_sem.at[k])
            for k, (src, dst) in enumerate(
                ((weight_in, w_ro), (both_in, both_ref), (state_in, state_ref))
            )
        ]
        for v in loads:
            v.start()
        begin(mi, 9)
        for i in range(2):
            db_core[i].wait_recv()
        for v in keep_out:
            v.start()
        combine(mi, 9)
        for v in loads:
            v.wait()
        send_on(mi, 9)
        begin(mi, 8)

        def keep_mixed(start, value):
            dmix_ref[pl.ds(start, chunk_rows), :] = value

        project(db_mine, db_theirs, lambda: stacked(w_ro), size, cols, keep_mixed)
        combine(mi, 8)
        send_on(mi, 8)
        recur_first(
            both_ref, state_ref, mask_ref, vec_ref, wr_ref, wi_ref, dmix_ref, dboth_ref, coef_ref, push_ref
        )
        for i, h in enumerate(halves):
            o_y[i].wait_recv()
            out_ref[h, :] = (
                mask_ref[h, 4:5] * (middle_ref[h, :] + oy_in[h, :].astype(f32))
            ).astype(bf16)
        out_move.start()
        scan_rows(coef_ref, push_ref, both_ref.shape[0] // held_buffers, True)
        recur_last(
            both_ref, state_ref, mask_ref, vec_ref, wr_ref, wi_ref, push_ref,
            dboth_ref, sums_ref, gr_ref, gi_ref,
        )
        keep_both = pltpu.make_async_copy(dboth_ref, dboth_out, out_sem.at[3])
        keep_both.start()
        block = gates_ref.shape[0]
        packed = [
            ref[h * block : (h + 1) * block, h * block : (h + 1) * block].astype(bf16)
            for ref in (gr_ref, gi_ref)
            for h in range(width // block)
        ]
        gates_ref[...] = jnp.concatenate(packed, axis=1)
        keep_both.wait()

    @pl.when(at.works)
    def _():
        term_ref[...] = jnp.zeros_like(term_ref)
        pl.run_scoped(
            mlp_part,
            pltpu.VMEM((2, own, model), bf16),
            pltpu.VMEM((2 * own, hidden), bf16),
            pltpu.VMEM((2 * own, 2 * hidden), bf16),
            pltpu.VMEM((2, size, 2 * hidden), bf16),
            pltpu.VMEM((own, model), f32),
        )
        pl.run_scoped(
            recur_part,
            pltpu.VMEM((blocks, size, width), bf16),
            pltpu.VMEM(both_in.shape, f32),
            pltpu.VMEM(state_in.shape, f32),
            pltpu.VMEM(dboth_out.shape, bf16),
            pltpu.VMEM(state_in.shape, f32),
            pltpu.VMEM(state_in.shape, f32),
            pltpu.VMEM((2 * own, width), f32),
            pltpu.VMEM((width, width), f32),
            pltpu.VMEM((width, width), f32),
        )
        for w in (mo, mi):
            settle(w)
        for w in (mo, mi):
            w.sent(*work_hops)
        for v in keep_out:
            v.wait()
        for moved in (*o_core, *o_y, mean_y, *db_y, *db_core, out_move):
            moved.wait_send()


def finish_kernel(
    count,
    *refs,
):
    sources, refs = refs[:9], refs[9:]
    (
        scale_ref, gain_ref, sums_ref, gates_ref, term_in,
        total_r, out_ref, recur_out, input_out, sums_out, term_out,
    ) = refs[:11]
    refs = refs[11:]
    one_mine, one_theirs, db_mine, db_theirs, dboth_ref, mixed_ref, w_ri, tok_left, dmid_ref = refs[:9]
    (
        d_r, land_r, part_out, part_in, part_sum, y_out, y_in, e_ref,
        mean_ref, mean_in, last_r, gates_in, gates_out, sums_in, term_ref, term_land,
        w_send, w_recv, m_send, m_recv, load_sem,
    ) = refs[9:]
    at = Place(count)
    size = w_ri.shape[1]
    cols = at.columns(size)
    own, half_model = dmid_ref.shape
    model = 2 * half_model
    rows = own // 2
    pair_width = dboth_ref.shape[1]
    w = Sums(at, d_r, land_r, total_r, w_send, w_recv)
    first, second = pl.ds(0, rows), pl.ds(rows, rows)
    left, right = pl.ds(0, half_model), pl.ds(half_model, half_model)
    halves = (first, second)

    def move(k, src, dst, where):
        return remote(src, dst, m_send.at[k], m_recv.at[k], where)

    e_core = [move(i, part_out.at[h], part_in.at[h], at.core) for i, h in enumerate(halves)]
    e_y = [move(2 + i, y_out.at[h], y_in.at[h], at.over_y) for i, h in enumerate(halves)]
    mean_y = move(4, mean_ref, mean_in, at.over_y)
    out_move = move(5, out_ref.at[second], out_ref.at[first], at.behind)
    gates_x = move(6, gates_ref, gates_in.at[0], at.beside)
    gates_z = move(7, gates_in.at[0], gates_in.at[1], at.ahead)
    gates_end = move(8, gates_out.at[0], gates_out.at[0], at.behind)
    gates_core = move(9, gates_out.at[0], gates_out.at[1], at.core)
    sums_x = move(10, sums_ref, sums_in.at[0], at.beside)
    sums_z = move(11, sums_in.at[0], sums_in.at[1], at.ahead)
    sums_end = move(12, sums_out.at[0], sums_out.at[0], at.behind)
    sums_core = move(13, sums_out.at[0], sums_out.at[1], at.core)
    term_x = move(14, term_ref, term_land.at[0], at.beside)
    term_z = move(15, term_land.at[0], term_land.at[1], at.ahead)
    term_core = move(16, term_land.at[1], term_land.at[2], at.core)
    term_end = move(17, term_out, term_out, at.behind)
    loads = [
        pltpu.make_async_copy(src, dst, load_sem.at[k]) for k, (src, dst) in enumerate(zip(sources, refs))
    ]

    def add(into, value):
        add_rows(into, value)

    def finish(parts):
        last_r[...] = parts[0][...]
        add_rows(last_r, parts[1], parts[2] if len(parts) == 3 else None)
        w.hop(11, last_r).start()
        w.total[at.c] = last_r[w.rows_of(at.c), :]

    def unpack(place, quarter):
        block = recur_out.shape[1]
        count_heads = recur_out.shape[0] // 2
        for k, out in enumerate((recur_out, input_out)):
            for h in range(count_heads):
                start = (k * count_heads + h) * block
                out[quarter * count_heads + h] = gates_out[place, :, start : start + block].astype(f32)

    at.meet()

    @pl.when(at.serves)
    def _():
        sums_end.wait_recv()
        sums_core.start()
        w.received(5, 6)
        w.start(10)
        gates_end.wait_recv()
        gates_core.start()
        w.received(9, 10)
        finish((w.land.at[2], w.land.at[3]))
        w.hop(11, last_r).wait()
        w.sent(*serve_hops)
        out_move.wait_recv()
        term_end.wait_recv()
        sums_core.wait()
        unpack(0, at.c)
        gates_core.wait()
        unpack(1, 1 - at.c)

    @pl.when(at.works)
    def _():
        gates_x.start()
        sums_x.start()
        for k in (4, 0, 1, 5, 2, 3, 6, 7, 8):
            loads[k].start()
        for k in (4, 0, 1, 5, 2, 3):
            loads[k].wait()

        def partial(b):
            here = columns_at(cols, b, size)

            def product(mine_ref, theirs_ref, column_ref):
                total = lax.dot_general(
                    mine_ref[:, here], column_ref[:own, :], contract_rows, preferred_element_type=f32
                )
                total = total + lax.dot_general(
                    theirs_ref[:, here], column_ref[own:, :], contract_rows, preferred_element_type=f32
                )
                return total.astype(bf16)

            d_r[b, :, :pair_width] = product(one_mine, one_theirs, dboth_ref)
            d_r[b, :, pair_width:] = product(db_mine, db_theirs, mixed_ref)

        for b, hops in ((7, (1, 2)), (5, (0,))):
            partial(b)
            w.start(*hops)
        sums_x.wait_recv()
        sums_in[0] = sums_in[0] + sums_ref[...]
        sums_z.start()
        gates_x.wait_recv()
        add_rows(gates_in.at[0], gates_ref)
        gates_z.start()
        for b, hops in ((6, (3,)), (3, (5,))):
            partial(b)
            w.start(*hops)

        def back(start, out, out_at):
            for b in range(blocks):
                out[out_at, columns_at(cols, b, size)] = lax.dot_general(
                    dboth_ref[pl.ds(start, rows), :], w_ri[b], contract_cols, preferred_element_type=f32
                ).astype(out.dtype)

        loads[6].wait()
        for i, h in enumerate(halves):
            back(own + i * rows, part_out, h)
            e_core[i].start()
        w.step(4, add)
        w.step(6, add)
        for b in (4, 1):
            partial(b)
        for i, h in enumerate(halves):
            back(i * rows, part_sum, first)
            e_core[i].wait_recv()
            e_ref[h, :] = part_sum[:, left] + part_in[h, left].astype(f32)
            y_out[h, :] = (part_sum[:, right] + part_in[h, right].astype(f32)).astype(bf16)
            e_y[i].start()
        sums_z.wait_recv()
        sums_out[0] = sums_in[0] + sums_in[1]
        sums_end.start()
        sums_core.start()
        gates_z.wait_recv()
        gates_out[0] = gates_in[0]
        add_rows(gates_out.at[0], gates_in.at[1])
        gates_end.start()
        gates_core.start()
        w.step(8, add)
        w.start(7)
        for b in (2, 0):
            partial(b)
        w.step(9, add)
        term_ref[...] = term_in[...]
        for k in (7, 8):
            loads[k].wait()
        for i in range(2):
            e_y[i].wait_recv()
            norm_sums(e_ref, y_in, tok_left, gain_ref, 0, mean_ref, i * rows, rows)
        mean_y.start()
        unpack(0, at.c)
        mean_y.wait_recv()

        def keep(row_at, value):
            out_ref[row_at, :] = (value + dmid_ref[row_at, :]).astype(bf16)

        for i in (1, 0):
            norm_rows_back(
                e_ref, tok_left, gain_ref, 0, scale_ref, mean_ref, mean_in, term_ref, model,
                i * rows, rows, keep,
            )
            if i == 1:
                out_move.start()
        term_x.start()
        term_x.wait_recv()
        term_land[0] = term_land[0] + term_ref[...]
        term_z.start()
        w.received(7, 8)
        finish((w.partial.at[0], w.land.at[3], w.land.at[4]))
        term_z.wait_recv()
        term_land[1] = term_land[0] + term_land[1]
        term_core.start()
        term_core.wait_recv()
        term_out[...] = term_land[1] + term_land[2]
        term_end.start()
        w.hop(11, last_r).wait()
        w.sent(*work_hops)
        sums_core.wait_recv()
        gates_core.wait_recv()
        unpack(1, 1 - at.c)
        for moved in (
            *e_core, *e_y, mean_y, out_move, gates_x, gates_z, gates_end, gates_core,
            sums_x, sums_z, sums_end, sums_core, term_x, term_z, term_core, term_end,
        ):
            moved.wait_send()


in_vmem = pl.BlockSpec(memory_space=pltpu.VMEM)
in_smem = pl.BlockSpec(memory_space=pltpu.SMEM)
in_any = pl.BlockSpec(memory_space=pl.ANY)
no_cost = pl.CostEstimate(flops=0, bytes_accessed=0, transcendentals=0)
kernel_params = pltpu.CompilerParams(vmem_limit_bytes=60 * 2**20)
copy_sem = pltpu.SemaphoreType.DMA


def lane_shape(rows, width):
    return (pl.cdiv(width, lanes), rows, lanes)


def run_forward(count, splits, tokens, out_grad, lengths, gains, taps, biases, recur_blocks, input_blocks):
    rows, half_model = tokens.shape
    own, model, width = 2 * rows, 2 * half_model, taps.shape[1] // 2
    size = 2 * splits[0].shape[1]
    columns = [v.shape[2] for v in splits[:3]] + [splits[3].shape[1] // 2]
    shape = jax.ShapeDtypeStruct
    gathered_shapes = [shape((blocks, size, n), bf16) for n in columns]
    wide = shape((own, model), bf16)
    kept = [
        shape((2 * own, 2 * width), f32),
        shape(lane_shape(2 * own, width), f32),
        shape((2 * own, width), bf16),
        shape((2 * own, lanes), f32),
        shape((own, half_model), f32),
        shape((own, half_model), bf16),
        *[wide] * 6,
        shape((2, own, lanes), f32),
        shape((8, width), f32),
        shape((width, width), bf16),
        shape((width, width), bf16),
    ]
    hidden = shape((2 * own, columns[3]), bf16)
    return pl.pallas_call(
        functools.partial(forward_kernel, count),
        out_shape=(*gathered_shapes, *kept, *[hidden] * 3),
        in_specs=[in_any] * 6 + [in_smem] + [in_vmem] * 5,
        out_specs=[in_any] * 23,
        scratch_shapes=[
            *[
                pltpu.VMEM(wide.shape if i == 5 else v.shape, v.dtype)
                for i, v in enumerate(kept)
                if i not in (0, 2)
            ],
            pltpu.VMEM((own, model), bf16),
            pltpu.VMEM((own, model), bf16),
            pltpu.VMEM((own, model), bf16),
            pltpu.VMEM((own, half_model), bf16),
            pltpu.VMEM((own, half_model), bf16),
            pltpu.VMEM((own, model), bf16),
            copy_sem((4, 9)),
            copy_sem((4, 9)),
            copy_sem((4,)),
            copy_sem((2, blocks)),
            copy_sem((18,)),
            copy_sem((18,)),
            copy_sem((2,)),
            copy_sem((16,)),
            copy_sem((2, 2, blocks)),
            copy_sem((2, 3)),
        ],
        compiler_params=comm_params(0),
        cost_estimate=no_cost,
        name="gather_and_recur",
    )(*splits, tokens, out_grad, lengths, gains, taps, biases, recur_blocks, input_blocks)


def comm_params(collective):
    return pltpu.CompilerParams(
        vmem_limit_bytes=255 * 2**18, collective_id=collective, has_side_effects=True
    )


def run_backward(
    count, weights, mlp_kept, normed_two, grad_low, middle, weight, both, state,
    scales, gains, mask, vectors, wr, wi, block,
):
    own, half_model = middle.shape
    model, width, rows = 2 * half_model, wr.shape[0], own // 2
    size = weight.shape[1]
    shape = jax.ShapeDtypeStruct
    hidden = [v.shape[2] for v in weights]
    wide = shape((own, model), bf16)
    kept = (shape((own, half_model), f32), wide, wide)
    return pl.pallas_call(
        functools.partial(backward_kernel, count),
        out_shape=(
            *[shape(v.shape, bf16) for v in weights],
            *[shape((5, size, n), bf16) for n in hidden],
            *[shape((2, size // 2, n), bf16) for n in hidden],
            *kept,
            shape((2 * own, 2 * width), bf16),
            shape((own, half_model), bf16),
            shape((8, width), f32),
            shape((block, 2 * width), bf16),
            shape((8, half_model), f32),
        ),
        in_specs=[in_any] * 13 + [in_vmem] * 6,
        out_specs=[in_any] * 10 + [in_vmem] * 4,
        scratch_shapes=[
            pltpu.VMEM((own, half_model), f32),
            *[pltpu.VMEM(v.shape, v.dtype) for v in kept],
            *[pltpu.VMEM((own, model), bf16)] * 3,
            *[pltpu.VMEM((own, half_model), bf16)] * 4,
            pltpu.VMEM((own, lanes), f32),
            pltpu.VMEM((own, lanes), f32),
            pltpu.VMEM((size, max(hidden)), bf16),
            pltpu.VMEM((size, max(hidden)), bf16),
            copy_sem((2, 12)),
            copy_sem((2, 12)),
            copy_sem((14,)),
            copy_sem((14,)),
            copy_sem((10,)),
            copy_sem((4,)),
            copy_sem((4,)),
            copy_sem((2, blocks)),
            copy_sem((2,)),
        ],
        compiler_params=comm_params(1),
        cost_estimate=no_cost,
        name="sum_and_back",
    )(
        *weights, *mlp_kept, *normed_two, *grad_low, middle, weight, both, state,
        scales, gains, mask, vectors, wr, wi,
    )


def run_finish(
    count, normed, d_branch, d_both, mixed, weight, tokens, d_middle, scales, gains, sums, gates, term
):
    own, half_model = d_middle.shape
    model, rows = 2 * half_model, own // 2
    size = weight.shape[1]
    width = weight.shape[2] + mixed.shape[1]
    shape = jax.ShapeDtypeStruct
    held = (*normed, *d_branch, d_both, mixed, weight, tokens, d_middle)
    block = gates.shape[0]
    square = shape((gates.shape[1] // block, block, block), f32)
    return pl.pallas_call(
        functools.partial(finish_kernel, count),
        out_shape=(
            shape((2, size // 2, width), bf16),
            shape((own, half_model), bf16),
            square,
            square,
            shape((2, *sums.shape), f32),
            shape(term.shape, f32),
        ),
        in_specs=[in_any] * 9 + [in_vmem] * 5,
        out_specs=[in_vmem] * 6,
        scratch_shapes=[
            *[pltpu.VMEM(v.shape, v.dtype) for v in held],
            pltpu.VMEM((blocks, size, width), bf16),
            pltpu.VMEM((5, size, width), bf16),
            pltpu.VMEM((own, model), bf16),
            pltpu.VMEM((own, model), bf16),
            pltpu.VMEM((rows, model), f32),
            pltpu.VMEM((own, half_model), bf16),
            pltpu.VMEM((own, half_model), bf16),
            pltpu.VMEM((own, half_model), f32),
            pltpu.VMEM((own, lanes), f32),
            pltpu.VMEM((own, lanes), f32),
            pltpu.VMEM((size, width), bf16),
            pltpu.VMEM((2, *gates.shape), bf16),
            pltpu.VMEM((2, *gates.shape), bf16),
            pltpu.VMEM((2, *sums.shape), f32),
            pltpu.VMEM(term.shape, f32),
            pltpu.VMEM((3, *term.shape), f32),
            copy_sem((12,)),
            copy_sem((12,)),
            copy_sem((18,)),
            copy_sem((18,)),
            copy_sem((9,)),
        ],
        compiler_params=comm_params(2),
        cost_estimate=no_cost,
        name="sum_and_finish",
    )(*held, scales, gains, sums, gates, term)


def local(
    n_dp,
    tokens,
    gain_rnn,
    rnn_in,
    gate_recur,
    gate_input,
    bias_recur,
    bias_input,
    decay_param,
    conv_weight,
    conv_bias,
    rnn_out,
    gain_mlp,
    mlp_in,
    mlp_out,
    lengths,
    out_grad,
):
    outer_count = n_dp // 16
    rows_here = rnn_in.shape[0]
    model = gain_rnn.shape[0]
    half_model = model // 2
    buffer_rows = tokens.shape[0]
    own_rows = 2 * buffer_rows
    index = lax.axis_index("dp")
    y = lax.axis_index("mp")
    c = index // outer_count % 2
    x = index // (2 * outer_count) % 2
    z = index // (4 * outer_count)
    outer = jnp.where(z < 2, 0, 3)
    far = 3 - z
    far_outer = 3 - outer

    def pick_c(first, second):
        return jnp.where(c == 0, first, second)

    def pick_y(first, second):
        return jnp.where(y == 0, first, second)

    group_rows = outer_count * rows_here
    block_rows = 2 * group_rows

    outer_groups = [[i * outer_count + w for w in range(outer_count)] for i in range(16)]

    def over_outer(value):
        if outer_count == 1:
            return value
        return lax.all_gather(value, "dp", axis_index_groups=outer_groups, axis=1, tiled=True)

    cols = jnp.stack(
        [
            ((at_z + 2 * y) % 4 * 2 + at_x) * block_rows
            for at_z in (z, outer, far, far_outer)
            for at_x in (x, 1 - x)
        ]
    ).astype(jnp.int32)

    def settle_grad(total):
        total = total.astype(f32)
        if outer_count > 1:
            total = lax.psum_scatter(
                total, "dp", axis_index_groups=outer_groups, scatter_dimension=1, tiled=True
            )
        return total

    def joined_pair(total):
        total = settle_grad(total)
        columns = total.shape[2] // 2
        return jnp.stack(
            [
                jnp.concatenate(
                    [total[q, :, k * columns : (k + 1) * columns] for q in range(2)], axis=1
                )
                for k in range(2)
            ],
            axis=1,
        )

    def joined_out(total):
        total = settle_grad(total)
        return jnp.concatenate([total[0], total[1]], axis=1)

    def over_groups(value):
        return lax.psum(value, "dp", axis_index_groups=outer_groups) if outer_count > 1 else value

    def relative(vector):
        first, second = vector[:half_model], vector[half_model:]
        return jnp.concatenate([pick_y(first, second), pick_y(second, first)])

    def quarters(value, axis):
        size = value.shape[axis] // 2
        return (
            lax.slice_in_dim(value, 0, size, axis=axis),
            lax.slice_in_dim(value, size, 2 * size, axis=axis),
        )

    def quarter(value, axis=0):
        return pick_c(*quarters(value, axis))

    gain_one, gain_two = relative(gain_rnn.astype(f32)), relative(gain_mlp.astype(f32))
    def split_pair(weight):
        row_count, _, columns = weight.shape
        parts = weight.reshape(row_count, 2, 2, columns // 2).transpose(2, 0, 1, 3)
        return over_outer(parts.reshape(2, row_count, columns))

    def split_out(weight):
        row_count, columns = weight.shape
        return over_outer(weight.reshape(row_count, 2, columns // 2).swapaxes(0, 1))

    def split_none(weight):
        if outer_count == 1:
            return weight
        return lax.all_gather(weight, "dp", axis_index_groups=outer_groups, axis=0, tiled=True)

    splits = (split_pair(rnn_in), split_out(rnn_out), split_pair(mlp_in), split_none(mlp_out))
    biases = jnp.stack([conv_bias, bias_recur, bias_input, decay_param])
    gains = jnp.stack([gain_one, gain_two])
    (
        rnn_in_all, rnn_out_all, mlp_in_all, mlp_out_all,
        both, state, mixed, mask, middle, tokens_all,
        *rows_kept, scales, vectors, wr, wi, act, gate_slope, gate_value,
    ) = run_forward(
        outer_count, splits, tokens, out_grad, lengths, gains, conv_weight, biases, gate_recur, gate_input
    )
    normed, normed_two, grad_low = rows_kept[0:2], rows_kept[2:4], rows_kept[4:6]

    (
        _, _, _, _, mlp_in_total, mlp_out_total, d_middle, d_branch, d_branch_theirs, d_both,
        output_two, sums, gates, term,
    ) = run_backward(
        outer_count,
        (mlp_in_all, mlp_out_all),
        (act, gate_slope, gate_value),
        normed_two,
        grad_low,
        middle,
        rnn_out_all,
        both,
        state,
        scales,
        gains,
        mask,
        vectors,
        wr,
        wi,
        gate_recur.shape[1],
    )
    rnn_total, tokens_grad_two, recur_grad, input_grad, sums, term = run_finish(
        outer_count,
        normed,
        (d_branch, d_branch_theirs),
        d_both,
        mixed,
        rnn_in_all,
        tokens_all,
        d_middle,
        scales,
        gains,
        sums,
        gates,
        term,
    )
    rnn_width = rnn_in.shape[2]
    rnn_in_total, rnn_out_total = rnn_total[:, :, :rnn_width], rnn_total[:, :, rnn_width:]
    layer_output, tokens_grad = output_two[:buffer_rows], tokens_grad_two[:buffer_rows]
    def both_quarters(pair, axis):
        return over_groups(
            pick_c(
                jnp.concatenate([pair[0], pair[1]], axis=axis),
                jnp.concatenate([pair[1], pair[0]], axis=axis),
            )
        )

    sums = both_quarters(sums, 1)
    recur_grad, input_grad = over_groups(recur_grad), over_groups(input_grad)
    gains_grad = over_groups(term[:2])

    return (
        layer_output,
        tokens_grad,
        gains_grad[0],
        joined_pair(rnn_in_total),
        recur_grad,
        input_grad,
        sums[5],
        sums[6],
        8.0 * jax.nn.sigmoid(-decay_param) * sums[7],
        sums[:4],
        sums[4],
        joined_out(rnn_out_total),
        gains_grad[1],
        joined_pair(mlp_in_total),
        joined_out(mlp_out_total),
    )


def solution(mesh):
    return jax.shard_map(
        functools.partial(local, mesh.shape["dp"]),
        mesh=mesh,
        in_specs=(
            P("dp", "mp"),
            P(),
            P("dp", None, "mp"),
            P("mp", None, None),
            P("mp", None, None),
            P("mp"),
            P("mp"),
            P("mp"),
            P(None, "mp"),
            P("mp"),
            P("dp", "mp"),
            P(),
            P("dp", None, "mp"),
            P("dp", "mp"),
            P("dp", None),
            P("dp", "mp"),
        ),
        out_specs=(
            P("dp", "mp"),
            P("dp", "mp"),
            P("mp"),
            P("dp", None, "mp"),
            P("mp", None, None),
            P("mp", None, None),
            P("mp"),
            P("mp"),
            P("mp"),
            P(None, "mp"),
            P("mp"),
            P("dp", "mp"),
            P("mp"),
            P("dp", None, "mp"),
            P("dp", "mp"),
        ),
        check_vma=False,
    )
```

```python
import functools

import jax
import jax.numpy as jnp
from jax import lax
from jax.experimental import pallas as pl
from jax.experimental.pallas import tpu as pltpu
from jax.sharding import PartitionSpec as P

norm_eps = 1e-06
root_eps = 0.001
bf16 = jnp.bfloat16
f32 = jnp.float32
contract_cols = (((1,), (1,)), ((), ()))
contract_rows = (((0,), (0,)), ((), ()))
gelu_scale = 0.7978845608028654
gelu_cubic = 0.044715
held_buffers = 4
scan_unroll = 8
blocks = 8
chunk_rows = 512
lanes = 128
by_mesh = pl.DeviceIdType.MESH


def pairs(n_dp, move):
    count = n_dp // 16
    found = []
    for i in range(n_dp):
        w, c, x, z = i % count, i // count % 2, i // count // 2 % 2, i // count // 4
        target = move(z, x, c)
        if target is not None:
            z, x, c = target
            found.append((i, ((z * 2 + x) * 2 + c) * count + w))
    return found


def gelu_parts(v):
    tanh_value = jnp.tanh(gelu_scale * (v + gelu_cubic * v * v * v))
    value = 0.5 * v * (1.0 + tanh_value)
    slope = 0.5 * (1.0 + tanh_value) + 0.5 * v * (1.0 - tanh_value * tanh_value) * (
        gelu_scale * (1.0 + 3.0 * gelu_cubic * v * v)
    )
    return value, slope


def shifted(value, offset):
    return pltpu.roll(value, offset % value.shape[0], 0)


def store_lanes(ref, at, value):
    chunks = ref.shape[0]
    spare = chunks * lanes - value.shape[1]
    if spare:
        value = jnp.concatenate([value, jnp.zeros((value.shape[0], spare), f32)], axis=1)
    for i in range(chunks):
        ref[i, at, :] = value[:, i * lanes : (i + 1) * lanes]


def load_lanes(ref, at, width):
    return jnp.concatenate([ref[i, at, :] for i in range(ref.shape[0])], axis=1)[:, :width]


def scan_rows(coef_ref, push_ref, rows, reverse):
    chunks = coef_ref.shape[0]

    def step(i, carried):
        carried = list(carried)
        for j in range(scan_unroll):
            t = i * scan_unroll + j
            at = pl.ds(rows - 1 - t if reverse else t, held_buffers, stride=rows)
            for k in range(chunks):
                if reverse:
                    value = push_ref[k, at, :] + carried[k]
                    carried[k] = coef_ref[k, at, :] * value
                else:
                    value = coef_ref[k, at, :] * carried[k] + push_ref[k, at, :]
                    carried[k] = value
                push_ref[k, at, :] = value
        return tuple(carried)

    start = tuple(jnp.zeros((held_buffers, lanes), f32) for _ in range(chunks))
    lax.fori_loop(0, rows // scan_unroll, step, start)


def columns_at(cols_ref, b, size):
    return pl.ds(pl.multiple_of(cols_ref[b], size), size)


def gathered(ref, at, cols_ref, size):
    return jnp.concatenate([ref[at, columns_at(cols_ref, b, size)] for b in range(blocks)], axis=1)


def stacked(refs, columns=slice(None)):
    return jnp.concatenate([ref[:, columns] for ref in refs], axis=0)


def project(mine_ref, theirs_ref, weight_refs, cols_ref, use):
    size = weight_refs[0].shape[0]
    own = mine_ref.shape[0]
    for part, ref in enumerate((mine_ref, theirs_ref)):

        def chunk(i, carry, part=part, ref=ref):
            at = pl.ds(pl.multiple_of(i * chunk_rows, chunk_rows), chunk_rows)
            rows = gathered(ref, at, cols_ref, size)
            use(
                pl.multiple_of(part * own + i * chunk_rows, chunk_rows),
                jnp.dot(rows, stacked(weight_refs), preferred_element_type=f32),
            )
            return carry

        lax.fori_loop(0, own // chunk_rows, chunk, 0)


def columns_at(cols, b, size):
    return pl.ds(pl.multiple_of(cols[b], size), size)


def gathered(ref, at, cols, size):
    return jnp.concatenate([ref[at, columns_at(cols, b, size)] for b in range(blocks)], axis=1)


def stacked(weight_ref):
    return weight_ref[...].reshape(-1, weight_ref.shape[2])


def project(mine_ref, theirs_ref, weight, size, cols, use):
    own = mine_ref.shape[0]
    for part, ref in enumerate((mine_ref, theirs_ref)):

        def chunk(i, carry, part=part, ref=ref):
            at = pl.ds(pl.multiple_of(i * chunk_rows, chunk_rows), chunk_rows)
            rows = gathered(ref, at, cols, size)
            use(
                pl.multiple_of(part * own + i * chunk_rows, chunk_rows),
                jnp.dot(rows, weight(), preferred_element_type=f32),
            )
            return carry

        lax.fori_loop(0, own // chunk_rows, chunk, 0)


def buffer_rows_at(b, rows):
    return pl.ds(pl.multiple_of(b * rows, rows), rows)


def conv_of(inner, mask, vec_ref):
    conv = vec_ref[4:5, :] + vec_ref[0:1, :] * inner
    for k in range(1, 4):
        conv = conv + vec_ref[k : k + 1, :] * (shifted(inner, k) * mask[:, k : k + 1])
    return conv


def gates_of(conv_low, vec_ref, wr_ref, wi_ref):
    rate = jax.nn.sigmoid(
        jnp.dot(conv_low, wr_ref[...], preferred_element_type=f32) + vec_ref[5:6, :]
    )
    igate = jax.nn.sigmoid(
        jnp.dot(conv_low, wi_ref[...], preferred_element_type=f32) + vec_ref[6:7, :]
    )
    return rate, igate


def recur_state(both_ref, mask_ref, vec_ref, wr_ref, wi_ref, coef_ref, push_ref):
    width = both_ref.shape[1] // 2
    rows = both_ref.shape[0] // held_buffers

    def gates(b, carry):
        at = buffer_rows_at(b, rows)
        mask = mask_ref[at, :]
        conv = conv_of(both_ref[at, :width], mask, vec_ref)
        rate, igate = gates_of(conv.astype(bf16), vec_ref, wr_ref, wi_ref)
        decay = jnp.exp(-8.0 * rate * vec_ref[7:8, :])
        root = jnp.sqrt(1.0 - decay * decay + root_eps)
        store_lanes(coef_ref, at, decay * mask[:, 0:1])
        store_lanes(push_ref, at, root * igate * conv)
        return carry

    lax.fori_loop(0, held_buffers, gates, 0)
    scan_rows(coef_ref, push_ref, rows, False)


def recur_mixed(both_ref, state_ref, mixed_ref):
    width = both_ref.shape[1] // 2
    rows = both_ref.shape[0] // held_buffers

    def mix(b, carry):
        at = buffer_rows_at(b, rows)
        gate = gelu_parts(both_ref[at, width:])[0]
        mixed_ref[at, :] = (load_lanes(state_ref, at, width) * gate).astype(bf16)
        return carry

    lax.fori_loop(0, held_buffers, mix, 0)


def stream_tiles(first, last, fetch, body):
    fetch(first, first % 2).start()

    def step(t, carry):
        slot = t % 2

        @pl.when(t + 1 < last)
        def _():
            fetch(t + 1, 1 - slot).start()

        fetch(t, slot).wait()
        body(t, slot)
        return carry

    lax.fori_loop(first, last, step, 0)


class Tile:
    def __init__(self, weight, room, sems, first_column, tile):
        at = pl.ds(pl.multiple_of(first_column, tile), tile)
        self.copies = [
            pltpu.make_async_copy(
                weight.at[b, :, at], room.at[:, pl.ds(b * tile, tile)], sems.at[b]
            )
            for b in range(blocks)
        ]

    def start(self):
        for v in self.copies:
            v.start()

    def wait(self):
        for v in self.copies:
            v.wait()


def tile_rows(room, tile):
    return jnp.concatenate([room[:, b * tile : (b + 1) * tile] for b in range(blocks)], axis=0)


class Place:
    def __init__(self, count):
        self.me = lax.axis_index("dp")
        self.y = lax.axis_index("mp")
        self.c = self.me // count % 2
        self.x = self.me // (2 * count) % 2
        self.z = self.me // (4 * count)
        self.core = {"dp": self.me + (1 - 2 * self.c) * count}
        self.beside = {"dp": self.me + (1 - 2 * self.x) * 2 * count}
        self.over_y = {"mp": 1 - self.y}
        sign = 1 - 2 * (self.z // 2)
        self.ahead = {"dp": self.me + sign * 4 * count}
        self.behind = {"dp": self.me - sign * 4 * count}
        self.works = (self.z + 1) // 2 == 1
        self.serves = (self.z + 1) // 2 != 1

    def columns(self, size):
        outer = self.z // 2 * 3
        far, far_outer = 3 - self.z, 3 - outer
        return [
            ((at_z + 2 * self.y) % 4 * 2 + at_x) * size
            for at_z in (self.z, outer, far, far_outer)
            for at_x in (self.x, 1 - self.x)
        ]

    def meet(self):
        barrier = pltpu.get_barrier_semaphore()

        def greet(partners):
            for partner in partners:
                pl.semaphore_signal(barrier, inc=1, device_id=partner, device_id_type=by_mesh)
            pl.semaphore_wait(barrier, len(partners))

        @pl.when(self.works)
        def _():
            greet((self.core, self.beside, self.over_y, self.ahead, self.behind))

        @pl.when(self.serves)
        def _():
            greet((self.core, self.beside, self.ahead))


def remote(src, dst, send, recv, where):
    return pltpu.make_async_remote_copy(
        src_ref=src,
        dst_ref=dst,
        send_sem=send,
        recv_sem=recv,
        device_id=where,
        device_id_type=by_mesh,
    )


def normed_rows(source_ref, gain_ref, gain_row, scale_ref, scale_row, out_ref, first, count):
    size = 128

    def chunk(i, carry):
        at = pl.ds(pl.multiple_of(first + i * size, size), size)
        rows = source_ref[at, :].astype(f32)
        scale = lax.rsqrt(jnp.mean(rows * rows, axis=1, keepdims=True) + norm_eps)
        scale_ref[scale_row, at, :] = jnp.broadcast_to(scale, (size, lanes))
        out_ref[at, :] = (rows * scale * gain_ref[gain_row : gain_row + 1, :]).astype(bf16)
        return carry

    lax.fori_loop(0, count // size, chunk, 0)


def forward_kernel(
    count,
    s_ri, s_ro, s_mi, s_mo,
    tokens_ref, grad_ref, lengths_ref, gain_ref, taps_ref, biases_ref, recur_blocks, input_blocks,
    g_ri, g_ro, g_mi, g_mo, *refs,
):
    results, mlp_out_refs, refs = refs[:16], refs[16:19], refs[19:]
    (
        state_ref, mask_ref, middle_ref, tok_ref,
        one_mine, one_theirs, two_mine, two_theirs, low_mine, low_theirs, scale_ref,
        vec_ref, wr_ref, wi_ref,
    ) = refs[:14]
    (
        grad_all, part_out, part_in, y_out, y_in, mid_ref,
        w_send, w_recv, w_local, load_sem, m_send, m_recv, m_local, out_sem, tile_sem, mlp_sem,
    ) = refs[14:]
    held = (
        None, state_ref, None, mask_ref, middle_ref, tok_ref,
        one_mine, one_theirs, two_mine, two_theirs, low_mine, low_theirs, scale_ref,
        vec_ref, wr_ref, wi_ref,
    )
    at = Place(count)
    half_rows = s_ri.shape[1]
    size = 2 * half_rows
    model = tok_ref.shape[1]
    half_model = model // 2
    rows = tokens_ref.shape[0]
    own = 2 * rows
    cols = at.columns(size)
    whole, splits = (g_ri, g_ro, g_mi, g_mo), (s_ri, s_ro, s_mi, s_mo)
    ri, ro, mi, mo = range(4)
    top, bottom = pl.ds(0, half_rows), pl.ds(half_rows, half_rows)
    core_rows = pl.ds(pl.multiple_of(at.c * half_rows, half_rows), half_rows)

    def split(w, quarter):
        if w == mo:
            columns = whole[w].shape[2]
            return s_mo.at[:, pl.ds(pl.multiple_of(quarter * columns, lanes), columns)]
        return splits[w].at[quarter]

    def hop(w, k):
        g = whole[w]
        src, dst, where = (
            (split(w, 1 - at.c), g.at[0, core_rows], at.core),
            (g.at[0], g.at[1], at.beside),
            (g.at[0], g.at[2], at.ahead),
            (g.at[1], g.at[3], at.ahead),
            (g.at[0], g.at[4], at.ahead),
            (g.at[4], g.at[5], at.beside),
            (g.at[2], g.at[6], at.ahead),
            (g.at[3, top], g.at[7, top], at.ahead),
            (g.at[6, bottom], g.at[7, bottom], at.beside),
        )[k]
        return remote(src, dst, w_send.at[w, k], w_recv.at[w, k], where)

    def kept(w):
        return pltpu.make_async_copy(split(w, at.c), whole[w].at[0, core_rows], w_local.at[w])

    def begin(w):
        kept(w).start()
        hop(w, 0).start()

    def own_block(w, hops):
        kept(w).wait()
        hop(w, 0).wait()
        for k in hops:
            hop(w, k).start()

    def pass_on(w, arrived, sent):
        hop(w, arrived).wait_recv()
        hop(w, sent).start()

    def move(k, src, dst, where):
        return remote(src, dst, m_send.at[k], m_recv.at[k], where)

    first, second = pl.ds(0, rows), pl.ds(rows, rows)
    left, right = pl.ds(0, half_model), pl.ds(half_model, half_model)
    mine_rows, their_rows = pl.ds(0, own), pl.ds(own, own)
    token_in = move(0, tokens_ref, tok_ref.at[second, left], at.ahead)
    token_y = move(1, tokens_ref, tok_ref.at[first, right], at.over_y)
    token_y_two = move(2, tok_ref.at[second, left], tok_ref.at[second, right], at.over_y)
    grad_in = move(3, grad_ref, grad_all.at[second, left], at.ahead)
    grad_y = move(4, grad_ref, grad_all.at[first, right], at.over_y)
    grad_y_two = move(5, grad_all.at[second, left], grad_all.at[second, right], at.over_y)
    mask_move = move(6, mask_ref.at[first], mask_ref.at[second], at.ahead)
    mask_core = move(7, mask_ref.at[mine_rows], mask_ref.at[their_rows], at.core)
    one_core = move(8, one_mine, one_theirs, at.core)
    low_core = move(9, low_mine, low_theirs, at.core)
    halves = (first, second)
    part_core = [move(10 + i, part_out.at[h], part_in.at[h], at.core) for i, h in enumerate(halves)]
    part_y = [move(12 + i, y_out.at[h], y_in.at[h], at.over_y) for i, h in enumerate(halves)]
    mid_y = [
        move(14 + i, mid_ref.at[h, left], mid_ref.at[h, right], at.over_y)
        for i, h in enumerate(halves)
    ]
    two_core = [move(16 + i, two_mine.at[h], two_theirs.at[h], at.core) for i, h in enumerate(halves)]
    token_here = pltpu.make_async_copy(tokens_ref, tok_ref.at[first, left], m_local.at[0])
    grad_here = pltpu.make_async_copy(grad_ref, grad_all.at[first, left], m_local.at[1])

    def load(w, target, b):
        return pltpu.make_async_copy(whole[w].at[b], target.at[b], load_sem.at[w, b])

    def keep_out(k, source=None):
        if source is None:
            source = held[k].at[:, left] if k == 5 else held[k]
        return pltpu.make_async_copy(source, results[k], out_sem.at[k])

    def make_mask():
        place = lax.broadcasted_iota(jnp.int32, (rows, lanes), 0)
        lane = lax.broadcasted_iota(jnp.int32, (rows, lanes), 1)
        ends = [lengths_ref[0, 0]]
        for k in (1, 2):
            ends.append(ends[-1] + lengths_ref[0, k])
        start = jnp.zeros((rows, lanes), jnp.int32)
        for end in ends:
            start = jnp.where(place >= end, end, start)
        offset = place - start
        bound = jnp.where(lane == 0, 1, jnp.where(lane == 4, place + 1 - ends[2] + offset, lane))
        mask_ref[first, :] = jnp.where((offset >= bound) & (lane < 5), 1.0, 0.0)

    def make_parameters():
        width = vec_ref.shape[1]

        def quarter(ref, row):
            value = ref[row : row + 1, :]
            return jnp.where(at.c == 0, value[:, :width], value[:, width:])

        for k in range(4):
            vec_ref[k : k + 1, :] = quarter(taps_ref, k)
        for k in range(3):
            vec_ref[4 + k : 5 + k, :] = quarter(biases_ref, k)
        turned = -quarter(biases_ref, 3)
        vec_ref[7:8, :] = jnp.maximum(turned, 0.0) + jnp.log1p(jnp.exp(-jnp.abs(turned)))
        block = recur_blocks.shape[1]
        count_heads = width // block
        for source, target in ((recur_blocks, wr_ref), (input_blocks, wi_ref)):
            for h in range(count_heads):
                parts = [source[at.c * count_heads + h]]
                if h > 0:
                    parts.insert(0, jnp.zeros((block, h * block), bf16))
                if h + 1 < count_heads:
                    parts.append(jnp.zeros((block, (count_heads - 1 - h) * block), bf16))
                target[h * block : (h + 1) * block, :] = jnp.concatenate(parts, axis=1)

    at.meet()

    @pl.when(at.serves)
    def _():
        for w in (ri, ro, mi, mo):
            begin(w)
        token_in.start()
        make_mask()
        mask_move.start()
        own_block(ri, (1, 2))
        pass_on(ri, 1, 3)
        own_block(ro, (1, 2))
        pass_on(ro, 1, 3)
        own_block(mi, (1, 2))
        grad_in.start()
        pass_on(mi, 1, 3)
        own_block(mo, (1, 2))
        pass_on(mo, 1, 3)
        for w in (ri, ro, mi, mo):
            for k in (1, 2, 3):
                hop(w, k).wait_send()
        for moved in (mask_move, token_in, grad_in):
            moved.wait_send()

    def recur_part(both_ref, mixed_ref, coef_ref, w_ri, w_ro, part_sum):
        for w, target in ((ri, w_ri), (ro, w_ro)):
            hop(w, 1).wait_recv()
            for k in (5, 7, 8):
                hop(w, k).wait_recv()
            for b in range(blocks):
                load(w, target, b).start()
        for b in range(blocks):
            load(ri, w_ri, b).wait()
        one_core.wait_recv()
        mask_core.wait_recv()

        def keep_both(start, value):
            both_ref[pl.ds(start, chunk_rows), :] = value

        for k in (3, 5, 6, 7):
            keep_out(k).start()
        project(one_mine, one_theirs, lambda: stacked(w_ri), size, cols, keep_both)
        keep_out(0, both_ref).start()
        grad_in.wait_recv()
        grad_y_two.start()
        recur_state(both_ref, mask_ref, vec_ref, wr_ref, wi_ref, coef_ref, state_ref)
        keep_out(1).start()
        pass_on(mi, 2, 6)
        pass_on(mi, 4, 5)
        recur_mixed(both_ref, state_ref, mixed_ref)
        keep_out(2, mixed_ref).start()
        for b in range(blocks):
            load(ro, w_ro, b).wait()

        def branch(start, out_ref, out_at):
            for b in range(blocks):
                out_ref[out_at, columns_at(cols, b, size)] = lax.dot_general(
                    mixed_ref[pl.ds(start, rows), :],
                    w_ro[b],
                    contract_cols,
                    preferred_element_type=f32,
                ).astype(out_ref.dtype)

        for i, h in enumerate(halves):
            branch(own + i * rows, part_out, h)
            part_core[i].start()
        for i, h in enumerate(halves):
            branch(i * rows, part_sum, first)
            part_core[i].wait_recv()
            middle_ref[h, :] = part_sum[:, left] + part_in[h, left].astype(f32)
            y_out[h, :] = (part_sum[:, right] + part_in[h, right].astype(f32)).astype(bf16)
            part_y[i].start()
        keep_out(0, both_ref).wait()
        keep_out(2, mixed_ref).wait()

    def mlp_part(gate_room, up_room, act_room, slope_room, value_room):
        hidden = mlp_out_refs[0].shape[1]
        tile = act_room.shape[2]
        rooms = (act_room, slope_room, value_room)

        class Both:
            def __init__(self, t, slot):
                self.tiles = (
                    Tile(g_mi, gate_room.at[slot], tile_sem.at[slot, 0], t * tile, tile),
                    Tile(g_mi, up_room.at[slot], tile_sem.at[slot, 1], hidden + t * tile, tile),
                )

            def start(self):
                for v in self.tiles:
                    v.start()

            def wait(self):
                for v in self.tiles:
                    v.wait()

        def results_of(t, slot):
            columns = pl.ds(pl.multiple_of(t * tile, tile), tile)
            return [
                pltpu.make_async_copy(room.at[slot], out.at[:, columns], mlp_sem.at[slot, k])
                for k, (room, out) in enumerate(zip(rooms, mlp_out_refs))
            ]

        def body(t, slot):
            @pl.when(t >= 2)
            def _():
                for v in results_of(t - 2, slot):
                    v.wait()

            for part, ref in enumerate((two_mine, two_theirs)):
                row_values = gathered(ref, slice(None), cols, size)
                gate = jnp.dot(
                    row_values, tile_rows(gate_room.at[slot], tile), preferred_element_type=f32
                )
                up = jnp.dot(
                    row_values, tile_rows(up_room.at[slot], tile), preferred_element_type=f32
                )
                value, slope = gelu_parts(gate)
                row_at = pl.ds(part * own, own)
                act_room[slot, row_at, :] = (value * up).astype(bf16)
                slope_room[slot, row_at, :] = (slope * up).astype(bf16)
                value_room[slot, row_at, :] = value.astype(bf16)
            for v in results_of(t, slot):
                v.start()

        count_tiles = hidden // tile
        stream_tiles(0, 2, Both, body)
        pass_on(mo, 2, 6)
        pass_on(mo, 4, 5)
        stream_tiles(2, count_tiles, Both, body)
        pass_on(mo, 3, 7)
        pass_on(mo, 6, 8)
        for t in (count_tiles - 2, count_tiles - 1):
            for v in results_of(t, t % 2):
                v.wait()

    @pl.when(at.works)
    def _():
        begin(ri)
        begin(ro)
        token_here.start()
        token_y.start()
        grad_here.start()
        begin(mi)
        begin(mo)
        own_block(ri, (1, 4))
        own_block(ro, (1, 4))
        make_mask()
        pass_on(ri, 4, 5)
        token_in.wait_recv()
        token_y_two.start()
        pass_on(ri, 2, 6)
        pass_on(ro, 4, 5)
        token_here.wait()
        token_y.wait_recv()
        normed_rows(tok_ref, gain_ref, 0, scale_ref, 0, one_mine, 0, rows)
        token_y_two.wait_recv()
        normed_rows(tok_ref, gain_ref, 0, scale_ref, 0, one_mine, rows, rows)
        one_core.start()
        own_block(mi, (1, 4))
        make_parameters()
        keep_out(13).start()
        keep_out(14).start()
        keep_out(15).start()
        mask_move.wait_recv()
        mask_core.start()
        pass_on(ri, 3, 7)
        pass_on(ri, 6, 8)
        pass_on(ro, 2, 6)
        pass_on(ro, 3, 7)
        pass_on(ro, 6, 8)
        grad_y.start()
        width = vec_ref.shape[1]
        pl.run_scoped(
            recur_part,
            pltpu.VMEM((2 * own, 2 * width), f32),
            pltpu.VMEM((2 * own, width), bf16),
            pltpu.VMEM(state_ref.shape, f32),
            pltpu.VMEM(g_ri.shape, bf16),
            pltpu.VMEM(g_ro.shape, bf16),
            pltpu.VMEM((rows, model), f32),
        )
        grad_here.wait()
        grad_y.wait_recv()
        grad_y_two.wait_recv()
        low_mine[...] = (grad_all[...].astype(f32) * mask_ref[mine_rows, 4:5]).astype(bf16)
        low_core.start()
        keep_out(10).start()
        for i, h in enumerate(halves):
            part_y[i].wait_recv()
            middle = middle_ref[h, :] + y_in[h, :].astype(f32) + tok_ref[h, left].astype(f32)
            middle_ref[h, :] = middle
            mid_ref[h, left] = middle.astype(bf16)
            mid_y[i].start()
        keep_out(4).start()
        pass_on(mi, 3, 7)
        pass_on(mi, 6, 8)
        own_block(mo, (1, 4))
        for i, h in enumerate(halves):
            mid_y[i].wait_recv()
            normed_rows(mid_ref, gain_ref, 1, scale_ref, 1, two_mine, i * rows, rows)
            two_core[i].start()
        keep_out(8).start()
        keep_out(12).start()
        low_core.wait_recv()
        keep_out(11).start()
        for moved in two_core:
            moved.wait_recv()
        keep_out(9).start()
        for k in (1, 5, 7, 8):
            hop(mi, k).wait_recv()
        tile = 256
        pl.run_scoped(
            mlp_part,
            *[pltpu.VMEM((2, size, blocks * tile), bf16)] * 2,
            *[pltpu.VMEM((2, 2 * own, tile), bf16)] * 3,
        )
        for k in (1, 5, 7, 8):
            hop(mo, k).wait_recv()
        for w in (ri, ro, mi, mo):
            for k in (1, 4, 5, 6, 7, 8):
                hop(w, k).wait_send()
        for moved in (
            token_y, token_y_two, grad_y, grad_y_two, mask_core, one_core, low_core,
            *part_core, *part_y, *mid_y, *two_core,
        ):
            moved.wait_send()
        for k in range(16):
            if k not in (0, 2):
                keep_out(k).wait()


def recur_first(both_ref, state_ref, mask_ref, vec_ref, wr_ref, wi_ref, dmix_ref, dboth_ref, coef_ref, push_ref):
    width = dmix_ref.shape[1]
    rows = both_ref.shape[0] // held_buffers

    def first(b, carry):
        at = buffer_rows_at(b, rows)
        gate, slope = gelu_parts(both_ref[at, width:])
        d_mixed = dmix_ref[at, :]
        mask = mask_ref[at, :]
        conv_low = conv_of(both_ref[at, :width], mask, vec_ref).astype(bf16)
        rate = gates_of(conv_low, vec_ref, wr_ref, wi_ref)[0]
        store_lanes(push_ref, at, d_mixed * gate)
        dboth_ref[at, width:] = (slope * d_mixed * load_lanes(state_ref, at, width)).astype(bf16)
        store_lanes(coef_ref, at, jnp.exp(-8.0 * rate * vec_ref[7:8, :]) * mask[:, 0:1])
        return carry

    lax.fori_loop(0, held_buffers, first, 0)


def recur_last(
    both_ref, state_ref, mask_ref, vec_ref, wr_ref, wi_ref, push_ref,
    dboth_ref, sums_ref, gr_ref, gi_ref,
):
    width = both_ref.shape[1] // 2
    rows = both_ref.shape[0] // held_buffers
    sums_ref[...] = jnp.zeros_like(sums_ref)
    gr_ref[...] = jnp.zeros_like(gr_ref)
    gi_ref[...] = jnp.zeros_like(gi_ref)
    def add_sum(k, value):
        sums_ref[k : k + 1, :] += jnp.sum(value, axis=0, keepdims=True)

    def last(b, carry):
        at = buffer_rows_at(b, rows)
        inner = both_ref[at, :width]
        mask = mask_ref[at, :]
        keep = mask[:, 0:1]
        softened = vec_ref[7:8, :]
        conv = conv_of(inner, mask, vec_ref)
        conv_low = conv.astype(bf16)
        rate, igate = gates_of(conv_low, vec_ref, wr_ref, wi_ref)
        d_push = load_lanes(push_ref, at, width)
        decay = jnp.exp(-8.0 * rate * softened)
        square = 1.0 - decay * decay + root_eps
        root = jnp.sqrt(square)
        d_root = d_push * igate * conv
        d_igate = d_push * root * conv
        before = shifted(load_lanes(state_ref, at, width), 1) * keep
        d_decay = d_push * before - d_root * decay / root
        d_log = d_decay * decay
        slow = d_log * rate
        d_pre_recur = (-8.0 * softened) * slow * (1.0 - rate)
        d_pre_input = d_igate * igate * (1.0 - igate)
        add_sum(7, slow)
        add_sum(5, d_pre_recur)
        add_sum(6, d_pre_input)
        low_recur = d_pre_recur.astype(bf16)
        low_input = d_pre_input.astype(bf16)
        gr_ref[...] += lax.dot_general(
            conv_low, low_recur, contract_rows, preferred_element_type=f32
        )
        gi_ref[...] += lax.dot_general(
            conv_low, low_input, contract_rows, preferred_element_type=f32
        )
        d_conv = d_push * root * igate
        d_conv = d_conv + lax.dot_general(
            low_recur, wr_ref[...], contract_cols, preferred_element_type=f32
        )
        d_conv = d_conv + lax.dot_general(
            low_input, wi_ref[...], contract_cols, preferred_element_type=f32
        )
        add_sum(4, d_conv)
        add_sum(0, d_conv * inner)
        d_inner = vec_ref[0:1, :] * d_conv
        for k in range(1, 4):
            kept = d_conv * mask[:, k : k + 1]
            add_sum(k, kept * shifted(inner, k))
            d_inner = d_inner + vec_ref[k : k + 1, :] * shifted(kept, -k)
        dboth_ref[at, :width] = d_inner.astype(bf16)
        return carry

    lax.fori_loop(0, held_buffers, last, 0)


class Sums:
    def __init__(self, at, partial, land, total, send, recv):
        self.at, self.partial, self.land, self.total = at, partial, land, total
        self.send, self.recv = send, recv
        self.half_rows = total.shape[1]
        self.top = pl.ds(0, self.half_rows)
        self.bottom = pl.ds(self.half_rows, self.half_rows)

    def rows_of(self, c):
        return pl.ds(pl.multiple_of(c * self.half_rows, self.half_rows), self.half_rows)

    def hop(self, k, last=None):
        d, land, at, top, bottom = self.partial, self.land, self.at, self.top, self.bottom
        src, dst, where = (
            lambda: (d.at[5, top], land.at[0, top], at.beside),
            lambda: (d.at[7, bottom], land.at[1, top], at.beside),
            lambda: (d.at[7, top], land.at[1, bottom], at.ahead),
            lambda: (d.at[6, top], land.at[2, top], at.ahead),
            lambda: (land.at[1, top], land.at[2, bottom], at.ahead),
            lambda: (d.at[3, bottom], land.at[0, bottom], at.behind),
            lambda: (land.at[1, bottom], land.at[0, top], at.behind),
            lambda: (d.at[1], land.at[3], at.beside),
            lambda: (land.at[0, top], land.at[4, top], at.ahead),
            lambda: (land.at[2, bottom], land.at[2, bottom], at.behind),
            lambda: (land.at[0], land.at[3], at.beside),
            lambda: (last.at[self.rows_of(1 - at.c)], self.total.at[at.c], at.core),
            lambda: (land.at[2, top], land.at[2, top], at.behind),
            lambda: (land.at[0, bottom], land.at[4, bottom], at.ahead),
            lambda: (d.at[5, bottom], land.at[0, bottom], at.beside),
        )[k]()
        return remote(src, dst, self.send.at[k], self.recv.at[k], where)

    def start(self, *hops):
        for k in hops:
            self.hop(k).start()

    def received(self, *hops):
        for k in hops:
            self.hop(k).wait_recv()

    def sent(self, *hops):
        for k in hops:
            self.hop(k).wait_send()

    def operands(self, k):
        d, land, top, bottom = self.partial, self.land, self.top, self.bottom
        return {
            4: (land.at[1, top], d.at[6, bottom]),
            6: (land.at[1, bottom], d.at[3, top]),
            8: (land.at[0, top], d.at[4, top]),
            9: (land.at[2, bottom], d.at[2, bottom]),
            12: (land.at[2, top], d.at[2, top]),
            13: (land.at[0, bottom], d.at[4, bottom]),
        }[k]

    def arrived(self, k):
        self.received({4: 1, 6: 2, 8: 0, 9: 4, 12: 3, 13: 14}[k])

    def step(self, k, add):
        self.arrived(k)
        add(*self.operands(k))
        self.start(k)


work_hops, serve_hops = (0, 1, 2, 3, 4, 5, 6, 7, 8, 9, 12, 13, 14), (10,)


def add_rows(into, value, other=None):
    size = 32 if into.shape[0] % 32 == 0 else 16

    def chunk(i, carry):
        at = pl.ds(pl.multiple_of(i * size, size), size)
        total = into[at, :].astype(f32) + value[at, :].astype(f32)
        if other is not None:
            total = total + other[at, :].astype(f32)
        into[at, :] = total.astype(bf16)
        return carry

    lax.fori_loop(0, into.shape[0] // size, chunk, 0)


def norm_sums(e_ref, y_in, source_ref, gain_ref, gain_row, mean_ref, first, count):
    size, half = 64, e_ref.shape[1]

    def chunk(i, carry):
        at = pl.ds(pl.multiple_of(first + i * size, size), size)
        e = e_ref[at, :] + y_in[at, :].astype(f32)
        e_ref[at, :] = e
        source = source_ref[at, :half].astype(bf16).astype(f32)
        part = jnp.sum(e * gain_ref[gain_row : gain_row + 1, :half] * source, axis=1, keepdims=True)
        mean_ref[at, :] = jnp.broadcast_to(part, (size, lanes))
        return carry

    lax.fori_loop(0, count // size, chunk, 0)


def norm_rows_back(
    e_ref, source_ref, gain_ref, gain_row, scale_ref, mean_ref, mean_in, term_ref, model, first, count, use
):
    size, half = 64, e_ref.shape[1]

    def chunk(i, carry):
        at = pl.ds(pl.multiple_of(first + i * size, size), size)
        e = e_ref[at, :]
        source = source_ref[at, :half].astype(bf16).astype(f32)
        scale = scale_ref[gain_row, at, 0:1]
        inner = (mean_ref[at, 0:1] + mean_in[at, 0:1]) / model
        weighted = e * gain_ref[gain_row : gain_row + 1, :half]
        term_ref[gain_row : gain_row + 1, :] += jnp.sum(e * source * scale, axis=0, keepdims=True)
        use(at, scale * weighted - source * (scale * scale * scale * inner))
        return carry

    lax.fori_loop(0, count // size, chunk, 0)


def backward_kernel(
    count,
    weight_mi, weight_mo, act_in, slope_in, value_in, two_mine, two_theirs, low_mine, low_theirs,
    middle_in, weight_in, both_in, state_in,
    scale_ref, gain_ref, mask_ref, vec_ref, wr_ref, wi_ref,
    d_mi, d_mo, land_mi, land_mo, total_mi, total_mo, dmid_out, mine_out, theirs_out, dboth_out,
    out_ref, sums_ref, gates_ref, term_ref,
    middle_ref, dmid_ref, db_mine, db_theirs,
    part_out, part_in, o_in, y_out, y_in, oy_out, oy_in, mean_ref, mean_in, stage_a, stage_b,
    w_send, w_recv, m_send, m_recv, local_sem, load_sem, out_sem, tile_sem, keep_sem,
):
    at = Place(count)
    size = weight_mi.shape[1]
    cols = at.columns(size)
    own, half_model = middle_ref.shape
    model = 2 * half_model
    rows = own // 2
    hidden = act_in.shape[1]
    width = weight_in.shape[2]
    e_ref, low_left = dmid_ref, y_out
    mi = Sums(at, d_mi, land_mi, total_mi, w_send.at[0], w_recv.at[0])
    mo = Sums(at, d_mo, land_mo, total_mo, w_send.at[1], w_recv.at[1])
    first, second = pl.ds(0, rows), pl.ds(rows, rows)
    left, right = pl.ds(0, half_model), pl.ds(half_model, half_model)
    halves = (first, second)

    def move(k, src, dst, where):
        return remote(src, dst, m_send.at[k], m_recv.at[k], where)

    e_core = [move(i, part_out.at[h], part_in.at[h], at.core) for i, h in enumerate(halves)]
    o_core = [move(2 + i, part_out.at[h], o_in.at[h], at.core) for i, h in enumerate(halves)]
    e_y = [move(4 + i, y_out.at[h], y_in.at[h], at.over_y) for i, h in enumerate(halves)]
    o_y = [move(6 + i, oy_out.at[h], oy_in.at[h], at.over_y) for i, h in enumerate(halves)]
    mean_y = move(8, mean_ref, mean_in, at.over_y)
    db_y = [
        move(9 + i, db_mine.at[h, left], db_mine.at[h, right], at.over_y)
        for i, h in enumerate(halves)
    ]
    db_core = [move(11 + i, db_mine.at[h], db_theirs.at[h], at.core) for i, h in enumerate(halves)]
    out_move = move(13, out_ref.at[second], out_ref.at[first], at.behind)
    low_load = pltpu.make_async_copy(low_mine.at[:, left], low_left, local_sem.at[6])
    middle_load = pltpu.make_async_copy(middle_in, middle_ref, local_sem.at[7])
    keep_out = [
        pltpu.make_async_copy(src, dst, out_sem.at[k])
        for k, (src, dst) in enumerate(
            ((dmid_ref, dmid_out), (db_mine, mine_out), (db_theirs, theirs_out))
        )
    ]

    def fetch(src, dst, k):
        return pltpu.make_async_copy(src, dst, local_sem.at[k])

    def staged(w, k):
        into, value = w.operands(k)
        count_rows, wide = into.shape
        low = k in (6, 9, 13)
        at_rows = pl.ds(count_rows, count_rows) if low else pl.ds(0, count_rows)
        place = 3 if low else 0
        a = stage_a.at[at_rows, pl.ds(0, wide)]
        b = stage_b.at[at_rows, pl.ds(0, wide)]
        return a, b, fetch(into, a, place), fetch(value, b, place + 1), fetch(a, into, place + 2)

    def begin(w, *hops):
        for k in hops:
            w.arrived(k)
            _, _, load_a, load_b, _ = staged(w, k)
            load_a.start()
            load_b.start()

    def combine(w, *hops):
        for k in hops:
            a, b, load_a, load_b, back = staged(w, k)
            load_a.wait()
            load_b.wait()
            add_rows(a, b)
            back.start()

    def send_on(w, *hops):
        for k in hops:
            staged(w, k)[4].wait()
            w.start(k)

    def finish(w, parts, last_hop=None):
        count_rows, wide = parts[0].shape
        a = stage_a.at[pl.ds(0, count_rows), pl.ds(0, wide)]
        b = stage_b.at[pl.ds(0, count_rows), pl.ds(0, wide)]
        loads = fetch(parts[0], a, 0), fetch(parts[1], b, 1)
        for v in loads:
            v.start()
        for v in loads:
            v.wait()
        add_rows(a, b)
        if len(parts) == 3:
            w.received(*last_hop)
            third = fetch(parts[2], b, 1)
            third.start()
            third.wait()
            add_rows(a, b)
        w.hop(11, a).start()
        kept = fetch(a.at[w.rows_of(at.c)], w.total.at[at.c], 2)
        kept.start()
        kept.wait()
        w.hop(11, a).wait()

    at.meet()

    @pl.when(at.serves)
    def _():
        for w in (mo, mi):
            w.received(5, 6)
            w.start(10)
        for w in (mo, mi):
            w.received(9, 12, 10)
            finish(w, (w.land.at[2], w.land.at[3]))
        out_move.wait_recv()
        for w in (mo, mi):
            w.sent(*serve_hops)

    block_order = (
        (7, (1, 2)), (5, (0, 14)), (6, (3,)), (3, (5,)), (1, (7,)), (4, ()), (2, ()), (0, ()),
    )

    def partial_blocks(w, lhs, column_ref, room, between=()):
        wide = column_ref.shape[1]
        between = dict(between)

        def write(i):
            return pltpu.make_async_copy(
                room.at[i % 2, :, pl.ds(0, wide)], w.partial.at[block_order[i][0]], keep_sem.at[i % 2]
            )

        def leave(i):
            write(i).wait()
            w.start(*block_order[i][1])

        for i in range(blocks):
            if i >= 2:
                leave(i - 2)
            here = columns_at(cols, block_order[i][0], size)
            rows_here = jnp.concatenate([lhs[0, :, here], lhs[1, :, here]], axis=0)
            room[i % 2, :, :wide] = lax.dot_general(
                rows_here, column_ref[...], contract_rows, preferred_element_type=f32
            ).astype(bf16)
            write(i).start()
            if i in between:
                between[i]()
        leave(blocks - 2)
        leave(blocks - 1)

    def rows_product(weight, row_ref, room, wide, theirs_out, mine_out, between=()):
        between = dict(between)

        def block(b):
            return pltpu.make_async_copy(
                weight.at[b], room.at[b % 2, :, pl.ds(0, wide)], tile_sem.at[b % 2, 0]
            )

        block(0).start()
        for b in range(blocks):
            if b + 1 < blocks:
                block(b + 1).start()
            block(b).wait()
            here = columns_at(cols, b, size)
            for which, out in ((1, theirs_out), (0, mine_out)):
                out[:, here] = lax.dot_general(
                    row_ref[which * own : (which + 1) * own, :],
                    room[b % 2, :, :wide],
                    contract_cols,
                    preferred_element_type=f32,
                ).astype(out.dtype)
            if b in between:
                between[b]()

    def settle(w):
        w.received(7)
        finish(w, (w.partial.at[0], w.land.at[3], w.land.at[4]), (8, 13))

    def join(i, h, mine_ref, arrived, landed, keep_value, sent_ref, over):
        arrived[i].wait_recv()
        keep_value(h, mine_ref[h, left] + landed[h, left].astype(f32))
        sent_ref[h, :] = (mine_ref[h, right] + landed[h, right].astype(f32)).astype(bf16)
        over[i].start()

    def mlp_part(lhs, act_ref, pair_ref, room, mine_ref):
        lhs_low = fetch(low_mine, lhs.at[0], 8), fetch(low_theirs, lhs.at[1], 9)
        lhs_two = fetch(two_mine, lhs.at[0], 8), fetch(two_theirs, lhs.at[1], 9)
        act_load = pltpu.make_async_copy(act_in, act_ref, load_sem.at[0])
        pair_load = [
            pltpu.make_async_copy(src, pair_ref.at[:, pl.ds(k * hidden, hidden)], load_sem.at[1 + k])
            for k, src in enumerate((slope_in, value_in))
        ]
        for v in (*lhs_low, act_load, *pair_load):
            v.start()
        middle_load.start()
        for v in (*lhs_low, act_load):
            v.wait()
        partial_blocks(mo, lhs, act_ref, room)
        for v in pair_load:
            v.wait()
        tile = 256

        def back(t, slot):
            gate_at = pl.ds(pl.multiple_of(t * tile, tile), tile)
            up_at = pl.ds(pl.multiple_of(hidden + t * tile, tile), tile)

            def use(start, d_act):
                row_at = pl.ds(start, chunk_rows)
                for where in (gate_at, up_at):
                    pair_ref[row_at, where] = (d_act * pair_ref[row_at, where].astype(f32)).astype(bf16)

            project(
                lhs.at[0], lhs.at[1], lambda: tile_rows(room.at[slot], tile), size, cols, use
            )

        stream_tiles(
            0,
            hidden // tile,
            lambda t, slot: Tile(weight_mo, room.at[slot], tile_sem.at[slot], t * tile, tile),
            back,
        )
        for v in lhs_two:
            v.start()
        begin(mo, 4, 6)
        rows_product(
            weight_mi,
            pair_ref,
            room,
            2 * hidden,
            part_out,
            mine_ref,
            (
                (1, lambda: combine(mo, 4, 6)),
                (2, lambda: send_on(mo, 4, 6)),
                (4, lambda: begin(mo, 8, 13)),
                (6, lambda: combine(mo, 8, 13)),
            ),
        )
        for moved in e_core:
            moved.start()
        send_on(mo, 8, 13)

        def keep_e(h, value):
            e_ref[h, :] = value

        for i, h in enumerate(halves):
            join(i, h, mine_ref, e_core, part_in, keep_e, y_out, e_y)
        for v in lhs_two:
            v.wait()
        partial_blocks(
            mi,
            lhs,
            pair_ref,
            room,
            (
                (2, lambda: begin(mo, 12, 9)),
                (4, lambda: combine(mo, 12, 9)),
                (5, lambda: send_on(mo, 12, 9)),
            ),
        )
        settle(mo)
        middle_load.wait()
        for i, h in enumerate(halves):
            e_y[i].wait_recv()
            norm_sums(e_ref, y_in, middle_ref, gain_ref, 1, mean_ref, i * rows, rows)
        mean_y.start()
        for moved in e_y:
            moved.wait_send()
        low_load.start()
        for moved in e_core:
            moved.wait_send()
        low_load.wait()
        mean_y.wait_recv()

        def keep(row_at, value):
            d_middle = value + low_left[row_at, :].astype(f32)
            dmid_ref[row_at, :] = d_middle
            db_mine[row_at, left] = d_middle.astype(bf16)

        for i in range(2):
            norm_rows_back(
                e_ref, middle_ref, gain_ref, 1, scale_ref, mean_ref, mean_in, term_ref, model,
                i * rows, rows, keep,
            )
            db_y[i].start()
        begin(mi, 4, 6)
        rows_product(
            weight_mo,
            act_ref,
            room,
            hidden,
            part_out,
            mine_ref,
            (
                (1, lambda: combine(mi, 4, 6)),
                (2, lambda: send_on(mi, 4, 6)),
                (3, lambda: begin(mi, 12)),
                (4, lambda: combine(mi, 12)),
                (5, lambda: (send_on(mi, 12), begin(mi, 8))),
                (6, lambda: combine(mi, 8)),
                (7, lambda: send_on(mi, 8)),
            ),
        )
        for moved in o_core:
            moved.start()

        def keep_o(h, value):
            middle_ref[h, :] = middle_ref[h, :] + value

        for i in range(2):
            db_y[i].wait_recv()
            db_core[i].start()
        for i, h in enumerate(halves):
            join(i, h, mine_ref, o_core, o_in, keep_o, oy_out, o_y)

    def recur_part(w_ro, both_ref, state_ref, dboth_ref, coef_ref, push_ref, dmix_ref, gr_ref, gi_ref):
        loads = [
            pltpu.make_async_copy(src, dst, load_sem.at[k])
            for k, (src, dst) in enumerate(
                ((weight_in, w_ro), (both_in, both_ref), (state_in, state_ref))
            )
        ]
        for v in loads:
            v.start()
        begin(mi, 9)
        for i in range(2):
            db_core[i].wait_recv()
        for v in keep_out:
            v.start()
        combine(mi, 9)
        for v in loads:
            v.wait()
        send_on(mi, 9)
        begin(mi, 13)

        def keep_mixed(start, value):
            dmix_ref[pl.ds(start, chunk_rows), :] = value

        project(db_mine, db_theirs, lambda: stacked(w_ro), size, cols, keep_mixed)
        combine(mi, 13)
        send_on(mi, 13)
        recur_first(
            both_ref, state_ref, mask_ref, vec_ref, wr_ref, wi_ref, dmix_ref, dboth_ref, coef_ref, push_ref
        )
        for i, h in enumerate(halves):
            o_y[i].wait_recv()
            out_ref[h, :] = (
                mask_ref[h, 4:5] * (middle_ref[h, :] + oy_in[h, :].astype(f32))
            ).astype(bf16)
        out_move.start()
        scan_rows(coef_ref, push_ref, both_ref.shape[0] // held_buffers, True)
        recur_last(
            both_ref, state_ref, mask_ref, vec_ref, wr_ref, wi_ref, push_ref,
            dboth_ref, sums_ref, gr_ref, gi_ref,
        )
        keep_both = pltpu.make_async_copy(dboth_ref, dboth_out, out_sem.at[3])
        keep_both.start()
        block = gates_ref.shape[0]
        packed = [
            ref[h * block : (h + 1) * block, h * block : (h + 1) * block].astype(bf16)
            for ref in (gr_ref, gi_ref)
            for h in range(width // block)
        ]
        gates_ref[...] = jnp.concatenate(packed, axis=1)
        keep_both.wait()

    @pl.when(at.works)
    def _():
        term_ref[...] = jnp.zeros_like(term_ref)
        pl.run_scoped(
            mlp_part,
            pltpu.VMEM((2, own, model), bf16),
            pltpu.VMEM((2 * own, hidden), bf16),
            pltpu.VMEM((2 * own, 2 * hidden), bf16),
            pltpu.VMEM((2, size, 2 * hidden), bf16),
            pltpu.VMEM((own, model), f32),
        )
        pl.run_scoped(
            recur_part,
            pltpu.VMEM((blocks, size, width), bf16),
            pltpu.VMEM(both_in.shape, f32),
            pltpu.VMEM(state_in.shape, f32),
            pltpu.VMEM(dboth_out.shape, bf16),
            pltpu.VMEM(state_in.shape, f32),
            pltpu.VMEM(state_in.shape, f32),
            pltpu.VMEM((2 * own, width), f32),
            pltpu.VMEM((width, width), f32),
            pltpu.VMEM((width, width), f32),
        )
        settle(mi)
        for w in (mo, mi):
            w.sent(*work_hops)
        for v in keep_out:
            v.wait()
        for moved in (*o_core, *o_y, mean_y, *db_y, *db_core, out_move):
            moved.wait_send()


def finish_kernel(
    count,
    *refs,
):
    sources, refs = refs[:9], refs[9:]
    (
        scale_ref, gain_ref, sums_ref, gates_ref, term_in,
        total_r, out_ref, recur_out, input_out, sums_out, term_out,
    ) = refs[:11]
    refs = refs[11:]
    one_mine, one_theirs, db_mine, db_theirs, dboth_ref, mixed_ref, w_ri, tok_left, dmid_ref = refs[:9]
    (
        d_r, land_r, part_out, part_in, part_sum, y_out, y_in, e_ref,
        mean_ref, mean_in, last_r, gates_in, gates_out, sums_in, term_ref, term_land,
        w_send, w_recv, m_send, m_recv, load_sem,
    ) = refs[9:]
    at = Place(count)
    size = w_ri.shape[1]
    cols = at.columns(size)
    own, half_model = dmid_ref.shape
    model = 2 * half_model
    rows = own // 2
    pair_width = dboth_ref.shape[1]
    w = Sums(at, d_r, land_r, total_r, w_send, w_recv)
    first, second = pl.ds(0, rows), pl.ds(rows, rows)
    left, right = pl.ds(0, half_model), pl.ds(half_model, half_model)
    halves = (first, second)

    def move(k, src, dst, where):
        return remote(src, dst, m_send.at[k], m_recv.at[k], where)

    e_core = [move(i, part_out.at[h], part_in.at[h], at.core) for i, h in enumerate(halves)]
    e_y = [move(2 + i, y_out.at[h], y_in.at[h], at.over_y) for i, h in enumerate(halves)]
    mean_y = move(4, mean_ref, mean_in, at.over_y)
    out_move = move(5, out_ref.at[second], out_ref.at[first], at.behind)
    gates_x = move(6, gates_ref, gates_in.at[0], at.beside)
    gates_z = move(7, gates_in.at[0], gates_in.at[1], at.ahead)
    gates_end = move(8, gates_out.at[0], gates_out.at[0], at.behind)
    gates_core = move(9, gates_out.at[0], gates_out.at[1], at.core)
    sums_x = move(10, sums_ref, sums_in.at[0], at.beside)
    sums_z = move(11, sums_in.at[0], sums_in.at[1], at.ahead)
    sums_end = move(12, sums_out.at[0], sums_out.at[0], at.behind)
    sums_core = move(13, sums_out.at[0], sums_out.at[1], at.core)
    term_x = move(14, term_ref, term_land.at[0], at.beside)
    term_z = move(15, term_land.at[0], term_land.at[1], at.ahead)
    term_core = move(16, term_land.at[1], term_land.at[2], at.core)
    term_end = move(17, term_out, term_out, at.behind)
    loads = [
        pltpu.make_async_copy(src, dst, load_sem.at[k]) for k, (src, dst) in enumerate(zip(sources, refs))
    ]

    def add(into, value):
        add_rows(into, value)

    def finish(parts, last_hop=None):
        last_r[...] = parts[0][...]
        add_rows(last_r, parts[1])
        if len(parts) == 3:
            w.received(*last_hop)
            add_rows(last_r, parts[2])
        w.hop(11, last_r).start()
        w.total[at.c] = last_r[w.rows_of(at.c), :]

    def unpack(place, quarter):
        block = recur_out.shape[1]
        count_heads = recur_out.shape[0] // 2
        for k, out in enumerate((recur_out, input_out)):
            for h in range(count_heads):
                start = (k * count_heads + h) * block
                out[quarter * count_heads + h] = gates_out[place, :, start : start + block].astype(f32)

    at.meet()

    @pl.when(at.serves)
    def _():
        sums_end.wait_recv()
        sums_core.start()
        w.received(5, 6)
        w.start(10)
        gates_end.wait_recv()
        gates_core.start()
        w.received(9, 12, 10)
        finish((w.land.at[2], w.land.at[3]))
        w.hop(11, last_r).wait()
        w.sent(*serve_hops)
        out_move.wait_recv()
        term_end.wait_recv()
        sums_core.wait()
        unpack(0, at.c)
        gates_core.wait()
        unpack(1, 1 - at.c)

    @pl.when(at.works)
    def _():
        gates_x.start()
        sums_x.start()
        for k in (4, 0, 1, 5, 2, 3, 6, 7, 8):
            loads[k].start()
        for k in (4, 0, 1, 5, 2, 3):
            loads[k].wait()

        def partial(b):
            here = columns_at(cols, b, size)

            def product(mine_ref, theirs_ref, column_ref):
                total = lax.dot_general(
                    mine_ref[:, here], column_ref[:own, :], contract_rows, preferred_element_type=f32
                )
                total = total + lax.dot_general(
                    theirs_ref[:, here], column_ref[own:, :], contract_rows, preferred_element_type=f32
                )
                return total.astype(bf16)

            d_r[b, :, :pair_width] = product(one_mine, one_theirs, dboth_ref)
            d_r[b, :, pair_width:] = product(db_mine, db_theirs, mixed_ref)

        for b, hops in ((7, (1, 2)), (3, (5,)), (5, (0, 14))):
            partial(b)
            w.start(*hops)
        sums_x.wait_recv()
        sums_in[0] = sums_in[0] + sums_ref[...]
        sums_z.start()
        gates_x.wait_recv()
        add_rows(gates_in.at[0], gates_ref)
        gates_z.start()
        for b, hops in ((6, (3,)),):
            partial(b)
            w.start(*hops)

        def back(start, out, out_at):
            for b in range(blocks):
                out[out_at, columns_at(cols, b, size)] = lax.dot_general(
                    dboth_ref[pl.ds(start, rows), :], w_ri[b], contract_cols, preferred_element_type=f32
                ).astype(out.dtype)

        loads[6].wait()
        for i, h in enumerate(halves):
            back(own + i * rows, part_out, h)
            e_core[i].start()
        w.step(4, add)
        w.step(6, add)
        for b in (4, 1):
            partial(b)
        for i, h in enumerate(halves):
            back(i * rows, part_sum, first)
            e_core[i].wait_recv()
            e_ref[h, :] = part_sum[:, left] + part_in[h, left].astype(f32)
            y_out[h, :] = (part_sum[:, right] + part_in[h, right].astype(f32)).astype(bf16)
            e_y[i].start()
        sums_z.wait_recv()
        sums_out[0] = sums_in[0] + sums_in[1]
        sums_end.start()
        sums_core.start()
        gates_z.wait_recv()
        gates_out[0] = gates_in[0]
        add_rows(gates_out.at[0], gates_in.at[1])
        gates_end.start()
        gates_core.start()
        w.step(8, add)
        w.step(13, add)
        w.start(7)
        for b in (2, 0):
            partial(b)
        w.step(12, add)
        w.step(9, add)
        term_ref[...] = term_in[...]
        for k in (7, 8):
            loads[k].wait()
        for i in range(2):
            e_y[i].wait_recv()
            norm_sums(e_ref, y_in, tok_left, gain_ref, 0, mean_ref, i * rows, rows)
        mean_y.start()
        unpack(0, at.c)
        mean_y.wait_recv()

        def keep(row_at, value):
            out_ref[row_at, :] = (value + dmid_ref[row_at, :]).astype(bf16)

        for i in (1, 0):
            norm_rows_back(
                e_ref, tok_left, gain_ref, 0, scale_ref, mean_ref, mean_in, term_ref, model,
                i * rows, rows, keep,
            )
            if i == 1:
                out_move.start()
        term_x.start()
        term_x.wait_recv()
        term_land[0] = term_land[0] + term_ref[...]
        term_z.start()
        w.received(7)
        finish((w.partial.at[0], w.land.at[3], w.land.at[4]), (8, 13))
        term_z.wait_recv()
        term_land[1] = term_land[0] + term_land[1]
        term_core.start()
        term_core.wait_recv()
        term_out[...] = term_land[1] + term_land[2]
        term_end.start()
        w.hop(11, last_r).wait()
        w.sent(*work_hops)
        sums_core.wait_recv()
        gates_core.wait_recv()
        unpack(1, 1 - at.c)
        for moved in (
            *e_core, *e_y, mean_y, out_move, gates_x, gates_z, gates_end, gates_core,
            sums_x, sums_z, sums_end, sums_core, term_x, term_z, term_core, term_end,
        ):
            moved.wait_send()


in_vmem = pl.BlockSpec(memory_space=pltpu.VMEM)
in_smem = pl.BlockSpec(memory_space=pltpu.SMEM)
in_any = pl.BlockSpec(memory_space=pl.ANY)
no_cost = pl.CostEstimate(flops=0, bytes_accessed=0, transcendentals=0)
kernel_params = pltpu.CompilerParams(vmem_limit_bytes=60 * 2**20)
copy_sem = pltpu.SemaphoreType.DMA


def lane_shape(rows, width):
    return (pl.cdiv(width, lanes), rows, lanes)


def run_forward(count, splits, tokens, out_grad, lengths, gains, taps, biases, recur_blocks, input_blocks):
    rows, half_model = tokens.shape
    own, model, width = 2 * rows, 2 * half_model, taps.shape[1] // 2
    size = 2 * splits[0].shape[1]
    columns = [v.shape[2] for v in splits[:3]] + [splits[3].shape[1] // 2]
    shape = jax.ShapeDtypeStruct
    gathered_shapes = [shape((blocks, size, n), bf16) for n in columns]
    wide = shape((own, model), bf16)
    kept = [
        shape((2 * own, 2 * width), f32),
        shape(lane_shape(2 * own, width), f32),
        shape((2 * own, width), bf16),
        shape((2 * own, lanes), f32),
        shape((own, half_model), f32),
        shape((own, half_model), bf16),
        *[wide] * 6,
        shape((2, own, lanes), f32),
        shape((8, width), f32),
        shape((width, width), bf16),
        shape((width, width), bf16),
    ]
    hidden = shape((2 * own, columns[3]), bf16)
    return pl.pallas_call(
        functools.partial(forward_kernel, count),
        out_shape=(*gathered_shapes, *kept, *[hidden] * 3),
        in_specs=[in_any] * 6 + [in_smem] + [in_vmem] * 5,
        out_specs=[in_any] * 23,
        scratch_shapes=[
            *[
                pltpu.VMEM(wide.shape if i == 5 else v.shape, v.dtype)
                for i, v in enumerate(kept)
                if i not in (0, 2)
            ],
            pltpu.VMEM((own, model), bf16),
            pltpu.VMEM((own, model), bf16),
            pltpu.VMEM((own, model), bf16),
            pltpu.VMEM((own, half_model), bf16),
            pltpu.VMEM((own, half_model), bf16),
            pltpu.VMEM((own, model), bf16),
            copy_sem((4, 9)),
            copy_sem((4, 9)),
            copy_sem((4,)),
            copy_sem((2, blocks)),
            copy_sem((18,)),
            copy_sem((18,)),
            copy_sem((2,)),
            copy_sem((16,)),
            copy_sem((2, 2, blocks)),
            copy_sem((2, 3)),
        ],
        compiler_params=comm_params(0),
        cost_estimate=no_cost,
        name="gather_and_recur",
    )(*splits, tokens, out_grad, lengths, gains, taps, biases, recur_blocks, input_blocks)


def comm_params(collective):
    return pltpu.CompilerParams(
        vmem_limit_bytes=255 * 2**18, collective_id=collective, has_side_effects=True
    )


def run_backward(
    count, weights, mlp_kept, normed_two, grad_low, middle, weight, both, state,
    scales, gains, mask, vectors, wr, wi, block,
):
    own, half_model = middle.shape
    model, width, rows = 2 * half_model, wr.shape[0], own // 2
    size = weight.shape[1]
    shape = jax.ShapeDtypeStruct
    hidden = [v.shape[2] for v in weights]
    wide = shape((own, model), bf16)
    kept = (shape((own, half_model), f32), wide, wide)
    return pl.pallas_call(
        functools.partial(backward_kernel, count),
        out_shape=(
            *[shape(v.shape, bf16) for v in weights],
            *[shape((5, size, n), bf16) for n in hidden],
            *[shape((2, size // 2, n), bf16) for n in hidden],
            *kept,
            shape((2 * own, 2 * width), bf16),
            shape((own, half_model), bf16),
            shape((8, width), f32),
            shape((block, 2 * width), bf16),
            shape((8, half_model), f32),
        ),
        in_specs=[in_any] * 13 + [in_vmem] * 6,
        out_specs=[in_any] * 10 + [in_vmem] * 4,
        scratch_shapes=[
            pltpu.VMEM((own, half_model), f32),
            *[pltpu.VMEM(v.shape, v.dtype) for v in kept],
            *[pltpu.VMEM((own, model), bf16)] * 3,
            *[pltpu.VMEM((own, half_model), bf16)] * 4,
            pltpu.VMEM((own, lanes), f32),
            pltpu.VMEM((own, lanes), f32),
            pltpu.VMEM((size, max(hidden)), bf16),
            pltpu.VMEM((size, max(hidden)), bf16),
            copy_sem((2, 15)),
            copy_sem((2, 15)),
            copy_sem((14,)),
            copy_sem((14,)),
            copy_sem((10,)),
            copy_sem((4,)),
            copy_sem((4,)),
            copy_sem((2, blocks)),
            copy_sem((2,)),
        ],
        compiler_params=comm_params(1),
        cost_estimate=no_cost,
        name="sum_and_back",
    )(
        *weights, *mlp_kept, *normed_two, *grad_low, middle, weight, both, state,
        scales, gains, mask, vectors, wr, wi,
    )


def run_finish(
    count, normed, d_branch, d_both, mixed, weight, tokens, d_middle, scales, gains, sums, gates, term
):
    own, half_model = d_middle.shape
    model, rows = 2 * half_model, own // 2
    size = weight.shape[1]
    width = weight.shape[2] + mixed.shape[1]
    shape = jax.ShapeDtypeStruct
    held = (*normed, *d_branch, d_both, mixed, weight, tokens, d_middle)
    block = gates.shape[0]
    square = shape((gates.shape[1] // block, block, block), f32)
    return pl.pallas_call(
        functools.partial(finish_kernel, count),
        out_shape=(
            shape((2, size // 2, width), bf16),
            shape((own, half_model), bf16),
            square,
            square,
            shape((2, *sums.shape), f32),
            shape(term.shape, f32),
        ),
        in_specs=[in_any] * 9 + [in_vmem] * 5,
        out_specs=[in_vmem] * 6,
        scratch_shapes=[
            *[pltpu.VMEM(v.shape, v.dtype) for v in held],
            pltpu.VMEM((blocks, size, width), bf16),
            pltpu.VMEM((5, size, width), bf16),
            pltpu.VMEM((own, model), bf16),
            pltpu.VMEM((own, model), bf16),
            pltpu.VMEM((rows, model), f32),
            pltpu.VMEM((own, half_model), bf16),
            pltpu.VMEM((own, half_model), bf16),
            pltpu.VMEM((own, half_model), f32),
            pltpu.VMEM((own, lanes), f32),
            pltpu.VMEM((own, lanes), f32),
            pltpu.VMEM((size, width), bf16),
            pltpu.VMEM((2, *gates.shape), bf16),
            pltpu.VMEM((2, *gates.shape), bf16),
            pltpu.VMEM((2, *sums.shape), f32),
            pltpu.VMEM(term.shape, f32),
            pltpu.VMEM((3, *term.shape), f32),
            copy_sem((15,)),
            copy_sem((15,)),
            copy_sem((18,)),
            copy_sem((18,)),
            copy_sem((9,)),
        ],
        compiler_params=comm_params(2),
        cost_estimate=no_cost,
        name="sum_and_finish",
    )(*held, scales, gains, sums, gates, term)


def local(
    n_dp,
    tokens,
    gain_rnn,
    rnn_in,
    gate_recur,
    gate_input,
    bias_recur,
    bias_input,
    decay_param,
    conv_weight,
    conv_bias,
    rnn_out,
    gain_mlp,
    mlp_in,
    mlp_out,
    lengths,
    out_grad,
):
    outer_count = n_dp // 16
    rows_here = rnn_in.shape[0]
    model = gain_rnn.shape[0]
    half_model = model // 2
    buffer_rows = tokens.shape[0]
    own_rows = 2 * buffer_rows
    index = lax.axis_index("dp")
    y = lax.axis_index("mp")
    c = index // outer_count % 2
    x = index // (2 * outer_count) % 2
    z = index // (4 * outer_count)
    outer = jnp.where(z < 2, 0, 3)
    far = 3 - z
    far_outer = 3 - outer

    def pick_c(first, second):
        return jnp.where(c == 0, first, second)

    def pick_y(first, second):
        return jnp.where(y == 0, first, second)

    group_rows = outer_count * rows_here
    block_rows = 2 * group_rows

    outer_groups = [[i * outer_count + w for w in range(outer_count)] for i in range(16)]

    def over_outer(value):
        if outer_count == 1:
            return value
        return lax.all_gather(value, "dp", axis_index_groups=outer_groups, axis=1, tiled=True)

    cols = jnp.stack(
        [
            ((at_z + 2 * y) % 4 * 2 + at_x) * block_rows
            for at_z in (z, outer, far, far_outer)
            for at_x in (x, 1 - x)
        ]
    ).astype(jnp.int32)

    def settle_grad(total):
        total = total.astype(f32)
        if outer_count > 1:
            total = lax.psum_scatter(
                total, "dp", axis_index_groups=outer_groups, scatter_dimension=1, tiled=True
            )
        return total

    def joined_pair(total):
        total = settle_grad(total)
        columns = total.shape[2] // 2
        return jnp.stack(
            [
                jnp.concatenate(
                    [total[q, :, k * columns : (k + 1) * columns] for q in range(2)], axis=1
                )
                for k in range(2)
            ],
            axis=1,
        )

    def joined_out(total):
        total = settle_grad(total)
        return jnp.concatenate([total[0], total[1]], axis=1)

    def over_groups(value):
        return lax.psum(value, "dp", axis_index_groups=outer_groups) if outer_count > 1 else value

    def relative(vector):
        first, second = vector[:half_model], vector[half_model:]
        return jnp.concatenate([pick_y(first, second), pick_y(second, first)])

    def quarters(value, axis):
        size = value.shape[axis] // 2
        return (
            lax.slice_in_dim(value, 0, size, axis=axis),
            lax.slice_in_dim(value, size, 2 * size, axis=axis),
        )

    def quarter(value, axis=0):
        return pick_c(*quarters(value, axis))

    gain_one, gain_two = relative(gain_rnn.astype(f32)), relative(gain_mlp.astype(f32))
    def split_pair(weight):
        row_count, _, columns = weight.shape
        parts = weight.reshape(row_count, 2, 2, columns // 2).transpose(2, 0, 1, 3)
        return over_outer(parts.reshape(2, row_count, columns))

    def split_out(weight):
        row_count, columns = weight.shape
        return over_outer(weight.reshape(row_count, 2, columns // 2).swapaxes(0, 1))

    def split_none(weight):
        if outer_count == 1:
            return weight
        return lax.all_gather(weight, "dp", axis_index_groups=outer_groups, axis=0, tiled=True)

    splits = (split_pair(rnn_in), split_out(rnn_out), split_pair(mlp_in), split_none(mlp_out))
    biases = jnp.stack([conv_bias, bias_recur, bias_input, decay_param])
    gains = jnp.stack([gain_one, gain_two])
    (
        rnn_in_all, rnn_out_all, mlp_in_all, mlp_out_all,
        both, state, mixed, mask, middle, tokens_all,
        *rows_kept, scales, vectors, wr, wi, act, gate_slope, gate_value,
    ) = run_forward(
        outer_count, splits, tokens, out_grad, lengths, gains, conv_weight, biases, gate_recur, gate_input
    )
    normed, normed_two, grad_low = rows_kept[0:2], rows_kept[2:4], rows_kept[4:6]

    (
        _, _, _, _, mlp_in_total, mlp_out_total, d_middle, d_branch, d_branch_theirs, d_both,
        output_two, sums, gates, term,
    ) = run_backward(
        outer_count,
        (mlp_in_all, mlp_out_all),
        (act, gate_slope, gate_value),
        normed_two,
        grad_low,
        middle,
        rnn_out_all,
        both,
        state,
        scales,
        gains,
        mask,
        vectors,
        wr,
        wi,
        gate_recur.shape[1],
    )
    rnn_total, tokens_grad_two, recur_grad, input_grad, sums, term = run_finish(
        outer_count,
        normed,
        (d_branch, d_branch_theirs),
        d_both,
        mixed,
        rnn_in_all,
        tokens_all,
        d_middle,
        scales,
        gains,
        sums,
        gates,
        term,
    )
    rnn_width = rnn_in.shape[2]
    rnn_in_total, rnn_out_total = rnn_total[:, :, :rnn_width], rnn_total[:, :, rnn_width:]
    layer_output, tokens_grad = output_two[:buffer_rows], tokens_grad_two[:buffer_rows]
    def both_quarters(pair, axis):
        return over_groups(
            pick_c(
                jnp.concatenate([pair[0], pair[1]], axis=axis),
                jnp.concatenate([pair[1], pair[0]], axis=axis),
            )
        )

    sums = both_quarters(sums, 1)
    recur_grad, input_grad = over_groups(recur_grad), over_groups(input_grad)
    gains_grad = over_groups(term[:2])

    return (
        layer_output,
        tokens_grad,
        gains_grad[0],
        joined_pair(rnn_in_total),
        recur_grad,
        input_grad,
        sums[5],
        sums[6],
        8.0 * jax.nn.sigmoid(-decay_param) * sums[7],
        sums[:4],
        sums[4],
        joined_out(rnn_out_total),
        gains_grad[1],
        joined_pair(mlp_in_total),
        joined_out(mlp_out_total),
    )


def solution(mesh):
    return jax.shard_map(
        functools.partial(local, mesh.shape["dp"]),
        mesh=mesh,
        in_specs=(
            P("dp", "mp"),
            P(),
            P("dp", None, "mp"),
            P("mp", None, None),
            P("mp", None, None),
            P("mp"),
            P("mp"),
            P("mp"),
            P(None, "mp"),
            P("mp"),
            P("dp", "mp"),
            P(),
            P("dp", None, "mp"),
            P("dp", "mp"),
            P("dp", None),
            P("dp", "mp"),
        ),
        out_specs=(
            P("dp", "mp"),
            P("dp", "mp"),
            P("mp"),
            P("dp", None, "mp"),
            P("mp", None, None),
            P("mp", None, None),
            P("mp"),
            P("mp"),
            P("mp"),
            P(None, "mp"),
            P("mp"),
            P("dp", "mp"),
            P("mp"),
            P("dp", None, "mp"),
            P("dp", "mp"),
        ),
        check_vma=False,
    )
```
